32 devices in a mesh: shard: 2 (over x), heads: 4 (over y, core), tensor: 4 (over z).
Axes of the slice: x: 2, y: 2, z: 4, core: 2. Of those that a mesh axis runs over, the one named last changes fastest.
Arguments:
- tokens: bfloat16 [12608, 768], P(('shard', 'heads', 'tensor')), may hold values from -6 to 6
- ln1_gain: bfloat16 [768], P('shard'), may hold values from 0.5 to 1.5
- ln1_bias: bfloat16 [768], P('shard'), may hold values from -2 to 2
- qkv_weight: bfloat16 [768, 2304], P('shard'), may hold values from -0.21875 to 0.21875
- out_weight: bfloat16 [768, 768], P('shard'), may hold values from -1.75 to 1.75
- ln2_gain: bfloat16 [768], P('shard'), may hold values from 0.5 to 1.5
- ln2_bias: bfloat16 [768], P('shard'), may hold values from -2 to 2
- router_weight: bfloat16 [768, 8], P('shard'), may hold values from -0.109375 to 0.109375
- expert_in: bfloat16 [8, 768, 3072], P(None, 'shard', 'tensor'), may hold values from -0.21875 to 0.21875
- expert_out: bfloat16 [8, 3072, 768], P(None, 'tensor', 'shard'), may hold values from -0.4375 to 0.4375
- route_noise: float32 [12608, 8], P(('shard', 'heads', 'tensor')), may hold values from -3 to 3
- expert_ids: int32 [12608, 2], P(('shard', 'heads', 'tensor')), may hold values from 0 to 7, all different within a row
- cotangent: bfloat16 [12608, 768], P(('shard', 'heads', 'tensor')), may hold values from -6 to 6
Outputs:
- mixed: bfloat16 [12608, 768], P(('shard', 'heads', 'tensor'))
- grad_tokens: bfloat16 [12608, 768], P(('shard', 'heads', 'tensor'))
- grad_ln1_gain: float32 [768], P('shard')
- grad_ln1_bias: float32 [768], P('shard')
- grad_qkv_weight: float32 [768, 2304], P('shard')
- grad_out_weight: float32 [768, 768], P('shard')
- grad_ln2_gain: float32 [768], P('shard')
- grad_ln2_bias: float32 [768], P('shard')
- grad_router_weight: float32 [768, 8], P('shard')
- grad_expert_in: float32 [8, 768, 3072], P(None, 'shard', 'tensor')
- grad_expert_out: float32 [8, 3072, 768], P(None, 'tensor', 'shard')
The draws below stay inside these ranges and needn't reach their ends.
Inputs may be any that keep to these rules, and one draw needn't show every extreme that they name: `expert_ids`: each row names 2 different experts.
All inputs are finite; a program needn't handle non-finite values.
Results may differ from the reference program's by a relative error of at most 0.02.
Values may be sent and summed in bfloat16 or wider, within the bound.
A program may use at most 320 MiB of HBM per device.

```python
import jax
import jax.numpy as jnp
from jax import lax

D = 768
HEADS = 12
HEAD_DIM = 64
FF = 3072
EXPERTS = 8
TOP = 2
SEQ = 197
HEAD_GROUP = 3
TOKENS = 12608
N_HEADS = 4


def level_of(own_key, shape, split, low, top_value):
    level, own = 1.0, jax.random.fold_in(own_key, 6)
    for dim, blocks in split:
        draws = jnp.exp(jax.random.uniform(jax.random.fold_in(own, dim), (blocks,), jnp.float32, low / len(split), top_value / len(split)))
        level = level * jnp.repeat(draws, shape[dim] // blocks).reshape([-1 if axis == dim else 1 for axis in range(len(shape))])
    return level


def different_ones(rng, rows, amount, top, lift):
    order = jax.random.permutation(jax.random.fold_in(rng, 1), amount)
    favour = order
    for power in range(3):
        favour = favour * favour // amount
    favour = favour * lift // amount
    lots = jax.random.randint(jax.random.fold_in(rng, 2), (rows, amount), 0, 4096) + favour
    sure = jax.random.permutation(jax.random.fold_in(rng, 3), rows)[jnp.arange(amount) % rows]
    lots = jnp.where(jnp.arange(rows)[:, None] == sure[None, :], 1 << 14, lots)
    score = lots * amount + jnp.arange(amount)
    return lax.top_k(score.astype(jnp.int32), top)[1].astype(jnp.int32)


def scatter_about(rng, shape, deviation, bound, shards=(), kind=jnp.bfloat16):
    values = deviation * jax.random.normal(rng, shape, jnp.float32)
    if shards:
        values = values * level_of(rng, shape, shards, -0.22, 0.18)
    return jnp.clip(values, -bound, bound).astype(kind)


def setup_inputs(seed: int = 0) -> dict:
    splits = jax.random.split(jax.random.key(seed), 14)
    tokens = scatter_about(splits[0], (TOKENS, D), 1.0, 6.0, ((0, 32),))
    ln1_gain = jnp.clip(1.0 + 0.1 * jax.random.normal(splits[1], (D,), jnp.float32), 0.5, 1.5).astype(jnp.bfloat16)
    ln1_bias = scatter_about(splits[2], (D,), 0.3, 2.0, ((0, 2),))
    qkv_weight = scatter_about(splits[3], (D, 3 * D), D ** -0.5, 0.21875, ((0, 2),))
    out_weight = scatter_about(splits[4], (D, D), (D // 64) ** -0.5, 1.75, ((0, 2),))
    ln2_gain = jnp.clip(1.0 + 0.1 * jax.random.normal(splits[5], (D,), jnp.float32), 0.5, 1.5).astype(jnp.bfloat16)
    ln2_bias = scatter_about(splits[6], (D,), 0.3, 2.0, ((0, 2),))
    router_weight = scatter_about(splits[7], (D, EXPERTS), (4 * D) ** -0.5, 0.109375, ((0, 2),))
    expert_in = scatter_about(splits[8], (EXPERTS, D, FF), D ** -0.5, 0.21875, ((1, 2), (2, 4)))
    expert_out = scatter_about(splits[9], (EXPERTS, FF, D), (FF // 16) ** -0.5, 0.4375, ((1, 4), (2, 2)))
    route_noise = scatter_about(splits[10], (TOKENS, EXPERTS), 0.5, 3.0, ((0, 32),), jnp.float32)
    expert_ids = different_ones(splits[11], TOKENS, EXPERTS, TOP, 0)
    cotangent = scatter_about(splits[12], (TOKENS, D), 1.0, 6.0, ((0, 32),))
    return dict(tokens=tokens, ln1_gain=ln1_gain, ln1_bias=ln1_bias, qkv_weight=qkv_weight, out_weight=out_weight, ln2_gain=ln2_gain, ln2_bias=ln2_bias, router_weight=router_weight, expert_in=expert_in, expert_out=expert_out, route_noise=route_noise, expert_ids=expert_ids, cotangent=cotangent)


EPS = 1e-06
HIGH = lax.Precision.HIGHEST

@jax.custom_vjp
def low(v):
    return lax.optimization_barrier(v.astype(jnp.bfloat16)).astype(jnp.float32)

@jax.custom_vjp
def low_back(v):
    return v

def low_keep(v):
    return (low(v), None)

def low_pass(kept, grad):
    return (grad,)

def back_keep(v):
    return (v, None)

def back_low(kept, grad):
    return (low(grad),)
low.defvjp(low_keep, low_pass)
low_back.defvjp(back_keep, back_low)

def layer_norm(values, gain, bias):
    mean = lax.optimization_barrier(jnp.mean(values, -1, keepdims=True))
    centred = values - mean
    spread = lax.optimization_barrier(jnp.mean(centred * centred, -1, keepdims=True))
    return centred * lax.rsqrt(spread + EPS) * gain + bias

def experts_apply(normed, gates, inner, outer):

    def one_expert(total, piece):
        weight_in, weight_out, column = piece
        hidden = low_back(jnp.dot(normed, weight_in, precision=HIGH))
        active = low(jax.nn.gelu(hidden) * column[:, None])
        return (total + jnp.dot(active, weight_out, precision=HIGH), None)
    start = jnp.zeros((normed.shape[0], normed.shape[1]), jnp.float32)
    total, unused = lax.scan(jax.checkpoint(one_expert), start, (inner, outer, gates.T))
    return total

def forward(tokens, gain_a, bias_a, proj_qkv, proj_out, gain_b, bias_b, router, inner, outer, noise, chosen):
    images = TOKENS // SEQ
    normed_a = low(layer_norm(tokens, gain_a, bias_a))
    packed = low(low_back(jnp.dot(normed_a, proj_qkv, precision=HIGH)))
    packed = packed.reshape(images, SEQ, N_HEADS, 3, HEAD_GROUP, HEAD_DIM)
    query = packed[:, :, :, 0].reshape(images, SEQ, HEADS, HEAD_DIM)
    keys = packed[:, :, :, 1].reshape(images, SEQ, HEADS, HEAD_DIM)
    values = packed[:, :, :, 2].reshape(images, SEQ, HEADS, HEAD_DIM)
    scores = low_back(jnp.einsum('nihd,njhd->nhij', query, keys, precision=HIGH) * HEAD_DIM ** (-0.5))
    weights = low(jax.nn.softmax(scores, -1))
    attended = low(low_back(jnp.einsum('nhij,njhd->nihd', weights, values, precision=HIGH)))
    middle = tokens + low_back(jnp.dot(attended.reshape(TOKENS, D), proj_out, precision=HIGH))
    normed_b = low(layer_norm(middle, gain_b, bias_b))
    gates = low(jax.nn.softmax(jnp.dot(normed_b, router, precision=HIGH) + noise, -1) * chosen)
    return middle + low_back(experts_apply(normed_b, gates, inner, outer))

def reference(tokens, ln1_gain, ln1_bias, qkv_weight, out_weight, ln2_gain, ln2_bias, router_weight, expert_in, expert_out, route_noise, expert_ids, cotangent):
    floats = tuple((item.astype(jnp.float32) for item in (tokens, ln1_gain, ln1_bias, qkv_weight, out_weight, ln2_gain, ln2_bias, router_weight, expert_in, expert_out)))
    labels = jnp.arange(EXPERTS, dtype=jnp.int32)
    chosen = lax.optimization_barrier(jnp.sum((expert_ids[:, :, None] == labels[None, None, :]).astype(jnp.float32), 1))

    def run(*items):
        return forward(*items, route_noise, chosen)
    result, pull = jax.vjp(run, *floats)
    grads = pull(cotangent.astype(jnp.float32))
    return (result.astype(jnp.bfloat16), grads[0].astype(jnp.bfloat16), grads[1], grads[2], grads[3], grads[4], grads[5], grads[6], grads[7], grads[8], grads[9])
```

```python
import jax
import jax.numpy as jnp
from jax import lax
from jax.sharding import PartitionSpec as P

HEAD_DIM = 64
SEQ = 197
EPS = 1e-06
HIGH = lax.Precision.HIGHEST
AXES = ("shard", "heads", "tensor")
BF = jnp.bfloat16
F32 = jnp.float32


def layer_norm(values, gain, bias):
    mean = jnp.mean(values, -1, keepdims=True)
    centred = values - mean
    spread = jnp.mean(centred * centred, -1, keepdims=True)
    return centred * lax.rsqrt(spread + EPS) * gain + bias


def route_gates(normed, router, noise, chosen):
    logits = jnp.dot(normed, router, precision=HIGH) + noise
    return jax.nn.softmax(logits, -1) * chosen


def contract_rows(left, right):
    return lax.dot_general(left, right, (((0,), (0,)), ((), ())), preferred_element_type=F32)


def contract_cols(left, right):
    return lax.dot_general(left, right, (((1,), (1,)), ((), ())), preferred_element_type=F32)


class Comm:
    def __init__(self):
        self.sizes = tuple(lax.axis_size(axis) for axis in AXES)
        self.shard = lax.axis_index("shard")
        self.head = lax.axis_index("heads")
        self.tensor = lax.axis_index("tensor")
        self.pair = self.head % 2

    def move(self, value, step):
        shards, heads, tensors = self.sizes
        pairs = []
        for s in range(shards):
            for h in range(heads):
                for t in range(tensors):
                    to = step(s, h, t)
                    if 0 <= to[2] < tensors:
                        source = (s * heads + h) * tensors + t
                        pairs.append((source, (to[0] * heads + to[1]) * tensors + to[2]))
        return lax.ppermute(value, AXES, pairs)

    def over_core(self, value):
        return self.move(value, lambda s, h, t: (s, h ^ 1, t))

    def over_heads(self, value):
        return self.move(value, lambda s, h, t: (s, (h + 2) % 4, t))

    def over_shard(self, value):
        return self.move(value, lambda s, h, t: (1 - s, h, t))

    def up(self, value):
        return self.move(value, lambda s, h, t: (s, h, t + 1))

    def down(self, value):
        return self.move(value, lambda s, h, t: (s, h, t - 1))

    def halves(self, value, index, axis):
        size = value.shape[axis] // 2
        mine = lax.dynamic_slice_in_dim(value, index * size, size, axis)
        other = lax.dynamic_slice_in_dim(value, (1 - index) * size, size, axis)
        return mine, other

    def join(self, mine, other, index, axis):
        first = jnp.where(index == 0, mine, other)
        second = jnp.where(index == 0, other, mine)
        return jnp.concatenate((first, second), axis)

    def gather_shard(self, value, axis):
        if self.sizes[0] != 2:
            return lax.all_gather(value, "shard", axis=axis, tiled=True)
        return self.join(value, self.over_shard(value), self.shard, axis)

    def gather_shard_split(self, value, axis, cut):
        if self.sizes[0] != 2:
            return lax.all_gather(value, "shard", axis=axis, tiled=True)
        mine, _ = self.halves(value, self.pair, cut)
        got = self.over_shard(mine)
        both = self.join(got, self.over_core(got), self.pair, cut)
        return self.join(value, both, self.shard, axis)

    def scatter_shard(self, value, axis):
        if self.sizes[0] != 2:
            return lax.psum_scatter(value.astype(BF), "shard", scatter_dimension=axis, tiled=True).astype(F32)
        mine, other = self.halves(value, self.shard, axis)
        return mine.astype(F32) + self.over_shard(other.astype(BF)).astype(F32)

    def scatter_core(self, value, axis):
        mine, other = self.halves(value, self.pair, axis)
        return mine.astype(F32) + self.over_core(other.astype(BF)).astype(F32)

    def scatter_heads(self, value, axis):
        mine, other = self.halves(value, self.head // 2, axis)
        return mine.astype(F32) + self.over_heads(other.astype(BF)).astype(F32)

    def line_gather(self, value):
        ups, downs = [value], [value]
        for _ in range(3):
            ups.append(self.up(ups[-1]))
            downs.append(self.down(downs[-1]))
        out = [value]
        for back in (1, 2, 3):
            out.append(jnp.where(self.tensor >= back, ups[back], downs[4 - back]))
        return out

    def line_scatter(self, parts):
        high, low = parts[1].astype(BF), parts[3].astype(BF)
        high = (parts[2].astype(F32) + self.up(high).astype(F32)).astype(BF)
        low = (parts[2].astype(F32) + self.down(low).astype(F32)).astype(BF)
        high = (parts[3].astype(F32) + self.up(high).astype(F32)).astype(BF)
        low = (parts[1].astype(F32) + self.down(low).astype(F32)).astype(BF)
        return parts[0].astype(F32) + self.up(high).astype(F32) + self.down(low).astype(F32)


def local(
    tokens,
    ln1_gain,
    ln1_bias,
    qkv_weight,
    out_weight,
    ln2_gain,
    ln2_bias,
    router_weight,
    expert_in,
    expert_out,
    route_noise,
    expert_ids,
    cotangent,
):
    comm = Comm()
    rows, width = tokens.shape
    experts = expert_in.shape[0]
    images = rows // SEQ
    heads = width // HEAD_DIM
    scale = HEAD_DIM ** (-0.5)
    half = experts // 2
    depth = ln1_gain.shape[0]

    smalls = jnp.concatenate(
        (ln1_gain[None], ln1_bias[None], ln2_gain[None], ln2_bias[None], router_weight.T), 0
    )
    smalls = comm.gather_shard(smalls, 1)
    gain_a, bias_a, gain_b, bias_b = (smalls[i].astype(F32) for i in range(4))
    router = smalls[4:].T
    dense = jnp.concatenate((qkv_weight, out_weight), 1)
    dense = comm.gather_shard_split(dense, 0, 1)
    proj_qkv, proj_out = dense[:, : 3 * width], dense[:, 3 * width :]
    own_in = lax.dynamic_slice_in_dim(expert_in, comm.pair * half, half, 0)
    own_out = lax.dynamic_slice_in_dim(expert_out, comm.pair * half, half, 0)
    inner = comm.gather_shard(own_in, 1)
    outer = comm.gather_shard(own_out, 2)
    grad_rows = jnp.concatenate(comm.line_gather(cotangent), 0)
    grad_rows = jnp.concatenate((grad_rows, comm.over_core(grad_rows)), 0)

    start_x = tokens.astype(F32)
    first_norm, first_pull = jax.vjp(layer_norm, start_x, gain_a, bias_a)
    normed_a = first_norm.astype(BF)
    packed = jnp.dot(normed_a, proj_qkv, preferred_element_type=F32).astype(BF)
    groups = heads // 3
    split = packed.reshape(images, SEQ, groups, 3, 3, HEAD_DIM)
    split = split.transpose(3, 0, 2, 4, 1, 5).reshape(3, images, heads, SEQ, HEAD_DIM)
    query, keys, values = split[0], split[1], split[2]
    scores = jnp.einsum("nhid,nhjd->nhij", query, keys, preferred_element_type=F32) * scale
    probs = jax.nn.softmax(scores, -1)
    weights = probs.astype(BF)
    attended = jnp.einsum("nhij,nhjd->nhid", weights, values, preferred_element_type=F32).astype(BF)
    returned = attended.transpose(0, 2, 1, 3).reshape(rows, width)
    middle = start_x + jnp.dot(returned, proj_out, preferred_element_type=F32)
    second_norm, second_pull = jax.vjp(layer_norm, middle, gain_b, bias_b)
    normed_b = second_norm.astype(BF)
    labels = jnp.arange(experts, dtype=jnp.int32)
    chosen = jnp.sum((expert_ids[:, :, None] == labels[None, None, :]).astype(F32), 1)

    def gate_function(normed, weight):
        return route_gates(normed, weight, route_noise, chosen)

    gates, gate_pull = jax.vjp(gate_function, normed_b.astype(F32), router.astype(F32))
    sent = jnp.concatenate((normed_b, jnp.pad(gates.astype(BF), ((0, 0), (0, 128 - experts)))), 1)
    rows_all = jnp.concatenate(comm.line_gather(sent), 0)
    rows_all = jnp.concatenate((rows_all, comm.over_core(rows_all)), 0)
    part_gates = lax.dynamic_slice_in_dim(rows_all[:, width:], comm.pair * half, half, 1).astype(F32)
    rows_all = rows_all[:, :width]

    total = jnp.zeros((rows_all.shape[0], width), F32)
    grad_rows_in = jnp.zeros((rows_all.shape[0], width), F32)
    gate_grads, inner_grads, outer_grads = [], [], []

    def reduce_expert(grad, axis, other):
        part = comm.scatter_shard(grad, axis)
        part = comm.scatter_heads(part, other).astype(BF)
        return comm.join(part, comm.over_heads(part), comm.head // 2, other)

    for expert in range(half):
        hidden = jnp.dot(rows_all, inner[expert], preferred_element_type=F32)
        activated, gelu_pull = jax.vjp(jax.nn.gelu, hidden)
        gate_column = part_gates[:, expert : expert + 1]
        active = (activated * gate_column).astype(BF)
        total = total + jnp.dot(active, outer[expert], preferred_element_type=F32)
        grad_active = contract_cols(grad_rows, outer[expert])
        gate_grads.append(jnp.sum(grad_active * activated, 1))
        grad_hidden = gelu_pull(grad_active * gate_column)[0].astype(BF)
        grad_rows_in = grad_rows_in + contract_cols(grad_hidden, inner[expert])
        outer_grads.append(reduce_expert(contract_rows(active, grad_rows), 1, 0))
        inner_grads.append(reduce_expert(contract_rows(rows_all, grad_hidden), 0, 1))

    count = rows * 4
    gate_table = jnp.stack(gate_grads, 1)
    spread = jnp.zeros((2 * count, 128), F32)
    spread = lax.dynamic_update_slice_in_dim(spread, gate_table, comm.pair * half, 1)
    back = jnp.concatenate((grad_rows_in, spread), 1).astype(BF)
    back = back[:count].astype(F32) + comm.over_core(back[count:]).astype(F32)
    back = comm.line_scatter([back[k * rows : (k + 1) * rows] for k in range(4)])
    grad_normed_moe, grad_gates = back[:, :width], back[:, width : width + experts]
    moe = total.astype(BF)
    moe = moe[:count].astype(F32) + comm.over_core(moe[count:]).astype(F32)
    moe = comm.line_scatter([moe[k * rows : (k + 1) * rows] for k in range(4)])
    mixed = (middle + moe).astype(BF)

    grad_out = cotangent.astype(F32)
    route_normed, grad_router = gate_pull(grad_gates)
    grad_mid, grad_gain_b, grad_bias_b = second_pull(grad_normed_moe + route_normed)
    grad_middle = grad_out + grad_mid
    grad_proj = grad_middle.astype(BF)
    grad_proj_out = contract_rows(returned, grad_proj)
    grad_returned = contract_cols(grad_proj, proj_out).astype(BF)
    grad_attended = grad_returned.reshape(images, SEQ, heads, HEAD_DIM).transpose(0, 2, 1, 3)
    grad_values = jnp.einsum("nhij,nhid->nhjd", weights, grad_attended, preferred_element_type=F32)
    grad_weights = jnp.einsum("nhid,nhjd->nhij", grad_attended, values, preferred_element_type=F32)
    inner_sum = jnp.sum(probs * grad_weights, -1, keepdims=True)
    grad_scores = (probs * (grad_weights - inner_sum)).astype(BF)
    grad_query = jnp.einsum("nhij,nhjd->nhid", grad_scores, keys, preferred_element_type=F32) * scale
    grad_keys = jnp.einsum("nhij,nhid->nhjd", grad_scores, query, preferred_element_type=F32) * scale
    stack = jnp.stack((grad_query, grad_keys, grad_values), 0).astype(BF)
    stack = stack.reshape(3, images, groups, 3, SEQ, HEAD_DIM).transpose(1, 4, 2, 0, 3, 5)
    grad_packed = stack.reshape(rows, 3 * width)
    grad_proj_qkv = contract_rows(normed_a, grad_packed)
    grad_normed_a = contract_cols(grad_packed, proj_qkv)
    grad_first, grad_gain_a, grad_bias_a = first_pull(grad_normed_a)
    grad_tokens = (grad_middle + grad_first).astype(BF)

    small = jnp.concatenate(
        (grad_gain_a[:, None], grad_bias_a[:, None], grad_gain_b[:, None], grad_bias_b[:, None], grad_router), 1
    )
    small = jnp.pad(small, ((0, 0), (0, 128 - small.shape[1])))
    shares = jnp.concatenate((grad_proj_qkv, grad_proj_out, small, jnp.zeros_like(small)), 1)
    shares = comm.scatter_core(shares, 1)
    shares = comm.scatter_shard(shares, 0)
    shares = comm.scatter_heads(shares, 1)
    cut = shares.shape[0] // 4
    rolled = [
        lax.dynamic_slice_in_dim(shares, ((comm.tensor + 4 - k) % 4) * cut, cut, 0) for k in range(4)
    ]
    summed = comm.line_scatter(rolled).astype(BF)
    pieces = comm.line_gather(summed)
    whole = jnp.zeros(shares.shape, BF)
    for k in range(4):
        whole = lax.dynamic_update_slice_in_dim(whole, pieces[k], ((comm.tensor + 4 - k) % 4) * cut, 0)
    whole = comm.join(whole, comm.over_heads(whole), comm.head // 2, 1)
    whole = comm.join(whole, comm.over_core(whole), comm.pair, 1).astype(F32)
    small = whole[:, 4 * width : 4 * width + 128]

    grad_in, grad_outer = jnp.stack(inner_grads, 0), jnp.stack(outer_grads, 0)
    grad_in = comm.join(grad_in, comm.over_core(grad_in), comm.pair, 0).astype(F32)
    grad_outer = comm.join(grad_outer, comm.over_core(grad_outer), comm.pair, 0).astype(F32)
    return (
        mixed,
        grad_tokens,
        small[:, 0],
        small[:, 1],
        whole[:, : 3 * width],
        whole[:, 3 * width : 4 * width],
        small[:, 2],
        small[:, 3],
        small[:, 4 : 4 + experts],
        grad_in,
        grad_outer,
    )


def solution(mesh):
    split = P(AXES, None)
    vector, matrix = P("shard"), P("shard", None)
    inner, outer = P(None, "shard", "tensor"), P(None, "tensor", "shard")
    return jax.shard_map(
        local,
        mesh=mesh,
        in_specs=(
            split, vector, vector, matrix, matrix, vector, vector, matrix, inner, outer, split, split, split,
        ),
        out_specs=(
            split, split, vector, vector, matrix, matrix, vector, vector, matrix, inner, outer,
        ),
        check_vma=False,
    )
```

```python
import jax
import jax.numpy as jnp
from jax import lax
from jax.experimental import pallas as pl
from jax.experimental.pallas import tpu as pltpu
from jax.sharding import PartitionSpec as P

HEAD_DIM = 64
SEQ = 197
EPS = 1e-06
AXES = ("shard", "heads", "tensor")
BF = jnp.bfloat16
F32 = jnp.float32


def contract_rows(left, right):
    return lax.dot_general(left, right, (((0,), (0,)), ((), ())), preferred_element_type=F32)


def contract_cols(left, right):
    return lax.dot_general(left, right, (((1,), (1,)), ((), ())), preferred_element_type=F32)


PAD = 208
TILE = 128
CHUNK = 256
FAR = 512.0
EXTRA = 128
MASKED = -1e30
CUBIC = 0.044715
ROOT = (2.0 / 3.141592653589793) ** 0.5
BIG = 60 * 1024 * 1024


def dot(left, right):
    return jnp.dot(left, right, preferred_element_type=F32)


def norm_parts(values):
    centred = values - jnp.mean(values, -1, keepdims=True)
    inverse = lax.rsqrt(jnp.mean(centred * centred, -1, keepdims=True) + EPS)
    return centred * inverse, inverse


def norm_back(grad, unit, inverse, gain):
    scaled = grad * gain
    along = jnp.mean(scaled * unit, -1, keepdims=True)
    return inverse * (scaled - jnp.mean(scaled, -1, keepdims=True) - unit * along)


def head_probs(query, keys, scale):
    scores = contract_cols(query, keys) * scale
    column = lax.broadcasted_iota(jnp.int32, scores.shape, 1)
    scores = jnp.where(column < SEQ, scores, MASKED)
    raised = jnp.exp(scores - jnp.max(scores, -1, keepdims=True))
    return raised / jnp.sum(raised, -1, keepdims=True)


def front_kernel(
    x_ref, small_ref, qkv_ref, out_ref, router_ref, noise_ref, ids_ref,
    normed_ref, packed_ref, attended_ref, middle_ref, sent_ref, prob_ref,
):
    width = x_ref.shape[1]
    images = x_ref.shape[0] // PAD
    group = 3 * HEAD_DIM
    groups = width // group
    scale = HEAD_DIM ** (-0.5)
    experts = 8
    for image in range(images):
        at = pl.ds(image * PAD, PAD)
        x = x_ref[at, :].astype(F32)
        unit, _ = norm_parts(x)
        normed = (unit * small_ref[0:1, :] + small_ref[1:2, :]).astype(BF)
        normed_ref[at, :] = normed
        lane = lax.broadcasted_iota(jnp.int32, (PAD, group), 1) // HEAD_DIM
        outs = []
        for double in range(groups // 2):
            cols = pl.ds(double * 6 * group, 6 * group)
            packed = dot(normed, qkv_ref[:, cols])
            packed_ref[at, cols] = packed.astype(BF)
            for side in range(2):
                query, keys, values = (
                    packed[:, (3 * side + k) * group : (3 * side + k + 1) * group].astype(BF)
                    for k in range(3)
                )
                total = jnp.zeros((PAD, group), F32)
                for head in range(3):
                    mask = lane == head
                    probs = head_probs(jnp.where(mask, query, jnp.zeros_like(query)), keys, scale)
                    total = jnp.where(mask, dot(probs.astype(BF), values), total)
                outs.append(total)
        attended = jnp.concatenate(outs, 1).astype(BF)
        attended_ref[at, :] = attended
        middle = x + dot(attended, out_ref[...])
        middle_ref[at, :] = middle
        unit, _ = norm_parts(middle)
        normed = (unit * small_ref[2:3, :] + small_ref[3:4, :]).astype(BF)
        lane = lax.broadcasted_iota(jnp.int32, (PAD, EXTRA), 1)
        logits = dot(normed, router_ref[...]) + noise_ref[at, :]
        logits = jnp.where(lane < experts, logits, MASKED)
        raised = jnp.exp(logits - jnp.max(logits, -1, keepdims=True))
        probs = raised / jnp.sum(raised, -1, keepdims=True)
        prob_ref[at, :] = probs
        first, second = ids_ref[at, 0:1], ids_ref[at, 1:2]
        chosen = ((lane == first) | (lane == second)).astype(F32)
        first, second = first + experts, second + experts
        flags = (((lane == first) | (lane == second)) & (lane >= experts)).astype(F32)
        sent_ref[at, 0:width] = normed
        sent_ref[at, width : width + EXTRA] = (probs * chosen + flags).astype(BF)


def front(x, small, qkv, out, router, noise, ids):
    rows, width = x.shape
    shape = jax.ShapeDtypeStruct
    return pl.pallas_call(
        front_kernel,
        out_shape=(
            shape((rows, width), BF),
            shape((rows, 3 * width), BF),
            shape((rows, width), BF),
            shape((rows, width), F32),
            shape((rows, width + EXTRA), BF),
            shape((rows, EXTRA), F32),
        ),
        compiler_params=pltpu.CompilerParams(vmem_limit_bytes=BIG),
        cost_estimate=pl.CostEstimate(flops=8 * 10**9, bytes_accessed=10**7, transcendentals=10**6),
        name="front",
    )(x, small, qkv, out, router, noise, ids)


def expert_kernel(
    place_ref, rows_ref, cot_ref, own_in, got_in, own_out, got_out,
    total_ref, back_ref, grad_in, grad_out,
    inner, outer, picked, grads, gate, active, hidden_grad, made, made_back, ranks, sum_in, sum_out, stage_in, stage_out,
    load_sem, store_sem,
):
    blocks, length, width = cot_ref.shape
    count = got_in.shape[0]
    depth = got_in.shape[1]
    pair, shard = place_ref[0], place_ref[1]
    experts = 2 * count
    capacity = blocks * TILE

    def loads(expert, slot):
        mine = pl.ds(pl.multiple_of(shard * depth, EXTRA), depth)
        other = pl.ds(pl.multiple_of((1 - shard) * depth, EXTRA), depth)
        index = pair * count + expert
        return (
            pltpu.make_async_copy(own_in.at[index], inner.at[slot, mine, :], load_sem.at[slot, 0]),
            pltpu.make_async_copy(got_in.at[expert], inner.at[slot, other, :], load_sem.at[slot, 1]),
            pltpu.make_async_copy(own_out.at[index], outer.at[slot, :, mine], load_sem.at[slot, 2]),
            pltpu.make_async_copy(got_out.at[expert], outer.at[slot, :, other], load_sem.at[slot, 3]),
        )

    def stores(expert, slot):
        return (
            pltpu.make_async_copy(stage_in.at[slot], grad_in.at[expert], store_sem.at[slot, 0]),
            pltpu.make_async_copy(stage_out.at[slot], grad_out.at[expert], store_sem.at[slot, 1]),
        )

    for copy in loads(0, 0):
        copy.start()
    ahead = lax.broadcasted_iota(jnp.int32, (length, length), 0)
    behind = lax.broadcasted_iota(jnp.int32, (length, length), 1)
    order = jnp.where(behind < ahead, 1.0, jnp.where(behind == ahead, FAR, 0.0)).astype(BF)

    def rank(block, carry):
        flags = rows_ref[block, :, width : width + EXTRA]
        place = lax.dot_general(flags, order, (((0,), (1,)), ((), ())), preferred_element_type=F32)
        ranks[block] = place[0:16, :] - FAR
        total_ref[block] = jnp.zeros(total_ref.shape[1:], BF)
        back_ref[block] = jnp.zeros(back_ref.shape[1:], BF)
        return carry

    lax.fori_loop(0, blocks, rank, 0)

    for expert in range(count):
        slot = expert % 2
        if expert + 1 < count:
            for copy in loads(expert + 1, 1 - slot):
                copy.start()
        line = pl.ds(experts + pair * count + expert, 1)
        highest = ranks[0, line, :]
        for block in range(1, blocks):
            highest = jnp.maximum(highest, ranks[block, line, :])
        passes = (jnp.maximum(jnp.max(highest), -1.0).astype(jnp.int32) + TILE) // TILE
        sum_in[...] = jnp.zeros(sum_in.shape, F32)
        sum_out[...] = jnp.zeros(sum_out.shape, F32)
        for copy in loads(expert, slot):
            copy.wait()

        def one_pass(step, carry):
            base = (step * TILE).astype(F32)
            slots = lax.broadcasted_iota(jnp.int32, (TILE, length), 0).astype(F32) + base

            def take(block, carry):
                choose = (ranks[block, line, :] == slots).astype(BF)
                at = pl.ds(pl.multiple_of(block * TILE, TILE), TILE)
                both = dot(choose, rows_ref[block])
                picked[at, :] = both[:, :width].astype(BF)
                lane = lax.broadcasted_iota(jnp.int32, (TILE, EXTRA), 1)
                column = jnp.where(lane == pair * count + expert, both[:, width:], 0.0)
                gate[at, :] = jnp.broadcast_to(jnp.sum(column, -1, keepdims=True), (TILE, EXTRA))
                grads[at, :] = dot(choose, cot_ref[block]).astype(BF)
                return carry

            lax.fori_loop(0, blocks, take, 0, unroll=2)

            def chunk(index, carry):
                at = pl.ds(pl.multiple_of(index * CHUNK, CHUNK), CHUNK)
                value = dot(picked[at, :], inner[slot])
                grad_active = contract_cols(grads[at, :], outer[slot])
                gate_column = gate[at, 0:1]
                square = value * value
                bent = jnp.tanh(ROOT * value * (1.0 + CUBIC * square))
                plus = 0.5 * (1.0 + bent)
                bowed = value * plus
                slope = plus + (0.5 * ROOT) * value * (1.0 - bent * bent) * (1.0 + (3.0 * CUBIC) * square)
                active[at, :] = (bowed * gate_column).astype(BF)
                back = (grad_active * gate_column * slope).astype(BF)
                hidden_grad[at, :] = back
                lane = lax.broadcasted_iota(jnp.int32, (CHUNK, EXTRA), 1)
                gate_grad = jnp.sum(grad_active * bowed, -1, keepdims=True)
                made_back[at, width : width + EXTRA] = jnp.where(
                    lane == pair * count + expert, gate_grad, 0.0
                ).astype(BF)
                made[at, :] = dot(active[at, :], outer[slot]).astype(BF)
                made_back[at, 0:width] = contract_cols(back, inner[slot]).astype(BF)
                return carry

            lax.fori_loop(0, capacity // CHUNK, chunk, 0)
            for third in range(3):
                at = pl.ds(third * CHUNK, CHUNK)
                sum_out[at, :] += contract_rows(active[:, at], grads[...])
                sum_in[at, :] += contract_rows(picked[:, at], hidden_grad[...])

            def give(block, carry):
                choose = (ranks[block, line, :] == slots).astype(BF)
                at = pl.ds(pl.multiple_of(block * TILE, TILE), TILE)
                total_ref[block] = (total_ref[block].astype(F32) + contract_rows(choose, made[at, :])).astype(BF)
                back_ref[block] = (back_ref[block].astype(F32) + contract_rows(choose, made_back[at, :])).astype(BF)
                return carry

            lax.fori_loop(0, blocks, give, 0, unroll=2)
            return carry

        lax.fori_loop(0, passes, one_pass, 0)
        if expert >= 2:
            for copy in stores(expert - 2, slot):
                copy.wait()
        stage_in[slot] = sum_in[...].astype(BF)
        stage_out[slot] = sum_out[...].astype(BF)
        for copy in stores(expert, slot):
            copy.start()
    for expert in range(max(count - 2, 0), count):
        for copy in stores(expert, expert % 2):
            copy.wait()


def expert_pass(place, rows, cot, own_in, got_in, own_out, got_out):
    blocks, length, width = cot.shape
    count, _, hidden = got_in.shape
    capacity = blocks * TILE
    shape = jax.ShapeDtypeStruct
    anywhere = pl.BlockSpec(memory_space=pl.ANY)
    vmem = pl.BlockSpec(memory_space=pltpu.VMEM)
    return pl.pallas_call(
        expert_kernel,
        out_shape=(
            shape((blocks, length, width), BF),
            shape((blocks, length, width + EXTRA), BF),
            shape((count, width, hidden), BF),
            shape((count, hidden, width), BF),
        ),
        in_specs=[pl.BlockSpec(memory_space=pltpu.SMEM), vmem, vmem] + [anywhere] * 4,
        out_specs=(vmem, vmem, anywhere, anywhere),
        scratch_shapes=[
            pltpu.VMEM((2, width, hidden), BF),
            pltpu.VMEM((2, hidden, width), BF),
            pltpu.VMEM((capacity, width), BF),
            pltpu.VMEM((capacity, width), BF),
            pltpu.VMEM((capacity, EXTRA), F32),
            pltpu.VMEM((capacity, hidden), BF),
            pltpu.VMEM((capacity, hidden), BF),
            pltpu.VMEM((capacity, width), BF),
            pltpu.VMEM((capacity, width + EXTRA), BF),
            pltpu.VMEM((blocks, 16, length), F32),
            pltpu.VMEM((width, hidden), F32),
            pltpu.VMEM((hidden, width), F32),
            pltpu.VMEM((2, width, hidden), BF),
            pltpu.VMEM((2, hidden, width), BF),
            pltpu.SemaphoreType.DMA((2, 4)),
            pltpu.SemaphoreType.DMA((2, 2)),
        ],
        compiler_params=pltpu.CompilerParams(vmem_limit_bytes=BIG),
        cost_estimate=pl.CostEstimate(flops=50 * 10**9, bytes_accessed=5 * 10**7, transcendentals=10**6),
        name="experts",
    )(place, rows, cot, own_in, got_in, own_out, got_out)


def back_kernel(
    moe_ref, cot_ref, x_ref, middle_ref, sent_ref, prob_ref, attended_ref, packed_ref, normed_ref,
    small_ref, qkv_ref, out_ref, router_ref,
    tokens_ref, grad_qkv, grad_out, grad_small, grad_router,
    stacked, projected,
):
    rows, width = x_ref.shape
    images = rows // PAD
    group = 3 * HEAD_DIM
    groups = width // group
    scale = HEAD_DIM ** (-0.5)
    experts = 8
    lane = lax.broadcasted_iota(jnp.int32, (PAD, EXTRA), 1)
    sums = [jnp.zeros((1, width), F32) for _ in range(4)]
    router_sum = jnp.zeros((EXTRA, width), F32)
    lanes = lax.broadcasted_iota(jnp.int32, (PAD, group), 1) // HEAD_DIM
    for image in range(images):
        at = pl.ds(image * PAD, PAD)
        moe = moe_ref[at, :].astype(F32)
        first_flags = sent_ref[at, width : width + EXTRA].astype(F32)
        chosen = jnp.where(lane < experts, pltpu.roll(first_flags, EXTRA - experts, 1), 0.0)
        probs = prob_ref[at, :]
        asked = moe[:, width:] * chosen
        grad_logits = probs * (asked - jnp.sum(probs * asked, -1, keepdims=True))
        coarse = grad_logits.astype(BF)
        fine = (grad_logits - coarse.astype(F32)).astype(BF)
        normed_b = sent_ref[at, 0:width]
        router_sum = router_sum + contract_rows(coarse, normed_b) + contract_rows(fine, normed_b)
        routed = contract_cols(coarse, router_ref[...]) + contract_cols(fine, router_ref[...])
        grad = moe[:, :width] + routed
        unit, inverse = norm_parts(middle_ref[at, :])
        sums[2] = sums[2] + jnp.sum(grad * unit, 0, keepdims=True)
        sums[3] = sums[3] + jnp.sum(grad, 0, keepdims=True)
        grad_middle = cot_ref[at, :].astype(F32) + norm_back(grad, unit, inverse, small_ref[2:3, :])
        grad_proj = grad_middle.astype(BF)
        projected[at, :] = grad_proj
        for double in range(groups // 2):
            made = []
            packed = packed_ref[at, pl.ds(double * 6 * group, 6 * group)]
            for side in range(2):
                query, keys, values = (
                    packed[:, (3 * side + k) * group : (3 * side + k + 1) * group] for k in range(3)
                )
                index = double * 2 + side
                grad_att = contract_cols(grad_proj, out_ref[pl.ds(index * group, group), :]).astype(BF)
                outs = [jnp.zeros((PAD, group), F32) for _ in range(3)]
                for head in range(3):
                    mask = lanes == head
                    probs = head_probs(jnp.where(mask, query, jnp.zeros_like(query)), keys, scale)
                    part = jnp.where(mask, grad_att, jnp.zeros_like(grad_att))
                    grad_weights = contract_cols(part, values)
                    inner_sum = jnp.sum(probs * grad_weights, -1, keepdims=True)
                    grad_scores = (probs * (grad_weights - inner_sum)).astype(BF)
                    outs[0] = jnp.where(mask, dot(grad_scores, keys), outs[0])
                    outs[1] = jnp.where(mask, contract_rows(grad_scores, query), outs[1])
                    outs[2] = jnp.where(mask, contract_rows(probs.astype(BF), grad_att), outs[2])
                made += [outs[0] * scale, outs[1] * scale, outs[2]]
            stacked[at, pl.ds(double * 6 * group, 6 * group)] = jnp.concatenate(made, 1).astype(BF)
        grad = contract_cols(stacked[at, :], qkv_ref[...])
        unit, inverse = norm_parts(x_ref[at, :].astype(F32))
        sums[0] = sums[0] + jnp.sum(grad * unit, 0, keepdims=True)
        sums[1] = sums[1] + jnp.sum(grad, 0, keepdims=True)
        tokens_ref[at, :] = (grad_middle + norm_back(grad, unit, inverse, small_ref[0:1, :])).astype(BF)
    grad_router[...] = router_sum[0:experts, :]
    for index in range(4):
        grad_small[index : index + 1, :] = sums[index]
    grad_out[...] = contract_rows(attended_ref[...], projected[...]).astype(BF)
    for third in range(3):
        cols = pl.ds(third * width, width)
        grad_qkv[:, cols] = contract_rows(normed_ref[...], stacked[:, cols]).astype(BF)


def back(moe, cot, x, middle, sent, prob, attended, packed, normed, small, qkv, out, router):
    rows, width = x.shape
    shape = jax.ShapeDtypeStruct
    return pl.pallas_call(
        back_kernel,
        out_shape=(
            shape((rows, width), BF),
            shape((width, 3 * width), BF),
            shape((width, width), BF),
            shape((4, width), F32),
            shape((8, width), F32),
        ),
        scratch_shapes=[pltpu.VMEM((rows, 3 * width), BF), pltpu.VMEM((rows, width), BF)],
        compiler_params=pltpu.CompilerParams(vmem_limit_bytes=BIG),
        cost_estimate=pl.CostEstimate(flops=16 * 10**9, bytes_accessed=2 * 10**7, transcendentals=10**6),
        name="back",
    )(moe, cot, x, middle, sent, prob, attended, packed, normed, small, qkv, out, router)


class Comm:
    def __init__(self):
        self.sizes = tuple(lax.axis_size(axis) for axis in AXES)
        self.shard = lax.axis_index("shard")
        self.head = lax.axis_index("heads")
        self.tensor = lax.axis_index("tensor")
        self.pair = self.head % 2

    def move(self, value, step):
        shards, heads, tensors = self.sizes
        pairs = []
        for s in range(shards):
            for h in range(heads):
                for t in range(tensors):
                    to = step(s, h, t)
                    if 0 <= to[2] < tensors:
                        source = (s * heads + h) * tensors + t
                        pairs.append((source, (to[0] * heads + to[1]) * tensors + to[2]))
        return lax.ppermute(value, AXES, pairs)

    def over_core(self, value):
        return self.move(value, lambda s, h, t: (s, h ^ 1, t))

    def over_heads(self, value):
        return self.move(value, lambda s, h, t: (s, (h + 2) % 4, t))

    def over_shard(self, value):
        return self.move(value, lambda s, h, t: (1 - s, h, t))

    def up(self, value):
        return self.move(value, lambda s, h, t: (s, h, t + 1))

    def down(self, value):
        return self.move(value, lambda s, h, t: (s, h, t - 1))

    def halves(self, value, index, axis):
        size = value.shape[axis] // 2
        mine = lax.dynamic_slice_in_dim(value, index * size, size, axis)
        other = lax.dynamic_slice_in_dim(value, (1 - index) * size, size, axis)
        return mine, other

    def join(self, mine, other, index, axis):
        first = jnp.where(index == 0, mine, other)
        second = jnp.where(index == 0, other, mine)
        return jnp.concatenate((first, second), axis)

    def gather_shard(self, value, axis):
        if self.sizes[0] != 2:
            return lax.all_gather(value, "shard", axis=axis, tiled=True)
        return self.join(value, self.over_shard(value), self.shard, axis)

    def gather_shard_split(self, value, axis, cut):
        if self.sizes[0] != 2:
            return lax.all_gather(value, "shard", axis=axis, tiled=True)
        mine, _ = self.halves(value, self.pair, cut)
        got = self.over_shard(mine)
        both = self.join(got, self.over_core(got), self.pair, cut)
        return self.join(value, both, self.shard, axis)

    def scatter_shard(self, value, axis):
        if self.sizes[0] != 2:
            return lax.psum_scatter(value.astype(BF), "shard", scatter_dimension=axis, tiled=True).astype(F32)
        mine, other = self.halves(value, self.shard, axis)
        return mine.astype(F32) + self.over_shard(other.astype(BF)).astype(F32)

    def scatter_core(self, value, axis):
        mine, other = self.halves(value, self.pair, axis)
        return mine.astype(F32) + self.over_core(other.astype(BF)).astype(F32)

    def scatter_heads(self, value, axis):
        mine, other = self.halves(value, self.head // 2, axis)
        return mine.astype(F32) + self.over_heads(other.astype(BF)).astype(F32)

    def line_gather(self, value):
        ups, downs = [value], [value]
        for _ in range(3):
            ups.append(self.up(ups[-1]))
            downs.append(self.down(downs[-1]))
        out = [value]
        for back in (1, 2, 3):
            out.append(jnp.where(self.tensor >= back, ups[back], downs[4 - back]))
        return out

    def line_scatter(self, parts):
        high, low = parts[1].astype(BF), parts[3].astype(BF)
        high = (parts[2].astype(F32) + self.up(high).astype(F32)).astype(BF)
        low = (parts[2].astype(F32) + self.down(low).astype(F32)).astype(BF)
        high = (parts[3].astype(F32) + self.up(high).astype(F32)).astype(BF)
        low = (parts[1].astype(F32) + self.down(low).astype(F32)).astype(BF)
        return parts[0].astype(F32) + self.up(high).astype(F32) + self.down(low).astype(F32)


def local(
    tokens, ln1_gain, ln1_bias, qkv_weight, out_weight, ln2_gain, ln2_bias, router_weight,
    expert_in, expert_out, route_noise, expert_ids, cotangent,
):
    comm = Comm()
    rows, width = tokens.shape
    experts = expert_in.shape[0]
    images = rows // SEQ
    half = experts // 2
    padded = images * PAD

    def pad(value, lanes=0, fill=0):
        value = value.reshape(images, SEQ, value.shape[1])
        value = jnp.pad(value, ((0, 0), (0, PAD - SEQ), (0, lanes)), constant_values=fill)
        return value.reshape(padded, value.shape[2])

    def unpad(value):
        return value.reshape(images, PAD, value.shape[1])[:, :SEQ].reshape(rows, value.shape[1])

    smalls = jnp.concatenate(
        (ln1_gain[None], ln1_bias[None], ln2_gain[None], ln2_bias[None], router_weight.T), 0
    )
    smalls = comm.gather_shard(smalls, 1)
    gains = smalls[:4].astype(F32)
    router = jnp.pad(smalls[4:].T, ((0, 0), (0, EXTRA - experts)))
    dense = jnp.concatenate((qkv_weight, out_weight), 1)
    dense = comm.gather_shard_split(dense, 0, 1)
    proj_qkv, proj_out = dense[:, : 3 * width], dense[:, 3 * width :]
    own_in = lax.dynamic_slice_in_dim(expert_in, comm.pair * half, half, 0)
    own_out = lax.dynamic_slice_in_dim(expert_out, comm.pair * half, half, 0)
    cot = pad(cotangent)
    grad_rows = jnp.stack(comm.line_gather(cot), 0)
    grad_rows = jnp.concatenate((grad_rows, comm.over_core(grad_rows)), 0)
    if comm.sizes[0] == 2:
        place = jnp.stack((comm.pair, comm.shard)).astype(jnp.int32)
        weights = (expert_in, comm.over_shard(own_in), expert_out, comm.over_shard(own_out))
    else:
        place = jnp.stack((0 * comm.pair, 0 * comm.shard)).astype(jnp.int32)
        place = place.at[0].set(comm.pair)
        inner = lax.all_gather(own_in, "shard", axis=1, tiled=True)
        outer = lax.all_gather(own_out, "shard", axis=2, tiled=True)
        inner = jnp.concatenate((inner, inner), 0)
        outer = jnp.concatenate((outer, outer), 0)
        middle_cut = width // 2
        weights = (
            inner[:, :middle_cut], inner[:half, middle_cut:], outer[:, :, :middle_cut], outer[:half, :, middle_cut:]
        )

    x = pad(tokens)
    normed_a, packed, attended, middle, sent, prob = front(
        x, gains, proj_qkv, proj_out, router, pad(route_noise, EXTRA - experts), pad(expert_ids, 0, -1)
    )
    rows_all = jnp.stack(comm.line_gather(sent), 0)
    rows_all = jnp.concatenate((rows_all, comm.over_core(rows_all)), 0)
    total, back_all, grads_in, grads_out = expert_pass(place, rows_all, grad_rows, *weights)

    def reduce_expert(grad, axis, other):
        part = comm.scatter_shard(grad, axis)
        part = comm.scatter_heads(part, other).astype(BF)
        return comm.join(part, comm.over_heads(part), comm.head // 2, other)

    inner_grads = [reduce_expert(grads_in[e], 0, 1) for e in range(half)]
    outer_grads = [reduce_expert(grads_out[e], 1, 0) for e in range(half)]

    def collect(value):
        value = value[:4].astype(F32) + comm.over_core(value[4:]).astype(F32)
        return comm.line_scatter([value[k] for k in range(4)])

    moe_grad = collect(back_all)
    moe = collect(total)
    mixed = (unpad(middle) + unpad(moe)).astype(BF)
    grad_tokens, grad_qkv, grad_out, grad_small, grad_router = back(
        moe_grad, cot, x, middle, sent, prob, attended, packed, normed_a, gains, proj_qkv, proj_out, router
    )
    grad_tokens = unpad(grad_tokens)

    small = jnp.concatenate((grad_small, grad_router), 0).T.astype(BF)
    small = jnp.pad(small, ((0, 0), (0, 128 - small.shape[1])))
    shares = jnp.concatenate((grad_qkv, grad_out, small, jnp.zeros_like(small)), 1)
    shares = comm.scatter_core(shares, 1)
    shares = comm.scatter_shard(shares, 0)
    shares = comm.scatter_heads(shares, 1)
    cut = shares.shape[0] // 4
    rolled = [
        lax.dynamic_slice_in_dim(shares, ((comm.tensor + 4 - k) % 4) * cut, cut, 0) for k in range(4)
    ]
    summed = comm.line_scatter(rolled).astype(BF)
    pieces = comm.line_gather(summed)
    whole = jnp.zeros(shares.shape, BF)
    for k in range(4):
        whole = lax.dynamic_update_slice_in_dim(whole, pieces[k], ((comm.tensor + 4 - k) % 4) * cut, 0)
    whole = comm.join(whole, comm.over_heads(whole), comm.head // 2, 1)
    whole = comm.join(whole, comm.over_core(whole), comm.pair, 1).astype(F32)
    small = whole[:, 4 * width : 4 * width + 128]

    grad_in, grad_outer = jnp.stack(inner_grads, 0), jnp.stack(outer_grads, 0)
    grad_in = comm.join(grad_in, comm.over_core(grad_in), comm.pair, 0).astype(F32)
    grad_outer = comm.join(grad_outer, comm.over_core(grad_outer), comm.pair, 0).astype(F32)
    return (
        mixed,
        grad_tokens,
        small[:, 0],
        small[:, 1],
        whole[:, : 3 * width],
        whole[:, 3 * width : 4 * width],
        small[:, 2],
        small[:, 3],
        small[:, 4 : 4 + experts],
        grad_in,
        grad_outer,
    )


def solution(mesh):
    split = P(AXES, None)
    vector, matrix = P("shard"), P("shard", None)
    inner, outer = P(None, "shard", "tensor"), P(None, "tensor", "shard")
    return jax.shard_map(
        local,
        mesh=mesh,
        in_specs=(
            split, vector, vector, matrix, matrix, vector, vector, matrix, inner, outer, split, split, split,
        ),
        out_specs=(
            split, split, vector, vector, matrix, matrix, vector, vector, matrix, inner, outer,
        ),
        check_vma=False,
    )
```

```python
import jax
import jax.numpy as jnp
from jax import lax
from jax.experimental import pallas as pl
from jax.experimental.pallas import tpu as pltpu
from jax.sharding import PartitionSpec as P

HEAD_DIM = 64
SEQ = 197
EPS = 1e-06
AXES = ("shard", "heads", "tensor")
BF = jnp.bfloat16
F32 = jnp.float32


def contract_rows(left, right):
    return lax.dot_general(left, right, (((0,), (0,)), ((), ())), preferred_element_type=F32)


def contract_cols(left, right):
    return lax.dot_general(left, right, (((1,), (1,)), ((), ())), preferred_element_type=F32)


PAD = 208
TILE = 128
CHUNK = 256
FAR = 512.0
TALL = 16
LANES = 128
MASKED = -1e30
CUBIC = 0.044715
ROOT = (2.0 / 3.141592653589793) ** 0.5
BIG = 60 * 1024 * 1024
MESH = pl.DeviceIdType.MESH


def dot(left, right):
    return jnp.dot(left, right, preferred_element_type=F32)


def norm_parts(values):
    centred = values - jnp.mean(values, -1, keepdims=True)
    inverse = lax.rsqrt(jnp.mean(centred * centred, -1, keepdims=True) + EPS)
    return centred * inverse, inverse


def norm_back(grad, unit, inverse, gain):
    scaled = grad * gain
    along = jnp.mean(scaled * unit, -1, keepdims=True)
    return inverse * (scaled - jnp.mean(scaled, -1, keepdims=True) - unit * along)


def head_probs(query, keys, scale):
    scores = contract_cols(query, keys) * scale
    column = lax.broadcasted_iota(jnp.int32, scores.shape, 1)
    scores = jnp.where(column < SEQ, scores, MASKED)
    raised = jnp.exp(scores - jnp.max(scores, -1, keepdims=True))
    return raised / jnp.sum(raised, -1, keepdims=True)


def gain_row(small_ref, experts, index):
    row = slice(experts + index, experts + index + 1)
    return jnp.concatenate((small_ref[0, row, :], small_ref[1, row, :]), 1).astype(F32)


def router_rows(small_ref):
    return jnp.concatenate((small_ref[0], small_ref[1]), 1)


def attend(normed, at, qkv_ref, packed_ref):
    width = normed.shape[1]
    group = 3 * HEAD_DIM
    scale = HEAD_DIM ** (-0.5)
    lane = lax.broadcasted_iota(jnp.int32, (PAD, group), 1) // HEAD_DIM
    outs = []
    for double in range(width // group // 2):
        cols = pl.ds(double * 6 * group, 6 * group)
        packed = dot(normed, qkv_ref[:, cols])
        packed_ref[at, cols] = packed.astype(BF)
        for side in range(2):
            query, keys, values = (
                packed[:, (3 * side + k) * group : (3 * side + k + 1) * group].astype(BF)
                for k in range(3)
            )
            total = jnp.zeros((PAD, group), F32)
            for head in range(3):
                mask = lane == head
                probs = head_probs(jnp.where(mask, query, jnp.zeros_like(query)), keys, scale)
                total = jnp.where(mask, dot(probs.astype(BF), values), total)
            outs.append(total)
    return jnp.concatenate(outs, 1).astype(BF)


def route(normed, small_ref, noise, ids, experts):
    logits = contract_cols(router_rows(small_ref), normed) + noise
    row = lax.broadcasted_iota(jnp.int32, logits.shape, 0)
    logits = jnp.where(row < experts, logits, MASKED)
    raised = jnp.exp(logits - jnp.max(logits, 0, keepdims=True))
    probs = raised / jnp.sum(raised, 0, keepdims=True)
    chosen = ((row == ids[0:1]) | (row == ids[1:2])).astype(F32)
    shifted = row - experts
    flags = (((shifted == ids[0:1]) | (shifted == ids[1:2])) & (shifted >= 0)).astype(F32)
    return probs, probs * chosen + flags


def front_image(image, experts, x_ref, small_ref, qkv_ref, out_ref, noise_ref, ids_ref, keep):
    normed_ref, packed_ref, attended_ref, middle_ref = keep
    at = pl.ds(image * PAD, PAD)
    x = x_ref[at, :].astype(F32)
    unit, _ = norm_parts(x)
    normed = (unit * gain_row(small_ref, experts, 0) + gain_row(small_ref, experts, 1)).astype(BF)
    normed_ref[at, :] = normed
    attended = attend(normed, at, qkv_ref, packed_ref)
    attended_ref[at, :] = attended
    middle = x + dot(attended, out_ref[...])
    middle_ref[at, :] = middle
    unit, _ = norm_parts(middle)
    normed = (unit * gain_row(small_ref, experts, 2) + gain_row(small_ref, experts, 3)).astype(BF)
    cols = slice(image * PAD, (image + 1) * PAD)
    probs, flags = route(normed, small_ref, noise_ref[:, cols], ids_ref[:, cols], experts)
    return normed, probs, flags


def front_kernel(
    x_ref, small_ref, qkv_ref, out_ref, noise_ref, ids_ref,
    normed_ref, packed_ref, attended_ref, middle_ref, rows_ref, flag_ref, prob_ref,
):
    keep = (normed_ref, packed_ref, attended_ref, middle_ref)
    probs, flags = [], []
    for image in range(x_ref.shape[0] // PAD):
        normed, prob, flag = front_image(
            image, TALL // 2, x_ref, small_ref, qkv_ref, out_ref, noise_ref, ids_ref, keep
        )
        rows_ref[pl.ds(image * PAD, PAD), :] = normed
        probs.append(prob)
        flags.append(flag)
    prob_ref[...] = jnp.concatenate(probs, 1)
    flag_ref[...] = jnp.concatenate(flags, 1).astype(BF)


def front(x, small, qkv, out, noise, ids):
    rows, width = x.shape
    shape = jax.ShapeDtypeStruct
    return pl.pallas_call(
        front_kernel,
        out_shape=(
            shape((rows, width), BF),
            shape((rows, 3 * width), BF),
            shape((rows, width), BF),
            shape((rows, width), F32),
            shape((rows, width), BF),
            shape((TALL, rows), BF),
            shape((TALL, rows), F32),
        ),
        compiler_params=pltpu.CompilerParams(vmem_limit_bytes=BIG),
        cost_estimate=pl.CostEstimate(flops=8 * 10**9, bytes_accessed=10**7, transcendentals=10**6),
        name="front",
    )(x, small, qkv, out, noise, ids)


class Place:
    def __init__(self):
        shard, head, tensor = (lax.axis_index(axis) for axis in AXES)
        self.shard, self.head, self.tensor = shard, head, tensor
        self.pair, self.side = lax.rem(head, 2), lax.div(head, 2)
        self.across = (1 - shard, head, tensor)
        self.beside = (shard, lax.rem(head + 2, 4), tensor)
        self.twin = (shard, head + 1 - 2 * self.pair, tensor)
        self.above = (shard, head, lax.rem(tensor + 1, 4))
        self.below = (shard, head, lax.rem(tensor + 3, 4))

    def greet(self):
        barrier = pltpu.get_barrier_semaphore()
        for device in (self.across, self.beside, self.twin, self.above, self.below):
            pl.semaphore_signal(barrier, inc=1, device_id=device, device_id_type=MESH)
        pl.semaphore_wait(barrier, 5)


class Links:
    def __init__(self, send, recv):
        self.send, self.recv, self.used = send, recv, 0
        self.sent = []

    def copy(self, source, target, device):
        index = self.used
        self.used += 1
        return pltpu.make_async_remote_copy(
            src_ref=source, dst_ref=target, send_sem=self.send.at[index], recv_sem=self.recv.at[index],
            device_id=device, device_id_type=MESH,
        )

    def start(self, source, target, device):
        copy = self.copy(source, target, device)
        copy.start()
        self.sent.append((None, copy))
        return copy

    def finish(self):
        for when, copy in self.sent:
            if when is None:
                copy.wait_send()
            else:
                pl.when(when)(copy.wait_send)


class LineGather:
    def __init__(self, links, place, view, own, parts):
        self.links, self.place, self.view, self.own = links, place, view, own
        self.copies = {}
        self.parts = parts

    def start(self, part, step):
        t = self.place.tensor
        for name, slot, device, sends in (
            ("up", t - step, self.place.above, (t >= step) & (t < 3)),
            ("down", t + step, self.place.below, (t + step <= 3) & (t > 0)),
        ):
            slot = jnp.clip(slot, 0, 3)
            source = self.own(part) if step == 0 else self.view(slot, part)
            copy = self.links.copy(source, self.view(slot, part), device)
            pl.when(sends)(copy.start)
            self.links.sent.append((sends, copy))
            self.copies[name, part, step] = copy

    def wait(self, part, step, then=None):
        t = self.place.tensor
        for name, slot, comes in (("up", t - 1 - step, t >= step + 1), ("down", t + 1 + step, t + 1 + step <= 3)):
            copy = self.copies[name, part, step]

            @pl.when(comes)
            def _():
                copy.wait_recv()

    def arrived(self, step):
        t = self.place.tensor
        return (
            (jnp.clip(t - 1 - step, 0, 3), t >= step + 1),
            (jnp.clip(t + 1 + step, 0, 3), t + 1 + step <= 3),
        )


def head_kernel(
    x_ref, cot_ref, small_own, qkv_own, out_own, expert_in, expert_out, noise_ref, ids_ref,
    small_ref, qkv_ref, out_ref, normed_ref, packed_ref, attended_ref, middle_ref, prob_ref,
    rows_all, flags_all, cot_all, got_in, got_out,
    sent_rows, sent_flags, send, recv, local_sem,
):
    place = Place()
    links = Links(send, recv)
    width = x_ref.shape[1]
    experts = expert_in.shape[0]
    depth = qkv_own.shape[0]
    quarter = depth // 4
    shard, pair, side, tensor = place.shard, place.pair, place.side, place.tensor
    mine = pair * 4 + tensor
    place.greet()

    def dense_rows(owner, across_side, across_pair, start, size):
        return pl.ds(pl.multiple_of(owner * depth + (across_side * 2 + across_pair) * quarter + start, TALL), size)

    pieces = ((qkv_own, qkv_ref, 0, quarter // 2), (qkv_own, qkv_ref, quarter // 2, quarter // 2), (out_own, out_ref, 0, quarter))
    smalls = links.start(small_own, small_ref.at[shard], place.across)
    cross = []
    for own, full, start, size in pieces:
        source = own.at[pl.ds(pl.multiple_of((side * 2 + pair) * quarter + start, TALL), size), :]
        cross.append(links.start(source, full.at[dense_rows(shard, side, pair, start, size), :], place.across))
    here = pl.ds(pl.multiple_of(shard * depth, TALL), depth)
    locals_ = [
        pltpu.make_async_copy(qkv_own, qkv_ref.at[here, :], local_sem.at[0]),
        pltpu.make_async_copy(out_own, out_ref.at[here, :], local_sem.at[1]),
        pltpu.make_async_copy(small_own, small_ref.at[shard], local_sem.at[2]),
        pltpu.make_async_copy(cot_ref, cot_all.at[mine], local_sem.at[3]),
    ]
    for copy in locals_:
        copy.start()

    def slots(array):
        def view(slot, part):
            return array.at[pair * 4 + slot, pl.ds(part * PAD, PAD), :]

        return view

    cot_line = LineGather(links, place, slots(cot_all), lambda part: cot_ref.at[pl.ds(part * PAD, PAD), :], 2)
    for part in range(2):
        cot_line.start(part, 0)

    beside, twins = [], []
    for index, (own, full, start, size) in enumerate(pieces):
        cross[index].wait_recv()
        rows = full.at[dense_rows(1 - shard, side, pair, start, size), :]
        beside.append(links.start(rows, rows, place.beside))
        twins.append(links.start(rows, rows, place.twin))
    for index, (own, full, start, size) in enumerate(pieces):
        beside[index].wait_recv()
        rows = full.at[dense_rows(1 - shard, 1 - side, pair, start, size), :]
        twins.append(links.start(rows, rows, place.twin))

    def expert_item(item):
        index = side * 2 + item // 2
        source, target = (expert_in, got_in) if item % 2 == 0 else (expert_out, got_out)
        return source.at[pair * (experts // 2) + index], target.at[index]

    fetched = [links.start(*expert_item(item), place.across) for item in range(4)]
    for part in range(2):
        cot_line.wait(part, 0)
        cot_line.start(part, 1)
    smalls.wait_recv()
    for copy in twins:
        copy.wait_recv()
    for copy in locals_:
        copy.wait()

    keep = (normed_ref, packed_ref, attended_ref, middle_ref)
    row_line = LineGather(links, place, slots(rows_all), lambda part: sent_rows.at[pl.ds(part * PAD, PAD), :], 2)
    flag_line = LineGather(links, place, lambda slot, part: flags_all.at[pair * 4 + slot], lambda part: sent_flags, 1)
    probs, flags = [], []
    twin_rows = []
    forwarded = []

    def forward_expert(item):
        fetched[item].wait_recv()
        _, target = expert_item(item)
        forwarded.append(links.start(target, target, place.beside))

    for image in range(2):
        normed, prob, flag = front_image(
            image, experts, x_ref, small_ref, qkv_ref, out_ref, noise_ref, ids_ref, keep
        )
        at = pl.ds(image * PAD, PAD)
        sent_rows[at, :] = normed
        row_line.start(image, 0)
        twin_rows.append(links.start(sent_rows.at[at, :], rows_all.at[mine, at, :], place.twin))
        probs.append(prob)
        flags.append(flag)
        if image == 0:
            for part in range(2):
                cot_line.wait(part, 1)
                cot_line.start(part, 2)
    prob_ref[...] = jnp.concatenate(probs, 1)
    sent_flags[...] = jnp.concatenate(flags, 1).astype(BF)
    flag_line.start(0, 0)
    twin_flags = [links.start(sent_flags, flags_all.at[mine], place.twin)]
    keep_own = [
        pltpu.make_async_copy(sent_rows, rows_all.at[mine], local_sem.at[0]),
        pltpu.make_async_copy(sent_flags, flags_all.at[mine], local_sem.at[1]),
    ]
    for copy in keep_own:
        copy.start()

    def share(line, array, part, step, copies, whole):
        for slot, comes in line.arrived(step):
            index = pair * 4 + slot
            ref = array.at[index] if whole else array.at[index, pl.ds(part * PAD, PAD), :]
            copy = links.copy(ref, ref, place.twin)
            pl.when(comes)(copy.start)
            links.sent.append((comes, copy))
            copies.append((comes, copy))

    twin_steps = []
    forward_expert(0)
    for step in range(3):
        for part in range(2):
            row_line.wait(part, step)
            if step < 2:
                row_line.start(part, step + 1)
            share(row_line, rows_all, part, step, twin_steps, False)
        flag_line.wait(0, step)
        if step < 2:
            flag_line.start(0, step + 1)
        share(flag_line, flags_all, 0, step, twin_steps, True)
        if step == 0:
            for part in range(2):
                cot_line.wait(part, 2)
            ours = cot_all.at[pl.ds(pair * 4, 4)]
            twin_cot = links.start(ours, ours, place.twin)
        forward_expert(step + 1)

    for copy in twin_rows + twin_flags + [twin_cot] + forwarded:
        copy.wait_recv()
    for comes, copy in twin_steps:
        pl.when(comes)(copy.wait_recv)
    for copy in keep_own:
        copy.wait()
    links.finish()


def head(x, cot, small, qkv, out, expert_in, expert_out, noise, ids):
    rows, width = x.shape
    depth = qkv.shape[0]
    count = expert_in.shape[0] // 2
    shape = jax.ShapeDtypeStruct
    anywhere = pl.BlockSpec(memory_space=pl.ANY)
    vmem = pl.BlockSpec(memory_space=pltpu.VMEM)
    return pl.pallas_call(
        head_kernel,
        out_shape=(
            shape((2, TALL, depth), BF),
            shape((width, 3 * width), BF),
            shape((width, width), BF),
            shape((rows, width), BF),
            shape((rows, 3 * width), BF),
            shape((rows, width), BF),
            shape((rows, width), F32),
            shape((TALL, rows), F32),
            shape((8, rows, width), BF),
            shape((8, TALL, rows), BF),
            shape((8, rows, width), BF),
            shape((count,) + expert_in.shape[1:], BF),
            shape((count,) + expert_out.shape[1:], BF),
        ),
        in_specs=[vmem] * 3 + [anywhere] * 4 + [vmem] * 2,
        out_specs=(vmem,) * 8 + (anywhere,) * 5,
        scratch_shapes=[
            pltpu.VMEM((rows, width), BF),
            pltpu.VMEM((TALL, rows), BF),
            pltpu.SemaphoreType.DMA((96,)),
            pltpu.SemaphoreType.DMA((96,)),
            pltpu.SemaphoreType.DMA((4,)),
        ],
        compiler_params=pltpu.CompilerParams(vmem_limit_bytes=BIG, collective_id=1, has_side_effects=True),
        cost_estimate=pl.CostEstimate(flops=8 * 10**9, bytes_accessed=3 * 10**7, transcendentals=10**6),
        name="head",
    )(x, cot, small, qkv, out, expert_in, expert_out, noise, ids)


def expert_kernel(
    place_ref, rows_ref, flag_ref, cot_ref, own_in, got_in, own_out, got_out,
    total_ref, back_ref, gate_ref, grad_in, grad_out,
    inner, outer, picked, grads, gate, active, hidden_grad, made, made_back, made_gate, ranks, sum_in, sum_out,
    stage_in, stage_out, load_sem, store_sem,
):
    blocks, length, width = cot_ref.shape
    count = got_in.shape[0]
    depth = got_in.shape[1]
    pair, shard = place_ref[0], place_ref[1]
    experts = 2 * count
    capacity = blocks * TILE

    def loads(expert, slot):
        mine = pl.ds(pl.multiple_of(shard * depth, LANES), depth)
        other = pl.ds(pl.multiple_of((1 - shard) * depth, LANES), depth)
        index = pair * count + expert
        return (
            pltpu.make_async_copy(own_in.at[index], inner.at[slot, mine, :], load_sem.at[slot, 0]),
            pltpu.make_async_copy(got_in.at[expert], inner.at[slot, other, :], load_sem.at[slot, 1]),
            pltpu.make_async_copy(own_out.at[index], outer.at[slot, :, mine], load_sem.at[slot, 2]),
            pltpu.make_async_copy(got_out.at[expert], outer.at[slot, :, other], load_sem.at[slot, 3]),
        )

    def stores(expert, slot):
        return (
            pltpu.make_async_copy(stage_in.at[slot], grad_in.at[expert], store_sem.at[slot, 0]),
            pltpu.make_async_copy(stage_out.at[slot], grad_out.at[expert], store_sem.at[slot, 1]),
        )

    for copy in loads(0, 0):
        copy.start()
    ahead = lax.broadcasted_iota(jnp.int32, (length, length), 0)
    behind = lax.broadcasted_iota(jnp.int32, (length, length), 1)
    order = jnp.where(behind < ahead, 1.0, jnp.where(behind == ahead, FAR, 0.0)).astype(BF)

    def rank(block, carry):
        ranks[block] = contract_cols(flag_ref[block], order) - FAR
        total_ref[block] = jnp.zeros(total_ref.shape[1:], BF)
        back_ref[block] = jnp.zeros(back_ref.shape[1:], BF)
        gate_ref[block] = jnp.zeros(gate_ref.shape[1:], BF)
        return carry

    lax.fori_loop(0, blocks, rank, 0)

    for expert in range(count):
        slot = expert % 2
        if expert + 1 < count:
            for copy in loads(expert + 1, 1 - slot):
                copy.start()
        line = pl.ds(experts + pair * count + expert, 1)
        highest = ranks[0, line, :]
        for block in range(1, blocks):
            highest = jnp.maximum(highest, ranks[block, line, :])
        passes = (jnp.maximum(jnp.max(highest), -1.0).astype(jnp.int32) + TILE) // TILE
        sum_in[...] = jnp.zeros(sum_in.shape, F32)
        sum_out[...] = jnp.zeros(sum_out.shape, F32)
        for copy in loads(expert, slot):
            copy.wait()

        def one_pass(step, carry):
            base = (step * TILE).astype(F32)
            slots = lax.broadcasted_iota(jnp.int32, (TILE, length), 0).astype(F32) + base

            def take(block, carry):
                choose = (ranks[block, line, :] == slots).astype(BF)
                at = pl.ds(pl.multiple_of(block * TILE, TILE), TILE)
                picked[at, :] = dot(choose, rows_ref[block]).astype(BF)
                grads[at, :] = dot(choose, cot_ref[block]).astype(BF)
                columns = contract_cols(choose, flag_ref[block])
                lane = lax.broadcasted_iota(jnp.int32, (TILE, TALL), 1)
                column = jnp.where(lane == pair * count + expert, columns, 0.0)
                gate[at, :] = jnp.broadcast_to(jnp.sum(column, -1, keepdims=True), (TILE, LANES))
                return carry

            lax.fori_loop(0, blocks, take, 0, unroll=2)

            def chunk(index, carry):
                at = pl.ds(pl.multiple_of(index * CHUNK, CHUNK), CHUNK)
                value = dot(picked[at, :], inner[slot])
                grad_active = contract_cols(grads[at, :], outer[slot])
                gate_column = gate[at, 0:1]
                square = value * value
                bent = jnp.tanh(ROOT * value * (1.0 + CUBIC * square))
                plus = 0.5 * (1.0 + bent)
                bowed = value * plus
                slope = plus + (0.5 * ROOT) * value * (1.0 - bent * bent) * (1.0 + (3.0 * CUBIC) * square)
                active[at, :] = (bowed * gate_column).astype(BF)
                back = (grad_active * gate_column * slope).astype(BF)
                hidden_grad[at, :] = back
                lane = lax.broadcasted_iota(jnp.int32, (CHUNK, TALL), 1)
                gate_grad = jnp.sum(grad_active * bowed, -1, keepdims=True)
                made_gate[at, :] = jnp.where(lane == pair * count + expert, gate_grad, 0.0).astype(BF)
                made[at, :] = dot(active[at, :], outer[slot]).astype(BF)
                made_back[at, :] = contract_cols(back, inner[slot]).astype(BF)
                return carry

            lax.fori_loop(0, capacity // CHUNK, chunk, 0)
            hidden = sum_in.shape[1]
            for start in range(0, hidden, CHUNK):
                at = pl.ds(start, CHUNK)
                sum_out[at, :] += contract_rows(active[:, at], grads[...])
            for start in range(0, width, CHUNK):
                at = pl.ds(start, CHUNK)
                sum_in[at, :] += contract_rows(picked[:, at], hidden_grad[...])

            def give(block, carry):
                choose = (ranks[block, line, :] == slots).astype(BF)
                at = pl.ds(pl.multiple_of(block * TILE, TILE), TILE)
                total_ref[block] = (total_ref[block].astype(F32) + contract_rows(choose, made[at, :])).astype(BF)
                back_ref[block] = (back_ref[block].astype(F32) + contract_rows(choose, made_back[at, :])).astype(BF)
                gate_ref[block] = (gate_ref[block].astype(F32) + contract_rows(made_gate[at, :], choose)).astype(BF)
                return carry

            lax.fori_loop(0, blocks, give, 0, unroll=2)
            return carry

        lax.fori_loop(0, passes, one_pass, 0)
        if expert >= 2:
            for copy in stores(expert - 2, slot):
                copy.wait()
        stage_in[slot] = sum_in[...].astype(BF)
        stage_out[slot] = sum_out[...].astype(BF)
        for copy in stores(expert, slot):
            copy.start()
    for expert in range(max(count - 2, 0), count):
        for copy in stores(expert, expert % 2):
            copy.wait()


def expert_pass(place, rows, flags, cot, own_in, got_in, own_out, got_out):
    blocks, length, width = cot.shape
    count, _, hidden = got_in.shape
    capacity = blocks * TILE
    shape = jax.ShapeDtypeStruct
    anywhere = pl.BlockSpec(memory_space=pl.ANY)
    vmem = pl.BlockSpec(memory_space=pltpu.VMEM)
    return pl.pallas_call(
        expert_kernel,
        out_shape=(
            shape((blocks, length, width), BF),
            shape((blocks, length, width), BF),
            shape((blocks, TALL, length), BF),
            shape((count, width, hidden), BF),
            shape((count, hidden, width), BF),
        ),
        in_specs=[pl.BlockSpec(memory_space=pltpu.SMEM), vmem, vmem, vmem] + [anywhere] * 4,
        out_specs=(vmem, vmem, vmem, anywhere, anywhere),
        scratch_shapes=[
            pltpu.VMEM((2, width, hidden), BF),
            pltpu.VMEM((2, hidden, width), BF),
            pltpu.VMEM((capacity, width), BF),
            pltpu.VMEM((capacity, width), BF),
            pltpu.VMEM((capacity, LANES), F32),
            pltpu.VMEM((capacity, hidden), BF),
            pltpu.VMEM((capacity, hidden), BF),
            pltpu.VMEM((capacity, width), BF),
            pltpu.VMEM((capacity, width), BF),
            pltpu.VMEM((capacity, TALL), BF),
            pltpu.VMEM((blocks, TALL, length), F32),
            pltpu.VMEM((width, hidden), F32),
            pltpu.VMEM((hidden, width), F32),
            pltpu.VMEM((2, width, hidden), BF),
            pltpu.VMEM((2, hidden, width), BF),
            pltpu.SemaphoreType.DMA((2, 4)),
            pltpu.SemaphoreType.DMA((2, 2)),
        ],
        compiler_params=pltpu.CompilerParams(vmem_limit_bytes=BIG),
        cost_estimate=pl.CostEstimate(flops=50 * 10**9, bytes_accessed=5 * 10**7, transcendentals=10**6),
        name="experts",
    )(place, rows, flags, cot, own_in, got_in, own_out, got_out)


def back_attention(at, grad_proj, packed_ref, out_ref, stacked):
    width = grad_proj.shape[1]
    group = 3 * HEAD_DIM
    scale = HEAD_DIM ** (-0.5)
    lanes = lax.broadcasted_iota(jnp.int32, (PAD, group), 1) // HEAD_DIM
    for double in range(width // group // 2):
        made = []
        packed = packed_ref[at, pl.ds(double * 6 * group, 6 * group)]
        for side in range(2):
            query, keys, values = (
                packed[:, (3 * side + k) * group : (3 * side + k + 1) * group] for k in range(3)
            )
            index = double * 2 + side
            grad_att = contract_cols(grad_proj, out_ref[pl.ds(index * group, group), :]).astype(BF)
            outs = [jnp.zeros((PAD, group), F32) for _ in range(3)]
            for head in range(3):
                mask = lanes == head
                probs = head_probs(jnp.where(mask, query, jnp.zeros_like(query)), keys, scale)
                part = jnp.where(mask, grad_att, jnp.zeros_like(grad_att))
                grad_weights = contract_cols(part, values)
                inner_sum = jnp.sum(probs * grad_weights, -1, keepdims=True)
                grad_scores = (probs * (grad_weights - inner_sum)).astype(BF)
                outs[0] = jnp.where(mask, dot(grad_scores, keys), outs[0])
                outs[1] = jnp.where(mask, contract_rows(grad_scores, query), outs[1])
                outs[2] = jnp.where(mask, contract_rows(probs.astype(BF), grad_att), outs[2])
            made += [outs[0] * scale, outs[1] * scale, outs[2]]
        stacked[at, pl.ds(double * 6 * group, 6 * group)] = jnp.concatenate(made, 1).astype(BF)


def back_middle(at, moe, gates, cot, middle, rows, probs, flags, small_ref, sums):
    experts = TALL // 2
    row = lax.broadcasted_iota(jnp.int32, flags.shape, 0)
    chosen = jnp.where(row < experts, pltpu.roll(flags, experts, 0), 0.0)
    asked = gates * chosen
    grad_logits = probs * (asked - jnp.sum(probs * asked, 0, keepdims=True))
    coarse = grad_logits.astype(BF)
    fine = (grad_logits - coarse.astype(F32)).astype(BF)
    router = router_rows(small_ref)
    sums[4] = sums[4] + dot(coarse, rows) + dot(fine, rows)
    grad = moe + contract_rows(coarse, router) + contract_rows(fine, router)
    unit, inverse = norm_parts(middle)
    sums[2] = sums[2] + jnp.sum(grad * unit, 0, keepdims=True)
    sums[3] = sums[3] + jnp.sum(grad, 0, keepdims=True)
    return cot + norm_back(grad, unit, inverse, gain_row(small_ref, experts, 2))


def back_kernel(
    moe_ref, gate_ref, cot_ref, x_ref, middle_ref, rows_ref, flag_ref, prob_ref, attended_ref, packed_ref, normed_ref,
    small_ref, qkv_ref, out_ref,
    tokens_ref, grad_qkv, grad_out, grad_small,
    stacked, projected,
):
    rows, width = x_ref.shape
    experts = TALL // 2
    sums = [jnp.zeros((1, width), F32) for _ in range(4)] + [jnp.zeros((TALL, width), F32)]
    for image in range(rows // PAD):
        at = pl.ds(image * PAD, PAD)
        cols = slice(image * PAD, (image + 1) * PAD)
        grad_middle = back_middle(
            at, moe_ref[at, :].astype(F32), gate_ref[:, cols].astype(F32), cot_ref[at, :].astype(F32),
            middle_ref[at, :], rows_ref[at, :], prob_ref[:, cols], flag_ref[:, cols].astype(F32), small_ref, sums,
        )
        grad_proj = grad_middle.astype(BF)
        projected[at, :] = grad_proj
        back_attention(at, grad_proj, packed_ref, out_ref, stacked)
        grad = contract_cols(stacked[at, :], qkv_ref[...])
        unit, inverse = norm_parts(x_ref[at, :].astype(F32))
        sums[0] = sums[0] + jnp.sum(grad * unit, 0, keepdims=True)
        sums[1] = sums[1] + jnp.sum(grad, 0, keepdims=True)
        tokens_ref[at, :] = (grad_middle + norm_back(grad, unit, inverse, gain_row(small_ref, experts, 0))).astype(BF)
    grad_small[...] = jnp.concatenate([sums[4][0:experts]] + sums[:4] + [jnp.zeros((4, width), F32)], 0).astype(BF)
    grad_out[...] = contract_rows(attended_ref[...], projected[...]).astype(BF)
    for third in range(3):
        cols = pl.ds(third * width, width)
        grad_qkv[:, cols] = contract_rows(normed_ref[...], stacked[:, cols]).astype(BF)


def back(moe, gates, cot, x, middle, sent, flags, prob, attended, packed, normed, small, qkv, out):
    rows, width = x.shape
    shape = jax.ShapeDtypeStruct
    return pl.pallas_call(
        back_kernel,
        out_shape=(
            shape((rows, width), BF),
            shape((width, 3 * width), BF),
            shape((width, width), BF),
            shape((TALL, width), BF),
        ),
        scratch_shapes=[pltpu.VMEM((rows, 3 * width), BF), pltpu.VMEM((rows, width), BF)],
        compiler_params=pltpu.CompilerParams(vmem_limit_bytes=BIG),
        cost_estimate=pl.CostEstimate(flops=16 * 10**9, bytes_accessed=2 * 10**7, transcendentals=10**6),
        name="back",
    )(moe, gates, cot, x, middle, sent, flags, prob, attended, packed, normed, small, qkv, out)


class Comm:
    def __init__(self):
        self.sizes = tuple(lax.axis_size(axis) for axis in AXES)
        self.shard = lax.axis_index("shard")
        self.head = lax.axis_index("heads")
        self.tensor = lax.axis_index("tensor")
        self.pair = self.head % 2

    def move(self, value, step):
        shards, heads, tensors = self.sizes
        pairs = []
        for s in range(shards):
            for h in range(heads):
                for t in range(tensors):
                    to = step(s, h, t)
                    if 0 <= to[2] < tensors:
                        source = (s * heads + h) * tensors + t
                        pairs.append((source, (to[0] * heads + to[1]) * tensors + to[2]))
        return lax.ppermute(value, AXES, pairs)

    def over_core(self, value):
        return self.move(value, lambda s, h, t: (s, h ^ 1, t))

    def over_heads(self, value):
        return self.move(value, lambda s, h, t: (s, (h + 2) % 4, t))

    def over_shard(self, value):
        return self.move(value, lambda s, h, t: (1 - s, h, t))

    def up(self, value):
        return self.move(value, lambda s, h, t: (s, h, t + 1))

    def down(self, value):
        return self.move(value, lambda s, h, t: (s, h, t - 1))

    def halves(self, value, index, axis):
        size = value.shape[axis] // 2
        mine = lax.dynamic_slice_in_dim(value, index * size, size, axis)
        other = lax.dynamic_slice_in_dim(value, (1 - index) * size, size, axis)
        return mine, other

    def join(self, mine, other, index, axis):
        first = jnp.where(index == 0, mine, other)
        second = jnp.where(index == 0, other, mine)
        return jnp.concatenate((first, second), axis)

    def gather_shard(self, value, axis):
        if self.sizes[0] != 2:
            return lax.all_gather(value, "shard", axis=axis, tiled=True)
        return self.join(value, self.over_shard(value), self.shard, axis)

    def gather_shard_split(self, value, axis, cut):
        if self.sizes[0] != 2:
            return lax.all_gather(value, "shard", axis=axis, tiled=True)
        mine, _ = self.halves(value, self.pair, cut)
        got = self.over_shard(mine)
        both = self.join(got, self.over_core(got), self.pair, cut)
        return self.join(value, both, self.shard, axis)

    def scatter_shard(self, value, axis):
        if self.sizes[0] != 2:
            return lax.psum_scatter(value.astype(BF), "shard", scatter_dimension=axis, tiled=True).astype(F32)
        mine, other = self.halves(value, self.shard, axis)
        return mine.astype(F32) + self.over_shard(other.astype(BF)).astype(F32)

    def scatter_core(self, value, axis):
        mine, other = self.halves(value, self.pair, axis)
        return mine.astype(F32) + self.over_core(other.astype(BF)).astype(F32)

    def scatter_heads(self, value, axis):
        mine, other = self.halves(value, self.head // 2, axis)
        return mine.astype(F32) + self.over_heads(other.astype(BF)).astype(F32)

    def line_gather(self, value):
        ups, downs = [value], [value]
        for _ in range(3):
            ups.append(self.up(ups[-1]))
            downs.append(self.down(downs[-1]))
        out = [value]
        for back in (1, 2, 3):
            out.append(jnp.where(self.tensor >= back, ups[back], downs[4 - back]))
        return out

    def line_scatter(self, parts):
        high, low = parts[1].astype(BF), parts[3].astype(BF)
        high = (parts[2].astype(F32) + self.up(high).astype(F32)).astype(BF)
        low = (parts[2].astype(F32) + self.down(low).astype(F32)).astype(BF)
        high = (parts[3].astype(F32) + self.up(high).astype(F32)).astype(BF)
        low = (parts[1].astype(F32) + self.down(low).astype(F32)).astype(BF)
        return parts[0].astype(F32) + self.up(high).astype(F32) + self.down(low).astype(F32)

    def join_slots(self, values):
        own = jnp.zeros((4,) + values[0].shape, values[0].dtype)
        for back, value in enumerate(values):
            own = lax.dynamic_update_index_in_dim(own, value, (self.tensor + 4 - back) % 4, 0)
        return self.join(own, self.over_core(own), self.pair, 0)

    def collect(self, value):
        mine, other = self.halves(value, self.pair, 0)
        mine = mine.astype(F32) + self.over_core(other).astype(F32)
        return self.line_scatter(
            [lax.dynamic_index_in_dim(mine, (self.tensor + 4 - k) % 4, 0, False) for k in range(4)]
        )


def local(
    tokens, ln1_gain, ln1_bias, qkv_weight, out_weight, ln2_gain, ln2_bias, router_weight,
    expert_in, expert_out, route_noise, expert_ids, cotangent,
):
    comm = Comm()
    rows, width = tokens.shape
    experts = expert_in.shape[0]
    images = rows // SEQ
    half = experts // 2
    padded = images * PAD

    def pad(value):
        value = value.reshape(images, SEQ, value.shape[1])
        return jnp.pad(value, ((0, 0), (0, PAD - SEQ), (0, 0))).reshape(padded, value.shape[2])

    def pad_turned(value, tall, fill):
        value = value.reshape(images, SEQ, value.shape[1]).transpose(2, 0, 1)
        value = jnp.pad(value, ((0, tall - value.shape[0]), (0, 0), (0, PAD - SEQ)), constant_values=fill)
        return value.reshape(tall, padded)

    def unpad(value):
        return value.reshape(images, PAD, value.shape[1])[:, :SEQ].reshape(rows, value.shape[1])

    small = jnp.concatenate(
        (router_weight.T, ln1_gain[None], ln1_bias[None], ln2_gain[None], ln2_bias[None]), 0
    )
    small = jnp.pad(small, ((0, TALL - small.shape[0]), (0, 0)))
    cot, x = pad(cotangent), pad(tokens)
    noise, ids = pad_turned(route_noise, TALL, 0), pad_turned(expert_ids, 8, -1)
    place = jnp.stack((comm.pair, comm.shard if comm.sizes[0] == 2 else 0 * comm.shard)).astype(jnp.int32)
    if comm.sizes[0] == 2:
        (
            small, proj_qkv, proj_out, normed_a, packed, attended, middle, prob,
            rows_all, flags_all, grad_rows, got_in, got_out,
        ) = head(x, cot, small, qkv_weight, out_weight, expert_in, expert_out, noise, ids)
        weights = (expert_in, got_in, expert_out, got_out)
        mine = comm.pair * 4 + comm.tensor
        sent = lax.dynamic_index_in_dim(rows_all, mine, 0, False)
        flags = lax.dynamic_index_in_dim(flags_all, mine, 0, False)
    else:
        small = lax.all_gather(small, "shard", axis=1, tiled=True)
        small = small.reshape(TALL, 2, width // 2).transpose(1, 0, 2)
        proj_qkv = lax.all_gather(qkv_weight, "shard", axis=0, tiled=True)
        proj_out = lax.all_gather(out_weight, "shard", axis=0, tiled=True)
        inner = lax.all_gather(lax.dynamic_slice_in_dim(expert_in, comm.pair * half, half, 0), "shard", axis=1, tiled=True)
        outer = lax.all_gather(lax.dynamic_slice_in_dim(expert_out, comm.pair * half, half, 0), "shard", axis=2, tiled=True)
        cut = width // 2
        weights = (
            jnp.concatenate((inner[:, :cut], inner[:, :cut]), 0), inner[:, cut:],
            jnp.concatenate((outer[:, :, :cut], outer[:, :, :cut]), 0), outer[:, :, cut:],
        )
        normed_a, packed, attended, middle, sent, flags, prob = front(x, small, proj_qkv, proj_out, noise, ids)

        def gather(value):
            return comm.join_slots(comm.line_gather(value))

        grad_rows, rows_all, flags_all = gather(cot), gather(sent), gather(flags)
    total, back_all, gate_all, grads_in, grads_out = expert_pass(place, rows_all, flags_all, grad_rows, *weights)

    def reduce_expert(grad, axis, other):
        part = comm.scatter_shard(grad, axis)
        part = comm.scatter_heads(part, other).astype(BF)
        return comm.join(part, comm.over_heads(part), comm.head // 2, other)

    inner_grads = [reduce_expert(grads_in[e], 0, 1) for e in range(half)]
    outer_grads = [reduce_expert(grads_out[e], 1, 0) for e in range(half)]

    moe_grad = comm.collect(back_all)
    gate_grad = comm.collect(gate_all)
    moe = comm.collect(total)
    mixed = (unpad(middle) + unpad(moe)).astype(BF)
    grad_tokens, grad_qkv, grad_out, grad_small = back(
        moe_grad, gate_grad, cot, x, middle, sent, flags, prob, attended, packed, normed_a, small, proj_qkv, proj_out
    )
    grad_tokens = unpad(grad_tokens)

    grad_small = jnp.pad(grad_small.T, ((0, 0), (0, 128 - TALL)))
    shares = jnp.concatenate((grad_qkv, grad_out, grad_small, jnp.zeros_like(grad_small)), 1)
    shares = comm.scatter_core(shares, 1)
    shares = comm.scatter_shard(shares, 0)
    shares = comm.scatter_heads(shares, 1)
    cut = shares.shape[0] // 4
    rolled = [
        lax.dynamic_slice_in_dim(shares, ((comm.tensor + 4 - k) % 4) * cut, cut, 0) for k in range(4)
    ]
    summed = comm.line_scatter(rolled).astype(BF)
    pieces = comm.line_gather(summed)
    whole = jnp.zeros(shares.shape, BF)
    for k in range(4):
        whole = lax.dynamic_update_slice_in_dim(whole, pieces[k], ((comm.tensor + 4 - k) % 4) * cut, 0)
    whole = comm.join(whole, comm.over_heads(whole), comm.head // 2, 1)
    whole = comm.join(whole, comm.over_core(whole), comm.pair, 1).astype(F32)
    small = whole[:, 4 * width : 4 * width + 128]

    grad_in, grad_outer = jnp.stack(inner_grads, 0), jnp.stack(outer_grads, 0)
    grad_in = comm.join(grad_in, comm.over_core(grad_in), comm.pair, 0).astype(F32)
    grad_outer = comm.join(grad_outer, comm.over_core(grad_outer), comm.pair, 0).astype(F32)
    return (
        mixed,
        grad_tokens,
        small[:, experts],
        small[:, experts + 1],
        whole[:, : 3 * width],
        whole[:, 3 * width : 4 * width],
        small[:, experts + 2],
        small[:, experts + 3],
        small[:, :experts],
        grad_in,
        grad_outer,
    )


def solution(mesh):
    split = P(AXES, None)
    vector, matrix = P("shard"), P("shard", None)
    inner, outer = P(None, "shard", "tensor"), P(None, "tensor", "shard")
    return jax.shard_map(
        local,
        mesh=mesh,
        in_specs=(
            split, vector, vector, matrix, matrix, vector, vector, matrix, inner, outer, split, split, split,
        ),
        out_specs=(
            split, split, vector, vector, matrix, matrix, vector, vector, matrix, inner, outer,
        ),
        check_vma=False,
    )
```

```python
import jax
import jax.numpy as jnp
from jax import lax
from jax.experimental import pallas as pl
from jax.experimental.pallas import tpu as pltpu
from jax.sharding import PartitionSpec as P

HEAD_DIM = 64
SEQ = 197
EPS = 1e-06
AXES = ("shard", "heads", "tensor")
BF = jnp.bfloat16
F32 = jnp.float32


def contract_rows(left, right):
    return lax.dot_general(left, right, (((0,), (0,)), ((), ())), preferred_element_type=F32)


def contract_cols(left, right):
    return lax.dot_general(left, right, (((1,), (1,)), ((), ())), preferred_element_type=F32)


PAD = 208
TILE = 128
CHUNK = 256
FAR = 512.0
TALL = 16
LANES = 128
MASKED = -1e30
CUBIC = 0.044715
ROOT = (2.0 / 3.141592653589793) ** 0.5
BIG = 60 * 1024 * 1024
MESH = pl.DeviceIdType.MESH


def dot(left, right):
    return jnp.dot(left, right, preferred_element_type=F32)


def norm_parts(values):
    centred = values - jnp.mean(values, -1, keepdims=True)
    inverse = lax.rsqrt(jnp.mean(centred * centred, -1, keepdims=True) + EPS)
    return centred * inverse, inverse


def norm_back(grad, unit, inverse, gain):
    scaled = grad * gain
    along = jnp.mean(scaled * unit, -1, keepdims=True)
    return inverse * (scaled - jnp.mean(scaled, -1, keepdims=True) - unit * along)


def head_probs(query, keys, scale):
    scores = contract_cols(query, keys) * scale
    column = lax.broadcasted_iota(jnp.int32, scores.shape, 1)
    scores = jnp.where(column < SEQ, scores, MASKED)
    raised = jnp.exp(scores - jnp.max(scores, -1, keepdims=True))
    return raised / jnp.sum(raised, -1, keepdims=True)


def gain_row(small_ref, experts, index):
    row = slice(experts + index, experts + index + 1)
    return jnp.concatenate((small_ref[0, row, :], small_ref[1, row, :]), 1).astype(F32)


def router_rows(small_ref):
    return jnp.concatenate((small_ref[0], small_ref[1]), 1)


def attend(normed, at, qkv_ref, packed_ref):
    width = normed.shape[1]
    group = 3 * HEAD_DIM
    scale = HEAD_DIM ** (-0.5)
    lane = lax.broadcasted_iota(jnp.int32, (PAD, group), 1) // HEAD_DIM
    outs = []
    for double in range(width // group // 2):
        cols = pl.ds(double * 6 * group, 6 * group)
        packed = dot(normed, qkv_ref[:, cols])
        packed_ref[at, cols] = packed.astype(BF)
        for side in range(2):
            query, keys, values = (
                packed[:, (3 * side + k) * group : (3 * side + k + 1) * group].astype(BF)
                for k in range(3)
            )
            total = jnp.zeros((PAD, group), F32)
            for head in range(3):
                mask = lane == head
                probs = head_probs(jnp.where(mask, query, jnp.zeros_like(query)), keys, scale)
                total = jnp.where(mask, dot(probs.astype(BF), values), total)
            outs.append(total)
    return jnp.concatenate(outs, 1).astype(BF)


def route(normed, small_ref, noise, ids, experts):
    logits = contract_cols(router_rows(small_ref), normed) + noise
    row = lax.broadcasted_iota(jnp.int32, logits.shape, 0)
    logits = jnp.where(row < experts, logits, MASKED)
    raised = jnp.exp(logits - jnp.max(logits, 0, keepdims=True))
    probs = raised / jnp.sum(raised, 0, keepdims=True)
    chosen = ((row == ids[0:1]) | (row == ids[1:2])).astype(F32)
    shifted = row - experts
    flags = (((shifted == ids[0:1]) | (shifted == ids[1:2])) & (shifted >= 0)).astype(F32)
    return probs, probs * chosen + flags


def front_image(image, experts, x_ref, small_ref, qkv_ref, out_ref, noise_ref, ids_ref, keep):
    normed_ref, packed_ref, attended_ref, middle_ref = keep
    at = pl.ds(image * PAD, PAD)
    x = x_ref[at, :].astype(F32)
    unit, _ = norm_parts(x)
    normed = (unit * gain_row(small_ref, experts, 0) + gain_row(small_ref, experts, 1)).astype(BF)
    normed_ref[at, :] = normed
    attended = attend(normed, at, qkv_ref, packed_ref)
    attended_ref[at, :] = attended
    middle = x + dot(attended, out_ref[...])
    middle_ref[at, :] = middle
    unit, _ = norm_parts(middle)
    normed = (unit * gain_row(small_ref, experts, 2) + gain_row(small_ref, experts, 3)).astype(BF)
    cols = slice(image * PAD, (image + 1) * PAD)
    probs, flags = route(normed, small_ref, noise_ref[:, cols], ids_ref[:, cols], experts)
    return normed, probs, flags


def front_kernel(
    x_ref, small_ref, qkv_ref, out_ref, noise_ref, ids_ref,
    normed_ref, packed_ref, attended_ref, middle_ref, rows_ref, flag_ref, prob_ref,
):
    keep = (normed_ref, packed_ref, attended_ref, middle_ref)
    probs, flags = [], []
    for image in range(x_ref.shape[0] // PAD):
        normed, prob, flag = front_image(
            image, TALL // 2, x_ref, small_ref, qkv_ref, out_ref, noise_ref, ids_ref, keep
        )
        rows_ref[pl.ds(image * PAD, PAD), :] = normed
        probs.append(prob)
        flags.append(flag)
    prob_ref[...] = jnp.concatenate(probs, 1)
    flag_ref[...] = jnp.concatenate(flags, 1).astype(BF)


def front(x, small, qkv, out, noise, ids):
    rows, width = x.shape
    shape = jax.ShapeDtypeStruct
    return pl.pallas_call(
        front_kernel,
        out_shape=(
            shape((rows, width), BF),
            shape((rows, 3 * width), BF),
            shape((rows, width), BF),
            shape((rows, width), F32),
            shape((rows, width), BF),
            shape((TALL, rows), BF),
            shape((TALL, rows), F32),
        ),
        compiler_params=pltpu.CompilerParams(vmem_limit_bytes=BIG),
        cost_estimate=pl.CostEstimate(flops=8 * 10**9, bytes_accessed=10**7, transcendentals=10**6),
        name="front",
    )(x, small, qkv, out, noise, ids)


class Place:
    def __init__(self):
        shard, head, tensor = (lax.axis_index(axis) for axis in AXES)
        self.shard, self.head, self.tensor = shard, head, tensor
        self.pair, self.side = lax.rem(head, 2), lax.div(head, 2)
        self.across = (1 - shard, head, tensor)
        self.beside = (shard, lax.rem(head + 2, 4), tensor)
        self.twin = (shard, head + 1 - 2 * self.pair, tensor)
        self.above = (shard, head, lax.rem(tensor + 1, 4))
        self.below = (shard, head, lax.rem(tensor + 3, 4))

    def greet(self, line=False):
        barrier = pltpu.get_barrier_semaphore()
        devices = [self.across, self.beside, self.twin, self.above, self.below]
        if line:
            devices.append((self.shard, self.head, lax.rem(self.tensor + 2, 4)))
        for device in devices:
            pl.semaphore_signal(barrier, inc=1, device_id=device, device_id_type=MESH)
        pl.semaphore_wait(barrier, len(devices))


class Links:
    def __init__(self, send, recv):
        self.send, self.recv, self.used = send, recv, 0
        self.sent = []

    def copy(self, source, target, device):
        index = self.used
        self.used += 1
        return pltpu.make_async_remote_copy(
            src_ref=source, dst_ref=target, send_sem=self.send.at[index], recv_sem=self.recv.at[index],
            device_id=device, device_id_type=MESH,
        )

    def start(self, source, target, device):
        copy = self.copy(source, target, device)
        copy.start()
        self.sent.append((None, copy))
        return copy

    def skip(self, done):
        self.sent = [(when, copy) for when, copy in self.sent if copy is not done]

    def finish(self):
        for when, copy in self.sent:
            if when is None:
                copy.wait_send()
            else:
                pl.when(when)(copy.wait_send)


class LineGather:
    def __init__(self, links, place, view, own, parts):
        self.links, self.place, self.view, self.own = links, place, view, own
        self.copies = {}
        self.parts = parts

    def start(self, part, step):
        t = self.place.tensor
        for name, slot, device, sends in (
            ("up", t - step, self.place.above, (t >= step) & (t < 3)),
            ("down", t + step, self.place.below, (t + step <= 3) & (t > 0)),
        ):
            slot = jnp.clip(slot, 0, 3)
            source = self.own(part) if step == 0 else self.view(slot, part)
            copy = self.links.copy(source, self.view(slot, part), device)
            pl.when(sends)(copy.start)
            self.links.sent.append((sends, copy))
            self.copies[name, part, step] = copy

    def wait(self, part, step, then=None):
        t = self.place.tensor
        for name, slot, comes in (("up", t - 1 - step, t >= step + 1), ("down", t + 1 + step, t + 1 + step <= 3)):
            copy = self.copies[name, part, step]

            @pl.when(comes)
            def _():
                copy.wait_recv()

    def arrived(self, step):
        t = self.place.tensor
        return (
            (jnp.clip(t - 1 - step, 0, 3), t >= step + 1),
            (jnp.clip(t + 1 + step, 0, 3), t + 1 + step <= 3),
        )


def head_kernel(
    x_ref, cot_ref, small_own, qkv_own, out_own, expert_in, expert_out, noise_ref, ids_ref,
    small_ref, qkv_ref, out_ref, normed_ref, packed_ref, attended_ref, middle_ref, prob_ref,
    rows_all, flags_all, cot_all, got_in, got_out,
    sent_rows, sent_flags, send, recv, local_sem,
):
    place = Place()
    links = Links(send, recv)
    width = x_ref.shape[1]
    experts = expert_in.shape[0]
    depth = qkv_own.shape[0]
    quarter = depth // 4
    shard, pair, side, tensor = place.shard, place.pair, place.side, place.tensor
    mine = pair * 4 + tensor
    place.greet()

    def dense_rows(owner, across_side, across_pair, start, size):
        return pl.ds(pl.multiple_of(owner * depth + (across_side * 2 + across_pair) * quarter + start, TALL), size)

    pieces = ((qkv_own, qkv_ref, 0, quarter // 2), (qkv_own, qkv_ref, quarter // 2, quarter // 2), (out_own, out_ref, 0, quarter))
    smalls = links.start(small_own, small_ref.at[shard], place.across)
    cross = []
    for own, full, start, size in pieces:
        source = own.at[pl.ds(pl.multiple_of((side * 2 + pair) * quarter + start, TALL), size), :]
        cross.append(links.start(source, full.at[dense_rows(shard, side, pair, start, size), :], place.across))
    here = pl.ds(pl.multiple_of(shard * depth, TALL), depth)
    locals_ = [
        pltpu.make_async_copy(qkv_own, qkv_ref.at[here, :], local_sem.at[0]),
        pltpu.make_async_copy(out_own, out_ref.at[here, :], local_sem.at[1]),
        pltpu.make_async_copy(small_own, small_ref.at[shard], local_sem.at[2]),
        pltpu.make_async_copy(cot_ref, cot_all.at[mine], local_sem.at[3]),
    ]
    for copy in locals_:
        copy.start()

    def slots(array):
        def view(slot, part):
            return array.at[pair * 4 + slot, pl.ds(part * PAD, PAD), :]

        return view

    cot_line = LineGather(links, place, slots(cot_all), lambda part: cot_ref.at[pl.ds(part * PAD, PAD), :], 2)
    for part in range(2):
        cot_line.start(part, 0)

    beside, twins = [], []
    for index, (own, full, start, size) in enumerate(pieces):
        cross[index].wait_recv()
        rows = full.at[dense_rows(1 - shard, side, pair, start, size), :]
        beside.append(links.start(rows, rows, place.beside))
        twins.append(links.start(rows, rows, place.twin))
    for index, (own, full, start, size) in enumerate(pieces):
        beside[index].wait_recv()
        rows = full.at[dense_rows(1 - shard, 1 - side, pair, start, size), :]
        twins.append(links.start(rows, rows, place.twin))

    def expert_item(item):
        index = side * 2 + item // 2
        source, target = (expert_in, got_in) if item % 2 == 0 else (expert_out, got_out)
        return source.at[pair * (experts // 2) + index], target.at[index]

    fetched = [links.start(*expert_item(item), place.across) for item in range(4)]
    for part in range(2):
        cot_line.wait(part, 0)
        cot_line.start(part, 1)
    smalls.wait_recv()
    for copy in twins:
        copy.wait_recv()
    for copy in locals_:
        copy.wait()

    keep = (normed_ref, packed_ref, attended_ref, middle_ref)
    row_line = LineGather(links, place, slots(rows_all), lambda part: sent_rows.at[pl.ds(part * PAD, PAD), :], 2)
    flag_line = LineGather(links, place, lambda slot, part: flags_all.at[pair * 4 + slot], lambda part: sent_flags, 1)
    probs, flags = [], []
    twin_rows = []
    forwarded = []

    def forward_expert(item):
        fetched[item].wait_recv()
        _, target = expert_item(item)
        forwarded.append(links.start(target, target, place.beside))

    for image in range(2):
        normed, prob, flag = front_image(
            image, experts, x_ref, small_ref, qkv_ref, out_ref, noise_ref, ids_ref, keep
        )
        at = pl.ds(image * PAD, PAD)
        sent_rows[at, :] = normed
        row_line.start(image, 0)
        twin_rows.append(links.start(sent_rows.at[at, :], rows_all.at[mine, at, :], place.twin))
        probs.append(prob)
        flags.append(flag)
        if image == 0:
            for part in range(2):
                cot_line.wait(part, 1)
                cot_line.start(part, 2)
    prob_ref[...] = jnp.concatenate(probs, 1)
    sent_flags[...] = jnp.concatenate(flags, 1).astype(BF)
    flag_line.start(0, 0)
    twin_flags = [links.start(sent_flags, flags_all.at[mine], place.twin)]
    keep_own = [
        pltpu.make_async_copy(sent_rows, rows_all.at[mine], local_sem.at[0]),
        pltpu.make_async_copy(sent_flags, flags_all.at[mine], local_sem.at[1]),
    ]
    for copy in keep_own:
        copy.start()

    def share(line, array, part, step, copies, whole):
        for slot, comes in line.arrived(step):
            index = pair * 4 + slot
            ref = array.at[index] if whole else array.at[index, pl.ds(part * PAD, PAD), :]
            copy = links.copy(ref, ref, place.twin)
            pl.when(comes)(copy.start)
            links.sent.append((comes, copy))
            copies.append((comes, copy))

    twin_steps = []
    forward_expert(0)
    for step in range(3):
        for part in range(2):
            row_line.wait(part, step)
            if step < 2:
                row_line.start(part, step + 1)
            share(row_line, rows_all, part, step, twin_steps, False)
        flag_line.wait(0, step)
        if step < 2:
            flag_line.start(0, step + 1)
        share(flag_line, flags_all, 0, step, twin_steps, True)
        if step == 0:
            for part in range(2):
                cot_line.wait(part, 2)
            ours = cot_all.at[pl.ds(pair * 4, 4)]
            twin_cot = links.start(ours, ours, place.twin)
        forward_expert(step + 1)

    for copy in twin_rows + twin_flags + [twin_cot] + forwarded:
        copy.wait_recv()
    for comes, copy in twin_steps:
        pl.when(comes)(copy.wait_recv)
    for copy in keep_own:
        copy.wait()
    links.finish()


def head(x, cot, small, qkv, out, expert_in, expert_out, noise, ids):
    rows, width = x.shape
    depth = qkv.shape[0]
    count = expert_in.shape[0] // 2
    shape = jax.ShapeDtypeStruct
    anywhere = pl.BlockSpec(memory_space=pl.ANY)
    vmem = pl.BlockSpec(memory_space=pltpu.VMEM)
    return pl.pallas_call(
        head_kernel,
        out_shape=(
            shape((2, TALL, depth), BF),
            shape((width, 3 * width), BF),
            shape((width, width), BF),
            shape((rows, width), BF),
            shape((rows, 3 * width), BF),
            shape((rows, width), BF),
            shape((rows, width), F32),
            shape((TALL, rows), F32),
            shape((8, rows, width), BF),
            shape((8, TALL, rows), BF),
            shape((8, rows, width), BF),
            shape((count,) + expert_in.shape[1:], BF),
            shape((count,) + expert_out.shape[1:], BF),
        ),
        in_specs=[vmem] * 3 + [anywhere] * 4 + [vmem] * 2,
        out_specs=(vmem,) * 8 + (anywhere,) * 5,
        scratch_shapes=[
            pltpu.VMEM((rows, width), BF),
            pltpu.VMEM((TALL, rows), BF),
            pltpu.SemaphoreType.DMA((96,)),
            pltpu.SemaphoreType.DMA((96,)),
            pltpu.SemaphoreType.DMA((4,)),
        ],
        compiler_params=pltpu.CompilerParams(vmem_limit_bytes=BIG, collective_id=1, has_side_effects=True),
        cost_estimate=pl.CostEstimate(flops=8 * 10**9, bytes_accessed=3 * 10**7, transcendentals=10**6),
        name="head",
    )(x, cot, small, qkv, out, expert_in, expert_out, noise, ids)


def expert_kernel(
    place_ref, rows_ref, flag_ref, cot_ref, own_in, got_in, own_out, got_out,
    total_ref, back_ref, gate_ref, grad_in, grad_out,
    inner, outer, picked, grads, gate, active, hidden_grad, made, made_back, made_gate, ranks, sum_in, sum_out,
    stage_in, stage_out, load_sem, store_sem,
):
    blocks, length, width = cot_ref.shape
    count = got_in.shape[0]
    depth = got_in.shape[1]
    pair, shard = place_ref[0], place_ref[1]
    experts = 2 * count
    capacity = blocks * TILE

    def loads(expert, slot):
        mine = pl.ds(pl.multiple_of(shard * depth, LANES), depth)
        other = pl.ds(pl.multiple_of((1 - shard) * depth, LANES), depth)
        index = pair * count + expert
        return (
            pltpu.make_async_copy(own_in.at[index], inner.at[slot, mine, :], load_sem.at[slot, 0]),
            pltpu.make_async_copy(got_in.at[expert], inner.at[slot, other, :], load_sem.at[slot, 1]),
            pltpu.make_async_copy(own_out.at[index], outer.at[slot, :, mine], load_sem.at[slot, 2]),
            pltpu.make_async_copy(got_out.at[expert], outer.at[slot, :, other], load_sem.at[slot, 3]),
        )

    def stores(expert, slot):
        return (
            pltpu.make_async_copy(stage_in.at[slot], grad_in.at[expert], store_sem.at[slot, 0]),
            pltpu.make_async_copy(stage_out.at[slot], grad_out.at[expert], store_sem.at[slot, 1]),
        )

    for copy in loads(0, 0):
        copy.start()
    ahead = lax.broadcasted_iota(jnp.int32, (length, length), 0)
    behind = lax.broadcasted_iota(jnp.int32, (length, length), 1)
    order = jnp.where(behind < ahead, 1.0, jnp.where(behind == ahead, FAR, 0.0)).astype(BF)

    def rank(block, carry):
        ranks[block] = contract_cols(flag_ref[block], order) - FAR
        total_ref[block] = jnp.zeros(total_ref.shape[1:], BF)
        back_ref[block] = jnp.zeros(back_ref.shape[1:], BF)
        gate_ref[block] = jnp.zeros(gate_ref.shape[1:], BF)
        return carry

    lax.fori_loop(0, blocks, rank, 0)

    for expert in range(count):
        slot = expert % 2
        if expert + 1 < count:
            for copy in loads(expert + 1, 1 - slot):
                copy.start()
        line = pl.ds(experts + pair * count + expert, 1)
        highest = ranks[0, line, :]
        for block in range(1, blocks):
            highest = jnp.maximum(highest, ranks[block, line, :])
        passes = (jnp.maximum(jnp.max(highest), -1.0).astype(jnp.int32) + TILE) // TILE
        sum_in[...] = jnp.zeros(sum_in.shape, F32)
        sum_out[...] = jnp.zeros(sum_out.shape, F32)
        for copy in loads(expert, slot):
            copy.wait()

        def one_pass(step, carry):
            base = (step * TILE).astype(F32)
            slots = lax.broadcasted_iota(jnp.int32, (TILE, length), 0).astype(F32) + base

            def take(block, carry):
                choose = (ranks[block, line, :] == slots).astype(BF)
                at = pl.ds(pl.multiple_of(block * TILE, TILE), TILE)
                picked[at, :] = dot(choose, rows_ref[block]).astype(BF)
                grads[at, :] = dot(choose, cot_ref[block]).astype(BF)
                columns = contract_cols(choose, flag_ref[block])
                lane = lax.broadcasted_iota(jnp.int32, (TILE, TALL), 1)
                column = jnp.where(lane == pair * count + expert, columns, 0.0)
                gate[at, :] = jnp.broadcast_to(jnp.sum(column, -1, keepdims=True), (TILE, LANES))
                return carry

            lax.fori_loop(0, blocks, take, 0, unroll=2)

            def chunk(index, carry):
                at = pl.ds(pl.multiple_of(index * CHUNK, CHUNK), CHUNK)
                value = dot(picked[at, :], inner[slot])
                grad_active = contract_cols(grads[at, :], outer[slot])
                gate_column = gate[at, 0:1]
                square = value * value
                bent = jnp.tanh(ROOT * value * (1.0 + CUBIC * square))
                plus = 0.5 * (1.0 + bent)
                bowed = value * plus
                slope = plus + (0.5 * ROOT) * value * (1.0 - bent * bent) * (1.0 + (3.0 * CUBIC) * square)
                active[at, :] = (bowed * gate_column).astype(BF)
                back = (grad_active * gate_column * slope).astype(BF)
                hidden_grad[at, :] = back
                lane = lax.broadcasted_iota(jnp.int32, (CHUNK, TALL), 1)
                gate_grad = jnp.sum(grad_active * bowed, -1, keepdims=True)
                made_gate[at, :] = jnp.where(lane == pair * count + expert, gate_grad, 0.0).astype(BF)
                made[at, :] = dot(active[at, :], outer[slot]).astype(BF)
                made_back[at, :] = contract_cols(back, inner[slot]).astype(BF)
                return carry

            lax.fori_loop(0, capacity // CHUNK, chunk, 0)
            hidden = sum_in.shape[1]
            for start in range(0, hidden, CHUNK):
                at = pl.ds(start, CHUNK)
                sum_out[at, :] += contract_rows(active[:, at], grads[...])
            for start in range(0, width, CHUNK):
                at = pl.ds(start, CHUNK)
                sum_in[at, :] += contract_rows(picked[:, at], hidden_grad[...])

            def give(block, carry):
                choose = (ranks[block, line, :] == slots).astype(BF)
                at = pl.ds(pl.multiple_of(block * TILE, TILE), TILE)
                total_ref[block] = (total_ref[block].astype(F32) + contract_rows(choose, made[at, :])).astype(BF)
                back_ref[block] = (back_ref[block].astype(F32) + contract_rows(choose, made_back[at, :])).astype(BF)
                gate_ref[block] = (gate_ref[block].astype(F32) + contract_rows(made_gate[at, :], choose)).astype(BF)
                return carry

            lax.fori_loop(0, blocks, give, 0, unroll=2)
            return carry

        lax.fori_loop(0, passes, one_pass, 0)
        if expert >= 2:
            for copy in stores(expert - 2, slot):
                copy.wait()
        stage_in[slot] = sum_in[...].astype(BF)
        stage_out[slot] = sum_out[...].astype(BF)
        for copy in stores(expert, slot):
            copy.start()
    for expert in range(max(count - 2, 0), count):
        for copy in stores(expert, expert % 2):
            copy.wait()


def expert_pass(place, rows, flags, cot, own_in, got_in, own_out, got_out):
    blocks, length, width = cot.shape
    count, _, hidden = got_in.shape
    capacity = blocks * TILE
    shape = jax.ShapeDtypeStruct
    anywhere = pl.BlockSpec(memory_space=pl.ANY)
    vmem = pl.BlockSpec(memory_space=pltpu.VMEM)
    return pl.pallas_call(
        expert_kernel,
        out_shape=(
            shape((blocks, length, width), BF),
            shape((blocks, length, width), BF),
            shape((blocks, TALL, length), BF),
            shape((count, width, hidden), BF),
            shape((count, hidden, width), BF),
        ),
        in_specs=[pl.BlockSpec(memory_space=pltpu.SMEM), vmem, vmem, vmem] + [anywhere] * 4,
        out_specs=(vmem, vmem, vmem, anywhere, anywhere),
        scratch_shapes=[
            pltpu.VMEM((2, width, hidden), BF),
            pltpu.VMEM((2, hidden, width), BF),
            pltpu.VMEM((capacity, width), BF),
            pltpu.VMEM((capacity, width), BF),
            pltpu.VMEM((capacity, LANES), F32),
            pltpu.VMEM((capacity, hidden), BF),
            pltpu.VMEM((capacity, hidden), BF),
            pltpu.VMEM((capacity, width), BF),
            pltpu.VMEM((capacity, width), BF),
            pltpu.VMEM((capacity, TALL), BF),
            pltpu.VMEM((blocks, TALL, length), F32),
            pltpu.VMEM((width, hidden), F32),
            pltpu.VMEM((hidden, width), F32),
            pltpu.VMEM((2, width, hidden), BF),
            pltpu.VMEM((2, hidden, width), BF),
            pltpu.SemaphoreType.DMA((2, 4)),
            pltpu.SemaphoreType.DMA((2, 2)),
        ],
        compiler_params=pltpu.CompilerParams(vmem_limit_bytes=BIG),
        cost_estimate=pl.CostEstimate(flops=50 * 10**9, bytes_accessed=5 * 10**7, transcendentals=10**6),
        name="experts",
    )(place, rows, flags, cot, own_in, got_in, own_out, got_out)


def back_middle(at, moe, gates, cot, middle, rows, probs, flags, small_ref, sums):
    experts = TALL // 2
    row = lax.broadcasted_iota(jnp.int32, flags.shape, 0)
    chosen = jnp.where(row < experts, pltpu.roll(flags, experts, 0), 0.0)
    asked = gates * chosen
    grad_logits = probs * (asked - jnp.sum(probs * asked, 0, keepdims=True))
    coarse = grad_logits.astype(BF)
    fine = (grad_logits - coarse.astype(F32)).astype(BF)
    router = router_rows(small_ref)
    sums[4] = sums[4] + dot(coarse, rows) + dot(fine, rows)
    grad = moe + contract_rows(coarse, router) + contract_rows(fine, router)
    unit, inverse = norm_parts(middle)
    sums[2] = sums[2] + jnp.sum(grad * unit, 0, keepdims=True)
    sums[3] = sums[3] + jnp.sum(grad, 0, keepdims=True)
    return cot + norm_back(grad, unit, inverse, gain_row(small_ref, experts, 2))


def back_heads(at, double, grad_proj, packed_ref, out_ref, stacked):
    width = grad_proj.shape[1]
    group = 3 * HEAD_DIM
    scale = HEAD_DIM ** (-0.5)
    lanes = lax.broadcasted_iota(jnp.int32, (PAD, group), 1) // HEAD_DIM
    made = []
    packed = packed_ref[at, pl.ds(double * 6 * group, 6 * group)]
    for side in range(2):
        query, keys, values = (packed[:, (3 * side + k) * group : (3 * side + k + 1) * group] for k in range(3))
        index = double * 2 + side
        grad_att = contract_cols(grad_proj, out_ref[pl.ds(index * group, group), :]).astype(BF)
        outs = [jnp.zeros((PAD, group), F32) for _ in range(3)]
        for head in range(3):
            mask = lanes == head
            probs = head_probs(jnp.where(mask, query, jnp.zeros_like(query)), keys, scale)
            part = jnp.where(mask, grad_att, jnp.zeros_like(grad_att))
            grad_weights = contract_cols(part, values)
            inner_sum = jnp.sum(probs * grad_weights, -1, keepdims=True)
            grad_scores = (probs * (grad_weights - inner_sum)).astype(BF)
            outs[0] = jnp.where(mask, dot(grad_scores, keys), outs[0])
            outs[1] = jnp.where(mask, contract_rows(grad_scores, query), outs[1])
            outs[2] = jnp.where(mask, contract_rows(probs.astype(BF), grad_att), outs[2])
        made += [outs[0] * scale, outs[1] * scale, outs[2]]
    stacked[at, pl.ds(double * 6 * group, 6 * group)] = jnp.concatenate(made, 1).astype(BF)


def back_kernel(
    moe_ref, gate_ref, cot_ref, x_ref, middle_ref, rows_ref, flag_ref, prob_ref, attended_ref, packed_ref, normed_ref,
    small_ref, qkv_ref, out_ref,
    tokens_ref, grad_qkv, grad_out, grad_small,
    stacked, projected,
):
    rows, width = x_ref.shape
    experts = TALL // 2
    sums = [jnp.zeros((1, width), F32) for _ in range(4)] + [jnp.zeros((TALL, width), F32)]
    for image in range(rows // PAD):
        at = pl.ds(image * PAD, PAD)
        cols = slice(image * PAD, (image + 1) * PAD)
        grad_middle = back_middle(
            at, moe_ref[at, :].astype(F32), gate_ref[:, cols].astype(F32), cot_ref[at, :].astype(F32),
            middle_ref[at, :], rows_ref[at, :], prob_ref[:, cols], flag_ref[:, cols].astype(F32), small_ref, sums,
        )
        grad_proj = grad_middle.astype(BF)
        projected[at, :] = grad_proj
        for double in range(width // (6 * HEAD_DIM)):
            back_heads(at, double, grad_proj, packed_ref, out_ref, stacked)
        grad = contract_cols(stacked[at, :], qkv_ref[...])
        unit, inverse = norm_parts(x_ref[at, :].astype(F32))
        sums[0] = sums[0] + jnp.sum(grad * unit, 0, keepdims=True)
        sums[1] = sums[1] + jnp.sum(grad, 0, keepdims=True)
        tokens_ref[at, :] = (grad_middle + norm_back(grad, unit, inverse, gain_row(small_ref, experts, 0))).astype(BF)
    grad_small[...] = jnp.concatenate([sums[4][0:experts]] + sums[:4] + [jnp.zeros((4, width), F32)], 0).astype(BF)
    grad_out[...] = contract_rows(attended_ref[...], projected[...]).astype(BF)
    for third in range(3):
        cols = pl.ds(third * width, width)
        grad_qkv[:, cols] = contract_rows(normed_ref[...], stacked[:, cols]).astype(BF)


def back(moe, gates, cot, x, middle, sent, flags, prob, attended, packed, normed, small, qkv, out):
    rows, width = x.shape
    shape = jax.ShapeDtypeStruct
    return pl.pallas_call(
        back_kernel,
        out_shape=(
            shape((rows, width), BF),
            shape((width, 3 * width), BF),
            shape((width, width), BF),
            shape((TALL, width), BF),
        ),
        scratch_shapes=[pltpu.VMEM((rows, 3 * width), BF), pltpu.VMEM((rows, width), BF)],
        compiler_params=pltpu.CompilerParams(vmem_limit_bytes=BIG),
        cost_estimate=pl.CostEstimate(flops=16 * 10**9, bytes_accessed=2 * 10**7, transcendentals=10**6),
        name="back",
    )(moe, gates, cot, x, middle, sent, flags, prob, attended, packed, normed, small, qkv, out)


class LineScatter:
    def __init__(self, links, place, sums, up, down):
        self.links, self.place = links, place
        self.sums, self.up, self.down = sums, up, down
        self.copies = {}

    def ways(self, step):
        t = self.place.tensor
        return (
            ("up", self.up, t + 3 - step, t <= step, t >= 1, self.place.above),
            ("down", self.down, t - 3 + step, t >= 3 - step, t <= 2, self.place.below),
        )

    def send(self, part, step):
        for name, got, slot, sends, comes, device in self.ways(step):
            slot = jnp.clip(slot, 0, 3)
            if step > 0:
                before = self.copies[name, part, step - 1]

                @pl.when(sends & comes)
                def _():
                    before.wait_recv()
                    ref = self.sums(slot, part)
                    ref[...] = (ref[...].astype(F32) + got(step - 1, part)[...].astype(F32)).astype(BF)

            copy = self.links.copy(self.sums(slot, part), got(step, part), device)
            pl.when(sends)(copy.start)
            self.links.sent.append((sends, copy))
            self.copies[name, part, step] = copy

    def finish(self, part, total):
        total[...] = self.sums(self.place.tensor, part)[...].astype(F32)
        for name, got, slot, sends, comes, device in self.ways(2):
            copy = self.copies[name, part, 2]

            @pl.when(comes)
            def _():
                copy.wait_recv()
                total[...] += got(2, part)[...].astype(F32)


def tail_kernel(
    back_all, gate_all, total_all, grads_in, grads_out, rows_all, flags_all,
    cot_ref, x_ref, middle_ref, prob_ref, attended_ref, packed_ref, normed_ref, small_ref, qkv_ref, out_ref,
    mixed_ref, tokens_ref, dense_ref, grad_small, final_in, final_out, beside_in, beside_out,
    back_sum, back_got, back_up, back_down, gate_sum, gate_got, gate_up, gate_down,
    total_sum, total_got, total_up, total_down, moe, gates, rows_ref, flag_ref, projected, stacked,
    chunks, core_got, across_sent, across_got, beside_sum, beside_sent, beside_got, line_sum, line_got, line_final,
    own_in, own_out, across_in, across_out, read_in, read_out,
    small_sent, small_core, small_half, small_across, small_side, small_beside, small_line_sent, small_line,
    send, recv, local_sem,
):
    place = Place()
    links = Links(send, recv)
    rows, width = x_ref.shape
    experts = TALL // 2
    count = grads_in.shape[0]
    depth = width // 2
    shard, pair, side, tensor = place.shard, place.pair, place.side, place.tensor
    mine = pair * 4 + tensor
    place.greet(True)
    ours, theirs = pl.ds(pair * 4, 4), pl.ds((1 - pair) * 4, 4)

    locals_ = [
        pltpu.make_async_copy(back_all.at[ours], back_sum, local_sem.at[0]),
        pltpu.make_async_copy(gate_all.at[ours], gate_sum, local_sem.at[1]),
        pltpu.make_async_copy(total_all.at[ours], total_sum, local_sem.at[2]),
        pltpu.make_async_copy(rows_all.at[mine], rows_ref, local_sem.at[3]),
        pltpu.make_async_copy(flags_all.at[mine], flag_ref, local_sem.at[4]),
    ]
    for copy in locals_:
        copy.start()
    from_twin = [
        links.start(back_all.at[theirs], back_got, place.twin),
        links.start(gate_all.at[theirs], gate_got, place.twin),
        links.start(total_all.at[theirs], total_got, place.twin),
    ]

    here = pl.ds(pl.multiple_of(shard * depth, LANES), depth)
    there = pl.ds(pl.multiple_of((1 - shard) * depth, LANES), depth)
    items = []
    for expert in range(count):
        items.append((grads_in.at[expert, there, :], grads_in.at[expert, here, :], across_in.at[expert],
                      beside_in.at[expert], final_in.at[pair * count + expert], own_in, read_in))
        items.append((grads_out.at[expert, :, there], grads_out.at[expert, :, here], across_out.at[expert],
                      beside_out.at[expert], final_out.at[pair * count + expert], own_out, read_out))
    item_loads = [pltpu.make_async_copy(item[1], item[5], local_sem.at[8 + m]) for m, item in enumerate(items)]
    item_across, item_beside, item_twin, item_keep = [], [], [], []
    todo = {"across": 0, "x": 0, "y": 0}

    def send_across():
        m = todo["across"]
        if m < len(items):
            item_across.append(links.start(items[m][0], items[m][2], place.across))
            todo["across"] += 1

    def take_across():
        m = todo["x"]
        if m >= len(items):
            return
        todo["x"] += 1
        item_across[m].wait_recv()
        send_across()
        item_loads[m].wait()
        total, own = items[m][2], items[m][5]
        total[...] = (total[...].astype(F32) + own[...].astype(F32)).astype(BF)
        item_beside.append(links.start(total, items[m][3], place.beside))
        if m + 2 < len(items):
            item_loads[m + 2].start()

    def take_beside():
        m = todo["y"]
        if m >= len(items):
            return
        todo["y"] += 1
        item_beside[m].wait_recv()
        total, got = items[m][2], items[m][6]
        load = pltpu.make_async_copy(items[m][3], got, local_sem.at[5])
        load.start()
        item_beside[m].wait_send()
        load.wait()
        total[...] = (total[...].astype(F32) + got[...].astype(F32)).astype(BF)
        item_twin.append(links.start(total, items[m][4], place.twin))
        keep = pltpu.make_async_copy(total, items[m][4], local_sem.at[16 + m])
        keep.start()
        item_keep.append(keep)

    send_across()
    send_across()
    item_loads[0].start()
    item_loads[1].start()

    share = depth // 2
    piece = share // 4
    half = width // 2
    stage = {}

    def dense_core(k):
        stage["core", k] = []
        for owner in range(2):
            source = chunks.at[k, pl.ds(pl.multiple_of(owner * depth + (1 - pair) * share, TALL), share), :]
            stage["core", k].append(links.start(source, core_got.at[k, owner], place.twin))

    def core_sum(k, owner):
        at = pl.ds(pl.multiple_of(owner * depth + pair * share, TALL), share)
        return chunks[k, at, :].astype(F32) + core_got[k, owner].astype(F32)

    def dense_across(k):
        for copy in stage["core", k]:
            copy.wait_recv()
        across_sent[k] = core_sum(k, 1 - shard).astype(BF)
        stage["across", k] = links.start(across_sent.at[k], across_got.at[k], place.across)

    def dense_beside(k):
        stage["across", k].wait_recv()
        beside_sum[k] = core_sum(k, shard) + across_got[k].astype(F32)
        other = pl.ds(pl.multiple_of((1 - side) * half, LANES), half)
        beside_sent[k] = beside_sum[k, :, other].astype(BF)
        stage["beside", k] = links.start(beside_sent.at[k], beside_got.at[k], place.beside)

    def around(offset):
        return (shard, place.head, lax.rem(tensor + offset, 4))

    def dense_line(k):
        stage["beside", k].wait_recv()
        own = pl.ds(pl.multiple_of(side * half, LANES), half)
        line_sum[k] = (beside_sum[k, :, own] + beside_got[k].astype(F32)).astype(BF)
        stage["line", k] = []
        for offset in (2, 1, 3):
            at = pl.ds(pl.multiple_of(lax.rem(tensor + offset, 4) * piece, TALL), piece)
            stage["line", k].append(links.start(line_sum.at[k, at, :], line_got.at[k, offset - 1], around(offset)))

    def dense_spread(k):
        for copy in stage["line", k]:
            copy.wait_recv()
        at = pl.ds(pl.multiple_of(tensor * piece, TALL), piece)
        value = line_sum[k, at, :].astype(F32)
        for offset in range(3):
            value = value + line_got[k, offset].astype(F32)
        line_final[k] = value.astype(BF)
        target = dense_ref.at[
            pl.ds(pl.multiple_of(pair * share + tensor * piece, TALL), piece),
            pl.ds(pl.multiple_of(k * width + side * half, LANES), half),
        ]
        stage["spread", k] = [links.start(line_final.at[k], target, around(offset)) for offset in (2, 1, 3)]
        stage["keep", k] = pltpu.make_async_copy(line_final.at[k], target, local_sem.at[24 + k])
        stage["keep", k].start()

    def dense_return(k):
        for copy in stage["spread", k]:
            copy.wait_recv()
        stage["keep", k].wait()
        block = dense_ref.at[
            pl.ds(pl.multiple_of(pair * share, TALL), share),
            pl.ds(pl.multiple_of(k * width + side * half, LANES), half),
        ]
        stage["return", k] = links.start(block, block, place.beside)

    def dense_twin(k):
        stage["return", k].wait_recv()
        block = dense_ref.at[pl.ds(pl.multiple_of(pair * share, TALL), share), pl.ds(k * width, width)]
        stage["twin", k] = links.start(block, block, place.twin)

    def slots(array):
        def view(slot, part):
            return array.at[slot, pl.ds(part * PAD, PAD), :]

        return view

    back_line = LineScatter(links, place, slots(back_sum), slots(back_up), slots(back_down))
    total_line = LineScatter(links, place, slots(total_sum), slots(total_up), slots(total_down))
    gate_line = LineScatter(
        links, place, lambda slot, part: gate_sum.at[slot], lambda step, part: gate_up.at[step],
        lambda step, part: gate_down.at[step],
    )

    def add_twin(sums, got):
        for slot in range(4):
            sums[slot] = (sums[slot].astype(F32) + got[slot].astype(F32)).astype(BF)

    for copy in (locals_[0], locals_[1]):
        copy.wait()
    from_twin[1].wait_recv()
    from_twin[0].wait_recv()
    add_twin(gate_sum, gate_got)
    add_twin(back_sum, back_got)
    gate_line.send(0, 0)
    for part in range(2):
        back_line.send(part, 0)
    locals_[2].wait()
    from_twin[2].wait_recv()
    add_twin(total_sum, total_got)
    gate_line.send(0, 1)
    for part in range(2):
        back_line.send(part, 1)
    take_across()
    gate_line.send(0, 2)
    for part in range(2):
        back_line.send(part, 2)
    take_across()
    take_beside()
    for part in range(2):
        total_line.send(part, 0)
    gate_line.finish(0, gates)
    locals_[3].wait()
    locals_[4].wait()

    sums = [jnp.zeros((1, width), F32) for _ in range(4)] + [jnp.zeros((TALL, width), F32)]
    for image in range(2):
        at = pl.ds(image * PAD, PAD)
        cols = slice(image * PAD, (image + 1) * PAD)
        back_line.finish(image, moe.at[at, :])
        grad = back_middle(
            at, moe[at, :], gates[:, cols], cot_ref[at, :].astype(F32), middle_ref[at, :], rows_ref[at, :],
            prob_ref[:, cols], flag_ref[:, cols].astype(F32), small_ref, sums,
        )
        moe[at, :] = grad
        projected[at, :] = grad.astype(BF)
    chunks[0] = contract_rows(attended_ref[...], projected[...]).astype(BF)
    dense_core(0)
    take_across()
    take_beside()
    for image in range(2):
        at = pl.ds(image * PAD, PAD)
        back_heads(at, 0, projected[at, :], packed_ref, out_ref, stacked)
    chunks[1] = contract_rows(normed_ref[...], stacked[:, pl.ds(0, width)]).astype(BF)
    dense_core(1)
    dense_across(0)
    for part in range(2):
        total_line.send(part, 1)
    take_across()
    dense_across(1)
    take_beside()
    for image in range(2):
        at = pl.ds(image * PAD, PAD)
        back_heads(at, 1, projected[at, :], packed_ref, out_ref, stacked)
    for k in (2, 3):
        chunks[k] = contract_rows(normed_ref[...], stacked[:, pl.ds((k - 1) * width, width)]).astype(BF)
        dense_core(k)
    dense_beside(0)
    for k in (2, 3):
        dense_across(k)
    for part in range(2):
        total_line.send(part, 2)
    for image in range(2):
        at = pl.ds(image * PAD, PAD)
        grad = contract_cols(stacked[at, :], qkv_ref[...])
        unit, inverse = norm_parts(x_ref[at, :].astype(F32))
        sums[0] = sums[0] + jnp.sum(grad * unit, 0, keepdims=True)
        sums[1] = sums[1] + jnp.sum(grad, 0, keepdims=True)
        tokens_ref[at, :] = (
            moe[at, :] + norm_back(grad, unit, inverse, gain_row(small_ref, experts, 0))
        ).astype(BF)
    small_sent[...] = jnp.concatenate([sums[4][0:experts]] + sums[:4] + [jnp.zeros((4, width), F32)], 0)
    small_copies = [links.start(small_sent, small_core, place.twin)]
    take_across()
    take_beside()
    dense_beside(1)
    dense_line(0)
    small_copies[0].wait_recv()
    other = pl.ds(pl.multiple_of((1 - shard) * depth, LANES), depth)
    small_half[...] = small_sent[:, other] + small_core[:, other]
    small_copies.append(links.start(small_half, small_across, place.across))
    take_across()
    take_beside()
    dense_line(1)
    dense_spread(0)
    dense_beside(2)
    small_copies[1].wait_recv()
    own = pl.ds(pl.multiple_of(shard * depth, LANES), depth)
    small_side[...] = small_sent[:, own] + small_core[:, own] + small_across[...]
    small_copies.append(links.start(small_side, small_beside, place.beside))
    dense_beside(3)
    dense_spread(1)
    dense_return(0)
    dense_line(2)
    take_across()
    take_beside()
    small_copies[2].wait_recv()
    small_line_sent[...] = small_side[...] + small_beside[...]
    small_line_copies = [links.start(small_line_sent, small_line.at[offset - 1], around(offset)) for offset in (2, 1, 3)]
    dense_line(3)
    dense_spread(2)
    dense_return(1)
    dense_twin(0)
    take_across()
    take_beside()
    dense_spread(3)
    dense_return(2)
    dense_twin(1)
    take_beside()
    dense_return(3)
    dense_twin(2)
    for copy in small_line_copies:
        copy.wait_recv()
    grad_small[...] = small_line_sent[...] + small_line[0] + small_line[1] + small_line[2]
    for part in range(2):
        at = pl.ds(part * PAD, PAD)
        total_line.finish(part, moe.at[at, :])
        mixed_ref[at, :] = (middle_ref[at, :] + moe[at, :]).astype(BF)
    for _ in items:
        take_across()
        take_beside()
    dense_twin(3)
    for copy in item_twin + [stage["twin", k] for k in range(4)]:
        copy.wait_recv()
    for copy in item_keep:
        copy.wait()
    for copy in item_beside:
        links.skip(copy)
    links.finish()


def tail(back_all, gate_all, total_all, grads_in, grads_out, rows_all, flags_all, cot, x, middle, prob, attended, packed, normed, small, qkv, out):
    rows, width = x.shape
    count, _, hidden = grads_in.shape
    depth = width // 2
    shape = jax.ShapeDtypeStruct
    anywhere = pl.BlockSpec(memory_space=pl.ANY)
    vmem = pl.BlockSpec(memory_space=pltpu.VMEM)
    share, piece, half = depth // 2, depth // 8, width // 2

    def scatter_buffers(tall, wide):
        return [pltpu.VMEM((4, tall, wide), BF)] * 2 + [pltpu.VMEM((3, tall, wide), BF)] * 2

    return pl.pallas_call(
        tail_kernel,
        out_shape=(
            shape((rows, width), BF),
            shape((rows, width), BF),
            shape((depth, 4 * width), BF),
            shape((TALL, depth), F32),
            shape((2 * count, depth, hidden), BF),
            shape((2 * count, hidden, depth), BF),
            shape((count, depth, hidden), BF),
            shape((count, hidden, depth), BF),
        ),
        in_specs=[anywhere] * 7 + [vmem] * 10,
        out_specs=(vmem,) * 4 + (anywhere,) * 4,
        scratch_shapes=scatter_buffers(rows, width)
        + scatter_buffers(TALL, rows)
        + scatter_buffers(rows, width)
        + [
            pltpu.VMEM((rows, width), F32),
            pltpu.VMEM((TALL, rows), F32),
            pltpu.VMEM((rows, width), BF),
            pltpu.VMEM((TALL, rows), BF),
            pltpu.VMEM((rows, width), BF),
            pltpu.VMEM((rows, 3 * width), BF),
            pltpu.VMEM((4, width, width), BF),
            pltpu.VMEM((4, 2, share, width), BF),
            pltpu.VMEM((4, share, width), BF),
            pltpu.VMEM((4, share, width), BF),
            pltpu.VMEM((4, share, width), F32),
            pltpu.VMEM((4, share, half), BF),
            pltpu.VMEM((4, share, half), BF),
            pltpu.VMEM((4, share, half), BF),
            pltpu.VMEM((4, 3, piece, half), BF),
            pltpu.VMEM((4, piece, half), BF),
        ]
        + [pltpu.VMEM((depth, hidden), BF), pltpu.VMEM((hidden, depth), BF)]
        + [pltpu.VMEM((count, depth, hidden), BF), pltpu.VMEM((count, hidden, depth), BF)]
        + [pltpu.VMEM((depth, hidden), BF), pltpu.VMEM((hidden, depth), BF)]
        + [
            pltpu.VMEM((TALL, width), F32),
            pltpu.VMEM((TALL, width), F32),
            pltpu.VMEM((TALL, depth), F32),
            pltpu.VMEM((TALL, depth), F32),
            pltpu.VMEM((TALL, depth), F32),
            pltpu.VMEM((TALL, depth), F32),
            pltpu.VMEM((TALL, depth), F32),
            pltpu.VMEM((3, TALL, depth), F32),
            pltpu.SemaphoreType.DMA((160,)),
            pltpu.SemaphoreType.DMA((160,)),
            pltpu.SemaphoreType.DMA((28,)),
        ],
        compiler_params=pltpu.CompilerParams(vmem_limit_bytes=BIG, collective_id=2, has_side_effects=True),
        cost_estimate=pl.CostEstimate(flops=16 * 10**9, bytes_accessed=5 * 10**7, transcendentals=10**6),
        name="tail",
    )(back_all, gate_all, total_all, grads_in, grads_out, rows_all, flags_all, cot, x, middle, prob, attended, packed, normed, small, qkv, out)


class Comm:
    def __init__(self):
        self.sizes = tuple(lax.axis_size(axis) for axis in AXES)
        self.shard = lax.axis_index("shard")
        self.head = lax.axis_index("heads")
        self.tensor = lax.axis_index("tensor")
        self.pair = self.head % 2

    def move(self, value, step):
        shards, heads, tensors = self.sizes
        pairs = []
        for s in range(shards):
            for h in range(heads):
                for t in range(tensors):
                    to = step(s, h, t)
                    if 0 <= to[2] < tensors:
                        source = (s * heads + h) * tensors + t
                        pairs.append((source, (to[0] * heads + to[1]) * tensors + to[2]))
        return lax.ppermute(value, AXES, pairs)

    def over_core(self, value):
        return self.move(value, lambda s, h, t: (s, h ^ 1, t))

    def over_heads(self, value):
        return self.move(value, lambda s, h, t: (s, (h + 2) % 4, t))

    def over_shard(self, value):
        return self.move(value, lambda s, h, t: (1 - s, h, t))

    def up(self, value):
        return self.move(value, lambda s, h, t: (s, h, t + 1))

    def down(self, value):
        return self.move(value, lambda s, h, t: (s, h, t - 1))

    def halves(self, value, index, axis):
        size = value.shape[axis] // 2
        mine = lax.dynamic_slice_in_dim(value, index * size, size, axis)
        other = lax.dynamic_slice_in_dim(value, (1 - index) * size, size, axis)
        return mine, other

    def join(self, mine, other, index, axis):
        first = jnp.where(index == 0, mine, other)
        second = jnp.where(index == 0, other, mine)
        return jnp.concatenate((first, second), axis)

    def gather_shard(self, value, axis):
        if self.sizes[0] != 2:
            return lax.all_gather(value, "shard", axis=axis, tiled=True)
        return self.join(value, self.over_shard(value), self.shard, axis)

    def gather_shard_split(self, value, axis, cut):
        if self.sizes[0] != 2:
            return lax.all_gather(value, "shard", axis=axis, tiled=True)
        mine, _ = self.halves(value, self.pair, cut)
        got = self.over_shard(mine)
        both = self.join(got, self.over_core(got), self.pair, cut)
        return self.join(value, both, self.shard, axis)

    def scatter_shard(self, value, axis):
        if self.sizes[0] != 2:
            return lax.psum_scatter(value.astype(BF), "shard", scatter_dimension=axis, tiled=True).astype(F32)
        mine, other = self.halves(value, self.shard, axis)
        return mine.astype(F32) + self.over_shard(other.astype(BF)).astype(F32)

    def scatter_core(self, value, axis):
        mine, other = self.halves(value, self.pair, axis)
        return mine.astype(F32) + self.over_core(other.astype(BF)).astype(F32)

    def scatter_heads(self, value, axis):
        mine, other = self.halves(value, self.head // 2, axis)
        return mine.astype(F32) + self.over_heads(other.astype(BF)).astype(F32)

    def line_gather(self, value):
        ups, downs = [value], [value]
        for _ in range(3):
            ups.append(self.up(ups[-1]))
            downs.append(self.down(downs[-1]))
        out = [value]
        for back in (1, 2, 3):
            out.append(jnp.where(self.tensor >= back, ups[back], downs[4 - back]))
        return out

    def line_scatter(self, parts):
        high, low = parts[1].astype(BF), parts[3].astype(BF)
        high = (parts[2].astype(F32) + self.up(high).astype(F32)).astype(BF)
        low = (parts[2].astype(F32) + self.down(low).astype(F32)).astype(BF)
        high = (parts[3].astype(F32) + self.up(high).astype(F32)).astype(BF)
        low = (parts[1].astype(F32) + self.down(low).astype(F32)).astype(BF)
        return parts[0].astype(F32) + self.up(high).astype(F32) + self.down(low).astype(F32)

    def join_slots(self, values):
        own = jnp.zeros((4,) + values[0].shape, values[0].dtype)
        for back, value in enumerate(values):
            own = lax.dynamic_update_index_in_dim(own, value, (self.tensor + 4 - back) % 4, 0)
        return self.join(own, self.over_core(own), self.pair, 0)

    def collect(self, value):
        mine, other = self.halves(value, self.pair, 0)
        mine = mine.astype(F32) + self.over_core(other).astype(F32)
        return self.line_scatter(
            [lax.dynamic_index_in_dim(mine, (self.tensor + 4 - k) % 4, 0, False) for k in range(4)]
        )


def local(
    tokens, ln1_gain, ln1_bias, qkv_weight, out_weight, ln2_gain, ln2_bias, router_weight,
    expert_in, expert_out, route_noise, expert_ids, cotangent,
):
    comm = Comm()
    rows, width = tokens.shape
    experts = expert_in.shape[0]
    images = rows // SEQ
    half = experts // 2
    padded = images * PAD

    def pad(value):
        value = value.reshape(images, SEQ, value.shape[1])
        return jnp.pad(value, ((0, 0), (0, PAD - SEQ), (0, 0))).reshape(padded, value.shape[2])

    def pad_turned(value, tall, fill):
        value = value.reshape(images, SEQ, value.shape[1]).transpose(2, 0, 1)
        value = jnp.pad(value, ((0, tall - value.shape[0]), (0, 0), (0, PAD - SEQ)), constant_values=fill)
        return value.reshape(tall, padded)

    def unpad(value):
        return value.reshape(images, PAD, value.shape[1])[:, :SEQ].reshape(rows, value.shape[1])

    small = jnp.concatenate(
        (router_weight.T, ln1_gain[None], ln1_bias[None], ln2_gain[None], ln2_bias[None]), 0
    )
    small = jnp.pad(small, ((0, TALL - small.shape[0]), (0, 0)))
    cot, x = pad(cotangent), pad(tokens)
    noise, ids = pad_turned(route_noise, TALL, 0), pad_turned(expert_ids, 8, -1)
    place = jnp.stack((comm.pair, comm.shard if comm.sizes[0] == 2 else 0 * comm.shard)).astype(jnp.int32)
    if comm.sizes[0] == 2:
        (
            small, proj_qkv, proj_out, normed_a, packed, attended, middle, prob,
            rows_all, flags_all, grad_rows, got_in, got_out,
        ) = head(x, cot, small, qkv_weight, out_weight, expert_in, expert_out, noise, ids)
        weights = (expert_in, got_in, expert_out, got_out)
    else:
        small = lax.all_gather(small, "shard", axis=1, tiled=True)
        small = small.reshape(TALL, 2, width // 2).transpose(1, 0, 2)
        proj_qkv = lax.all_gather(qkv_weight, "shard", axis=0, tiled=True)
        proj_out = lax.all_gather(out_weight, "shard", axis=0, tiled=True)
        inner = lax.all_gather(lax.dynamic_slice_in_dim(expert_in, comm.pair * half, half, 0), "shard", axis=1, tiled=True)
        outer = lax.all_gather(lax.dynamic_slice_in_dim(expert_out, comm.pair * half, half, 0), "shard", axis=2, tiled=True)
        cut = width // 2
        weights = (
            jnp.concatenate((inner[:, :cut], inner[:, :cut]), 0), inner[:, cut:],
            jnp.concatenate((outer[:, :, :cut], outer[:, :, :cut]), 0), outer[:, :, cut:],
        )
        normed_a, packed, attended, middle, sent, flags, prob = front(x, small, proj_qkv, proj_out, noise, ids)

        def gather(value):
            return comm.join_slots(comm.line_gather(value))

        grad_rows, rows_all, flags_all = gather(cot), gather(sent), gather(flags)
    total, back_all, gate_all, grads_in, grads_out = expert_pass(place, rows_all, flags_all, grad_rows, *weights)

    if comm.sizes[0] == 2:
        mixed, grad_tokens, dense, grad_small, grad_in, grad_outer, _, _ = tail(
            back_all, gate_all, total, grads_in, grads_out, rows_all, flags_all,
            cot, x, middle, prob, attended, packed, normed_a, small, proj_qkv, proj_out,
        )
        dense = dense.astype(F32)
        return (
            unpad(mixed),
            unpad(grad_tokens),
            grad_small[experts],
            grad_small[experts + 1],
            dense[:, width:],
            dense[:, :width],
            grad_small[experts + 2],
            grad_small[experts + 3],
            grad_small[:experts].T,
            grad_in.astype(F32),
            grad_outer.astype(F32),
        )

    def reduce_expert(grad, axis, other):
        part = comm.scatter_shard(grad, axis)
        part = comm.scatter_heads(part, other).astype(BF)
        return comm.join(part, comm.over_heads(part), comm.head // 2, other)

    inner_grads = [reduce_expert(grads_in[e], 0, 1) for e in range(half)]
    outer_grads = [reduce_expert(grads_out[e], 1, 0) for e in range(half)]

    moe_grad = comm.collect(back_all)
    gate_grad = comm.collect(gate_all)
    moe = comm.collect(total)
    mixed = (unpad(middle) + unpad(moe)).astype(BF)
    grad_tokens, grad_qkv, grad_out, grad_small = back(
        moe_grad, gate_grad, cot, x, middle, sent, flags, prob, attended, packed, normed_a, small, proj_qkv, proj_out
    )
    grad_tokens = unpad(grad_tokens)

    grad_small = jnp.pad(grad_small.T, ((0, 0), (0, 128 - TALL)))
    shares = jnp.concatenate((grad_qkv, grad_out, grad_small, jnp.zeros_like(grad_small)), 1)
    shares = comm.scatter_core(shares, 1)
    shares = comm.scatter_shard(shares, 0)
    shares = comm.scatter_heads(shares, 1)
    cut = shares.shape[0] // 4
    rolled = [
        lax.dynamic_slice_in_dim(shares, ((comm.tensor + 4 - k) % 4) * cut, cut, 0) for k in range(4)
    ]
    summed = comm.line_scatter(rolled).astype(BF)
    pieces = comm.line_gather(summed)
    whole = jnp.zeros(shares.shape, BF)
    for k in range(4):
        whole = lax.dynamic_update_slice_in_dim(whole, pieces[k], ((comm.tensor + 4 - k) % 4) * cut, 0)
    whole = comm.join(whole, comm.over_heads(whole), comm.head // 2, 1)
    whole = comm.join(whole, comm.over_core(whole), comm.pair, 1).astype(F32)
    small = whole[:, 4 * width : 4 * width + 128]

    grad_in, grad_outer = jnp.stack(inner_grads, 0), jnp.stack(outer_grads, 0)
    grad_in = comm.join(grad_in, comm.over_core(grad_in), comm.pair, 0).astype(F32)
    grad_outer = comm.join(grad_outer, comm.over_core(grad_outer), comm.pair, 0).astype(F32)
    return (
        mixed,
        grad_tokens,
        small[:, experts],
        small[:, experts + 1],
        whole[:, : 3 * width],
        whole[:, 3 * width : 4 * width],
        small[:, experts + 2],
        small[:, experts + 3],
        small[:, :experts],
        grad_in,
        grad_outer,
    )


def solution(mesh):
    split = P(AXES, None)
    vector, matrix = P("shard"), P("shard", None)
    inner, outer = P(None, "shard", "tensor"), P(None, "tensor", "shard")
    return jax.shard_map(
        local,
        mesh=mesh,
        in_specs=(
            split, vector, vector, matrix, matrix, vector, vector, matrix, inner, outer, split, split, split,
        ),
        out_specs=(
            split, split, vector, vector, matrix, matrix, vector, vector, matrix, inner, outer,
        ),
        check_vma=False,
    )
```

```python
import jax
import jax.numpy as jnp
from jax import lax
from jax.experimental import pallas as pl
from jax.experimental.pallas import tpu as pltpu
from jax.sharding import PartitionSpec as P

HEAD_DIM = 64
SEQ = 197
EPS = 1e-06
AXES = ("shard", "heads", "tensor")
BF = jnp.bfloat16
F32 = jnp.float32


def contract_rows(left, right):
    return lax.dot_general(left, right, (((0,), (0,)), ((), ())), preferred_element_type=F32)


def contract_cols(left, right):
    return lax.dot_general(left, right, (((1,), (1,)), ((), ())), preferred_element_type=F32)


PAD = 208
TILE = 128
CHUNK = 256
FAR = 512.0
TALL = 16
LANES = 128
MASKED = -1e30
CUBIC = 0.044715
ROOT = (2.0 / 3.141592653589793) ** 0.5
BIG = 60 * 1024 * 1024
MESH = pl.DeviceIdType.MESH


def dot(left, right):
    return jnp.dot(left, right, preferred_element_type=F32)


def norm_parts(values):
    centred = values - jnp.mean(values, -1, keepdims=True)
    inverse = lax.rsqrt(jnp.mean(centred * centred, -1, keepdims=True) + EPS)
    return centred * inverse, inverse


def norm_back(grad, unit, inverse, gain):
    scaled = grad * gain
    along = jnp.mean(scaled * unit, -1, keepdims=True)
    return inverse * (scaled - jnp.mean(scaled, -1, keepdims=True) - unit * along)


def head_probs(query, keys, scale):
    scores = contract_cols(query, keys) * scale
    column = lax.broadcasted_iota(jnp.int32, scores.shape, 1)
    scores = jnp.where(column < SEQ, scores, MASKED)
    raised = jnp.exp(scores - jnp.max(scores, -1, keepdims=True))
    return raised / jnp.sum(raised, -1, keepdims=True)


def gain_row(small_ref, experts, index):
    row = slice(experts + index, experts + index + 1)
    return jnp.concatenate((small_ref[0, row, :], small_ref[1, row, :]), 1).astype(F32)


def router_rows(small_ref):
    return jnp.concatenate((small_ref[0], small_ref[1]), 1)


def attend(normed, at, qkv_ref, packed_ref):
    width = normed.shape[1]
    group = 3 * HEAD_DIM
    scale = HEAD_DIM ** (-0.5)
    lane = lax.broadcasted_iota(jnp.int32, (PAD, group), 1) // HEAD_DIM
    outs = []
    for double in range(width // group // 2):
        cols = pl.ds(double * 6 * group, 6 * group)
        packed = dot(normed, qkv_ref[:, cols])
        packed_ref[at, cols] = packed.astype(BF)
        for side in range(2):
            query, keys, values = (
                packed[:, (3 * side + k) * group : (3 * side + k + 1) * group].astype(BF)
                for k in range(3)
            )
            total = jnp.zeros((PAD, group), F32)
            for head in range(3):
                mask = lane == head
                probs = head_probs(jnp.where(mask, query, jnp.zeros_like(query)), keys, scale)
                total = jnp.where(mask, dot(probs.astype(BF), values), total)
            outs.append(total)
    return jnp.concatenate(outs, 1).astype(BF)


def route(normed, small_ref, noise, ids, experts):
    logits = contract_cols(router_rows(small_ref), normed) + noise
    row = lax.broadcasted_iota(jnp.int32, logits.shape, 0)
    logits = jnp.where(row < experts, logits, MASKED)
    raised = jnp.exp(logits - jnp.max(logits, 0, keepdims=True))
    probs = raised / jnp.sum(raised, 0, keepdims=True)
    chosen = ((row == ids[0:1]) | (row == ids[1:2])).astype(F32)
    shifted = row - experts
    flags = (((shifted == ids[0:1]) | (shifted == ids[1:2])) & (shifted >= 0)).astype(F32)
    return probs, probs * chosen + flags


def front_image(image, experts, x_ref, small_ref, qkv_ref, out_ref, noise_ref, ids_ref, keep, ready=None):
    normed_ref, packed_ref, attended_ref, middle_ref = keep
    at = pl.ds(image * PAD, PAD)
    x = x_ref[at, :].astype(F32)
    unit, _ = norm_parts(x)
    normed = (unit * gain_row(small_ref, experts, 0) + gain_row(small_ref, experts, 1)).astype(BF)
    normed_ref[at, :] = normed
    attended = attend(normed, at, qkv_ref, packed_ref)
    attended_ref[at, :] = attended
    if ready is not None:
        ready()
    middle = x + dot(attended, out_ref[...])
    middle_ref[at, :] = middle
    unit, _ = norm_parts(middle)
    normed = (unit * gain_row(small_ref, experts, 2) + gain_row(small_ref, experts, 3)).astype(BF)
    cols = slice(image * PAD, (image + 1) * PAD)
    probs, flags = route(normed, small_ref, noise_ref[:, cols], ids_ref[:, cols], experts)
    return normed, probs, flags


def front_kernel(
    x_ref, small_ref, qkv_ref, out_ref, noise_ref, ids_ref,
    normed_ref, packed_ref, attended_ref, middle_ref, rows_ref, flag_ref, prob_ref,
):
    keep = (normed_ref, packed_ref, attended_ref, middle_ref)
    probs, flags = [], []
    for image in range(x_ref.shape[0] // PAD):
        normed, prob, flag = front_image(
            image, TALL // 2, x_ref, small_ref, qkv_ref, out_ref, noise_ref, ids_ref, keep
        )
        rows_ref[pl.ds(image * PAD, PAD), :] = normed
        probs.append(prob)
        flags.append(flag)
    prob_ref[...] = jnp.concatenate(probs, 1)
    flag_ref[...] = jnp.concatenate(flags, 1).astype(BF)


def front(x, small, qkv, out, noise, ids):
    rows, width = x.shape
    shape = jax.ShapeDtypeStruct
    return pl.pallas_call(
        front_kernel,
        out_shape=(
            shape((rows, width), BF),
            shape((rows, 3 * width), BF),
            shape((rows, width), BF),
            shape((rows, width), F32),
            shape((rows, width), BF),
            shape((TALL, rows), BF),
            shape((TALL, rows), F32),
        ),
        compiler_params=pltpu.CompilerParams(vmem_limit_bytes=BIG),
        cost_estimate=pl.CostEstimate(flops=8 * 10**9, bytes_accessed=10**7, transcendentals=10**6),
        name="front",
    )(x, small, qkv, out, noise, ids)


class Place:
    def __init__(self):
        shard, head, tensor = (lax.axis_index(axis) for axis in AXES)
        self.shard, self.head, self.tensor = shard, head, tensor
        self.pair, self.side = lax.rem(head, 2), lax.div(head, 2)
        self.across = (1 - shard, head, tensor)
        self.beside = (shard, lax.rem(head + 2, 4), tensor)
        self.twin = (shard, head + 1 - 2 * self.pair, tensor)
        self.above = (shard, head, lax.rem(tensor + 1, 4))
        self.below = (shard, head, lax.rem(tensor + 3, 4))

    def greet(self, line=False):
        barrier = pltpu.get_barrier_semaphore()
        devices = [self.across, self.beside, self.twin, self.above, self.below]
        if line:
            devices.append((self.shard, self.head, lax.rem(self.tensor + 2, 4)))
        for device in devices:
            pl.semaphore_signal(barrier, inc=1, device_id=device, device_id_type=MESH)
        pl.semaphore_wait(barrier, len(devices))


class Links:
    def __init__(self, send, recv):
        self.send, self.recv, self.used = send, recv, 0
        self.sent = []

    def copy(self, source, target, device):
        index = self.used
        self.used += 1
        return pltpu.make_async_remote_copy(
            src_ref=source, dst_ref=target, send_sem=self.send.at[index], recv_sem=self.recv.at[index],
            device_id=device, device_id_type=MESH,
        )

    def start(self, source, target, device):
        copy = self.copy(source, target, device)
        copy.start()
        self.sent.append((None, copy))
        return copy

    def skip(self, done):
        self.sent = [(when, copy) for when, copy in self.sent if copy is not done]

    def finish(self):
        for when, copy in self.sent:
            if when is None:
                copy.wait_send()
            else:
                pl.when(when)(copy.wait_send)


class LineGather:
    def __init__(self, links, place, view, own, parts):
        self.links, self.place, self.view, self.own = links, place, view, own
        self.copies = {}
        self.parts = parts

    def start(self, part, step):
        t = self.place.tensor
        for name, slot, device, sends in (
            ("up", t - step, self.place.above, (t >= step) & (t < 3)),
            ("down", t + step, self.place.below, (t + step <= 3) & (t > 0)),
        ):
            slot = jnp.clip(slot, 0, 3)
            source = self.own(part) if step == 0 else self.view(slot, part)
            copy = self.links.copy(source, self.view(slot, part), device)
            pl.when(sends)(copy.start)
            self.links.sent.append((sends, copy))
            self.copies[name, part, step] = copy

    def wait(self, part, step, then=None):
        t = self.place.tensor
        for name, slot, comes in (("up", t - 1 - step, t >= step + 1), ("down", t + 1 + step, t + 1 + step <= 3)):
            copy = self.copies[name, part, step]

            @pl.when(comes)
            def _():
                copy.wait_recv()

    def arrived(self, step):
        t = self.place.tensor
        return (
            (jnp.clip(t - 1 - step, 0, 3), t >= step + 1),
            (jnp.clip(t + 1 + step, 0, 3), t + 1 + step <= 3),
        )


def head_kernel(
    x_ref, cot_ref, small_own, qkv_own, out_own, expert_in, expert_out, noise_ref, ids_ref,
    small_ref, qkv_ref, out_ref, normed_ref, packed_ref, attended_ref, middle_ref, prob_ref,
    rows_all, flags_all, cot_all, got_in, got_out,
    sent_rows, sent_flags, send, recv, local_sem,
):
    place = Place()
    links = Links(send, recv)
    width = x_ref.shape[1]
    experts = expert_in.shape[0]
    depth = qkv_own.shape[0]
    quarter = depth // 4
    shard, pair, side, tensor = place.shard, place.pair, place.side, place.tensor
    mine = pair * 4 + tensor
    place.greet()

    def dense_rows(owner, across_side, across_pair, start, size):
        return pl.ds(pl.multiple_of(owner * depth + (across_side * 2 + across_pair) * quarter + start, TALL), size)

    pieces = ((qkv_own, qkv_ref, 0, quarter // 2), (qkv_own, qkv_ref, quarter // 2, quarter // 2), (out_own, out_ref, 0, quarter))
    smalls = links.start(small_own, small_ref.at[shard], place.across)
    cross = []
    for own, full, start, size in pieces:
        source = own.at[pl.ds(pl.multiple_of((side * 2 + pair) * quarter + start, TALL), size), :]
        cross.append(links.start(source, full.at[dense_rows(shard, side, pair, start, size), :], place.across))

    def expert_item(item):
        index = side * 2 + item // 2
        source, target = (expert_in, got_in) if item % 2 == 0 else (expert_out, got_out)
        return source.at[pair * (experts // 2) + index], target.at[index]

    fetched = [links.start(*expert_item(item), place.across) for item in range(4)]
    here = pl.ds(pl.multiple_of(shard * depth, TALL), depth)
    locals_ = [
        pltpu.make_async_copy(qkv_own, qkv_ref.at[here, :], local_sem.at[0]),
        pltpu.make_async_copy(out_own, out_ref.at[here, :], local_sem.at[1]),
        pltpu.make_async_copy(small_own, small_ref.at[shard], local_sem.at[2]),
        pltpu.make_async_copy(cot_ref, cot_all.at[mine], local_sem.at[3]),
    ]
    for copy in locals_:
        copy.start()

    def slots(array):
        def view(slot, part):
            return array.at[pair * 4 + slot, pl.ds(part * PAD, PAD), :]

        return view

    cot_line = LineGather(links, place, slots(cot_all), lambda part: cot_ref.at[pl.ds(part * PAD, PAD), :], 2)
    for part in range(2):
        cot_line.start(part, 0)

    beside, twins = [], []
    for index, (own, full, start, size) in enumerate(pieces):
        cross[index].wait_recv()
        rows = full.at[dense_rows(1 - shard, side, pair, start, size), :]
        beside.append(links.start(rows, rows, place.beside))
        twins.append(links.start(rows, rows, place.twin))
    for part in range(2):
        cot_line.wait(part, 0)
        cot_line.start(part, 1)
    for index, (own, full, start, size) in enumerate(pieces):
        beside[index].wait_recv()
        rows = full.at[dense_rows(1 - shard, 1 - side, pair, start, size), :]
        twins.append(links.start(rows, rows, place.twin))

    for part in range(2):
        cot_line.wait(part, 1)
        cot_line.start(part, 2)
    smalls.wait_recv()
    for index, copy in enumerate(twins):
        if index % len(pieces) < 2:
            copy.wait_recv()
    for copy in locals_:
        copy.wait()

    keep = (normed_ref, packed_ref, attended_ref, middle_ref)
    row_line = LineGather(links, place, slots(rows_all), lambda part: sent_rows.at[pl.ds(part * PAD, PAD), :], 2)
    flag_line = LineGather(links, place, lambda slot, part: flags_all.at[pair * 4 + slot], lambda part: sent_flags, 1)
    probs, flags = [], []

    def out_ready():
        for index, copy in enumerate(twins):
            if index % len(pieces) == 2:
                copy.wait_recv()

    twin_rows = []
    forwarded = []

    def forward_expert(item):
        fetched[item].wait_recv()
        _, target = expert_item(item)
        forwarded.append(links.start(target, target, place.beside))

    for image in range(2):
        normed, prob, flag = front_image(
            image, experts, x_ref, small_ref, qkv_ref, out_ref, noise_ref, ids_ref, keep,
            out_ready if image == 0 else None,
        )
        at = pl.ds(image * PAD, PAD)
        sent_rows[at, :] = normed
        row_line.start(image, 0)
        twin_rows.append(links.start(sent_rows.at[at, :], rows_all.at[mine, at, :], place.twin))
        probs.append(prob)
        flags.append(flag)
        forward_expert(image)
    prob_ref[...] = jnp.concatenate(probs, 1)
    sent_flags[...] = jnp.concatenate(flags, 1).astype(BF)
    flag_line.start(0, 0)
    twin_flags = [links.start(sent_flags, flags_all.at[mine], place.twin)]
    keep_own = [
        pltpu.make_async_copy(sent_rows, rows_all.at[mine], local_sem.at[0]),
        pltpu.make_async_copy(sent_flags, flags_all.at[mine], local_sem.at[1]),
    ]
    for copy in keep_own:
        copy.start()

    def share(line, array, part, step, copies, whole):
        for slot, comes in line.arrived(step):
            index = pair * 4 + slot
            ref = array.at[index] if whole else array.at[index, pl.ds(part * PAD, PAD), :]
            copy = links.copy(ref, ref, place.twin)
            pl.when(comes)(copy.start)
            links.sent.append((comes, copy))
            copies.append((comes, copy))

    twin_steps = []
    for step in range(3):
        for part in range(2):
            row_line.wait(part, step)
            if step < 2:
                row_line.start(part, step + 1)
            share(row_line, rows_all, part, step, twin_steps, False)
        if step < 2:
            forward_expert(step + 2)
        flag_line.wait(0, step)
        if step < 2:
            flag_line.start(0, step + 1)
        share(flag_line, flags_all, 0, step, twin_steps, True)
        if step == 0:
            for part in range(2):
                cot_line.wait(part, 2)
            ours = cot_all.at[pl.ds(pair * 4, 4)]
            twin_cot = links.start(ours, ours, place.twin)

    for copy in twin_rows + twin_flags + [twin_cot] + forwarded:
        copy.wait_recv()
    for comes, copy in twin_steps:
        pl.when(comes)(copy.wait_recv)
    for copy in keep_own:
        copy.wait()
    links.finish()


def head(x, cot, small, qkv, out, expert_in, expert_out, noise, ids):
    rows, width = x.shape
    depth = qkv.shape[0]
    count = expert_in.shape[0] // 2
    shape = jax.ShapeDtypeStruct
    anywhere = pl.BlockSpec(memory_space=pl.ANY)
    vmem = pl.BlockSpec(memory_space=pltpu.VMEM)
    return pl.pallas_call(
        head_kernel,
        out_shape=(
            shape((2, TALL, depth), BF),
            shape((width, 3 * width), BF),
            shape((width, width), BF),
            shape((rows, width), BF),
            shape((rows, 3 * width), BF),
            shape((rows, width), BF),
            shape((rows, width), F32),
            shape((TALL, rows), F32),
            shape((8, rows, width), BF),
            shape((8, TALL, rows), BF),
            shape((8, rows, width), BF),
            shape((count,) + expert_in.shape[1:], BF),
            shape((count,) + expert_out.shape[1:], BF),
        ),
        in_specs=[vmem] * 3 + [anywhere] * 4 + [vmem] * 2,
        out_specs=(vmem,) * 8 + (anywhere,) * 5,
        scratch_shapes=[
            pltpu.VMEM((rows, width), BF),
            pltpu.VMEM((TALL, rows), BF),
            pltpu.SemaphoreType.DMA((96,)),
            pltpu.SemaphoreType.DMA((96,)),
            pltpu.SemaphoreType.DMA((4,)),
        ],
        compiler_params=pltpu.CompilerParams(vmem_limit_bytes=BIG, collective_id=1, has_side_effects=True),
        cost_estimate=pl.CostEstimate(flops=8 * 10**9, bytes_accessed=3 * 10**7, transcendentals=10**6),
        name="head",
    )(x, cot, small, qkv, out, expert_in, expert_out, noise, ids)


def expert_kernel(
    place_ref, rows_ref, flag_ref, cot_ref, own_in, got_in, own_out, got_out,
    total_ref, back_ref, gate_ref, grad_in, grad_out,
    inner, outer, picked, grads, gate, active, hidden_grad, made, made_back, made_gate, ranks, sum_in, sum_out,
    stage_in, stage_out, load_sem, store_sem,
):
    blocks, length, width = cot_ref.shape
    count = got_in.shape[0]
    depth = got_in.shape[1]
    pair, shard = place_ref[0], place_ref[1]
    experts = 2 * count
    capacity = blocks * TILE

    def loads(expert, slot):
        mine = pl.ds(pl.multiple_of(shard * depth, LANES), depth)
        other = pl.ds(pl.multiple_of((1 - shard) * depth, LANES), depth)
        index = pair * count + expert
        return (
            pltpu.make_async_copy(own_in.at[index], inner.at[slot, mine, :], load_sem.at[slot, 0]),
            pltpu.make_async_copy(got_in.at[expert], inner.at[slot, other, :], load_sem.at[slot, 1]),
            pltpu.make_async_copy(own_out.at[index], outer.at[slot, :, mine], load_sem.at[slot, 2]),
            pltpu.make_async_copy(got_out.at[expert], outer.at[slot, :, other], load_sem.at[slot, 3]),
        )

    def stores(expert, slot):
        return (
            pltpu.make_async_copy(stage_in.at[slot], grad_in.at[expert], store_sem.at[slot, 0]),
            pltpu.make_async_copy(stage_out.at[slot], grad_out.at[expert], store_sem.at[slot, 1]),
        )

    for copy in loads(0, 0):
        copy.start()
    ahead = lax.broadcasted_iota(jnp.int32, (length, length), 0)
    behind = lax.broadcasted_iota(jnp.int32, (length, length), 1)
    order = jnp.where(behind < ahead, 1.0, jnp.where(behind == ahead, FAR, 0.0)).astype(BF)

    def rank(block, carry):
        ranks[block] = contract_cols(flag_ref[block], order) - FAR
        total_ref[block] = jnp.zeros(total_ref.shape[1:], BF)
        back_ref[block] = jnp.zeros(back_ref.shape[1:], BF)
        gate_ref[block] = jnp.zeros(gate_ref.shape[1:], BF)
        return carry

    lax.fori_loop(0, blocks, rank, 0)

    for expert in range(count):
        slot = expert % 2
        if expert + 1 < count:
            for copy in loads(expert + 1, 1 - slot):
                copy.start()
        line = pl.ds(experts + pair * count + expert, 1)
        highest = ranks[0, line, :]
        for block in range(1, blocks):
            highest = jnp.maximum(highest, ranks[block, line, :])
        passes = (jnp.maximum(jnp.max(highest), -1.0).astype(jnp.int32) + TILE) // TILE
        sum_in[...] = jnp.zeros(sum_in.shape, F32)
        sum_out[...] = jnp.zeros(sum_out.shape, F32)
        for copy in loads(expert, slot):
            copy.wait()

        def one_pass(step, carry):
            base = (step * TILE).astype(F32)
            slots = lax.broadcasted_iota(jnp.int32, (TILE, length), 0).astype(F32) + base

            def take(block, carry):
                choose = (ranks[block, line, :] == slots).astype(BF)
                at = pl.ds(pl.multiple_of(block * TILE, TILE), TILE)
                picked[at, :] = dot(choose, rows_ref[block]).astype(BF)
                grads[at, :] = dot(choose, cot_ref[block]).astype(BF)
                columns = contract_cols(choose, flag_ref[block])
                lane = lax.broadcasted_iota(jnp.int32, (TILE, TALL), 1)
                column = jnp.where(lane == pair * count + expert, columns, 0.0)
                gate[at, :] = jnp.broadcast_to(jnp.sum(column, -1, keepdims=True), (TILE, LANES))
                return carry

            lax.fori_loop(0, blocks, take, 0, unroll=2)

            def chunk(index, carry):
                at = pl.ds(pl.multiple_of(index * CHUNK, CHUNK), CHUNK)
                value = dot(picked[at, :], inner[slot])
                grad_active = contract_cols(grads[at, :], outer[slot])
                gate_column = gate[at, 0:1]
                square = value * value
                bent = jnp.tanh(ROOT * value * (1.0 + CUBIC * square))
                plus = 0.5 * (1.0 + bent)
                bowed = value * plus
                slope = plus + (0.5 * ROOT) * value * (1.0 - bent * bent) * (1.0 + (3.0 * CUBIC) * square)
                active[at, :] = (bowed * gate_column).astype(BF)
                back = (grad_active * gate_column * slope).astype(BF)
                hidden_grad[at, :] = back
                lane = lax.broadcasted_iota(jnp.int32, (CHUNK, TALL), 1)
                gate_grad = jnp.sum(grad_active * bowed, -1, keepdims=True)
                made_gate[at, :] = jnp.where(lane == pair * count + expert, gate_grad, 0.0).astype(BF)
                made[at, :] = dot(active[at, :], outer[slot]).astype(BF)
                made_back[at, :] = contract_cols(back, inner[slot]).astype(BF)
                return carry

            lax.fori_loop(0, capacity // CHUNK, chunk, 0)
            hidden = sum_in.shape[1]
            for start in range(0, hidden, CHUNK):
                at = pl.ds(start, CHUNK)
                sum_out[at, :] += contract_rows(active[:, at], grads[...])
            for start in range(0, width, CHUNK):
                at = pl.ds(start, CHUNK)
                sum_in[at, :] += contract_rows(picked[:, at], hidden_grad[...])

            def give(block, carry):
                choose = (ranks[block, line, :] == slots).astype(BF)
                at = pl.ds(pl.multiple_of(block * TILE, TILE), TILE)
                total_ref[block] = (total_ref[block].astype(F32) + contract_rows(choose, made[at, :])).astype(BF)
                back_ref[block] = (back_ref[block].astype(F32) + contract_rows(choose, made_back[at, :])).astype(BF)
                gate_ref[block] = (gate_ref[block].astype(F32) + contract_rows(made_gate[at, :], choose)).astype(BF)
                return carry

            lax.fori_loop(0, blocks, give, 0, unroll=2)
            return carry

        lax.fori_loop(0, passes, one_pass, 0)
        if expert >= 2:
            for copy in stores(expert - 2, slot):
                copy.wait()
        stage_in[slot] = sum_in[...].astype(BF)
        stage_out[slot] = sum_out[...].astype(BF)
        for copy in stores(expert, slot):
            copy.start()
    for expert in range(max(count - 2, 0), count):
        for copy in stores(expert, expert % 2):
            copy.wait()


def expert_pass(place, rows, flags, cot, own_in, got_in, own_out, got_out):
    blocks, length, width = cot.shape
    count, _, hidden = got_in.shape
    capacity = blocks * TILE
    shape = jax.ShapeDtypeStruct
    anywhere = pl.BlockSpec(memory_space=pl.ANY)
    vmem = pl.BlockSpec(memory_space=pltpu.VMEM)
    return pl.pallas_call(
        expert_kernel,
        out_shape=(
            shape((blocks, length, width), BF),
            shape((blocks, length, width), BF),
            shape((blocks, TALL, length), BF),
            shape((count, width, hidden), BF),
            shape((count, hidden, width), BF),
        ),
        in_specs=[pl.BlockSpec(memory_space=pltpu.SMEM), vmem, vmem, vmem] + [anywhere] * 4,
        out_specs=(vmem, vmem, vmem, anywhere, anywhere),
        scratch_shapes=[
            pltpu.VMEM((2, width, hidden), BF),
            pltpu.VMEM((2, hidden, width), BF),
            pltpu.VMEM((capacity, width), BF),
            pltpu.VMEM((capacity, width), BF),
            pltpu.VMEM((capacity, LANES), F32),
            pltpu.VMEM((capacity, hidden), BF),
            pltpu.VMEM((capacity, hidden), BF),
            pltpu.VMEM((capacity, width), BF),
            pltpu.VMEM((capacity, width), BF),
            pltpu.VMEM((capacity, TALL), BF),
            pltpu.VMEM((blocks, TALL, length), F32),
            pltpu.VMEM((width, hidden), F32),
            pltpu.VMEM((hidden, width), F32),
            pltpu.VMEM((2, width, hidden), BF),
            pltpu.VMEM((2, hidden, width), BF),
            pltpu.SemaphoreType.DMA((2, 4)),
            pltpu.SemaphoreType.DMA((2, 2)),
        ],
        compiler_params=pltpu.CompilerParams(vmem_limit_bytes=BIG),
        cost_estimate=pl.CostEstimate(flops=50 * 10**9, bytes_accessed=5 * 10**7, transcendentals=10**6),
        name="experts",
    )(place, rows, flags, cot, own_in, got_in, own_out, got_out)


def back_middle(at, moe, gates, cot, middle, rows, probs, flags, small_ref, sums):
    experts = TALL // 2
    row = lax.broadcasted_iota(jnp.int32, flags.shape, 0)
    chosen = jnp.where(row < experts, pltpu.roll(flags, experts, 0), 0.0)
    asked = gates * chosen
    grad_logits = probs * (asked - jnp.sum(probs * asked, 0, keepdims=True))
    coarse = grad_logits.astype(BF)
    fine = (grad_logits - coarse.astype(F32)).astype(BF)
    router = router_rows(small_ref)
    sums[4] = sums[4] + dot(coarse, rows) + dot(fine, rows)
    grad = moe + contract_rows(coarse, router) + contract_rows(fine, router)
    unit, inverse = norm_parts(middle)
    sums[2] = sums[2] + jnp.sum(grad * unit, 0, keepdims=True)
    sums[3] = sums[3] + jnp.sum(grad, 0, keepdims=True)
    return cot + norm_back(grad, unit, inverse, gain_row(small_ref, experts, 2))


def back_heads(at, double, grad_proj, packed_ref, out_ref, stacked):
    width = grad_proj.shape[1]
    group = 3 * HEAD_DIM
    scale = HEAD_DIM ** (-0.5)
    lanes = lax.broadcasted_iota(jnp.int32, (PAD, group), 1) // HEAD_DIM
    made = []
    packed = packed_ref[at, pl.ds(double * 6 * group, 6 * group)]
    for side in range(2):
        query, keys, values = (packed[:, (3 * side + k) * group : (3 * side + k + 1) * group] for k in range(3))
        index = double * 2 + side
        grad_att = contract_cols(grad_proj, out_ref[pl.ds(index * group, group), :]).astype(BF)
        outs = [jnp.zeros((PAD, group), F32) for _ in range(3)]
        for head in range(3):
            mask = lanes == head
            probs = head_probs(jnp.where(mask, query, jnp.zeros_like(query)), keys, scale)
            part = jnp.where(mask, grad_att, jnp.zeros_like(grad_att))
            grad_weights = contract_cols(part, values)
            inner_sum = jnp.sum(probs * grad_weights, -1, keepdims=True)
            grad_scores = (probs * (grad_weights - inner_sum)).astype(BF)
            outs[0] = jnp.where(mask, dot(grad_scores, keys), outs[0])
            outs[1] = jnp.where(mask, contract_rows(grad_scores, query), outs[1])
            outs[2] = jnp.where(mask, contract_rows(probs.astype(BF), grad_att), outs[2])
        made += [outs[0] * scale, outs[1] * scale, outs[2]]
    stacked[at, pl.ds(double * 6 * group, 6 * group)] = jnp.concatenate(made, 1).astype(BF)


def back_kernel(
    moe_ref, gate_ref, cot_ref, x_ref, middle_ref, rows_ref, flag_ref, prob_ref, attended_ref, packed_ref, normed_ref,
    small_ref, qkv_ref, out_ref,
    tokens_ref, grad_qkv, grad_out, grad_small,
    stacked, projected,
):
    rows, width = x_ref.shape
    experts = TALL // 2
    sums = [jnp.zeros((1, width), F32) for _ in range(4)] + [jnp.zeros((TALL, width), F32)]
    for image in range(rows // PAD):
        at = pl.ds(image * PAD, PAD)
        cols = slice(image * PAD, (image + 1) * PAD)
        grad_middle = back_middle(
            at, moe_ref[at, :].astype(F32), gate_ref[:, cols].astype(F32), cot_ref[at, :].astype(F32),
            middle_ref[at, :], rows_ref[at, :], prob_ref[:, cols], flag_ref[:, cols].astype(F32), small_ref, sums,
        )
        grad_proj = grad_middle.astype(BF)
        projected[at, :] = grad_proj
        for double in range(width // (6 * HEAD_DIM)):
            back_heads(at, double, grad_proj, packed_ref, out_ref, stacked)
        grad = contract_cols(stacked[at, :], qkv_ref[...])
        unit, inverse = norm_parts(x_ref[at, :].astype(F32))
        sums[0] = sums[0] + jnp.sum(grad * unit, 0, keepdims=True)
        sums[1] = sums[1] + jnp.sum(grad, 0, keepdims=True)
        tokens_ref[at, :] = (grad_middle + norm_back(grad, unit, inverse, gain_row(small_ref, experts, 0))).astype(BF)
    grad_small[...] = jnp.concatenate([sums[4][0:experts]] + sums[:4] + [jnp.zeros((4, width), F32)], 0).astype(BF)
    grad_out[...] = contract_rows(attended_ref[...], projected[...]).astype(BF)
    for third in range(3):
        cols = pl.ds(third * width, width)
        grad_qkv[:, cols] = contract_rows(normed_ref[...], stacked[:, cols]).astype(BF)


def back(moe, gates, cot, x, middle, sent, flags, prob, attended, packed, normed, small, qkv, out):
    rows, width = x.shape
    shape = jax.ShapeDtypeStruct
    return pl.pallas_call(
        back_kernel,
        out_shape=(
            shape((rows, width), BF),
            shape((width, 3 * width), BF),
            shape((width, width), BF),
            shape((TALL, width), BF),
        ),
        scratch_shapes=[pltpu.VMEM((rows, 3 * width), BF), pltpu.VMEM((rows, width), BF)],
        compiler_params=pltpu.CompilerParams(vmem_limit_bytes=BIG),
        cost_estimate=pl.CostEstimate(flops=16 * 10**9, bytes_accessed=2 * 10**7, transcendentals=10**6),
        name="back",
    )(moe, gates, cot, x, middle, sent, flags, prob, attended, packed, normed, small, qkv, out)


ORDER = [[('x', 0), ('x', 1)], [('x', 2)], [('a', 0), ('x', 3), ('a', 1), ('x', 4), ('y', 0), ('x', 5)], [], [], [], [], [('b', 0), ('x', 6)], [('da', 0), ('b', 1), ('y', 1), ('da', 2), ('da', 3), ('y', 2), ('dl', 0), ('da', 1), ('x', 7)], [('dl', 2), ('y', 3), ('x', 8), ('dl', 3), ('db', 0), ('x', 9), ('y', 4), ('db', 2), ('y', 5), ('y', 6), ('dl', 1), ('y', 7), ('ds', 0), ('db', 3), ('c', 0), ('y', 8), ('s', 0), ('x', 10), ('c', 1), ('ds', 2), ('y', 9), ('s', 1), ('y', 10), ('s', 2), ('db', 1), ('ds', 3), ('dt', 0), ('ds', 1), ('dt', 2), ('x', 11), ('y', 11)], [('s', 3), ('dt', 3), ('dt', 1)]]


class LineScatter:
    def __init__(self, links, place, sums, up, down):
        self.links, self.place = links, place
        self.sums, self.up, self.down = sums, up, down
        self.copies = {}

    def ways(self, step):
        t = self.place.tensor
        return (
            ("up", self.up, t + 3 - step, t <= step, t >= 1, self.place.above),
            ("down", self.down, t - 3 + step, t >= 3 - step, t <= 2, self.place.below),
        )

    def send(self, part, step):
        for name, got, slot, sends, comes, device in self.ways(step):
            slot = jnp.clip(slot, 0, 3)
            if step > 0:
                before = self.copies[name, part, step - 1]

                @pl.when(sends & comes)
                def _():
                    before.wait_recv()
                    ref = self.sums(slot, part)
                    ref[...] = (ref[...].astype(F32) + got(step - 1, part)[...].astype(F32)).astype(BF)

            copy = self.links.copy(self.sums(slot, part), got(step, part), device)
            pl.when(sends)(copy.start)
            self.links.sent.append((sends, copy))
            self.copies[name, part, step] = copy

    def finish(self, part, total):
        total[...] = self.sums(self.place.tensor, part)[...].astype(F32)
        for name, got, slot, sends, comes, device in self.ways(2):
            copy = self.copies[name, part, 2]

            @pl.when(comes)
            def _():
                copy.wait_recv()
                total[...] += got(2, part)[...].astype(F32)


def tail_kernel(
    back_all, gate_all, total_all, grads_in, grads_out, rows_all, flags_all,
    cot_ref, x_ref, middle_ref, prob_ref, attended_ref, packed_ref, normed_ref, small_ref, qkv_ref, out_ref,
    mixed_ref, tokens_ref, dense_ref, grad_small, final_in, final_out, beside_in, beside_out,
    back_sum, back_got, back_up, back_down, gate_sum, gate_got, gate_up, gate_down,
    total_sum, total_got, total_up, total_down, moe, gates, rows_ref, flag_ref, projected, stacked,
    chunks, core_got, across_sent, across_got, line_sum, line_got, side_sum, side_got, line_final,
    own_in, own_out, across_in, across_out, read_in, read_out, half_in, half_out, mine_in, mine_out, both_in, both_out,
    small_sent, small_core, small_half, small_across, small_side, small_beside, small_line_sent, small_line,
    send, recv, local_sem,
):
    place = Place()
    links = Links(send, recv)
    rows, width = x_ref.shape
    experts = TALL // 2
    count = grads_in.shape[0]
    depth = width // 2
    shard, pair, side, tensor = place.shard, place.pair, place.side, place.tensor
    mine = pair * 4 + tensor
    place.greet(True)
    ours, theirs = pl.ds(pair * 4, 4), pl.ds((1 - pair) * 4, 4)

    locals_ = [
        pltpu.make_async_copy(back_all.at[ours], back_sum, local_sem.at[0]),
        pltpu.make_async_copy(gate_all.at[ours], gate_sum, local_sem.at[1]),
        pltpu.make_async_copy(total_all.at[ours], total_sum, local_sem.at[2]),
        pltpu.make_async_copy(rows_all.at[mine], rows_ref, local_sem.at[3]),
        pltpu.make_async_copy(flags_all.at[mine], flag_ref, local_sem.at[4]),
    ]
    for copy in locals_:
        copy.start()
    from_twin = [links.start(gate_all.at[theirs], gate_got, place.twin)]
    for part in range(2):
        at = pl.ds(part * PAD, PAD)
        from_twin.append(links.start(back_all.at[theirs, at, :], back_got.at[:, at, :], place.twin))
    from_twin.append(links.start(total_all.at[theirs], total_got, place.twin))

    here = pl.ds(pl.multiple_of(shard * depth, LANES), depth)
    there = pl.ds(pl.multiple_of((1 - shard) * depth, LANES), depth)
    hidden = grads_in.shape[2]
    tall, wide = depth // 2, hidden // 2
    pieces = []
    for expert in range(1, count):
        for half in range(2):
            at = pl.ds(half * tall, tall)
            pieces.append((
                grads_in.at[expert, pl.ds(pl.multiple_of((1 - shard) * depth + half * tall, TALL), tall), :],
                grads_in.at[expert, pl.ds(pl.multiple_of(shard * depth + half * tall, TALL), tall), :],
                across_in.at[expert - 1, at, :], beside_in.at[expert - 1, at, :],
                final_in.at[pair * count + expert, at, :], own_in.at[at, :], read_in.at[at, :],
            ))
        for half in range(2):
            at = pl.ds(half * wide, wide)
            pieces.append((
                grads_out.at[expert, at, there], grads_out.at[expert, at, here],
                across_out.at[expert - 1, at, :], beside_out.at[expert - 1, at, :],
                final_out.at[pair * count + expert, at, :], own_out.at[at, :], read_out.at[at, :],
            ))
    loads = [pltpu.make_async_copy(piece[1], piece[5], local_sem.at[8 + m]) for m, piece in enumerate(pieces)]
    at_across, at_beside, at_twin, kept = {}, {}, [], []
    started = [0]

    def add(target, source):
        target[...] = (target[...].astype(F32) + source[...].astype(F32)).astype(BF)

    def keep(source, target):
        copy = pltpu.make_async_copy(source, target, local_sem.at[32 + len(kept)])
        copy.start()
        kept.append(copy)

    def send_across():
        m = started[0]
        if m < len(pieces):
            at_across[m] = links.start(pieces[m][0], pieces[m][2], place.across)
            started[0] += 1

    def take_across(m):
        at_across[m].wait_recv()
        send_across()
        loads[m].wait()
        add(pieces[m][2], pieces[m][5])
        at_beside[m] = links.start(pieces[m][2], pieces[m][3], place.beside)
        if m + 4 < len(pieces):
            loads[m + 4].start()

    def take_beside(m):
        at_beside[m].wait_recv()
        load = pltpu.make_async_copy(pieces[m][3], pieces[m][6], local_sem.at[5])
        load.start()
        at_beside[m].wait_send()
        links.skip(at_beside[m])
        load.wait()
        add(pieces[m][2], pieces[m][6])
        at_twin.append(links.start(pieces[m][2], pieces[m][4], place.twin))
        keep(pieces[m][2], pieces[m][4])

    our_half = pl.ds(pl.multiple_of(side * wide, LANES), wide)
    other_half = pl.ds(pl.multiple_of((1 - side) * wide, LANES), wide)
    first = (
        (grads_in.at[0, :, other_half], grads_in.at[0, :, our_half], half_in, mine_in,
         half_in.at[there, :], half_in.at[here, :], both_in,
         final_in.at[pair * count, :, our_half], final_in.at[pair * count, :, other_half]),
        (grads_out.at[0, other_half, :], grads_out.at[0, our_half, :], half_out, mine_out,
         half_out.at[:, there], half_out.at[:, here], both_out,
         final_out.at[pair * count, our_half, :], final_out.at[pair * count, other_half, :]),
    )
    first_loads = [pltpu.make_async_copy(item[1], item[3], local_sem.at[6 + q]) for q, item in enumerate(first)]
    first_beside, first_across, first_back = {}, {}, {}

    def first_send(q):
        first_loads[q].start()
        first_beside[q] = links.start(first[q][0], first[q][2], place.beside)

    def first_sum(q):
        first_beside[q].wait_recv()
        first_loads[q].wait()
        add(first[q][2], first[q][3])
        first_across[q] = links.start(first[q][4], first[q][6], place.across)

    def first_total(q):
        first_across[q].wait_recv()
        add(first[q][6], first[q][5])
        first_back[q] = links.start(first[q][6], first[q][7], place.beside)
        at_twin.append(links.start(first[q][6], first[q][7], place.twin))
        keep(first[q][6], first[q][7])

    def first_share(q):
        first_back[q].wait_recv()
        at_twin.append(links.start(first[q][8], first[q][8], place.twin))

    share = depth // 2
    piece = share // 4
    stage = {}

    def dense_core(k):
        stage["core", k] = []
        for owner in range(2):
            source = chunks.at[k, pl.ds(pl.multiple_of(owner * depth + (1 - pair) * share, TALL), share), :]
            stage["core", k].append(links.start(source, core_got.at[k, owner], place.twin))

    def core_sum(k, owner):
        at = pl.ds(pl.multiple_of(owner * depth + pair * share, TALL), share)
        return chunks[k, at, :].astype(F32) + core_got[k, owner].astype(F32)

    def dense_across(k):
        for copy in stage["core", k]:
            copy.wait_recv()
        across_sent[k] = core_sum(k, 1 - shard).astype(BF)
        stage["across", k] = links.start(across_sent.at[k], across_got.at[k], place.across)

    def around(offset):
        return (shard, place.head, lax.rem(tensor + offset, 4))

    def dense_line(k):
        stage["across", k].wait_recv()
        line_sum[k] = (core_sum(k, shard) + across_got[k].astype(F32)).astype(BF)
        stage["line", k] = []
        for offset in (2, 1, 3):
            at = pl.ds(pl.multiple_of(lax.rem(tensor + offset, 4) * piece, TALL), piece)
            stage["line", k].append(links.start(line_sum.at[k, at, :], line_got.at[k, offset - 1], around(offset)))

    def dense_beside(k):
        for copy in stage["line", k]:
            copy.wait_recv()
        at = pl.ds(pl.multiple_of(tensor * piece, TALL), piece)
        value = line_sum[k, at, :].astype(F32)
        for offset in range(3):
            value = value + line_got[k, offset].astype(F32)
        side_sum[k] = value.astype(BF)
        stage["beside", k] = links.start(side_sum.at[k], side_got.at[k], place.beside)

    def dense_spread(k):
        stage["beside", k].wait_recv()
        line_final[k] = (side_sum[k].astype(F32) + side_got[k].astype(F32)).astype(BF)
        target = dense_ref.at[
            pl.ds(pl.multiple_of(pair * share + tensor * piece, TALL), piece), pl.ds(k * width, width)
        ]
        stage["spread", k] = [links.start(line_final.at[k], target, around(offset)) for offset in (2, 1, 3)]
        stage["keep", k] = pltpu.make_async_copy(line_final.at[k], target, local_sem.at[24 + k])
        stage["keep", k].start()

    def dense_twin(k):
        for copy in stage["spread", k]:
            copy.wait_recv()
        stage["keep", k].wait()
        block = dense_ref.at[pl.ds(pl.multiple_of(pair * share, TALL), share), pl.ds(k * width, width)]
        stage["twin", k] = links.start(block, block, place.twin)

    def small_core_stage():
        small_core_copy.wait_recv()
        other = pl.ds(pl.multiple_of((1 - shard) * depth, LANES), depth)
        small_half[...] = small_sent[:, other] + small_core[:, other]
        stage["small", 1] = links.start(small_half, small_across, place.across)

    def small_across_stage():
        stage["small", 1].wait_recv()
        own = pl.ds(pl.multiple_of(shard * depth, LANES), depth)
        small_side[...] = small_sent[:, own] + small_core[:, own] + small_across[...]
        stage["small", 2] = links.start(small_side, small_beside, place.beside)

    def small_beside_stage():
        stage["small", 2].wait_recv()
        small_line_sent[...] = small_side[...] + small_beside[...]
        stage["small", 3] = [
            links.start(small_line_sent, small_line.at[offset - 1], around(offset)) for offset in (2, 1, 3)
        ]

    def small_line_stage():
        for copy in stage["small", 3]:
            copy.wait_recv()
        grad_small[...] = small_line_sent[...] + small_line[0] + small_line[1] + small_line[2]

    def slots(array):
        def view(slot, part):
            return array.at[slot, pl.ds(part * PAD, PAD), :]

        return view

    back_line = LineScatter(links, place, slots(back_sum), slots(back_up), slots(back_down))
    total_line = LineScatter(links, place, slots(total_sum), slots(total_up), slots(total_down))
    gate_line = LineScatter(
        links, place, lambda slot, part: gate_sum.at[slot], lambda step, part: gate_up.at[step],
        lambda step, part: gate_down.at[step],
    )

    steps = {
        "x": take_across, "y": take_beside, "a": first_sum, "b": first_total, "c": first_share,
        "da": dense_across, "dl": dense_line, "db": dense_beside, "ds": dense_spread, "dt": dense_twin,
        "s": lambda index: (small_core_stage, small_across_stage, small_beside_stage, small_line_stage)[index](),
    }

    def go(slot):
        for name, index in ORDER[slot]:
            steps[name](index)

    first_send(0)
    for _ in range(3):
        send_across()
    first_send(1)
    for m in range(4):
        loads[m].start()
    locals_[1].wait()
    from_twin[0].wait_recv()
    add(gate_sum, gate_got)
    gate_line.send(0, 0)
    locals_[0].wait()
    for part in range(2):
        from_twin[1 + part].wait_recv()
        at = pl.ds(part * PAD, PAD)
        for slot in range(4):
            add(back_sum.at[slot, at, :], back_got.at[slot, at, :])
        back_line.send(part, 0)
    locals_[2].wait()
    from_twin[3].wait_recv()
    for slot in range(4):
        add(total_sum.at[slot], total_got.at[slot])
    go(0)
    gate_line.send(0, 1)
    for part in range(2):
        back_line.send(part, 1)
    go(1)
    gate_line.send(0, 2)
    for part in range(2):
        back_line.send(part, 2)
    go(2)
    for part in range(2):
        total_line.send(part, 0)
    gate_line.finish(0, gates)
    locals_[3].wait()
    locals_[4].wait()

    sums = [jnp.zeros((1, width), F32) for _ in range(4)] + [jnp.zeros((TALL, width), F32)]
    for image in range(2):
        at = pl.ds(image * PAD, PAD)
        cols = slice(image * PAD, (image + 1) * PAD)
        back_line.finish(image, moe.at[at, :])
        grad = back_middle(
            at, moe[at, :], gates[:, cols], cot_ref[at, :].astype(F32), middle_ref[at, :], rows_ref[at, :],
            prob_ref[:, cols], flag_ref[:, cols].astype(F32), small_ref, sums,
        )
        moe[at, :] = grad
        projected[at, :] = grad.astype(BF)
    go(3)
    chunks[0] = contract_rows(attended_ref[...], projected[...]).astype(BF)
    dense_core(0)
    go(4)
    for image in range(2):
        at = pl.ds(image * PAD, PAD)
        back_heads(at, 0, projected[at, :], packed_ref, out_ref, stacked)
        if image == 0:
            go(5)
    chunks[1] = contract_rows(normed_ref[...], stacked[:, pl.ds(0, width)]).astype(BF)
    dense_core(1)
    for part in range(2):
        total_line.send(part, 1)
    go(6)
    for image in range(2):
        at = pl.ds(image * PAD, PAD)
        back_heads(at, 1, projected[at, :], packed_ref, out_ref, stacked)
        if image == 0:
            go(7)
    for k in (2, 3):
        chunks[k] = contract_rows(normed_ref[...], stacked[:, pl.ds((k - 1) * width, width)]).astype(BF)
        dense_core(k)
    for part in range(2):
        total_line.send(part, 2)
    go(8)
    for image in range(2):
        at = pl.ds(image * PAD, PAD)
        grad = contract_cols(stacked[at, :], qkv_ref[...])
        unit, inverse = norm_parts(x_ref[at, :].astype(F32))
        sums[0] = sums[0] + jnp.sum(grad * unit, 0, keepdims=True)
        sums[1] = sums[1] + jnp.sum(grad, 0, keepdims=True)
        tokens_ref[at, :] = (
            moe[at, :] + norm_back(grad, unit, inverse, gain_row(small_ref, experts, 0))
        ).astype(BF)
    small_sent[...] = jnp.concatenate([sums[4][0:experts]] + sums[:4] + [jnp.zeros((4, width), F32)], 0)
    small_core_copy = links.start(small_sent, small_core, place.twin)
    go(9)
    for part in range(2):
        at = pl.ds(part * PAD, PAD)
        total_line.finish(part, moe.at[at, :])
        mixed_ref[at, :] = (middle_ref[at, :] + moe[at, :]).astype(BF)
    go(10)
    for copy in at_twin + [stage["twin", k] for k in range(4)]:
        copy.wait_recv()
    for copy in kept:
        copy.wait()
    links.finish()


def tail(back_all, gate_all, total_all, grads_in, grads_out, rows_all, flags_all, cot, x, middle, prob, attended, packed, normed, small, qkv, out):
    rows, width = x.shape
    count, _, hidden = grads_in.shape
    depth = width // 2
    shape = jax.ShapeDtypeStruct
    anywhere = pl.BlockSpec(memory_space=pl.ANY)
    vmem = pl.BlockSpec(memory_space=pltpu.VMEM)
    share, piece = depth // 2, depth // 8

    def scatter_buffers(tall, wide):
        return [pltpu.VMEM((4, tall, wide), BF)] * 2 + [pltpu.VMEM((3, tall, wide), BF)] * 2

    return pl.pallas_call(
        tail_kernel,
        out_shape=(
            shape((rows, width), BF),
            shape((rows, width), BF),
            shape((depth, 4 * width), BF),
            shape((TALL, depth), F32),
            shape((2 * count, depth, hidden), BF),
            shape((2 * count, hidden, depth), BF),
            shape((count - 1, depth, hidden), BF),
            shape((count - 1, hidden, depth), BF),
        ),
        in_specs=[anywhere] * 7 + [vmem] * 10,
        out_specs=(vmem,) * 4 + (anywhere,) * 4,
        scratch_shapes=scatter_buffers(rows, width)
        + scatter_buffers(TALL, rows)
        + scatter_buffers(rows, width)
        + [
            pltpu.VMEM((rows, width), F32),
            pltpu.VMEM((TALL, rows), F32),
            pltpu.VMEM((rows, width), BF),
            pltpu.VMEM((TALL, rows), BF),
            pltpu.VMEM((rows, width), BF),
            pltpu.VMEM((rows, 3 * width), BF),
            pltpu.VMEM((4, width, width), BF),
            pltpu.VMEM((4, 2, share, width), BF),
            pltpu.VMEM((4, share, width), BF),
            pltpu.VMEM((4, share, width), BF),
            pltpu.VMEM((4, share, width), BF),
            pltpu.VMEM((4, 3, piece, width), BF),
            pltpu.VMEM((4, piece, width), BF),
            pltpu.VMEM((4, piece, width), BF),
            pltpu.VMEM((4, piece, width), BF),
        ]
        + [pltpu.VMEM((depth, hidden), BF), pltpu.VMEM((hidden, depth), BF)]
        + [pltpu.VMEM((count - 1, depth, hidden), BF), pltpu.VMEM((count - 1, hidden, depth), BF)]
        + [pltpu.VMEM((depth, hidden), BF), pltpu.VMEM((hidden, depth), BF)]
        + [pltpu.VMEM((width, hidden // 2), BF), pltpu.VMEM((hidden // 2, width), BF)] * 2
        + [pltpu.VMEM((depth, hidden // 2), BF), pltpu.VMEM((hidden // 2, depth), BF)]
        + [
            pltpu.VMEM((TALL, width), F32),
            pltpu.VMEM((TALL, width), F32),
            pltpu.VMEM((TALL, depth), F32),
            pltpu.VMEM((TALL, depth), F32),
            pltpu.VMEM((TALL, depth), F32),
            pltpu.VMEM((TALL, depth), F32),
            pltpu.VMEM((TALL, depth), F32),
            pltpu.VMEM((3, TALL, depth), F32),
            pltpu.SemaphoreType.DMA((192,)),
            pltpu.SemaphoreType.DMA((192,)),
            pltpu.SemaphoreType.DMA((48,)),
        ],
        compiler_params=pltpu.CompilerParams(vmem_limit_bytes=BIG, collective_id=2, has_side_effects=True),
        cost_estimate=pl.CostEstimate(flops=16 * 10**9, bytes_accessed=5 * 10**7, transcendentals=10**6),
        name="tail",
    )(back_all, gate_all, total_all, grads_in, grads_out, rows_all, flags_all, cot, x, middle, prob, attended, packed, normed, small, qkv, out)


class Comm:
    def __init__(self):
        self.sizes = tuple(lax.axis_size(axis) for axis in AXES)
        self.shard = lax.axis_index("shard")
        self.head = lax.axis_index("heads")
        self.tensor = lax.axis_index("tensor")
        self.pair = self.head % 2

    def move(self, value, step):
        shards, heads, tensors = self.sizes
        pairs = []
        for s in range(shards):
            for h in range(heads):
                for t in range(tensors):
                    to = step(s, h, t)
                    if 0 <= to[2] < tensors:
                        source = (s * heads + h) * tensors + t
                        pairs.append((source, (to[0] * heads + to[1]) * tensors + to[2]))
        return lax.ppermute(value, AXES, pairs)

    def over_core(self, value):
        return self.move(value, lambda s, h, t: (s, h ^ 1, t))

    def over_heads(self, value):
        return self.move(value, lambda s, h, t: (s, (h + 2) % 4, t))

    def over_shard(self, value):
        return self.move(value, lambda s, h, t: (1 - s, h, t))

    def up(self, value):
        return self.move(value, lambda s, h, t: (s, h, t + 1))

    def down(self, value):
        return self.move(value, lambda s, h, t: (s, h, t - 1))

    def halves(self, value, index, axis):
        size = value.shape[axis] // 2
        mine = lax.dynamic_slice_in_dim(value, index * size, size, axis)
        other = lax.dynamic_slice_in_dim(value, (1 - index) * size, size, axis)
        return mine, other

    def join(self, mine, other, index, axis):
        first = jnp.where(index == 0, mine, other)
        second = jnp.where(index == 0, other, mine)
        return jnp.concatenate((first, second), axis)

    def gather_shard(self, value, axis):
        if self.sizes[0] != 2:
            return lax.all_gather(value, "shard", axis=axis, tiled=True)
        return self.join(value, self.over_shard(value), self.shard, axis)

    def gather_shard_split(self, value, axis, cut):
        if self.sizes[0] != 2:
            return lax.all_gather(value, "shard", axis=axis, tiled=True)
        mine, _ = self.halves(value, self.pair, cut)
        got = self.over_shard(mine)
        both = self.join(got, self.over_core(got), self.pair, cut)
        return self.join(value, both, self.shard, axis)

    def scatter_shard(self, value, axis):
        if self.sizes[0] != 2:
            return lax.psum_scatter(value.astype(BF), "shard", scatter_dimension=axis, tiled=True).astype(F32)
        mine, other = self.halves(value, self.shard, axis)
        return mine.astype(F32) + self.over_shard(other.astype(BF)).astype(F32)

    def scatter_core(self, value, axis):
        mine, other = self.halves(value, self.pair, axis)
        return mine.astype(F32) + self.over_core(other.astype(BF)).astype(F32)

    def scatter_heads(self, value, axis):
        mine, other = self.halves(value, self.head // 2, axis)
        return mine.astype(F32) + self.over_heads(other.astype(BF)).astype(F32)

    def line_gather(self, value):
        ups, downs = [value], [value]
        for _ in range(3):
            ups.append(self.up(ups[-1]))
            downs.append(self.down(downs[-1]))
        out = [value]
        for back in (1, 2, 3):
            out.append(jnp.where(self.tensor >= back, ups[back], downs[4 - back]))
        return out

    def line_scatter(self, parts):
        high, low = parts[1].astype(BF), parts[3].astype(BF)
        high = (parts[2].astype(F32) + self.up(high).astype(F32)).astype(BF)
        low = (parts[2].astype(F32) + self.down(low).astype(F32)).astype(BF)
        high = (parts[3].astype(F32) + self.up(high).astype(F32)).astype(BF)
        low = (parts[1].astype(F32) + self.down(low).astype(F32)).astype(BF)
        return parts[0].astype(F32) + self.up(high).astype(F32) + self.down(low).astype(F32)

    def join_slots(self, values):
        own = jnp.zeros((4,) + values[0].shape, values[0].dtype)
        for back, value in enumerate(values):
            own = lax.dynamic_update_index_in_dim(own, value, (self.tensor + 4 - back) % 4, 0)
        return self.join(own, self.over_core(own), self.pair, 0)

    def collect(self, value):
        mine, other = self.halves(value, self.pair, 0)
        mine = mine.astype(F32) + self.over_core(other).astype(F32)
        return self.line_scatter(
            [lax.dynamic_index_in_dim(mine, (self.tensor + 4 - k) % 4, 0, False) for k in range(4)]
        )


def local(
    tokens, ln1_gain, ln1_bias, qkv_weight, out_weight, ln2_gain, ln2_bias, router_weight,
    expert_in, expert_out, route_noise, expert_ids, cotangent,
):
    comm = Comm()
    rows, width = tokens.shape
    experts = expert_in.shape[0]
    images = rows // SEQ
    half = experts // 2
    padded = images * PAD

    def pad(value):
        value = value.reshape(images, SEQ, value.shape[1])
        return jnp.pad(value, ((0, 0), (0, PAD - SEQ), (0, 0))).reshape(padded, value.shape[2])

    def pad_turned(value, tall, fill):
        value = value.reshape(images, SEQ, value.shape[1]).transpose(2, 0, 1)
        value = jnp.pad(value, ((0, tall - value.shape[0]), (0, 0), (0, PAD - SEQ)), constant_values=fill)
        return value.reshape(tall, padded)

    def unpad(value):
        return value.reshape(images, PAD, value.shape[1])[:, :SEQ].reshape(rows, value.shape[1])

    small = jnp.concatenate(
        (router_weight.T, ln1_gain[None], ln1_bias[None], ln2_gain[None], ln2_bias[None]), 0
    )
    small = jnp.pad(small, ((0, TALL - small.shape[0]), (0, 0)))
    cot, x = pad(cotangent), pad(tokens)
    noise, ids = pad_turned(route_noise, TALL, 0), pad_turned(expert_ids, 8, -1)
    place = jnp.stack((comm.pair, comm.shard if comm.sizes[0] == 2 else 0 * comm.shard)).astype(jnp.int32)
    if comm.sizes[0] == 2:
        (
            small, proj_qkv, proj_out, normed_a, packed, attended, middle, prob,
            rows_all, flags_all, grad_rows, got_in, got_out,
        ) = head(x, cot, small, qkv_weight, out_weight, expert_in, expert_out, noise, ids)
        weights = (expert_in, got_in, expert_out, got_out)
    else:
        small = lax.all_gather(small, "shard", axis=1, tiled=True)
        small = small.reshape(TALL, 2, width // 2).transpose(1, 0, 2)
        proj_qkv = lax.all_gather(qkv_weight, "shard", axis=0, tiled=True)
        proj_out = lax.all_gather(out_weight, "shard", axis=0, tiled=True)
        inner = lax.all_gather(lax.dynamic_slice_in_dim(expert_in, comm.pair * half, half, 0), "shard", axis=1, tiled=True)
        outer = lax.all_gather(lax.dynamic_slice_in_dim(expert_out, comm.pair * half, half, 0), "shard", axis=2, tiled=True)
        cut = width // 2
        weights = (
            jnp.concatenate((inner[:, :cut], inner[:, :cut]), 0), inner[:, cut:],
            jnp.concatenate((outer[:, :, :cut], outer[:, :, :cut]), 0), outer[:, :, cut:],
        )
        normed_a, packed, attended, middle, sent, flags, prob = front(x, small, proj_qkv, proj_out, noise, ids)

        def gather(value):
            return comm.join_slots(comm.line_gather(value))

        grad_rows, rows_all, flags_all = gather(cot), gather(sent), gather(flags)
    total, back_all, gate_all, grads_in, grads_out = expert_pass(place, rows_all, flags_all, grad_rows, *weights)

    if comm.sizes[0] == 2:
        mixed, grad_tokens, dense, grad_small, grad_in, grad_outer, _, _ = tail(
            back_all, gate_all, total, grads_in, grads_out, rows_all, flags_all,
            cot, x, middle, prob, attended, packed, normed_a, small, proj_qkv, proj_out,
        )
        dense = dense.astype(F32)
        return (
            unpad(mixed),
            unpad(grad_tokens),
            grad_small[experts],
            grad_small[experts + 1],
            dense[:, width:],
            dense[:, :width],
            grad_small[experts + 2],
            grad_small[experts + 3],
            grad_small[:experts].T,
            grad_in.astype(F32),
            grad_outer.astype(F32),
        )

    def reduce_expert(grad, axis, other):
        part = comm.scatter_shard(grad, axis)
        part = comm.scatter_heads(part, other).astype(BF)
        return comm.join(part, comm.over_heads(part), comm.head // 2, other)

    inner_grads = [reduce_expert(grads_in[e], 0, 1) for e in range(half)]
    outer_grads = [reduce_expert(grads_out[e], 1, 0) for e in range(half)]

    moe_grad = comm.collect(back_all)
    gate_grad = comm.collect(gate_all)
    moe = comm.collect(total)
    mixed = (unpad(middle) + unpad(moe)).astype(BF)
    grad_tokens, grad_qkv, grad_out, grad_small = back(
        moe_grad, gate_grad, cot, x, middle, sent, flags, prob, attended, packed, normed_a, small, proj_qkv, proj_out
    )
    grad_tokens = unpad(grad_tokens)

    grad_small = jnp.pad(grad_small.T, ((0, 0), (0, 128 - TALL)))
    shares = jnp.concatenate((grad_qkv, grad_out, grad_small, jnp.zeros_like(grad_small)), 1)
    shares = comm.scatter_core(shares, 1)
    shares = comm.scatter_shard(shares, 0)
    shares = comm.scatter_heads(shares, 1)
    cut = shares.shape[0] // 4
    rolled = [
        lax.dynamic_slice_in_dim(shares, ((comm.tensor + 4 - k) % 4) * cut, cut, 0) for k in range(4)
    ]
    summed = comm.line_scatter(rolled).astype(BF)
    pieces = comm.line_gather(summed)
    whole = jnp.zeros(shares.shape, BF)
    for k in range(4):
        whole = lax.dynamic_update_slice_in_dim(whole, pieces[k], ((comm.tensor + 4 - k) % 4) * cut, 0)
    whole = comm.join(whole, comm.over_heads(whole), comm.head // 2, 1)
    whole = comm.join(whole, comm.over_core(whole), comm.pair, 1).astype(F32)
    small = whole[:, 4 * width : 4 * width + 128]

    grad_in, grad_outer = jnp.stack(inner_grads, 0), jnp.stack(outer_grads, 0)
    grad_in = comm.join(grad_in, comm.over_core(grad_in), comm.pair, 0).astype(F32)
    grad_outer = comm.join(grad_outer, comm.over_core(grad_outer), comm.pair, 0).astype(F32)
    return (
        mixed,
        grad_tokens,
        small[:, experts],
        small[:, experts + 1],
        whole[:, : 3 * width],
        whole[:, 3 * width : 4 * width],
        small[:, experts + 2],
        small[:, experts + 3],
        small[:, :experts],
        grad_in,
        grad_outer,
    )


def solution(mesh):
    split = P(AXES, None)
    vector, matrix = P("shard"), P("shard", None)
    inner, outer = P(None, "shard", "tensor"), P(None, "tensor", "shard")
    return jax.shard_map(
        local,
        mesh=mesh,
        in_specs=(
            split, vector, vector, matrix, matrix, vector, vector, matrix, inner, outer, split, split, split,
        ),
        out_specs=(
            split, split, vector, vector, matrix, matrix, vector, vector, matrix, inner, outer,
        ),
        check_vma=False,
    )
```

```python
import jax
import jax.numpy as jnp
from jax import lax
from jax.experimental import pallas as pl
from jax.experimental.pallas import tpu as pltpu
from jax.sharding import PartitionSpec as P

HEAD_DIM = 64
SEQ = 197
EPS = 1e-06
AXES = ("shard", "heads", "tensor")
BF = jnp.bfloat16
F32 = jnp.float32


def contract_rows(left, right):
    return lax.dot_general(left, right, (((0,), (0,)), ((), ())), preferred_element_type=F32)


def contract_cols(left, right):
    return lax.dot_general(left, right, (((1,), (1,)), ((), ())), preferred_element_type=F32)


PAD = 208
TILE = 128
CHUNK = 256
FAR = 512.0
TALL = 16
LANES = 128
MASKED = -1e30
CUBIC = 0.044715
ROOT = (2.0 / 3.141592653589793) ** 0.5
BIG = 60 * 1024 * 1024
MESH = pl.DeviceIdType.MESH


def dot(left, right):
    return jnp.dot(left, right, preferred_element_type=F32)


def norm_parts(values):
    centred = values - jnp.mean(values, -1, keepdims=True)
    inverse = lax.rsqrt(jnp.mean(centred * centred, -1, keepdims=True) + EPS)
    return centred * inverse, inverse


def norm_back(grad, unit, inverse, gain):
    scaled = grad * gain
    along = jnp.mean(scaled * unit, -1, keepdims=True)
    return inverse * (scaled - jnp.mean(scaled, -1, keepdims=True) - unit * along)


def head_probs(query, keys, scale):
    scores = contract_cols(query, keys) * scale
    column = lax.broadcasted_iota(jnp.int32, scores.shape, 1)
    scores = jnp.where(column < SEQ, scores, MASKED)
    raised = jnp.exp(scores - jnp.max(scores, -1, keepdims=True))
    return raised / jnp.sum(raised, -1, keepdims=True)


def gain_row(small_ref, experts, index):
    row = slice(experts + index, experts + index + 1)
    return jnp.concatenate((small_ref[0, row, :], small_ref[1, row, :]), 1).astype(F32)


def router_rows(small_ref):
    return jnp.concatenate((small_ref[0], small_ref[1]), 1)


def attend(normed, at, qkv_ref, packed_ref):
    width = normed.shape[1]
    group = 3 * HEAD_DIM
    scale = HEAD_DIM ** (-0.5)
    lane = lax.broadcasted_iota(jnp.int32, (PAD, group), 1) // HEAD_DIM
    outs = []
    for double in range(width // group // 2):
        cols = pl.ds(double * 6 * group, 6 * group)
        packed = dot(normed, qkv_ref[:, cols])
        packed_ref[at, cols] = packed.astype(BF)
        for side in range(2):
            query, keys, values = (
                packed[:, (3 * side + k) * group : (3 * side + k + 1) * group].astype(BF)
                for k in range(3)
            )
            total = jnp.zeros((PAD, group), F32)
            for head in range(3):
                mask = lane == head
                probs = head_probs(jnp.where(mask, query, jnp.zeros_like(query)), keys, scale)
                total = jnp.where(mask, dot(probs.astype(BF), values), total)
            outs.append(total)
    return jnp.concatenate(outs, 1).astype(BF)


def route(normed, small_ref, noise, ids, experts):
    logits = contract_cols(router_rows(small_ref), normed) + noise
    row = lax.broadcasted_iota(jnp.int32, logits.shape, 0)
    logits = jnp.where(row < experts, logits, MASKED)
    raised = jnp.exp(logits - jnp.max(logits, 0, keepdims=True))
    probs = raised / jnp.sum(raised, 0, keepdims=True)
    chosen = ((row == ids[0:1]) | (row == ids[1:2])).astype(F32)
    shifted = row - experts
    flags = (((shifted == ids[0:1]) | (shifted == ids[1:2])) & (shifted >= 0)).astype(F32)
    return probs, probs * chosen + flags


def front_image(image, experts, x_ref, small_ref, qkv_ref, out_ref, noise_ref, ids_ref, keep, ready=None):
    normed_ref, packed_ref, attended_ref, middle_ref = keep
    at = pl.ds(image * PAD, PAD)
    x = x_ref[at, :].astype(F32)
    unit, _ = norm_parts(x)
    normed = (unit * gain_row(small_ref, experts, 0) + gain_row(small_ref, experts, 1)).astype(BF)
    normed_ref[at, :] = normed
    attended = attend(normed, at, qkv_ref, packed_ref)
    attended_ref[at, :] = attended
    if ready is not None:
        ready()
    middle = x + dot(attended, out_ref[...])
    middle_ref[at, :] = middle
    unit, _ = norm_parts(middle)
    normed = (unit * gain_row(small_ref, experts, 2) + gain_row(small_ref, experts, 3)).astype(BF)
    cols = slice(image * PAD, (image + 1) * PAD)
    probs, flags = route(normed, small_ref, noise_ref[:, cols], ids_ref[:, cols], experts)
    return normed, probs, flags


def front_kernel(
    x_ref, small_ref, qkv_ref, out_ref, noise_ref, ids_ref,
    normed_ref, packed_ref, attended_ref, middle_ref, rows_ref, flag_ref, prob_ref,
):
    keep = (normed_ref, packed_ref, attended_ref, middle_ref)
    probs, flags = [], []
    for image in range(x_ref.shape[0] // PAD):
        normed, prob, flag = front_image(
            image, TALL // 2, x_ref, small_ref, qkv_ref, out_ref, noise_ref, ids_ref, keep
        )
        rows_ref[pl.ds(image * PAD, PAD), :] = normed
        probs.append(prob)
        flags.append(flag)
    prob_ref[...] = jnp.concatenate(probs, 1)
    flag_ref[...] = jnp.concatenate(flags, 1).astype(BF)


def front(x, small, qkv, out, noise, ids):
    rows, width = x.shape
    shape = jax.ShapeDtypeStruct
    return pl.pallas_call(
        front_kernel,
        out_shape=(
            shape((rows, width), BF),
            shape((rows, 3 * width), BF),
            shape((rows, width), BF),
            shape((rows, width), F32),
            shape((rows, width), BF),
            shape((TALL, rows), BF),
            shape((TALL, rows), F32),
        ),
        compiler_params=pltpu.CompilerParams(vmem_limit_bytes=BIG),
        cost_estimate=pl.CostEstimate(flops=8 * 10**9, bytes_accessed=10**7, transcendentals=10**6),
        name="front",
    )(x, small, qkv, out, noise, ids)


class Place:
    def __init__(self):
        shard, head, tensor = (lax.axis_index(axis) for axis in AXES)
        self.shard, self.head, self.tensor = shard, head, tensor
        self.pair, self.side = lax.rem(head, 2), lax.div(head, 2)
        self.across = (1 - shard, head, tensor)
        self.beside = (shard, lax.rem(head + 2, 4), tensor)
        self.twin = (shard, head + 1 - 2 * self.pair, tensor)
        self.above = (shard, head, lax.rem(tensor + 1, 4))
        self.below = (shard, head, lax.rem(tensor + 3, 4))

    def greet(self, line=False):
        barrier = pltpu.get_barrier_semaphore()
        devices = [self.across, self.beside, self.twin, self.above, self.below]
        if line:
            devices.append((self.shard, self.head, lax.rem(self.tensor + 2, 4)))
        for device in devices:
            pl.semaphore_signal(barrier, inc=1, device_id=device, device_id_type=MESH)
        pl.semaphore_wait(barrier, len(devices))


class Links:
    def __init__(self, send, recv):
        self.send, self.recv, self.used = send, recv, 0
        self.sent = []

    def copy(self, source, target, device):
        index = self.used
        self.used += 1
        return pltpu.make_async_remote_copy(
            src_ref=source, dst_ref=target, send_sem=self.send.at[index], recv_sem=self.recv.at[index],
            device_id=device, device_id_type=MESH,
        )

    def start(self, source, target, device):
        copy = self.copy(source, target, device)
        copy.start()
        self.sent.append((None, copy))
        return copy

    def skip(self, done):
        self.sent = [(when, copy) for when, copy in self.sent if copy is not done]

    def finish(self):
        for when, copy in self.sent:
            if when is None:
                copy.wait_send()
            else:
                pl.when(when)(copy.wait_send)


class LineGather:
    def __init__(self, links, place, view, own, parts):
        self.links, self.place, self.view, self.own = links, place, view, own
        self.copies = {}
        self.parts = parts

    def start(self, part, step):
        t = self.place.tensor
        for name, slot, device, sends in (
            ("up", t - step, self.place.above, (t >= step) & (t < 3)),
            ("down", t + step, self.place.below, (t + step <= 3) & (t > 0)),
        ):
            slot = jnp.clip(slot, 0, 3)
            source = self.own(part) if step == 0 else self.view(slot, part)
            copy = self.links.copy(source, self.view(slot, part), device)
            pl.when(sends)(copy.start)
            self.links.sent.append((sends, copy))
            self.copies[name, part, step] = copy

    def wait(self, part, step, then=None):
        t = self.place.tensor
        for name, slot, comes in (("up", t - 1 - step, t >= step + 1), ("down", t + 1 + step, t + 1 + step <= 3)):
            copy = self.copies[name, part, step]

            @pl.when(comes)
            def _():
                copy.wait_recv()

    def arrived(self, step):
        t = self.place.tensor
        return (
            (jnp.clip(t - 1 - step, 0, 3), t >= step + 1),
            (jnp.clip(t + 1 + step, 0, 3), t + 1 + step <= 3),
        )


def head_kernel(
    x_ref, cot_ref, small_own, qkv_own, out_own, expert_in, expert_out, noise_ref, ids_ref,
    small_ref, qkv_ref, out_ref, normed_ref, packed_ref, attended_ref, middle_ref, prob_ref,
    rows_all, flags_all, cot_all, got_in, got_out,
    sent_rows, sent_flags, send, recv, local_sem,
):
    place = Place()
    links = Links(send, recv)
    width = x_ref.shape[1]
    experts = expert_in.shape[0]
    depth = qkv_own.shape[0]
    quarter = depth // 4
    shard, pair, side, tensor = place.shard, place.pair, place.side, place.tensor
    mine = pair * 4 + tensor
    place.greet()

    def dense_rows(owner, across_side, across_pair, start, size):
        return pl.ds(pl.multiple_of(owner * depth + (across_side * 2 + across_pair) * quarter + start, TALL), size)

    pieces = ((qkv_own, qkv_ref, 0, quarter // 2), (qkv_own, qkv_ref, quarter // 2, quarter // 2), (out_own, out_ref, 0, quarter))
    smalls = links.start(small_own, small_ref.at[shard], place.across)
    cross = []
    for own, full, start, size in pieces:
        source = own.at[pl.ds(pl.multiple_of((side * 2 + pair) * quarter + start, TALL), size), :]
        cross.append(links.start(source, full.at[dense_rows(shard, side, pair, start, size), :], place.across))

    def expert_item(item):
        index = side * 2 + item // 2
        source, target = (expert_in, got_in) if item % 2 == 0 else (expert_out, got_out)
        return source.at[pair * (experts // 2) + index], target.at[index]

    fetched = [links.start(*expert_item(item), place.across) for item in range(4)]
    here = pl.ds(pl.multiple_of(shard * depth, TALL), depth)
    locals_ = [
        pltpu.make_async_copy(qkv_own, qkv_ref.at[here, :], local_sem.at[0]),
        pltpu.make_async_copy(out_own, out_ref.at[here, :], local_sem.at[1]),
        pltpu.make_async_copy(small_own, small_ref.at[shard], local_sem.at[2]),
        pltpu.make_async_copy(cot_ref, cot_all.at[mine], local_sem.at[3]),
    ]
    for copy in locals_:
        copy.start()

    def slots(array):
        def view(slot, part):
            return array.at[pair * 4 + slot, pl.ds(part * PAD, PAD), :]

        return view

    cot_line = LineGather(links, place, slots(cot_all), lambda part: cot_ref.at[pl.ds(part * PAD, PAD), :], 2)
    for part in range(2):
        cot_line.start(part, 0)

    beside, twins = [], []
    for index, (own, full, start, size) in enumerate(pieces):
        cross[index].wait_recv()
        rows = full.at[dense_rows(1 - shard, side, pair, start, size), :]
        beside.append(links.start(rows, rows, place.beside))
        twins.append(links.start(rows, rows, place.twin))
    for part in range(2):
        cot_line.wait(part, 0)
        cot_line.start(part, 1)
    for index, (own, full, start, size) in enumerate(pieces):
        beside[index].wait_recv()
        rows = full.at[dense_rows(1 - shard, 1 - side, pair, start, size), :]
        twins.append(links.start(rows, rows, place.twin))

    for part in range(2):
        cot_line.wait(part, 1)
        cot_line.start(part, 2)
    smalls.wait_recv()
    for index, copy in enumerate(twins):
        if index % len(pieces) < 2:
            copy.wait_recv()
    for copy in locals_:
        copy.wait()

    keep = (normed_ref, packed_ref, attended_ref, middle_ref)
    row_line = LineGather(links, place, slots(rows_all), lambda part: sent_rows.at[pl.ds(part * PAD, PAD), :], 2)
    flag_line = LineGather(links, place, lambda slot, part: flags_all.at[pair * 4 + slot], lambda part: sent_flags, 1)
    probs, flags = [], []

    def out_ready():
        for index, copy in enumerate(twins):
            if index % len(pieces) == 2:
                copy.wait_recv()

    twin_rows = []
    forwarded = []

    def forward_expert(item):
        fetched[item].wait_recv()
        _, target = expert_item(item)
        forwarded.append(links.start(target, target, place.beside))

    for image in range(2):
        normed, prob, flag = front_image(
            image, experts, x_ref, small_ref, qkv_ref, out_ref, noise_ref, ids_ref, keep,
            out_ready if image == 0 else None,
        )
        at = pl.ds(image * PAD, PAD)
        sent_rows[at, :] = normed
        row_line.start(image, 0)
        twin_rows.append(links.start(sent_rows.at[at, :], rows_all.at[mine, at, :], place.twin))
        probs.append(prob)
        flags.append(flag)
        forward_expert(image)
    prob_ref[...] = jnp.concatenate(probs, 1)
    sent_flags[...] = jnp.concatenate(flags, 1).astype(BF)
    flag_line.start(0, 0)
    twin_flags = [links.start(sent_flags, flags_all.at[mine], place.twin)]
    keep_own = [
        pltpu.make_async_copy(sent_rows, rows_all.at[mine], local_sem.at[0]),
        pltpu.make_async_copy(sent_flags, flags_all.at[mine], local_sem.at[1]),
    ]
    for copy in keep_own:
        copy.start()

    def share(line, array, part, step, copies, whole):
        for slot, comes in line.arrived(step):
            index = pair * 4 + slot
            ref = array.at[index] if whole else array.at[index, pl.ds(part * PAD, PAD), :]
            copy = links.copy(ref, ref, place.twin)
            pl.when(comes)(copy.start)
            links.sent.append((comes, copy))
            copies.append((comes, copy))

    twin_steps = []
    for step in range(3):
        for part in range(2):
            row_line.wait(part, step)
            if step < 2:
                row_line.start(part, step + 1)
            share(row_line, rows_all, part, step, twin_steps, False)
        if step < 2:
            forward_expert(step + 2)
        flag_line.wait(0, step)
        if step < 2:
            flag_line.start(0, step + 1)
        share(flag_line, flags_all, 0, step, twin_steps, True)
        if step == 0:
            for part in range(2):
                cot_line.wait(part, 2)
            ours = cot_all.at[pl.ds(pair * 4, 4)]
            twin_cot = links.start(ours, ours, place.twin)

    for copy in twin_rows + twin_flags + [twin_cot] + forwarded:
        copy.wait_recv()
    for comes, copy in twin_steps:
        pl.when(comes)(copy.wait_recv)
    for copy in keep_own:
        copy.wait()
    links.finish()


def head(x, cot, small, qkv, out, expert_in, expert_out, noise, ids):
    rows, width = x.shape
    depth = qkv.shape[0]
    count = expert_in.shape[0] // 2
    shape = jax.ShapeDtypeStruct
    anywhere = pl.BlockSpec(memory_space=pl.ANY)
    vmem = pl.BlockSpec(memory_space=pltpu.VMEM)
    return pl.pallas_call(
        head_kernel,
        out_shape=(
            shape((2, TALL, depth), BF),
            shape((width, 3 * width), BF),
            shape((width, width), BF),
            shape((rows, width), BF),
            shape((rows, 3 * width), BF),
            shape((rows, width), BF),
            shape((rows, width), F32),
            shape((TALL, rows), F32),
            shape((8, rows, width), BF),
            shape((8, TALL, rows), BF),
            shape((8, rows, width), BF),
            shape((count,) + expert_in.shape[1:], BF),
            shape((count,) + expert_out.shape[1:], BF),
        ),
        in_specs=[vmem] * 3 + [anywhere] * 4 + [vmem] * 2,
        out_specs=(vmem,) * 8 + (anywhere,) * 5,
        scratch_shapes=[
            pltpu.VMEM((rows, width), BF),
            pltpu.VMEM((TALL, rows), BF),
            pltpu.SemaphoreType.DMA((96,)),
            pltpu.SemaphoreType.DMA((96,)),
            pltpu.SemaphoreType.DMA((4,)),
        ],
        compiler_params=pltpu.CompilerParams(vmem_limit_bytes=BIG, collective_id=1, has_side_effects=True),
        cost_estimate=pl.CostEstimate(flops=8 * 10**9, bytes_accessed=3 * 10**7, transcendentals=10**6),
        name="head",
    )(x, cot, small, qkv, out, expert_in, expert_out, noise, ids)


def expert_kernel(
    place_ref, flag_ref, rows_all, cot_all, own_in, got_in, own_out, got_out,
    total_all, back_all, gate_ref, grad_in, grad_out,
    inner, outer, picked, grads, gate, active, hidden_grad, made, made_back, made_gate, ranks,
    rows_buf, cot_buf, total_buf, back_buf, stage_in, stage_out, load_sem, store_sem, fetch_sem, put_sem, old_sem,
):
    blocks, length, width = cot_all.shape
    count = got_in.shape[0]
    depth = got_in.shape[1]
    pair, shard = place_ref[0], place_ref[1]
    experts = 2 * count

    def loads(expert):
        slot = expert % 2
        mine = pl.ds(pl.multiple_of(shard * depth, LANES), depth)
        other = pl.ds(pl.multiple_of((1 - shard) * depth, LANES), depth)
        index = pair * count + expert
        return (
            pltpu.make_async_copy(own_in.at[index], inner.at[slot, mine, :], load_sem.at[slot, 0]),
            pltpu.make_async_copy(got_in.at[expert], inner.at[slot, other, :], load_sem.at[slot, 1]),
            pltpu.make_async_copy(own_out.at[index], outer.at[slot, :, mine], load_sem.at[slot, 2]),
            pltpu.make_async_copy(got_out.at[expert], outer.at[slot, :, other], load_sem.at[slot, 3]),
        )

    def stores(expert):
        slot = expert % 2
        return (
            pltpu.make_async_copy(stage_in.at[slot], grad_in.at[expert], store_sem.at[slot, 0]),
            pltpu.make_async_copy(stage_out.at[slot], grad_out.at[expert], store_sem.at[slot, 1]),
        )

    def fetches(block):
        slot = block % 2
        return (
            pltpu.make_async_copy(rows_all.at[block], rows_buf.at[slot], fetch_sem.at[slot, 0]),
            pltpu.make_async_copy(cot_all.at[block], cot_buf.at[slot], fetch_sem.at[slot, 1]),
        )

    def puts(block):
        slot = block % 2
        return (
            pltpu.make_async_copy(total_buf.at[slot], total_all.at[block], put_sem.at[slot, 0]),
            pltpu.make_async_copy(back_buf.at[slot], back_all.at[block], put_sem.at[slot, 1]),
        )

    def start(copies):
        for copy in copies:
            copy.start()

    def wait(copies):
        for copy in copies:
            copy.wait()

    def reload(pairs):
        copies = [pltpu.make_async_copy(source, target, old_sem.at[n]) for n, (source, target) in enumerate(pairs)]
        start(copies)
        wait(copies)

    start(fetches(0) + fetches(1) + loads(0))
    ahead = lax.broadcasted_iota(jnp.int32, (length, length), 0)
    behind = lax.broadcasted_iota(jnp.int32, (length, length), 1)
    order = jnp.where(behind < ahead, 1.0, jnp.where(behind == ahead, FAR, 0.0)).astype(BF)
    for block in range(blocks):
        ranks[block] = contract_cols(flag_ref[block], order) - FAR

    def line(expert):
        return pl.ds(experts + pair * count + expert, 1)

    passes = []
    for expert in range(count):
        highest = ranks[0, line(expert), :]
        for block in range(1, blocks):
            highest = jnp.maximum(highest, ranks[block, line(expert), :])
        passes.append((jnp.maximum(jnp.max(highest), -1.0).astype(jnp.int32) + TILE) // TILE)
    rounds = jnp.int32(1)
    for value in passes:
        rounds = jnp.maximum(rounds, value)

    def one_round(step, carry):
        again = step > 0
        slots = lax.broadcasted_iota(jnp.int32, (TILE, length), 0).astype(F32) + (step * TILE).astype(F32)

        def choices(block):
            return jnp.concatenate(
                [(ranks[block, line(expert), :] == slots).astype(BF) for expert in range(count)], 0
            )

        @pl.when(again)
        def _():
            start(fetches(0) + fetches(1) + loads(0))

        lane = lax.broadcasted_iota(jnp.int32, (count * TILE, TALL), 1)
        wanted = lax.broadcasted_iota(jnp.int32, (count * TILE, TALL), 0) // TILE + pair * count
        for block in range(blocks):
            slot = block % 2
            at = pl.ds(block * TILE, TILE)
            choose = choices(block)
            columns = jnp.where(lane == wanted, contract_cols(choose, flag_ref[block]), 0.0)
            column = jnp.broadcast_to(jnp.sum(columns, -1, keepdims=True), (count * TILE, LANES))
            wait(fetches(block))
            both = dot(choose, rows_buf[slot]).astype(BF)
            other = dot(choose, cot_buf[slot]).astype(BF)
            for expert in range(count):
                part = slice(expert * TILE, (expert + 1) * TILE)
                picked[expert, at, :] = both[part]
                grads[expert, at, :] = other[part]
                gate[expert, at, :] = column[part]
            if block + 2 < blocks:
                start(fetches(block + 2))

        for expert in range(count):
            slot = expert % 2
            runs = jnp.logical_or(step == 0, passes[expert] > step)
            if expert + 1 < count:
                start(loads(expert + 1))
            wait(loads(expert))

            @pl.when(runs)
            def _():
                def chunk(index, carry):
                    at = pl.ds(pl.multiple_of(index * CHUNK, CHUNK), CHUNK)
                    value = dot(picked[expert, at, :], inner[slot])
                    grad_active = contract_cols(grads[expert, at, :], outer[slot])
                    gate_column = gate[expert, at, 0:1]
                    square = value * value
                    bent = jnp.tanh(ROOT * value * (1.0 + CUBIC * square))
                    plus = 0.5 * (1.0 + bent)
                    bowed = value * plus
                    slope = plus + (0.5 * ROOT) * value * (1.0 - bent * bent) * (1.0 + (3.0 * CUBIC) * square)
                    active[at, :] = (bowed * gate_column).astype(BF)
                    back = (grad_active * gate_column * slope).astype(BF)
                    hidden_grad[at, :] = back
                    lane = lax.broadcasted_iota(jnp.int32, (CHUNK, TALL), 1)
                    gate_grad = jnp.sum(grad_active * bowed, -1, keepdims=True)
                    made_gate[expert, at, :] = jnp.where(lane == pair * count + expert, gate_grad, 0.0).astype(BF)
                    made[expert, at, :] = dot(active[at, :], outer[slot]).astype(BF)
                    made_back[expert, at, :] = contract_cols(back, inner[slot]).astype(BF)
                    return carry

                lax.fori_loop(0, blocks * TILE // CHUNK, chunk, 0)

            if expert >= 2:
                before = jnp.logical_or(step == 0, passes[expert - 2] > step)

                @pl.when(before)
                def _():
                    wait(stores(expert - 2))

            @pl.when(runs)
            def _():
                for stage, grad, left, right in (
                    (stage_out, grad_out, active, grads.at[expert]), (stage_in, grad_in, picked.at[expert], hidden_grad),
                ):
                    @pl.when(again)
                    def _():
                        reload([(grad.at[expert], stage.at[slot])])

                    for begin in range(0, left.shape[1], CHUNK):
                        at = pl.ds(begin, CHUNK)
                        value = contract_rows(left[:, at], right[...])
                        old = stage[slot, at, :].astype(F32)
                        stage[slot, at, :] = (value + jnp.where(again, old, 0.0)).astype(BF)
                start(stores(expert))

        for block in range(blocks):
            slot = block % 2
            at = pl.ds(block * TILE, TILE)
            choose = choices(block)
            if block >= 2:
                wait(puts(block - 2))

            def joined(source):
                return jnp.concatenate([source[expert, at, :] for expert in range(count)], 0)

            @pl.when(again)
            def _():
                reload([(total_all.at[block], rows_buf.at[0]), (back_all.at[block], rows_buf.at[1])])

            for target, source, old in ((total_buf, made, 0), (back_buf, made_back, 1)):
                target[slot] = contract_rows(choose, joined(source)).astype(BF)

                @pl.when(again)
                def _():
                    target[slot] = (target[slot].astype(F32) + rows_buf[old].astype(F32)).astype(BF)

            start(puts(block))
            gates = contract_rows(joined(made_gate), choose)
            gate_ref[block] = (gates + jnp.where(again, gate_ref[block].astype(F32), 0.0)).astype(BF)
        for block in range(blocks - 2, blocks):
            wait(puts(block))
        for expert in range(count - 2, count):

            @pl.when(jnp.logical_or(step == 0, passes[expert] > step))
            def _():
                wait(stores(expert))

        return carry

    lax.fori_loop(0, rounds, one_round, 0)


def expert_pass(place, rows, flags, cot, own_in, got_in, own_out, got_out):
    blocks, length, width = cot.shape
    count, _, hidden = got_in.shape
    capacity = blocks * TILE
    shape = jax.ShapeDtypeStruct
    anywhere = pl.BlockSpec(memory_space=pl.ANY)
    vmem = pl.BlockSpec(memory_space=pltpu.VMEM)
    return pl.pallas_call(
        expert_kernel,
        out_shape=(
            shape((blocks, length, width), BF),
            shape((blocks, length, width), BF),
            shape((blocks, TALL, length), BF),
            shape((count, width, hidden), BF),
            shape((count, hidden, width), BF),
        ),
        in_specs=[pl.BlockSpec(memory_space=pltpu.SMEM), vmem] + [anywhere] * 6,
        out_specs=(anywhere, anywhere, vmem, anywhere, anywhere),
        scratch_shapes=[
            pltpu.VMEM((2, width, hidden), BF),
            pltpu.VMEM((2, hidden, width), BF),
            pltpu.VMEM((count, capacity, width), BF),
            pltpu.VMEM((count, capacity, width), BF),
            pltpu.VMEM((count, capacity, LANES), F32),
            pltpu.VMEM((capacity, hidden), BF),
            pltpu.VMEM((capacity, hidden), BF),
            pltpu.VMEM((count, capacity, width), BF),
            pltpu.VMEM((count, capacity, width), BF),
            pltpu.VMEM((count, capacity, TALL), BF),
            pltpu.VMEM((blocks, TALL, length), F32),
            pltpu.VMEM((2, length, width), BF),
            pltpu.VMEM((2, length, width), BF),
            pltpu.VMEM((2, length, width), BF),
            pltpu.VMEM((2, length, width), BF),
            pltpu.VMEM((2, width, hidden), BF),
            pltpu.VMEM((2, hidden, width), BF),
            pltpu.SemaphoreType.DMA((2, 4)),
            pltpu.SemaphoreType.DMA((2, 2)),
            pltpu.SemaphoreType.DMA((2, 2)),
            pltpu.SemaphoreType.DMA((2, 2)),
            pltpu.SemaphoreType.DMA((2,)),
        ],
        compiler_params=pltpu.CompilerParams(vmem_limit_bytes=BIG),
        cost_estimate=pl.CostEstimate(flops=50 * 10**9, bytes_accessed=5 * 10**7, transcendentals=10**6),
        name="experts",
    )(place, flags, rows, cot, own_in, got_in, own_out, got_out)


def back_middle(at, moe, gates, cot, middle, rows, probs, flags, small_ref, sums):
    experts = TALL // 2
    row = lax.broadcasted_iota(jnp.int32, flags.shape, 0)
    chosen = jnp.where(row < experts, pltpu.roll(flags, experts, 0), 0.0)
    asked = gates * chosen
    grad_logits = probs * (asked - jnp.sum(probs * asked, 0, keepdims=True))
    coarse = grad_logits.astype(BF)
    fine = (grad_logits - coarse.astype(F32)).astype(BF)
    router = router_rows(small_ref)
    sums[4] = sums[4] + dot(coarse, rows) + dot(fine, rows)
    grad = moe + contract_rows(coarse, router) + contract_rows(fine, router)
    unit, inverse = norm_parts(middle)
    sums[2] = sums[2] + jnp.sum(grad * unit, 0, keepdims=True)
    sums[3] = sums[3] + jnp.sum(grad, 0, keepdims=True)
    return cot + norm_back(grad, unit, inverse, gain_row(small_ref, experts, 2))


def back_heads(at, double, grad_proj, packed_ref, out_ref, stacked):
    width = grad_proj.shape[1]
    group = 3 * HEAD_DIM
    scale = HEAD_DIM ** (-0.5)
    lanes = lax.broadcasted_iota(jnp.int32, (PAD, group), 1) // HEAD_DIM
    made = []
    packed = packed_ref[at, pl.ds(double * 6 * group, 6 * group)]
    for side in range(2):
        query, keys, values = (packed[:, (3 * side + k) * group : (3 * side + k + 1) * group] for k in range(3))
        index = double * 2 + side
        grad_att = contract_cols(grad_proj, out_ref[pl.ds(index * group, group), :]).astype(BF)
        outs = [jnp.zeros((PAD, group), F32) for _ in range(3)]
        for head in range(3):
            mask = lanes == head
            probs = head_probs(jnp.where(mask, query, jnp.zeros_like(query)), keys, scale)
            part = jnp.where(mask, grad_att, jnp.zeros_like(grad_att))
            grad_weights = contract_cols(part, values)
            inner_sum = jnp.sum(probs * grad_weights, -1, keepdims=True)
            grad_scores = (probs * (grad_weights - inner_sum)).astype(BF)
            outs[0] = jnp.where(mask, dot(grad_scores, keys), outs[0])
            outs[1] = jnp.where(mask, contract_rows(grad_scores, query), outs[1])
            outs[2] = jnp.where(mask, contract_rows(probs.astype(BF), grad_att), outs[2])
        made += [outs[0] * scale, outs[1] * scale, outs[2]]
    stacked[at, pl.ds(double * 6 * group, 6 * group)] = jnp.concatenate(made, 1).astype(BF)


def back_kernel(
    moe_ref, gate_ref, cot_ref, x_ref, middle_ref, rows_ref, flag_ref, prob_ref, attended_ref, packed_ref, normed_ref,
    small_ref, qkv_ref, out_ref,
    tokens_ref, grad_qkv, grad_out, grad_small,
    stacked, projected,
):
    rows, width = x_ref.shape
    experts = TALL // 2
    sums = [jnp.zeros((1, width), F32) for _ in range(4)] + [jnp.zeros((TALL, width), F32)]
    for image in range(rows // PAD):
        at = pl.ds(image * PAD, PAD)
        cols = slice(image * PAD, (image + 1) * PAD)
        grad_middle = back_middle(
            at, moe_ref[at, :].astype(F32), gate_ref[:, cols].astype(F32), cot_ref[at, :].astype(F32),
            middle_ref[at, :], rows_ref[at, :], prob_ref[:, cols], flag_ref[:, cols].astype(F32), small_ref, sums,
        )
        grad_proj = grad_middle.astype(BF)
        projected[at, :] = grad_proj
        for double in range(width // (6 * HEAD_DIM)):
            back_heads(at, double, grad_proj, packed_ref, out_ref, stacked)
        grad = contract_cols(stacked[at, :], qkv_ref[...])
        unit, inverse = norm_parts(x_ref[at, :].astype(F32))
        sums[0] = sums[0] + jnp.sum(grad * unit, 0, keepdims=True)
        sums[1] = sums[1] + jnp.sum(grad, 0, keepdims=True)
        tokens_ref[at, :] = (grad_middle + norm_back(grad, unit, inverse, gain_row(small_ref, experts, 0))).astype(BF)
    grad_small[...] = jnp.concatenate([sums[4][0:experts]] + sums[:4] + [jnp.zeros((4, width), F32)], 0).astype(BF)
    grad_out[...] = contract_rows(attended_ref[...], projected[...]).astype(BF)
    for third in range(3):
        cols = pl.ds(third * width, width)
        grad_qkv[:, cols] = contract_rows(normed_ref[...], stacked[:, cols]).astype(BF)


def back(moe, gates, cot, x, middle, sent, flags, prob, attended, packed, normed, small, qkv, out):
    rows, width = x.shape
    shape = jax.ShapeDtypeStruct
    return pl.pallas_call(
        back_kernel,
        out_shape=(
            shape((rows, width), BF),
            shape((width, 3 * width), BF),
            shape((width, width), BF),
            shape((TALL, width), BF),
        ),
        scratch_shapes=[pltpu.VMEM((rows, 3 * width), BF), pltpu.VMEM((rows, width), BF)],
        compiler_params=pltpu.CompilerParams(vmem_limit_bytes=BIG),
        cost_estimate=pl.CostEstimate(flops=16 * 10**9, bytes_accessed=2 * 10**7, transcendentals=10**6),
        name="back",
    )(moe, gates, cot, x, middle, sent, flags, prob, attended, packed, normed, small, qkv, out)


ORDER = [[('x', 0), ('x', 1)], [('x', 2)], [('a', 0), ('x', 3), ('a', 1), ('x', 4), ('y', 0), ('x', 5)], [], [], [], [], [('b', 0), ('x', 6)], [('da', 0), ('b', 1), ('y', 1), ('da', 2), ('da', 3), ('y', 2), ('dl', 0), ('da', 1), ('x', 7)], [('dl', 2), ('y', 3), ('x', 8), ('dl', 3), ('db', 0), ('x', 9), ('y', 4), ('db', 2), ('y', 5), ('y', 6), ('dl', 1), ('y', 7), ('ds', 0), ('db', 3), ('c', 0), ('y', 8), ('s', 0), ('x', 10), ('c', 1), ('ds', 2), ('y', 9), ('s', 1), ('y', 10), ('s', 2), ('db', 1), ('ds', 3), ('dt', 0), ('ds', 1), ('dt', 2), ('x', 11), ('y', 11)], [('s', 3), ('dt', 3), ('dt', 1)]]


class LineScatter:
    def __init__(self, links, place, sums, up, down):
        self.links, self.place = links, place
        self.sums, self.up, self.down = sums, up, down
        self.copies = {}

    def ways(self, step):
        t = self.place.tensor
        return (
            ("up", self.up, t + 3 - step, t <= step, t >= 1, self.place.above),
            ("down", self.down, t - 3 + step, t >= 3 - step, t <= 2, self.place.below),
        )

    def send(self, part, step):
        for name, got, slot, sends, comes, device in self.ways(step):
            slot = jnp.clip(slot, 0, 3)
            if step > 0:
                before = self.copies[name, part, step - 1]

                @pl.when(sends & comes)
                def _():
                    before.wait_recv()
                    ref = self.sums(slot, part)
                    ref[...] = (ref[...].astype(F32) + got(step - 1, part)[...].astype(F32)).astype(BF)

            copy = self.links.copy(self.sums(slot, part), got(step, part), device)
            pl.when(sends)(copy.start)
            self.links.sent.append((sends, copy))
            self.copies[name, part, step] = copy

    def finish(self, part, total):
        total[...] = self.sums(self.place.tensor, part)[...].astype(F32)
        for name, got, slot, sends, comes, device in self.ways(2):
            copy = self.copies[name, part, 2]

            @pl.when(comes)
            def _():
                copy.wait_recv()
                total[...] += got(2, part)[...].astype(F32)


def tail_kernel(
    back_all, gate_all, total_all, grads_in, grads_out, rows_all, flags_all,
    cot_ref, x_ref, middle_ref, prob_ref, attended_ref, packed_ref, normed_ref, small_ref, qkv_ref, out_ref,
    mixed_ref, tokens_ref, dense_ref, grad_small, final_in, final_out, beside_in, beside_out,
    back_sum, back_got, back_up, back_down, gate_sum, gate_got, gate_up, gate_down,
    total_sum, total_got, total_up, total_down, moe, gates, rows_ref, flag_ref, projected, stacked,
    chunks, core_got, across_sent, across_got, line_sum, line_got, side_sum, side_got, line_final,
    own_in, own_out, across_in, across_out, read_in, read_out, half_in, half_out, mine_in, mine_out, both_in, both_out,
    small_sent, small_core, small_half, small_across, small_side, small_beside, small_line_sent, small_line,
    send, recv, local_sem,
):
    place = Place()
    links = Links(send, recv)
    rows, width = x_ref.shape
    experts = TALL // 2
    count = grads_in.shape[0]
    depth = width // 2
    shard, pair, side, tensor = place.shard, place.pair, place.side, place.tensor
    mine = pair * 4 + tensor
    place.greet(True)
    ours, theirs = pl.ds(pair * 4, 4), pl.ds((1 - pair) * 4, 4)

    locals_ = [
        pltpu.make_async_copy(back_all.at[ours], back_sum, local_sem.at[0]),
        pltpu.make_async_copy(gate_all.at[ours], gate_sum, local_sem.at[1]),
        pltpu.make_async_copy(total_all.at[ours], total_sum, local_sem.at[2]),
        pltpu.make_async_copy(rows_all.at[mine], rows_ref, local_sem.at[3]),
        pltpu.make_async_copy(flags_all.at[mine], flag_ref, local_sem.at[4]),
    ]
    for copy in locals_:
        copy.start()
    from_twin = [links.start(gate_all.at[theirs], gate_got, place.twin)]
    for part in range(2):
        at = pl.ds(part * PAD, PAD)
        from_twin.append(links.start(back_all.at[theirs, at, :], back_got.at[:, at, :], place.twin))
    from_twin.append(links.start(total_all.at[theirs], total_got, place.twin))

    here = pl.ds(pl.multiple_of(shard * depth, LANES), depth)
    there = pl.ds(pl.multiple_of((1 - shard) * depth, LANES), depth)
    hidden = grads_in.shape[2]
    tall, wide = depth // 2, hidden // 2
    pieces = []
    for expert in range(1, count):
        for half in range(2):
            at = pl.ds(half * tall, tall)
            pieces.append((
                grads_in.at[expert, pl.ds(pl.multiple_of((1 - shard) * depth + half * tall, TALL), tall), :],
                grads_in.at[expert, pl.ds(pl.multiple_of(shard * depth + half * tall, TALL), tall), :],
                across_in.at[expert - 1, at, :], beside_in.at[expert - 1, at, :],
                final_in.at[pair * count + expert, at, :], own_in.at[at, :], read_in.at[at, :],
            ))
        for half in range(2):
            at = pl.ds(half * wide, wide)
            pieces.append((
                grads_out.at[expert, at, there], grads_out.at[expert, at, here],
                across_out.at[expert - 1, at, :], beside_out.at[expert - 1, at, :],
                final_out.at[pair * count + expert, at, :], own_out.at[at, :], read_out.at[at, :],
            ))
    loads = [pltpu.make_async_copy(piece[1], piece[5], local_sem.at[8 + m]) for m, piece in enumerate(pieces)]
    at_across, at_beside, at_twin, kept = {}, {}, [], []
    started = [0]

    def add(target, source):
        target[...] = (target[...].astype(F32) + source[...].astype(F32)).astype(BF)

    def keep(source, target):
        copy = pltpu.make_async_copy(source, target, local_sem.at[32 + len(kept)])
        copy.start()
        kept.append(copy)

    def send_across():
        m = started[0]
        if m < len(pieces):
            at_across[m] = links.start(pieces[m][0], pieces[m][2], place.across)
            started[0] += 1

    def take_across(m):
        at_across[m].wait_recv()
        send_across()
        loads[m].wait()
        add(pieces[m][2], pieces[m][5])
        at_beside[m] = links.start(pieces[m][2], pieces[m][3], place.beside)
        if m + 4 < len(pieces):
            loads[m + 4].start()

    def take_beside(m):
        at_beside[m].wait_recv()
        load = pltpu.make_async_copy(pieces[m][3], pieces[m][6], local_sem.at[5])
        load.start()
        at_beside[m].wait_send()
        links.skip(at_beside[m])
        load.wait()
        add(pieces[m][2], pieces[m][6])
        at_twin.append(links.start(pieces[m][2], pieces[m][4], place.twin))
        keep(pieces[m][2], pieces[m][4])

    our_half = pl.ds(pl.multiple_of(side * wide, LANES), wide)
    other_half = pl.ds(pl.multiple_of((1 - side) * wide, LANES), wide)
    first = (
        (grads_in.at[0, :, other_half], grads_in.at[0, :, our_half], half_in, mine_in,
         half_in.at[there, :], half_in.at[here, :], both_in,
         final_in.at[pair * count, :, our_half], final_in.at[pair * count, :, other_half]),
        (grads_out.at[0, other_half, :], grads_out.at[0, our_half, :], half_out, mine_out,
         half_out.at[:, there], half_out.at[:, here], both_out,
         final_out.at[pair * count, our_half, :], final_out.at[pair * count, other_half, :]),
    )
    first_loads = [pltpu.make_async_copy(item[1], item[3], local_sem.at[6 + q]) for q, item in enumerate(first)]
    first_beside, first_across, first_back = {}, {}, {}

    def first_send(q):
        first_loads[q].start()
        first_beside[q] = links.start(first[q][0], first[q][2], place.beside)

    def first_sum(q):
        first_beside[q].wait_recv()
        first_loads[q].wait()
        add(first[q][2], first[q][3])
        first_across[q] = links.start(first[q][4], first[q][6], place.across)

    def first_total(q):
        first_across[q].wait_recv()
        add(first[q][6], first[q][5])
        first_back[q] = links.start(first[q][6], first[q][7], place.beside)
        at_twin.append(links.start(first[q][6], first[q][7], place.twin))
        keep(first[q][6], first[q][7])

    def first_share(q):
        first_back[q].wait_recv()
        at_twin.append(links.start(first[q][8], first[q][8], place.twin))

    share = depth // 2
    piece = share // 4
    stage = {}

    def dense_core(k):
        stage["core", k] = []
        for owner in range(2):
            source = chunks.at[k, pl.ds(pl.multiple_of(owner * depth + (1 - pair) * share, TALL), share), :]
            stage["core", k].append(links.start(source, core_got.at[k, owner], place.twin))

    def core_sum(k, owner):
        at = pl.ds(pl.multiple_of(owner * depth + pair * share, TALL), share)
        return chunks[k, at, :].astype(F32) + core_got[k, owner].astype(F32)

    def dense_across(k):
        for copy in stage["core", k]:
            copy.wait_recv()
        across_sent[k] = core_sum(k, 1 - shard).astype(BF)
        stage["across", k] = links.start(across_sent.at[k], across_got.at[k], place.across)

    def around(offset):
        return (shard, place.head, lax.rem(tensor + offset, 4))

    def dense_line(k):
        stage["across", k].wait_recv()
        line_sum[k] = (core_sum(k, shard) + across_got[k].astype(F32)).astype(BF)
        stage["line", k] = []
        for offset in (2, 1, 3):
            at = pl.ds(pl.multiple_of(lax.rem(tensor + offset, 4) * piece, TALL), piece)
            stage["line", k].append(links.start(line_sum.at[k, at, :], line_got.at[k, offset - 1], around(offset)))

    def dense_beside(k):
        for copy in stage["line", k]:
            copy.wait_recv()
        at = pl.ds(pl.multiple_of(tensor * piece, TALL), piece)
        value = line_sum[k, at, :].astype(F32)
        for offset in range(3):
            value = value + line_got[k, offset].astype(F32)
        side_sum[k] = value.astype(BF)
        stage["beside", k] = links.start(side_sum.at[k], side_got.at[k], place.beside)

    def dense_spread(k):
        stage["beside", k].wait_recv()
        line_final[k] = (side_sum[k].astype(F32) + side_got[k].astype(F32)).astype(BF)
        target = dense_ref.at[
            pl.ds(pl.multiple_of(pair * share + tensor * piece, TALL), piece), pl.ds(k * width, width)
        ]
        stage["spread", k] = [links.start(line_final.at[k], target, around(offset)) for offset in (2, 1, 3)]
        stage["keep", k] = pltpu.make_async_copy(line_final.at[k], target, local_sem.at[24 + k])
        stage["keep", k].start()

    def dense_twin(k):
        for copy in stage["spread", k]:
            copy.wait_recv()
        stage["keep", k].wait()
        block = dense_ref.at[pl.ds(pl.multiple_of(pair * share, TALL), share), pl.ds(k * width, width)]
        stage["twin", k] = links.start(block, block, place.twin)

    def small_core_stage():
        small_core_copy.wait_recv()
        other = pl.ds(pl.multiple_of((1 - shard) * depth, LANES), depth)
        small_half[...] = small_sent[:, other] + small_core[:, other]
        stage["small", 1] = links.start(small_half, small_across, place.across)

    def small_across_stage():
        stage["small", 1].wait_recv()
        own = pl.ds(pl.multiple_of(shard * depth, LANES), depth)
        small_side[...] = small_sent[:, own] + small_core[:, own] + small_across[...]
        stage["small", 2] = links.start(small_side, small_beside, place.beside)

    def small_beside_stage():
        stage["small", 2].wait_recv()
        small_line_sent[...] = small_side[...] + small_beside[...]
        stage["small", 3] = [
            links.start(small_line_sent, small_line.at[offset - 1], around(offset)) for offset in (2, 1, 3)
        ]

    def small_line_stage():
        for copy in stage["small", 3]:
            copy.wait_recv()
        grad_small[...] = small_line_sent[...] + small_line[0] + small_line[1] + small_line[2]

    def slots(array):
        def view(slot, part):
            return array.at[slot, pl.ds(part * PAD, PAD), :]

        return view

    back_line = LineScatter(links, place, slots(back_sum), slots(back_up), slots(back_down))
    total_line = LineScatter(links, place, slots(total_sum), slots(total_up), slots(total_down))
    gate_line = LineScatter(
        links, place, lambda slot, part: gate_sum.at[slot], lambda step, part: gate_up.at[step],
        lambda step, part: gate_down.at[step],
    )

    steps = {
        "x": take_across, "y": take_beside, "a": first_sum, "b": first_total, "c": first_share,
        "da": dense_across, "dl": dense_line, "db": dense_beside, "ds": dense_spread, "dt": dense_twin,
        "s": lambda index: (small_core_stage, small_across_stage, small_beside_stage, small_line_stage)[index](),
    }

    def go(slot):
        for name, index in ORDER[slot]:
            steps[name](index)

    first_send(0)
    for _ in range(3):
        send_across()
    first_send(1)
    for m in range(4):
        loads[m].start()
    locals_[1].wait()
    from_twin[0].wait_recv()
    add(gate_sum, gate_got)
    gate_line.send(0, 0)
    locals_[0].wait()
    for part in range(2):
        from_twin[1 + part].wait_recv()
        at = pl.ds(part * PAD, PAD)
        for slot in range(4):
            add(back_sum.at[slot, at, :], back_got.at[slot, at, :])
        back_line.send(part, 0)
    locals_[2].wait()
    from_twin[3].wait_recv()
    for slot in range(4):
        add(total_sum.at[slot], total_got.at[slot])
    go(0)
    gate_line.send(0, 1)
    for part in range(2):
        back_line.send(part, 1)
    go(1)
    gate_line.send(0, 2)
    for part in range(2):
        back_line.send(part, 2)
    go(2)
    for part in range(2):
        total_line.send(part, 0)
    gate_line.finish(0, gates)
    locals_[3].wait()
    locals_[4].wait()

    sums = [jnp.zeros((1, width), F32) for _ in range(4)] + [jnp.zeros((TALL, width), F32)]
    for image in range(2):
        at = pl.ds(image * PAD, PAD)
        cols = slice(image * PAD, (image + 1) * PAD)
        back_line.finish(image, moe.at[at, :])
        grad = back_middle(
            at, moe[at, :], gates[:, cols], cot_ref[at, :].astype(F32), middle_ref[at, :], rows_ref[at, :],
            prob_ref[:, cols], flag_ref[:, cols].astype(F32), small_ref, sums,
        )
        moe[at, :] = grad
        projected[at, :] = grad.astype(BF)
    go(3)
    chunks[0] = contract_rows(attended_ref[...], projected[...]).astype(BF)
    dense_core(0)
    go(4)
    for image in range(2):
        at = pl.ds(image * PAD, PAD)
        back_heads(at, 0, projected[at, :], packed_ref, out_ref, stacked)
        if image == 0:
            go(5)
    chunks[1] = contract_rows(normed_ref[...], stacked[:, pl.ds(0, width)]).astype(BF)
    dense_core(1)
    for part in range(2):
        total_line.send(part, 1)
    go(6)
    for image in range(2):
        at = pl.ds(image * PAD, PAD)
        back_heads(at, 1, projected[at, :], packed_ref, out_ref, stacked)
        if image == 0:
            go(7)
    for k in (2, 3):
        chunks[k] = contract_rows(normed_ref[...], stacked[:, pl.ds((k - 1) * width, width)]).astype(BF)
        dense_core(k)
    for part in range(2):
        total_line.send(part, 2)
    go(8)
    for image in range(2):
        at = pl.ds(image * PAD, PAD)
        grad = contract_cols(stacked[at, :], qkv_ref[...])
        unit, inverse = norm_parts(x_ref[at, :].astype(F32))
        sums[0] = sums[0] + jnp.sum(grad * unit, 0, keepdims=True)
        sums[1] = sums[1] + jnp.sum(grad, 0, keepdims=True)
        tokens_ref[at, :] = (
            moe[at, :] + norm_back(grad, unit, inverse, gain_row(small_ref, experts, 0))
        ).astype(BF)
    small_sent[...] = jnp.concatenate([sums[4][0:experts]] + sums[:4] + [jnp.zeros((4, width), F32)], 0)
    small_core_copy = links.start(small_sent, small_core, place.twin)
    go(9)
    for part in range(2):
        at = pl.ds(part * PAD, PAD)
        total_line.finish(part, moe.at[at, :])
        mixed_ref[at, :] = (middle_ref[at, :] + moe[at, :]).astype(BF)
    go(10)
    for copy in at_twin + [stage["twin", k] for k in range(4)]:
        copy.wait_recv()
    for copy in kept:
        copy.wait()
    links.finish()


def tail(back_all, gate_all, total_all, grads_in, grads_out, rows_all, flags_all, cot, x, middle, prob, attended, packed, normed, small, qkv, out):
    rows, width = x.shape
    count, _, hidden = grads_in.shape
    depth = width // 2
    shape = jax.ShapeDtypeStruct
    anywhere = pl.BlockSpec(memory_space=pl.ANY)
    vmem = pl.BlockSpec(memory_space=pltpu.VMEM)
    share, piece = depth // 2, depth // 8

    def scatter_buffers(tall, wide):
        return [pltpu.VMEM((4, tall, wide), BF)] * 2 + [pltpu.VMEM((3, tall, wide), BF)] * 2

    return pl.pallas_call(
        tail_kernel,
        out_shape=(
            shape((rows, width), BF),
            shape((rows, width), BF),
            shape((depth, 4 * width), BF),
            shape((TALL, depth), F32),
            shape((2 * count, depth, hidden), BF),
            shape((2 * count, hidden, depth), BF),
            shape((count - 1, depth, hidden), BF),
            shape((count - 1, hidden, depth), BF),
        ),
        in_specs=[anywhere] * 7 + [vmem] * 10,
        out_specs=(vmem,) * 4 + (anywhere,) * 4,
        scratch_shapes=scatter_buffers(rows, width)
        + scatter_buffers(TALL, rows)
        + scatter_buffers(rows, width)
        + [
            pltpu.VMEM((rows, width), F32),
            pltpu.VMEM((TALL, rows), F32),
            pltpu.VMEM((rows, width), BF),
            pltpu.VMEM((TALL, rows), BF),
            pltpu.VMEM((rows, width), BF),
            pltpu.VMEM((rows, 3 * width), BF),
            pltpu.VMEM((4, width, width), BF),
            pltpu.VMEM((4, 2, share, width), BF),
            pltpu.VMEM((4, share, width), BF),
            pltpu.VMEM((4, share, width), BF),
            pltpu.VMEM((4, share, width), BF),
            pltpu.VMEM((4, 3, piece, width), BF),
            pltpu.VMEM((4, piece, width), BF),
            pltpu.VMEM((4, piece, width), BF),
            pltpu.VMEM((4, piece, width), BF),
        ]
        + [pltpu.VMEM((depth, hidden), BF), pltpu.VMEM((hidden, depth), BF)]
        + [pltpu.VMEM((count - 1, depth, hidden), BF), pltpu.VMEM((count - 1, hidden, depth), BF)]
        + [pltpu.VMEM((depth, hidden), BF), pltpu.VMEM((hidden, depth), BF)]
        + [pltpu.VMEM((width, hidden // 2), BF), pltpu.VMEM((hidden // 2, width), BF)] * 2
        + [pltpu.VMEM((depth, hidden // 2), BF), pltpu.VMEM((hidden // 2, depth), BF)]
        + [
            pltpu.VMEM((TALL, width), F32),
            pltpu.VMEM((TALL, width), F32),
            pltpu.VMEM((TALL, depth), F32),
            pltpu.VMEM((TALL, depth), F32),
            pltpu.VMEM((TALL, depth), F32),
            pltpu.VMEM((TALL, depth), F32),
            pltpu.VMEM((TALL, depth), F32),
            pltpu.VMEM((3, TALL, depth), F32),
            pltpu.SemaphoreType.DMA((192,)),
            pltpu.SemaphoreType.DMA((192,)),
            pltpu.SemaphoreType.DMA((48,)),
        ],
        compiler_params=pltpu.CompilerParams(vmem_limit_bytes=BIG, collective_id=2, has_side_effects=True),
        cost_estimate=pl.CostEstimate(flops=16 * 10**9, bytes_accessed=5 * 10**7, transcendentals=10**6),
        name="tail",
    )(back_all, gate_all, total_all, grads_in, grads_out, rows_all, flags_all, cot, x, middle, prob, attended, packed, normed, small, qkv, out)


class Comm:
    def __init__(self):
        self.sizes = tuple(lax.axis_size(axis) for axis in AXES)
        self.shard = lax.axis_index("shard")
        self.head = lax.axis_index("heads")
        self.tensor = lax.axis_index("tensor")
        self.pair = self.head % 2

    def move(self, value, step):
        shards, heads, tensors = self.sizes
        pairs = []
        for s in range(shards):
            for h in range(heads):
                for t in range(tensors):
                    to = step(s, h, t)
                    if 0 <= to[2] < tensors:
                        source = (s * heads + h) * tensors + t
                        pairs.append((source, (to[0] * heads + to[1]) * tensors + to[2]))
        return lax.ppermute(value, AXES, pairs)

    def over_core(self, value):
        return self.move(value, lambda s, h, t: (s, h ^ 1, t))

    def over_heads(self, value):
        return self.move(value, lambda s, h, t: (s, (h + 2) % 4, t))

    def over_shard(self, value):
        return self.move(value, lambda s, h, t: (1 - s, h, t))

    def up(self, value):
        return self.move(value, lambda s, h, t: (s, h, t + 1))

    def down(self, value):
        return self.move(value, lambda s, h, t: (s, h, t - 1))

    def halves(self, value, index, axis):
        size = value.shape[axis] // 2
        mine = lax.dynamic_slice_in_dim(value, index * size, size, axis)
        other = lax.dynamic_slice_in_dim(value, (1 - index) * size, size, axis)
        return mine, other

    def join(self, mine, other, index, axis):
        first = jnp.where(index == 0, mine, other)
        second = jnp.where(index == 0, other, mine)
        return jnp.concatenate((first, second), axis)

    def gather_shard(self, value, axis):
        if self.sizes[0] != 2:
            return lax.all_gather(value, "shard", axis=axis, tiled=True)
        return self.join(value, self.over_shard(value), self.shard, axis)

    def gather_shard_split(self, value, axis, cut):
        if self.sizes[0] != 2:
            return lax.all_gather(value, "shard", axis=axis, tiled=True)
        mine, _ = self.halves(value, self.pair, cut)
        got = self.over_shard(mine)
        both = self.join(got, self.over_core(got), self.pair, cut)
        return self.join(value, both, self.shard, axis)

    def scatter_shard(self, value, axis):
        if self.sizes[0] != 2:
            return lax.psum_scatter(value.astype(BF), "shard", scatter_dimension=axis, tiled=True).astype(F32)
        mine, other = self.halves(value, self.shard, axis)
        return mine.astype(F32) + self.over_shard(other.astype(BF)).astype(F32)

    def scatter_core(self, value, axis):
        mine, other = self.halves(value, self.pair, axis)
        return mine.astype(F32) + self.over_core(other.astype(BF)).astype(F32)

    def scatter_heads(self, value, axis):
        mine, other = self.halves(value, self.head // 2, axis)
        return mine.astype(F32) + self.over_heads(other.astype(BF)).astype(F32)

    def line_gather(self, value):
        ups, downs = [value], [value]
        for _ in range(3):
            ups.append(self.up(ups[-1]))
            downs.append(self.down(downs[-1]))
        out = [value]
        for back in (1, 2, 3):
            out.append(jnp.where(self.tensor >= back, ups[back], downs[4 - back]))
        return out

    def line_scatter(self, parts):
        high, low = parts[1].astype(BF), parts[3].astype(BF)
        high = (parts[2].astype(F32) + self.up(high).astype(F32)).astype(BF)
        low = (parts[2].astype(F32) + self.down(low).astype(F32)).astype(BF)
        high = (parts[3].astype(F32) + self.up(high).astype(F32)).astype(BF)
        low = (parts[1].astype(F32) + self.down(low).astype(F32)).astype(BF)
        return parts[0].astype(F32) + self.up(high).astype(F32) + self.down(low).astype(F32)

    def join_slots(self, values):
        own = jnp.zeros((4,) + values[0].shape, values[0].dtype)
        for back, value in enumerate(values):
            own = lax.dynamic_update_index_in_dim(own, value, (self.tensor + 4 - back) % 4, 0)
        return self.join(own, self.over_core(own), self.pair, 0)

    def collect(self, value):
        mine, other = self.halves(value, self.pair, 0)
        mine = mine.astype(F32) + self.over_core(other).astype(F32)
        return self.line_scatter(
            [lax.dynamic_index_in_dim(mine, (self.tensor + 4 - k) % 4, 0, False) for k in range(4)]
        )


def local(
    tokens, ln1_gain, ln1_bias, qkv_weight, out_weight, ln2_gain, ln2_bias, router_weight,
    expert_in, expert_out, route_noise, expert_ids, cotangent,
):
    comm = Comm()
    rows, width = tokens.shape
    experts = expert_in.shape[0]
    images = rows // SEQ
    half = experts // 2
    padded = images * PAD

    def pad(value):
        value = value.reshape(images, SEQ, value.shape[1])
        return jnp.pad(value, ((0, 0), (0, PAD - SEQ), (0, 0))).reshape(padded, value.shape[2])

    def pad_turned(value, tall, fill):
        value = value.reshape(images, SEQ, value.shape[1]).transpose(2, 0, 1)
        value = jnp.pad(value, ((0, tall - value.shape[0]), (0, 0), (0, PAD - SEQ)), constant_values=fill)
        return value.reshape(tall, padded)

    def unpad(value):
        return value.reshape(images, PAD, value.shape[1])[:, :SEQ].reshape(rows, value.shape[1])

    small = jnp.concatenate(
        (router_weight.T, ln1_gain[None], ln1_bias[None], ln2_gain[None], ln2_bias[None]), 0
    )
    small = jnp.pad(small, ((0, TALL - small.shape[0]), (0, 0)))
    cot, x = pad(cotangent), pad(tokens)
    noise, ids = pad_turned(route_noise, TALL, 0), pad_turned(expert_ids, 8, -1)
    place = jnp.stack((comm.pair, comm.shard if comm.sizes[0] == 2 else 0 * comm.shard)).astype(jnp.int32)
    if comm.sizes[0] == 2:
        (
            small, proj_qkv, proj_out, normed_a, packed, attended, middle, prob,
            rows_all, flags_all, grad_rows, got_in, got_out,
        ) = head(x, cot, small, qkv_weight, out_weight, expert_in, expert_out, noise, ids)
        weights = (expert_in, got_in, expert_out, got_out)
    else:
        small = lax.all_gather(small, "shard", axis=1, tiled=True)
        small = small.reshape(TALL, 2, width // 2).transpose(1, 0, 2)
        proj_qkv = lax.all_gather(qkv_weight, "shard", axis=0, tiled=True)
        proj_out = lax.all_gather(out_weight, "shard", axis=0, tiled=True)
        inner = lax.all_gather(lax.dynamic_slice_in_dim(expert_in, comm.pair * half, half, 0), "shard", axis=1, tiled=True)
        outer = lax.all_gather(lax.dynamic_slice_in_dim(expert_out, comm.pair * half, half, 0), "shard", axis=2, tiled=True)
        cut = width // 2
        weights = (
            jnp.concatenate((inner[:, :cut], inner[:, :cut]), 0), inner[:, cut:],
            jnp.concatenate((outer[:, :, :cut], outer[:, :, :cut]), 0), outer[:, :, cut:],
        )
        normed_a, packed, attended, middle, sent, flags, prob = front(x, small, proj_qkv, proj_out, noise, ids)

        def gather(value):
            return comm.join_slots(comm.line_gather(value))

        grad_rows, rows_all, flags_all = gather(cot), gather(sent), gather(flags)
    total, back_all, gate_all, grads_in, grads_out = expert_pass(place, rows_all, flags_all, grad_rows, *weights)

    if comm.sizes[0] == 2:
        mixed, grad_tokens, dense, grad_small, grad_in, grad_outer, _, _ = tail(
            back_all, gate_all, total, grads_in, grads_out, rows_all, flags_all,
            cot, x, middle, prob, attended, packed, normed_a, small, proj_qkv, proj_out,
        )
        dense = dense.astype(F32)
        return (
            unpad(mixed),
            unpad(grad_tokens),
            grad_small[experts],
            grad_small[experts + 1],
            dense[:, width:],
            dense[:, :width],
            grad_small[experts + 2],
            grad_small[experts + 3],
            grad_small[:experts].T,
            grad_in.astype(F32),
            grad_outer.astype(F32),
        )

    def reduce_expert(grad, axis, other):
        part = comm.scatter_shard(grad, axis)
        part = comm.scatter_heads(part, other).astype(BF)
        return comm.join(part, comm.over_heads(part), comm.head // 2, other)

    inner_grads = [reduce_expert(grads_in[e], 0, 1) for e in range(half)]
    outer_grads = [reduce_expert(grads_out[e], 1, 0) for e in range(half)]

    moe_grad = comm.collect(back_all)
    gate_grad = comm.collect(gate_all)
    moe = comm.collect(total)
    mixed = (unpad(middle) + unpad(moe)).astype(BF)
    grad_tokens, grad_qkv, grad_out, grad_small = back(
        moe_grad, gate_grad, cot, x, middle, sent, flags, prob, attended, packed, normed_a, small, proj_qkv, proj_out
    )
    grad_tokens = unpad(grad_tokens)

    grad_small = jnp.pad(grad_small.T, ((0, 0), (0, 128 - TALL)))
    shares = jnp.concatenate((grad_qkv, grad_out, grad_small, jnp.zeros_like(grad_small)), 1)
    shares = comm.scatter_core(shares, 1)
    shares = comm.scatter_shard(shares, 0)
    shares = comm.scatter_heads(shares, 1)
    cut = shares.shape[0] // 4
    rolled = [
        lax.dynamic_slice_in_dim(shares, ((comm.tensor + 4 - k) % 4) * cut, cut, 0) for k in range(4)
    ]
    summed = comm.line_scatter(rolled).astype(BF)
    pieces = comm.line_gather(summed)
    whole = jnp.zeros(shares.shape, BF)
    for k in range(4):
        whole = lax.dynamic_update_slice_in_dim(whole, pieces[k], ((comm.tensor + 4 - k) % 4) * cut, 0)
    whole = comm.join(whole, comm.over_heads(whole), comm.head // 2, 1)
    whole = comm.join(whole, comm.over_core(whole), comm.pair, 1).astype(F32)
    small = whole[:, 4 * width : 4 * width + 128]

    grad_in, grad_outer = jnp.stack(inner_grads, 0), jnp.stack(outer_grads, 0)
    grad_in = comm.join(grad_in, comm.over_core(grad_in), comm.pair, 0).astype(F32)
    grad_outer = comm.join(grad_outer, comm.over_core(grad_outer), comm.pair, 0).astype(F32)
    return (
        mixed,
        grad_tokens,
        small[:, experts],
        small[:, experts + 1],
        whole[:, : 3 * width],
        whole[:, 3 * width : 4 * width],
        small[:, experts + 2],
        small[:, experts + 3],
        small[:, :experts],
        grad_in,
        grad_outer,
    )


def solution(mesh):
    split = P(AXES, None)
    vector, matrix = P("shard"), P("shard", None)
    inner, outer = P(None, "shard", "tensor"), P(None, "tensor", "shard")
    return jax.shard_map(
        local,
        mesh=mesh,
        in_specs=(
            split, vector, vector, matrix, matrix, vector, vector, matrix, inner, outer, split, split, split,
        ),
        out_specs=(
            split, split, vector, vector, matrix, matrix, vector, vector, matrix, inner, outer,
        ),
        check_vma=False,
    )
```

```python
import jax
import jax.numpy as jnp
from jax import lax
from jax.experimental import pallas as pl
from jax.experimental.pallas import tpu as pltpu
from jax.sharding import PartitionSpec as P

HEAD_DIM = 64
SEQ = 197
EPS = 1e-06
AXES = ("shard", "heads", "tensor")
BF = jnp.bfloat16
F32 = jnp.float32


def contract_rows(left, right):
    return lax.dot_general(left, right, (((0,), (0,)), ((), ())), preferred_element_type=F32)


def contract_cols(left, right):
    return lax.dot_general(left, right, (((1,), (1,)), ((), ())), preferred_element_type=F32)


PAD = 208
TILE = 128
CHUNK = 256
FAR = 512.0
TALL = 16
LANES = 128
MASKED = -1e30
CUBIC = 0.044715
ROOT = (2.0 / 3.141592653589793) ** 0.5
BIG = 60 * 1024 * 1024
MESH = pl.DeviceIdType.MESH


def dot(left, right):
    return jnp.dot(left, right, preferred_element_type=F32)


def norm_parts(values):
    centred = values - jnp.mean(values, -1, keepdims=True)
    inverse = lax.rsqrt(jnp.mean(centred * centred, -1, keepdims=True) + EPS)
    return centred * inverse, inverse


def norm_back(grad, unit, inverse, gain):
    scaled = grad * gain
    along = jnp.mean(scaled * unit, -1, keepdims=True)
    return inverse * (scaled - jnp.mean(scaled, -1, keepdims=True) - unit * along)


def head_probs(query, keys, scale):
    scores = contract_cols(query, keys) * scale
    column = lax.broadcasted_iota(jnp.int32, scores.shape, 1)
    scores = jnp.where(column < SEQ, scores, MASKED)
    raised = jnp.exp(scores - jnp.max(scores, -1, keepdims=True))
    return raised / jnp.sum(raised, -1, keepdims=True)


def gain_row(small_ref, experts, index):
    row = slice(experts + index, experts + index + 1)
    return jnp.concatenate((small_ref[0, row, :], small_ref[1, row, :]), 1).astype(F32)


def router_rows(small_ref):
    return jnp.concatenate((small_ref[0], small_ref[1]), 1)


def attend(normed, at, qkv_ref, packed_ref):
    width = normed.shape[1]
    group = 3 * HEAD_DIM
    scale = HEAD_DIM ** (-0.5)
    lane = lax.broadcasted_iota(jnp.int32, (PAD, group), 1) // HEAD_DIM
    outs = []
    for double in range(width // group // 2):
        cols = pl.ds(double * 6 * group, 6 * group)
        packed = dot(normed, qkv_ref[:, cols])
        packed_ref[at, cols] = packed.astype(BF)
        for side in range(2):
            query, keys, values = (
                packed[:, (3 * side + k) * group : (3 * side + k + 1) * group].astype(BF)
                for k in range(3)
            )
            total = jnp.zeros((PAD, group), F32)
            for head in range(3):
                mask = lane == head
                probs = head_probs(jnp.where(mask, query, jnp.zeros_like(query)), keys, scale)
                total = jnp.where(mask, dot(probs.astype(BF), values), total)
            outs.append(total)
    return jnp.concatenate(outs, 1).astype(BF)


def route(normed, small_ref, noise, ids, experts):
    logits = contract_cols(router_rows(small_ref), normed) + noise
    row = lax.broadcasted_iota(jnp.int32, logits.shape, 0)
    logits = jnp.where(row < experts, logits, MASKED)
    raised = jnp.exp(logits - jnp.max(logits, 0, keepdims=True))
    probs = raised / jnp.sum(raised, 0, keepdims=True)
    chosen = ((row == ids[0:1]) | (row == ids[1:2])).astype(F32)
    shifted = row - experts
    flags = (((shifted == ids[0:1]) | (shifted == ids[1:2])) & (shifted >= 0)).astype(F32)
    return probs, probs * chosen + flags


def front_image(image, experts, x_ref, small_ref, qkv_ref, out_ref, noise_ref, ids_ref, keep, ready=None):
    normed_ref, packed_ref, attended_ref, middle_ref = keep
    at = pl.ds(image * PAD, PAD)
    x = x_ref[at, :].astype(F32)
    unit, _ = norm_parts(x)
    normed = (unit * gain_row(small_ref, experts, 0) + gain_row(small_ref, experts, 1)).astype(BF)
    normed_ref[at, :] = normed
    attended = attend(normed, at, qkv_ref, packed_ref)
    attended_ref[at, :] = attended
    if ready is not None:
        ready()
    middle = x + dot(attended, out_ref[...])
    middle_ref[at, :] = middle
    unit, _ = norm_parts(middle)
    normed = (unit * gain_row(small_ref, experts, 2) + gain_row(small_ref, experts, 3)).astype(BF)
    cols = slice(image * PAD, (image + 1) * PAD)
    probs, flags = route(normed, small_ref, noise_ref[:, cols], ids_ref[:, cols], experts)
    return normed, probs, flags


def front_kernel(
    x_ref, small_ref, qkv_ref, out_ref, noise_ref, ids_ref,
    normed_ref, packed_ref, attended_ref, middle_ref, rows_ref, flag_ref, prob_ref,
):
    keep = (normed_ref, packed_ref, attended_ref, middle_ref)
    probs, flags = [], []
    for image in range(x_ref.shape[0] // PAD):
        normed, prob, flag = front_image(
            image, TALL // 2, x_ref, small_ref, qkv_ref, out_ref, noise_ref, ids_ref, keep
        )
        rows_ref[pl.ds(image * PAD, PAD), :] = normed
        probs.append(prob)
        flags.append(flag)
    prob_ref[...] = jnp.concatenate(probs, 1)
    flag_ref[...] = jnp.concatenate(flags, 1).astype(BF)


def front(x, small, qkv, out, noise, ids):
    rows, width = x.shape
    shape = jax.ShapeDtypeStruct
    return pl.pallas_call(
        front_kernel,
        out_shape=(
            shape((rows, width), BF),
            shape((rows, 3 * width), BF),
            shape((rows, width), BF),
            shape((rows, width), F32),
            shape((rows, width), BF),
            shape((TALL, rows), BF),
            shape((TALL, rows), F32),
        ),
        compiler_params=pltpu.CompilerParams(vmem_limit_bytes=BIG),
        cost_estimate=pl.CostEstimate(flops=8 * 10**9, bytes_accessed=10**7, transcendentals=10**6),
        name="front",
    )(x, small, qkv, out, noise, ids)


class Place:
    def __init__(self):
        shard, head, tensor = (lax.axis_index(axis) for axis in AXES)
        self.shard, self.head, self.tensor = shard, head, tensor
        self.pair, self.side = lax.rem(head, 2), lax.div(head, 2)
        self.across = (1 - shard, head, tensor)
        self.beside = (shard, lax.rem(head + 2, 4), tensor)
        self.twin = (shard, head + 1 - 2 * self.pair, tensor)
        self.above = (shard, head, lax.rem(tensor + 1, 4))
        self.below = (shard, head, lax.rem(tensor + 3, 4))

    def greet(self, line=False):
        barrier = pltpu.get_barrier_semaphore()
        devices = [self.across, self.beside, self.twin, self.above, self.below]
        if line:
            devices.append((self.shard, self.head, lax.rem(self.tensor + 2, 4)))
        for device in devices:
            pl.semaphore_signal(barrier, inc=1, device_id=device, device_id_type=MESH)
        pl.semaphore_wait(barrier, len(devices))


class Links:
    def __init__(self, send, recv):
        self.send, self.recv, self.used = send, recv, 0
        self.sent = []

    def copy(self, source, target, device):
        index = self.used
        self.used += 1
        return pltpu.make_async_remote_copy(
            src_ref=source, dst_ref=target, send_sem=self.send.at[index], recv_sem=self.recv.at[index],
            device_id=device, device_id_type=MESH,
        )

    def start(self, source, target, device):
        copy = self.copy(source, target, device)
        copy.start()
        self.sent.append((None, copy))
        return copy

    def skip(self, done):
        self.sent = [(when, copy) for when, copy in self.sent if copy is not done]

    def finish(self):
        for when, copy in self.sent:
            if when is None:
                copy.wait_send()
            else:
                pl.when(when)(copy.wait_send)


class LineGather:
    def __init__(self, links, place, view, own, parts):
        self.links, self.place, self.view, self.own = links, place, view, own
        self.copies = {}
        self.parts = parts

    def start(self, part, step):
        t = self.place.tensor
        for name, slot, device, sends in (
            ("up", t - step, self.place.above, (t >= step) & (t < 3)),
            ("down", t + step, self.place.below, (t + step <= 3) & (t > 0)),
        ):
            slot = jnp.clip(slot, 0, 3)
            source = self.own(part) if step == 0 else self.view(slot, part)
            copy = self.links.copy(source, self.view(slot, part), device)
            pl.when(sends)(copy.start)
            self.links.sent.append((sends, copy))
            self.copies[name, part, step] = copy

    def wait(self, part, step, then=None):
        t = self.place.tensor
        for name, slot, comes in (("up", t - 1 - step, t >= step + 1), ("down", t + 1 + step, t + 1 + step <= 3)):
            copy = self.copies[name, part, step]

            @pl.when(comes)
            def _():
                copy.wait_recv()

    def arrived(self, step):
        t = self.place.tensor
        return (
            (jnp.clip(t - 1 - step, 0, 3), t >= step + 1),
            (jnp.clip(t + 1 + step, 0, 3), t + 1 + step <= 3),
        )


def head_kernel(
    x_ref, cot_ref, small_own, qkv_own, out_own, expert_in, expert_out, noise_ref, ids_ref,
    small_ref, qkv_ref, out_ref, normed_ref, packed_ref, attended_ref, middle_ref, prob_ref,
    rows_all, flags_all, cot_all, got_in, got_out,
    sent_rows, sent_flags, send, recv, local_sem,
):
    place = Place()
    links = Links(send, recv)
    width = x_ref.shape[1]
    experts = expert_in.shape[0]
    depth = qkv_own.shape[0]
    quarter = depth // 4
    shard, pair, side, tensor = place.shard, place.pair, place.side, place.tensor
    mine = pair * 4 + tensor
    place.greet()

    def dense_rows(owner, across_side, across_pair, start, size):
        return pl.ds(pl.multiple_of(owner * depth + (across_side * 2 + across_pair) * quarter + start, TALL), size)

    pieces = ((qkv_own, qkv_ref, 0, quarter // 2), (qkv_own, qkv_ref, quarter // 2, quarter // 2), (out_own, out_ref, 0, quarter))
    smalls = links.start(small_own, small_ref.at[shard], place.across)
    cross = []
    for own, full, start, size in pieces:
        source = own.at[pl.ds(pl.multiple_of((side * 2 + pair) * quarter + start, TALL), size), :]
        cross.append(links.start(source, full.at[dense_rows(shard, side, pair, start, size), :], place.across))

    def expert_item(item):
        index = side * 2 + item // 2
        source, target = (expert_in, got_in) if item % 2 == 0 else (expert_out, got_out)
        return source.at[pair * (experts // 2) + index], target.at[index]

    fetched = [links.start(*expert_item(item), place.across) for item in range(4)]
    here = pl.ds(pl.multiple_of(shard * depth, TALL), depth)
    locals_ = [
        pltpu.make_async_copy(qkv_own, qkv_ref.at[here, :], local_sem.at[0]),
        pltpu.make_async_copy(out_own, out_ref.at[here, :], local_sem.at[1]),
        pltpu.make_async_copy(small_own, small_ref.at[shard], local_sem.at[2]),
        pltpu.make_async_copy(cot_ref, cot_all.at[mine], local_sem.at[3]),
    ]
    for copy in locals_:
        copy.start()

    def slots(array):
        def view(slot, part):
            return array.at[pair * 4 + slot, pl.ds(part * PAD, PAD), :]

        return view

    cot_line = LineGather(links, place, slots(cot_all), lambda part: cot_ref.at[pl.ds(part * PAD, PAD), :], 2)
    for part in range(2):
        cot_line.start(part, 0)

    beside, twins = [], []
    for index, (own, full, start, size) in enumerate(pieces):
        cross[index].wait_recv()
        rows = full.at[dense_rows(1 - shard, side, pair, start, size), :]
        beside.append(links.start(rows, rows, place.beside))
        twins.append(links.start(rows, rows, place.twin))
    for part in range(2):
        cot_line.wait(part, 0)
        cot_line.start(part, 1)
    for index, (own, full, start, size) in enumerate(pieces):
        beside[index].wait_recv()
        rows = full.at[dense_rows(1 - shard, 1 - side, pair, start, size), :]
        twins.append(links.start(rows, rows, place.twin))

    for part in range(2):
        cot_line.wait(part, 1)
        cot_line.start(part, 2)
    smalls.wait_recv()
    for index, copy in enumerate(twins):
        if index % len(pieces) < 2:
            copy.wait_recv()
    for copy in locals_:
        copy.wait()

    keep = (normed_ref, packed_ref, attended_ref, middle_ref)
    row_line = LineGather(links, place, slots(rows_all), lambda part: sent_rows.at[pl.ds(part * PAD, PAD), :], 2)
    flag_line = LineGather(links, place, lambda slot, part: flags_all.at[pair * 4 + slot], lambda part: sent_flags, 1)
    probs, flags = [], []

    def out_ready():
        for index, copy in enumerate(twins):
            if index % len(pieces) == 2:
                copy.wait_recv()

    twin_rows = []
    forwarded = []

    def forward_expert(item):
        fetched[item].wait_recv()
        _, target = expert_item(item)
        forwarded.append(links.start(target, target, place.beside))

    for image in range(2):
        normed, prob, flag = front_image(
            image, experts, x_ref, small_ref, qkv_ref, out_ref, noise_ref, ids_ref, keep,
            out_ready if image == 0 else None,
        )
        at = pl.ds(image * PAD, PAD)
        sent_rows[at, :] = normed
        row_line.start(image, 0)
        twin_rows.append(links.start(sent_rows.at[at, :], rows_all.at[mine, at, :], place.twin))
        probs.append(prob)
        flags.append(flag)
        forward_expert(image)
    prob_ref[...] = jnp.concatenate(probs, 1)
    sent_flags[...] = jnp.concatenate(flags, 1).astype(BF)
    flag_line.start(0, 0)
    twin_flags = [links.start(sent_flags, flags_all.at[mine], place.twin)]
    keep_own = [
        pltpu.make_async_copy(sent_rows, rows_all.at[mine], local_sem.at[0]),
        pltpu.make_async_copy(sent_flags, flags_all.at[mine], local_sem.at[1]),
    ]
    for copy in keep_own:
        copy.start()

    def share(line, array, part, step, copies, whole):
        for slot, comes in line.arrived(step):
            index = pair * 4 + slot
            ref = array.at[index] if whole else array.at[index, pl.ds(part * PAD, PAD), :]
            copy = links.copy(ref, ref, place.twin)
            pl.when(comes)(copy.start)
            links.sent.append((comes, copy))
            copies.append((comes, copy))

    twin_steps = []
    for step in range(3):
        for part in range(2):
            row_line.wait(part, step)
            if step < 2:
                row_line.start(part, step + 1)
            share(row_line, rows_all, part, step, twin_steps, False)
        if step < 2:
            forward_expert(step + 2)
        flag_line.wait(0, step)
        if step < 2:
            flag_line.start(0, step + 1)
        share(flag_line, flags_all, 0, step, twin_steps, True)
        if step == 0:
            for part in range(2):
                cot_line.wait(part, 2)
            ours = cot_all.at[pl.ds(pair * 4, 4)]
            twin_cot = links.start(ours, ours, place.twin)

    for copy in twin_rows + twin_flags + [twin_cot] + forwarded:
        copy.wait_recv()
    for comes, copy in twin_steps:
        pl.when(comes)(copy.wait_recv)
    for copy in keep_own:
        copy.wait()
    links.finish()


def head(x, cot, small, qkv, out, expert_in, expert_out, noise, ids):
    rows, width = x.shape
    depth = qkv.shape[0]
    count = expert_in.shape[0] // 2
    shape = jax.ShapeDtypeStruct
    anywhere = pl.BlockSpec(memory_space=pl.ANY)
    vmem = pl.BlockSpec(memory_space=pltpu.VMEM)
    return pl.pallas_call(
        head_kernel,
        out_shape=(
            shape((2, TALL, depth), BF),
            shape((width, 3 * width), BF),
            shape((width, width), BF),
            shape((rows, width), BF),
            shape((rows, 3 * width), BF),
            shape((rows, width), BF),
            shape((rows, width), F32),
            shape((TALL, rows), F32),
            shape((8, rows, width), BF),
            shape((8, TALL, rows), BF),
            shape((8, rows, width), BF),
            shape((count,) + expert_in.shape[1:], BF),
            shape((count,) + expert_out.shape[1:], BF),
        ),
        in_specs=[vmem] * 3 + [anywhere] * 4 + [vmem] * 2,
        out_specs=(vmem,) * 8 + (anywhere,) * 5,
        scratch_shapes=[
            pltpu.VMEM((rows, width), BF),
            pltpu.VMEM((TALL, rows), BF),
            pltpu.SemaphoreType.DMA((96,)),
            pltpu.SemaphoreType.DMA((96,)),
            pltpu.SemaphoreType.DMA((4,)),
        ],
        compiler_params=pltpu.CompilerParams(vmem_limit_bytes=BIG, collective_id=1, has_side_effects=True),
        cost_estimate=pl.CostEstimate(flops=8 * 10**9, bytes_accessed=3 * 10**7, transcendentals=10**6),
        name="head",
    )(x, cot, small, qkv, out, expert_in, expert_out, noise, ids)


def expert_kernel(
    place_ref, flag_ref, rows_all, cot_all, own_in, got_in, own_out, got_out,
    total_all, back_all, gate_ref, grad_in, grad_out,
    inner, outer, picked, grads, gate, active, hidden_grad, made, made_back, made_gate, ranks,
    rows_buf, cot_buf, total_buf, back_buf, stage_in, stage_out, load_sem, store_sem, fetch_sem, put_sem, old_sem,
):
    blocks, length, width = cot_all.shape
    count = got_in.shape[0]
    depth = got_in.shape[1]
    pair, shard = place_ref[0], place_ref[1]
    experts = 2 * count

    def loads(expert, slot):
        mine = pl.ds(pl.multiple_of(shard * depth, LANES), depth)
        other = pl.ds(pl.multiple_of((1 - shard) * depth, LANES), depth)
        index = pair * count + expert
        return (
            pltpu.make_async_copy(own_in.at[index], inner.at[slot, mine, :], load_sem.at[slot, 0]),
            pltpu.make_async_copy(got_in.at[expert], inner.at[slot, other, :], load_sem.at[slot, 1]),
            pltpu.make_async_copy(own_out.at[index], outer.at[slot, :, mine], load_sem.at[slot, 2]),
            pltpu.make_async_copy(got_out.at[expert], outer.at[slot, :, other], load_sem.at[slot, 3]),
        )

    def stores(expert, slot):
        return (
            pltpu.make_async_copy(stage_in.at[slot], grad_in.at[expert], store_sem.at[slot, 0]),
            pltpu.make_async_copy(stage_out.at[slot], grad_out.at[expert], store_sem.at[slot, 1]),
        )

    def fetches(block, slot):
        return (
            pltpu.make_async_copy(rows_all.at[block], rows_buf.at[slot], fetch_sem.at[slot, 0]),
            pltpu.make_async_copy(cot_all.at[block], cot_buf.at[slot], fetch_sem.at[slot, 1]),
        )

    def puts(block, slot):
        return (
            pltpu.make_async_copy(total_buf.at[slot], total_all.at[block], put_sem.at[slot, 0]),
            pltpu.make_async_copy(back_buf.at[slot], back_all.at[block], put_sem.at[slot, 1]),
        )

    def start(copies):
        for copy in copies:
            copy.start()

    def wait(copies):
        for copy in copies:
            copy.wait()

    def reload(pairs):
        copies = [pltpu.make_async_copy(source, target, old_sem.at[n]) for n, (source, target) in enumerate(pairs)]
        start(copies)
        wait(copies)

    start(fetches(0, 0) + fetches(1, 1) + loads(0, 0))
    ahead = lax.broadcasted_iota(jnp.int32, (length, length), 0)
    behind = lax.broadcasted_iota(jnp.int32, (length, length), 1)
    order = jnp.where(behind < ahead, 1.0, jnp.where(behind == ahead, FAR, 0.0)).astype(BF)
    for block in range(blocks):
        ranks[block] = contract_cols(flag_ref[block], order) - FAR

    def line(expert):
        return pl.ds(experts + pair * count + expert, 1)

    def passes_of(expert):
        highest = ranks[0, line(expert), :]
        for block in range(1, blocks):
            highest = jnp.maximum(highest, ranks[block, line(expert), :])
        return (jnp.maximum(jnp.max(highest), -1.0).astype(jnp.int32) + TILE) // TILE

    highest = ranks[0, line(0), :]
    for block in range(blocks):
        for expert in range(count):
            highest = jnp.maximum(highest, ranks[block, line(expert), :])
    rounds = (jnp.maximum(jnp.max(highest), 0.0).astype(jnp.int32) + TILE) // TILE

    def take(block, slot, step):
        at = pl.ds(pl.multiple_of(block * TILE, TILE), TILE)
        choose = choices(block, step)
        columns = jnp.where(lane == wanted, contract_cols(choose, flag_ref[block]), 0.0)
        column = jnp.broadcast_to(jnp.sum(columns, -1, keepdims=True), (count * TILE, LANES))
        wait(fetches(block, slot))
        both = dot(choose, rows_buf[slot]).astype(BF)
        other = dot(choose, cot_buf[slot]).astype(BF)
        for expert in range(count):
            part = slice(expert * TILE, (expert + 1) * TILE)
            picked[expert, at, :] = both[part]
            grads[expert, at, :] = other[part]
            gate[expert, at, :] = column[part]

    def compute(expert, slot):
        def chunk(index, carry):
            at = pl.ds(pl.multiple_of(index * CHUNK, CHUNK), CHUNK)
            value = dot(picked[expert, at, :], inner[slot])
            grad_active = contract_cols(grads[expert, at, :], outer[slot])
            gate_column = gate[expert, at, 0:1]
            square = value * value
            bent = jnp.tanh(ROOT * value * (1.0 + CUBIC * square))
            plus = 0.5 * (1.0 + bent)
            bowed = value * plus
            slope = plus + (0.5 * ROOT) * value * (1.0 - bent * bent) * (1.0 + (3.0 * CUBIC) * square)
            active[at, :] = (bowed * gate_column).astype(BF)
            back = (grad_active * gate_column * slope).astype(BF)
            hidden_grad[at, :] = back
            lane = lax.broadcasted_iota(jnp.int32, (CHUNK, TALL), 1)
            gate_grad = jnp.sum(grad_active * bowed, -1, keepdims=True)
            made_gate[expert, at, :] = jnp.where(lane == pair * count + expert, gate_grad, 0.0).astype(BF)
            made[expert, at, :] = dot(active[at, :], outer[slot]).astype(BF)
            made_back[expert, at, :] = contract_cols(back, inner[slot]).astype(BF)
            return carry

        lax.fori_loop(0, blocks * TILE // CHUNK, chunk, 0)

    def weigh(expert, slot, again):
        for stage, grad, left, right in (
            (stage_out, grad_out, active, grads.at[expert]), (stage_in, grad_in, picked.at[expert], hidden_grad),
        ):
            if again:
                reload([(grad.at[expert], stage.at[slot])])
            for begin in range(0, left.shape[1], CHUNK):
                at = pl.ds(begin, CHUNK)
                value = contract_rows(left[:, at], right[...])
                if again:
                    value = value + stage[slot, at, :].astype(F32)
                stage[slot, at, :] = value.astype(BF)

    def give(block, slot, step, again):
        at = pl.ds(pl.multiple_of(block * TILE, TILE), TILE)
        choose = choices(block, step)

        def joined(source):
            return jnp.concatenate([source[expert, at, :] for expert in range(count)], 0)

        if again:
            reload([(total_all.at[block], rows_buf.at[0]), (back_all.at[block], rows_buf.at[1])])
        for target, source, old in ((total_buf, made, 0), (back_buf, made_back, 1)):
            value = contract_rows(choose, joined(source))
            if again:
                value = value + rows_buf[old].astype(F32)
            target[slot] = value.astype(BF)
        start(puts(block, slot))
        gates = contract_rows(joined(made_gate), choose)
        if again:
            gates = gates + gate_ref[block].astype(F32)
        gate_ref[block] = gates.astype(BF)

    def choices(block, step):
        slots = lax.broadcasted_iota(jnp.int32, (TILE, length), 0).astype(F32) + (step * TILE).astype(F32)
        return jnp.concatenate([(ranks[block, line(expert), :] == slots).astype(BF) for expert in range(count)], 0)

    lane = lax.broadcasted_iota(jnp.int32, (count * TILE, TALL), 1)
    wanted = lax.broadcasted_iota(jnp.int32, (count * TILE, TALL), 0) // TILE + pair * count
    first = jnp.int32(0)
    for block in range(blocks):
        take(block, block % 2, first)
        if block + 2 < blocks:
            start(fetches(block + 2, block % 2))
    for expert in range(count):
        slot = expert % 2
        if expert + 1 < count:
            start(loads(expert + 1, 1 - slot))
        wait(loads(expert, slot))
        compute(expert, slot)
        if expert >= 2:
            wait(stores(expert - 2, slot))
        weigh(expert, slot, False)
        start(stores(expert, slot))
    for block in range(blocks):
        if block >= 2:
            wait(puts(block - 2, block % 2))
        give(block, block % 2, first, False)
    for block in range(blocks - 2, blocks):
        wait(puts(block, block % 2))
    for expert in range(count - 2, count):
        wait(stores(expert, expert % 2))

    def more(step, carry):
        def take_one(block, carry):
            start(fetches(block, 0))
            take(block, 0, step)
            return carry

        def expert_one(expert, carry):
            @pl.when(passes_of(expert) > step)
            def _():
                start(loads(expert, 0))
                wait(loads(expert, 0))
                compute(expert, 0)
                weigh(expert, 0, True)
                start(stores(expert, 0))
                wait(stores(expert, 0))

            return carry

        def give_one(block, carry):
            give(block, 0, step, True)
            wait(puts(block, 0))
            return carry

        lax.fori_loop(0, blocks, take_one, 0)
        lax.fori_loop(0, count, expert_one, 0)
        lax.fori_loop(0, blocks, give_one, 0)
        return carry

    lax.fori_loop(1, rounds, more, 0)


def expert_pass(place, rows, flags, cot, own_in, got_in, own_out, got_out):
    blocks, length, width = cot.shape
    count, _, hidden = got_in.shape
    capacity = blocks * TILE
    shape = jax.ShapeDtypeStruct
    anywhere = pl.BlockSpec(memory_space=pl.ANY)
    vmem = pl.BlockSpec(memory_space=pltpu.VMEM)
    return pl.pallas_call(
        expert_kernel,
        out_shape=(
            shape((blocks, length, width), BF),
            shape((blocks, length, width), BF),
            shape((blocks, TALL, length), BF),
            shape((count, width, hidden), BF),
            shape((count, hidden, width), BF),
        ),
        in_specs=[pl.BlockSpec(memory_space=pltpu.SMEM), vmem] + [anywhere] * 6,
        out_specs=(anywhere, anywhere, vmem, anywhere, anywhere),
        scratch_shapes=[
            pltpu.VMEM((2, width, hidden), BF),
            pltpu.VMEM((2, hidden, width), BF),
            pltpu.VMEM((count, capacity, width), BF),
            pltpu.VMEM((count, capacity, width), BF),
            pltpu.VMEM((count, capacity, LANES), F32),
            pltpu.VMEM((capacity, hidden), BF),
            pltpu.VMEM((capacity, hidden), BF),
            pltpu.VMEM((count, capacity, width), BF),
            pltpu.VMEM((count, capacity, width), BF),
            pltpu.VMEM((count, capacity, TALL), BF),
            pltpu.VMEM((blocks, TALL, length), F32),
            pltpu.VMEM((2, length, width), BF),
            pltpu.VMEM((2, length, width), BF),
            pltpu.VMEM((2, length, width), BF),
            pltpu.VMEM((2, length, width), BF),
            pltpu.VMEM((2, width, hidden), BF),
            pltpu.VMEM((2, hidden, width), BF),
            pltpu.SemaphoreType.DMA((2, 4)),
            pltpu.SemaphoreType.DMA((2, 2)),
            pltpu.SemaphoreType.DMA((2, 2)),
            pltpu.SemaphoreType.DMA((2, 2)),
            pltpu.SemaphoreType.DMA((2,)),
        ],
        compiler_params=pltpu.CompilerParams(vmem_limit_bytes=BIG),
        cost_estimate=pl.CostEstimate(flops=50 * 10**9, bytes_accessed=5 * 10**7, transcendentals=10**6),
        name="experts",
    )(place, flags, rows, cot, own_in, got_in, own_out, got_out)


def back_middle(at, moe, gates, cot, middle, rows, probs, flags, small_ref, sums):
    experts = TALL // 2
    row = lax.broadcasted_iota(jnp.int32, flags.shape, 0)
    chosen = jnp.where(row < experts, pltpu.roll(flags, experts, 0), 0.0)
    asked = gates * chosen
    grad_logits = probs * (asked - jnp.sum(probs * asked, 0, keepdims=True))
    coarse = grad_logits.astype(BF)
    fine = (grad_logits - coarse.astype(F32)).astype(BF)
    router = router_rows(small_ref)
    sums[4] = sums[4] + dot(coarse, rows) + dot(fine, rows)
    grad = moe + contract_rows(coarse, router) + contract_rows(fine, router)
    unit, inverse = norm_parts(middle)
    sums[2] = sums[2] + jnp.sum(grad * unit, 0, keepdims=True)
    sums[3] = sums[3] + jnp.sum(grad, 0, keepdims=True)
    return cot + norm_back(grad, unit, inverse, gain_row(small_ref, experts, 2))


def back_heads(at, double, grad_proj, packed_ref, out_ref, stacked):
    width = grad_proj.shape[1]
    group = 3 * HEAD_DIM
    scale = HEAD_DIM ** (-0.5)
    lanes = lax.broadcasted_iota(jnp.int32, (PAD, group), 1) // HEAD_DIM
    made = []
    packed = packed_ref[at, pl.ds(double * 6 * group, 6 * group)]
    for side in range(2):
        query, keys, values = (packed[:, (3 * side + k) * group : (3 * side + k + 1) * group] for k in range(3))
        index = double * 2 + side
        grad_att = contract_cols(grad_proj, out_ref[pl.ds(index * group, group), :]).astype(BF)
        outs = [jnp.zeros((PAD, group), F32) for _ in range(3)]
        for head in range(3):
            mask = lanes == head
            probs = head_probs(jnp.where(mask, query, jnp.zeros_like(query)), keys, scale)
            part = jnp.where(mask, grad_att, jnp.zeros_like(grad_att))
            grad_weights = contract_cols(part, values)
            inner_sum = jnp.sum(probs * grad_weights, -1, keepdims=True)
            grad_scores = (probs * (grad_weights - inner_sum)).astype(BF)
            outs[0] = jnp.where(mask, dot(grad_scores, keys), outs[0])
            outs[1] = jnp.where(mask, contract_rows(grad_scores, query), outs[1])
            outs[2] = jnp.where(mask, contract_rows(probs.astype(BF), grad_att), outs[2])
        made += [outs[0] * scale, outs[1] * scale, outs[2]]
    stacked[at, pl.ds(double * 6 * group, 6 * group)] = jnp.concatenate(made, 1).astype(BF)


def back_kernel(
    moe_ref, gate_ref, cot_ref, x_ref, middle_ref, rows_ref, flag_ref, prob_ref, attended_ref, packed_ref, normed_ref,
    small_ref, qkv_ref, out_ref,
    tokens_ref, grad_qkv, grad_out, grad_small,
    stacked, projected,
):
    rows, width = x_ref.shape
    experts = TALL // 2
    sums = [jnp.zeros((1, width), F32) for _ in range(4)] + [jnp.zeros((TALL, width), F32)]
    for image in range(rows // PAD):
        at = pl.ds(image * PAD, PAD)
        cols = slice(image * PAD, (image + 1) * PAD)
        grad_middle = back_middle(
            at, moe_ref[at, :].astype(F32), gate_ref[:, cols].astype(F32), cot_ref[at, :].astype(F32),
            middle_ref[at, :], rows_ref[at, :], prob_ref[:, cols], flag_ref[:, cols].astype(F32), small_ref, sums,
        )
        grad_proj = grad_middle.astype(BF)
        projected[at, :] = grad_proj
        for double in range(width // (6 * HEAD_DIM)):
            back_heads(at, double, grad_proj, packed_ref, out_ref, stacked)
        grad = contract_cols(stacked[at, :], qkv_ref[...])
        unit, inverse = norm_parts(x_ref[at, :].astype(F32))
        sums[0] = sums[0] + jnp.sum(grad * unit, 0, keepdims=True)
        sums[1] = sums[1] + jnp.sum(grad, 0, keepdims=True)
        tokens_ref[at, :] = (grad_middle + norm_back(grad, unit, inverse, gain_row(small_ref, experts, 0))).astype(BF)
    grad_small[...] = jnp.concatenate([sums[4][0:experts]] + sums[:4] + [jnp.zeros((4, width), F32)], 0).astype(BF)
    grad_out[...] = contract_rows(attended_ref[...], projected[...]).astype(BF)
    for third in range(3):
        cols = pl.ds(third * width, width)
        grad_qkv[:, cols] = contract_rows(normed_ref[...], stacked[:, cols]).astype(BF)


def back(moe, gates, cot, x, middle, sent, flags, prob, attended, packed, normed, small, qkv, out):
    rows, width = x.shape
    shape = jax.ShapeDtypeStruct
    return pl.pallas_call(
        back_kernel,
        out_shape=(
            shape((rows, width), BF),
            shape((width, 3 * width), BF),
            shape((width, width), BF),
            shape((TALL, width), BF),
        ),
        scratch_shapes=[pltpu.VMEM((rows, 3 * width), BF), pltpu.VMEM((rows, width), BF)],
        compiler_params=pltpu.CompilerParams(vmem_limit_bytes=BIG),
        cost_estimate=pl.CostEstimate(flops=16 * 10**9, bytes_accessed=2 * 10**7, transcendentals=10**6),
        name="back",
    )(moe, gates, cot, x, middle, sent, flags, prob, attended, packed, normed, small, qkv, out)


ORDER = [[('x', 0), ('x', 1)], [('x', 2)], [('a', 0), ('x', 3), ('a', 1), ('x', 4), ('y', 0), ('x', 5)], [], [], [], [], [('b', 0), ('x', 6)], [('da', 0), ('b', 1), ('y', 1), ('da', 2), ('da', 3), ('y', 2), ('dl', 0), ('da', 1), ('x', 7)], [('dl', 2), ('y', 3), ('x', 8), ('dl', 3), ('db', 0), ('x', 9), ('y', 4), ('db', 2), ('y', 5), ('y', 6), ('dl', 1), ('y', 7), ('ds', 0), ('db', 3), ('c', 0), ('y', 8), ('s', 0), ('x', 10), ('c', 1), ('ds', 2), ('y', 9), ('s', 1), ('y', 10), ('s', 2), ('db', 1), ('ds', 3), ('dt', 0), ('ds', 1), ('dt', 2), ('x', 11), ('y', 11)], [('s', 3), ('dt', 3), ('dt', 1)]]


class LineScatter:
    def __init__(self, links, place, sums, up, down):
        self.links, self.place = links, place
        self.sums, self.up, self.down = sums, up, down
        self.copies = {}

    def ways(self, step):
        t = self.place.tensor
        return (
            ("up", self.up, t + 3 - step, t <= step, t >= 1, self.place.above),
            ("down", self.down, t - 3 + step, t >= 3 - step, t <= 2, self.place.below),
        )

    def send(self, part, step):
        for name, got, slot, sends, comes, device in self.ways(step):
            slot = jnp.clip(slot, 0, 3)
            if step > 0:
                before = self.copies[name, part, step - 1]

                @pl.when(sends & comes)
                def _():
                    before.wait_recv()
                    ref = self.sums(slot, part)
                    ref[...] = (ref[...].astype(F32) + got(step - 1, part)[...].astype(F32)).astype(BF)

            copy = self.links.copy(self.sums(slot, part), got(step, part), device)
            pl.when(sends)(copy.start)
            self.links.sent.append((sends, copy))
            self.copies[name, part, step] = copy

    def finish(self, part, total):
        total[...] = self.sums(self.place.tensor, part)[...].astype(F32)
        for name, got, slot, sends, comes, device in self.ways(2):
            copy = self.copies[name, part, 2]

            @pl.when(comes)
            def _():
                copy.wait_recv()
                total[...] += got(2, part)[...].astype(F32)


def tail_kernel(
    back_all, gate_all, total_all, grads_in, grads_out, rows_all, flags_all,
    cot_ref, x_ref, middle_ref, prob_ref, attended_ref, packed_ref, normed_ref, small_ref, qkv_ref, out_ref,
    mixed_ref, tokens_ref, dense_ref, grad_small, final_in, final_out, beside_in, beside_out,
    back_sum, back_got, back_up, back_down, gate_sum, gate_got, gate_up, gate_down,
    total_sum, total_got, total_up, total_down, moe, gates, rows_ref, flag_ref, projected, stacked,
    chunks, core_got, across_sent, across_got, line_sum, line_got, side_sum, side_got, line_final,
    own_in, own_out, across_in, across_out, read_in, read_out, half_in, half_out, mine_in, mine_out, both_in, both_out,
    small_sent, small_core, small_half, small_across, small_side, small_beside, small_line_sent, small_line,
    send, recv, local_sem,
):
    place = Place()
    links = Links(send, recv)
    rows, width = x_ref.shape
    experts = TALL // 2
    count = grads_in.shape[0]
    depth = width // 2
    shard, pair, side, tensor = place.shard, place.pair, place.side, place.tensor
    mine = pair * 4 + tensor
    place.greet(True)
    ours, theirs = pl.ds(pair * 4, 4), pl.ds((1 - pair) * 4, 4)

    locals_ = [
        pltpu.make_async_copy(back_all.at[ours], back_sum, local_sem.at[0]),
        pltpu.make_async_copy(gate_all.at[ours], gate_sum, local_sem.at[1]),
        pltpu.make_async_copy(total_all.at[ours], total_sum, local_sem.at[2]),
        pltpu.make_async_copy(rows_all.at[mine], rows_ref, local_sem.at[3]),
        pltpu.make_async_copy(flags_all.at[mine], flag_ref, local_sem.at[4]),
    ]
    for copy in locals_:
        copy.start()
    from_twin = [links.start(gate_all.at[theirs], gate_got, place.twin)]
    for part in range(2):
        at = pl.ds(part * PAD, PAD)
        from_twin.append(links.start(back_all.at[theirs, at, :], back_got.at[:, at, :], place.twin))
    from_twin.append(links.start(total_all.at[theirs], total_got, place.twin))

    here = pl.ds(pl.multiple_of(shard * depth, LANES), depth)
    there = pl.ds(pl.multiple_of((1 - shard) * depth, LANES), depth)
    hidden = grads_in.shape[2]
    tall, wide = depth // 2, hidden // 2
    pieces = []
    for expert in range(1, count):
        for half in range(2):
            at = pl.ds(half * tall, tall)
            pieces.append((
                grads_in.at[expert, pl.ds(pl.multiple_of((1 - shard) * depth + half * tall, TALL), tall), :],
                grads_in.at[expert, pl.ds(pl.multiple_of(shard * depth + half * tall, TALL), tall), :],
                across_in.at[expert - 1, at, :], beside_in.at[expert - 1, at, :],
                final_in.at[pair * count + expert, at, :], own_in.at[at, :], read_in.at[at, :],
            ))
        for half in range(2):
            at = pl.ds(half * wide, wide)
            pieces.append((
                grads_out.at[expert, at, there], grads_out.at[expert, at, here],
                across_out.at[expert - 1, at, :], beside_out.at[expert - 1, at, :],
                final_out.at[pair * count + expert, at, :], own_out.at[at, :], read_out.at[at, :],
            ))
    loads = [pltpu.make_async_copy(piece[1], piece[5], local_sem.at[8 + m]) for m, piece in enumerate(pieces)]
    at_across, at_beside, at_twin, kept = {}, {}, [], []
    started = [0]

    def add(target, source):
        target[...] = (target[...].astype(F32) + source[...].astype(F32)).astype(BF)

    def keep(source, target):
        copy = pltpu.make_async_copy(source, target, local_sem.at[32 + len(kept)])
        copy.start()
        kept.append(copy)

    def send_across():
        m = started[0]
        if m < len(pieces):
            at_across[m] = links.start(pieces[m][0], pieces[m][2], place.across)
            started[0] += 1

    def take_across(m):
        at_across[m].wait_recv()
        send_across()
        loads[m].wait()
        add(pieces[m][2], pieces[m][5])
        at_beside[m] = links.start(pieces[m][2], pieces[m][3], place.beside)
        if m + 4 < len(pieces):
            loads[m + 4].start()

    def take_beside(m):
        at_beside[m].wait_recv()
        load = pltpu.make_async_copy(pieces[m][3], pieces[m][6], local_sem.at[5])
        load.start()
        at_beside[m].wait_send()
        links.skip(at_beside[m])
        load.wait()
        add(pieces[m][2], pieces[m][6])
        at_twin.append(links.start(pieces[m][2], pieces[m][4], place.twin))
        keep(pieces[m][2], pieces[m][4])

    our_half = pl.ds(pl.multiple_of(side * wide, LANES), wide)
    other_half = pl.ds(pl.multiple_of((1 - side) * wide, LANES), wide)
    first = (
        (grads_in.at[0, :, other_half], grads_in.at[0, :, our_half], half_in, mine_in,
         half_in.at[there, :], half_in.at[here, :], both_in,
         final_in.at[pair * count, :, our_half], final_in.at[pair * count, :, other_half]),
        (grads_out.at[0, other_half, :], grads_out.at[0, our_half, :], half_out, mine_out,
         half_out.at[:, there], half_out.at[:, here], both_out,
         final_out.at[pair * count, our_half, :], final_out.at[pair * count, other_half, :]),
    )
    first_loads = [pltpu.make_async_copy(item[1], item[3], local_sem.at[6 + q]) for q, item in enumerate(first)]
    first_beside, first_across, first_back = {}, {}, {}

    def first_send(q):
        first_loads[q].start()
        first_beside[q] = links.start(first[q][0], first[q][2], place.beside)

    def first_sum(q):
        first_beside[q].wait_recv()
        first_loads[q].wait()
        add(first[q][2], first[q][3])
        first_across[q] = links.start(first[q][4], first[q][6], place.across)

    def first_total(q):
        first_across[q].wait_recv()
        add(first[q][6], first[q][5])
        first_back[q] = links.start(first[q][6], first[q][7], place.beside)
        at_twin.append(links.start(first[q][6], first[q][7], place.twin))
        keep(first[q][6], first[q][7])

    def first_share(q):
        first_back[q].wait_recv()
        at_twin.append(links.start(first[q][8], first[q][8], place.twin))

    share = depth // 2
    piece = share // 4
    stage = {}

    def dense_core(k):
        stage["core", k] = []
        for owner in range(2):
            source = chunks.at[k, pl.ds(pl.multiple_of(owner * depth + (1 - pair) * share, TALL), share), :]
            stage["core", k].append(links.start(source, core_got.at[k, owner], place.twin))

    def core_sum(k, owner):
        at = pl.ds(pl.multiple_of(owner * depth + pair * share, TALL), share)
        return chunks[k, at, :].astype(F32) + core_got[k, owner].astype(F32)

    def dense_across(k):
        for copy in stage["core", k]:
            copy.wait_recv()
        across_sent[k] = core_sum(k, 1 - shard).astype(BF)
        stage["across", k] = links.start(across_sent.at[k], across_got.at[k], place.across)

    def around(offset):
        return (shard, place.head, lax.rem(tensor + offset, 4))

    def dense_line(k):
        stage["across", k].wait_recv()
        line_sum[k] = (core_sum(k, shard) + across_got[k].astype(F32)).astype(BF)
        stage["line", k] = []
        for offset in (2, 1, 3):
            at = pl.ds(pl.multiple_of(lax.rem(tensor + offset, 4) * piece, TALL), piece)
            stage["line", k].append(links.start(line_sum.at[k, at, :], line_got.at[k, offset - 1], around(offset)))

    def dense_beside(k):
        for copy in stage["line", k]:
            copy.wait_recv()
        at = pl.ds(pl.multiple_of(tensor * piece, TALL), piece)
        value = line_sum[k, at, :].astype(F32)
        for offset in range(3):
            value = value + line_got[k, offset].astype(F32)
        side_sum[k] = value.astype(BF)
        stage["beside", k] = links.start(side_sum.at[k], side_got.at[k], place.beside)

    def dense_spread(k):
        stage["beside", k].wait_recv()
        line_final[k] = (side_sum[k].astype(F32) + side_got[k].astype(F32)).astype(BF)
        target = dense_ref.at[
            pl.ds(pl.multiple_of(pair * share + tensor * piece, TALL), piece), pl.ds(k * width, width)
        ]
        stage["spread", k] = [links.start(line_final.at[k], target, around(offset)) for offset in (2, 1, 3)]
        stage["keep", k] = pltpu.make_async_copy(line_final.at[k], target, local_sem.at[24 + k])
        stage["keep", k].start()

    def dense_twin(k):
        for copy in stage["spread", k]:
            copy.wait_recv()
        stage["keep", k].wait()
        block = dense_ref.at[pl.ds(pl.multiple_of(pair * share, TALL), share), pl.ds(k * width, width)]
        stage["twin", k] = links.start(block, block, place.twin)

    def small_core_stage():
        small_core_copy.wait_recv()
        other = pl.ds(pl.multiple_of((1 - shard) * depth, LANES), depth)
        small_half[...] = small_sent[:, other] + small_core[:, other]
        stage["small", 1] = links.start(small_half, small_across, place.across)

    def small_across_stage():
        stage["small", 1].wait_recv()
        own = pl.ds(pl.multiple_of(shard * depth, LANES), depth)
        small_side[...] = small_sent[:, own] + small_core[:, own] + small_across[...]
        stage["small", 2] = links.start(small_side, small_beside, place.beside)

    def small_beside_stage():
        stage["small", 2].wait_recv()
        small_line_sent[...] = small_side[...] + small_beside[...]
        stage["small", 3] = [
            links.start(small_line_sent, small_line.at[offset - 1], around(offset)) for offset in (2, 1, 3)
        ]

    def small_line_stage():
        for copy in stage["small", 3]:
            copy.wait_recv()
        grad_small[...] = small_line_sent[...] + small_line[0] + small_line[1] + small_line[2]

    def slots(array):
        def view(slot, part):
            return array.at[slot, pl.ds(part * PAD, PAD), :]

        return view

    back_line = LineScatter(links, place, slots(back_sum), slots(back_up), slots(back_down))
    total_line = LineScatter(links, place, slots(total_sum), slots(total_up), slots(total_down))
    gate_line = LineScatter(
        links, place, lambda slot, part: gate_sum.at[slot], lambda step, part: gate_up.at[step],
        lambda step, part: gate_down.at[step],
    )

    steps = {
        "x": take_across, "y": take_beside, "a": first_sum, "b": first_total, "c": first_share,
        "da": dense_across, "dl": dense_line, "db": dense_beside, "ds": dense_spread, "dt": dense_twin,
        "s": lambda index: (small_core_stage, small_across_stage, small_beside_stage, small_line_stage)[index](),
    }

    def go(slot):
        for name, index in ORDER[slot]:
            steps[name](index)

    first_send(0)
    for _ in range(3):
        send_across()
    first_send(1)
    for m in range(4):
        loads[m].start()
    locals_[1].wait()
    from_twin[0].wait_recv()
    add(gate_sum, gate_got)
    gate_line.send(0, 0)
    locals_[0].wait()
    for part in range(2):
        from_twin[1 + part].wait_recv()
        at = pl.ds(part * PAD, PAD)
        for slot in range(4):
            add(back_sum.at[slot, at, :], back_got.at[slot, at, :])
        back_line.send(part, 0)
    locals_[2].wait()
    from_twin[3].wait_recv()
    for slot in range(4):
        add(total_sum.at[slot], total_got.at[slot])
    go(0)
    gate_line.send(0, 1)
    for part in range(2):
        back_line.send(part, 1)
    go(1)
    gate_line.send(0, 2)
    for part in range(2):
        back_line.send(part, 2)
    go(2)
    for part in range(2):
        total_line.send(part, 0)
    gate_line.finish(0, gates)
    locals_[3].wait()
    locals_[4].wait()

    sums = [jnp.zeros((1, width), F32) for _ in range(4)] + [jnp.zeros((TALL, width), F32)]
    for image in range(2):
        at = pl.ds(image * PAD, PAD)
        cols = slice(image * PAD, (image + 1) * PAD)
        back_line.finish(image, moe.at[at, :])
        grad = back_middle(
            at, moe[at, :], gates[:, cols], cot_ref[at, :].astype(F32), middle_ref[at, :], rows_ref[at, :],
            prob_ref[:, cols], flag_ref[:, cols].astype(F32), small_ref, sums,
        )
        moe[at, :] = grad
        projected[at, :] = grad.astype(BF)
    go(3)
    chunks[0] = contract_rows(attended_ref[...], projected[...]).astype(BF)
    dense_core(0)
    go(4)
    for image in range(2):
        at = pl.ds(image * PAD, PAD)
        back_heads(at, 0, projected[at, :], packed_ref, out_ref, stacked)
        if image == 0:
            go(5)
    chunks[1] = contract_rows(normed_ref[...], stacked[:, pl.ds(0, width)]).astype(BF)
    dense_core(1)
    for part in range(2):
        total_line.send(part, 1)
    go(6)
    for image in range(2):
        at = pl.ds(image * PAD, PAD)
        back_heads(at, 1, projected[at, :], packed_ref, out_ref, stacked)
        if image == 0:
            go(7)
    for k in (2, 3):
        chunks[k] = contract_rows(normed_ref[...], stacked[:, pl.ds((k - 1) * width, width)]).astype(BF)
        dense_core(k)
    for part in range(2):
        total_line.send(part, 2)
    go(8)
    for image in range(2):
        at = pl.ds(image * PAD, PAD)
        grad = contract_cols(stacked[at, :], qkv_ref[...])
        unit, inverse = norm_parts(x_ref[at, :].astype(F32))
        sums[0] = sums[0] + jnp.sum(grad * unit, 0, keepdims=True)
        sums[1] = sums[1] + jnp.sum(grad, 0, keepdims=True)
        tokens_ref[at, :] = (
            moe[at, :] + norm_back(grad, unit, inverse, gain_row(small_ref, experts, 0))
        ).astype(BF)
    small_sent[...] = jnp.concatenate([sums[4][0:experts]] + sums[:4] + [jnp.zeros((4, width), F32)], 0)
    small_core_copy = links.start(small_sent, small_core, place.twin)
    go(9)
    for part in range(2):
        at = pl.ds(part * PAD, PAD)
        total_line.finish(part, moe.at[at, :])
        mixed_ref[at, :] = (middle_ref[at, :] + moe[at, :]).astype(BF)
    go(10)
    for copy in at_twin + [stage["twin", k] for k in range(4)]:
        copy.wait_recv()
    for copy in kept:
        copy.wait()
    links.finish()


def tail(back_all, gate_all, total_all, grads_in, grads_out, rows_all, flags_all, cot, x, middle, prob, attended, packed, normed, small, qkv, out):
    rows, width = x.shape
    count, _, hidden = grads_in.shape
    depth = width // 2
    shape = jax.ShapeDtypeStruct
    anywhere = pl.BlockSpec(memory_space=pl.ANY)
    vmem = pl.BlockSpec(memory_space=pltpu.VMEM)
    share, piece = depth // 2, depth // 8

    def scatter_buffers(tall, wide):
        return [pltpu.VMEM((4, tall, wide), BF)] * 2 + [pltpu.VMEM((3, tall, wide), BF)] * 2

    return pl.pallas_call(
        tail_kernel,
        out_shape=(
            shape((rows, width), BF),
            shape((rows, width), BF),
            shape((depth, 4 * width), BF),
            shape((TALL, depth), F32),
            shape((2 * count, depth, hidden), BF),
            shape((2 * count, hidden, depth), BF),
            shape((count - 1, depth, hidden), BF),
            shape((count - 1, hidden, depth), BF),
        ),
        in_specs=[anywhere] * 7 + [vmem] * 10,
        out_specs=(vmem,) * 4 + (anywhere,) * 4,
        scratch_shapes=scatter_buffers(rows, width)
        + scatter_buffers(TALL, rows)
        + scatter_buffers(rows, width)
        + [
            pltpu.VMEM((rows, width), F32),
            pltpu.VMEM((TALL, rows), F32),
            pltpu.VMEM((rows, width), BF),
            pltpu.VMEM((TALL, rows), BF),
            pltpu.VMEM((rows, width), BF),
            pltpu.VMEM((rows, 3 * width), BF),
            pltpu.VMEM((4, width, width), BF),
            pltpu.VMEM((4, 2, share, width), BF),
            pltpu.VMEM((4, share, width), BF),
            pltpu.VMEM((4, share, width), BF),
            pltpu.VMEM((4, share, width), BF),
            pltpu.VMEM((4, 3, piece, width), BF),
            pltpu.VMEM((4, piece, width), BF),
            pltpu.VMEM((4, piece, width), BF),
            pltpu.VMEM((4, piece, width), BF),
        ]
        + [pltpu.VMEM((depth, hidden), BF), pltpu.VMEM((hidden, depth), BF)]
        + [pltpu.VMEM((count - 1, depth, hidden), BF), pltpu.VMEM((count - 1, hidden, depth), BF)]
        + [pltpu.VMEM((depth, hidden), BF), pltpu.VMEM((hidden, depth), BF)]
        + [pltpu.VMEM((width, hidden // 2), BF), pltpu.VMEM((hidden // 2, width), BF)] * 2
        + [pltpu.VMEM((depth, hidden // 2), BF), pltpu.VMEM((hidden // 2, depth), BF)]
        + [
            pltpu.VMEM((TALL, width), F32),
            pltpu.VMEM((TALL, width), F32),
            pltpu.VMEM((TALL, depth), F32),
            pltpu.VMEM((TALL, depth), F32),
            pltpu.VMEM((TALL, depth), F32),
            pltpu.VMEM((TALL, depth), F32),
            pltpu.VMEM((TALL, depth), F32),
            pltpu.VMEM((3, TALL, depth), F32),
            pltpu.SemaphoreType.DMA((192,)),
            pltpu.SemaphoreType.DMA((192,)),
            pltpu.SemaphoreType.DMA((48,)),
        ],
        compiler_params=pltpu.CompilerParams(vmem_limit_bytes=BIG, collective_id=2, has_side_effects=True),
        cost_estimate=pl.CostEstimate(flops=16 * 10**9, bytes_accessed=5 * 10**7, transcendentals=10**6),
        name="tail",
    )(back_all, gate_all, total_all, grads_in, grads_out, rows_all, flags_all, cot, x, middle, prob, attended, packed, normed, small, qkv, out)


class Comm:
    def __init__(self):
        self.sizes = tuple(lax.axis_size(axis) for axis in AXES)
        self.shard = lax.axis_index("shard")
        self.head = lax.axis_index("heads")
        self.tensor = lax.axis_index("tensor")
        self.pair = self.head % 2

    def move(self, value, step):
        shards, heads, tensors = self.sizes
        pairs = []
        for s in range(shards):
            for h in range(heads):
                for t in range(tensors):
                    to = step(s, h, t)
                    if 0 <= to[2] < tensors:
                        source = (s * heads + h) * tensors + t
                        pairs.append((source, (to[0] * heads + to[1]) * tensors + to[2]))
        return lax.ppermute(value, AXES, pairs)

    def over_core(self, value):
        return self.move(value, lambda s, h, t: (s, h ^ 1, t))

    def over_heads(self, value):
        return self.move(value, lambda s, h, t: (s, (h + 2) % 4, t))

    def over_shard(self, value):
        return self.move(value, lambda s, h, t: (1 - s, h, t))

    def up(self, value):
        return self.move(value, lambda s, h, t: (s, h, t + 1))

    def down(self, value):
        return self.move(value, lambda s, h, t: (s, h, t - 1))

    def halves(self, value, index, axis):
        size = value.shape[axis] // 2
        mine = lax.dynamic_slice_in_dim(value, index * size, size, axis)
        other = lax.dynamic_slice_in_dim(value, (1 - index) * size, size, axis)
        return mine, other

    def join(self, mine, other, index, axis):
        first = jnp.where(index == 0, mine, other)
        second = jnp.where(index == 0, other, mine)
        return jnp.concatenate((first, second), axis)

    def gather_shard(self, value, axis):
        if self.sizes[0] != 2:
            return lax.all_gather(value, "shard", axis=axis, tiled=True)
        return self.join(value, self.over_shard(value), self.shard, axis)

    def gather_shard_split(self, value, axis, cut):
        if self.sizes[0] != 2:
            return lax.all_gather(value, "shard", axis=axis, tiled=True)
        mine, _ = self.halves(value, self.pair, cut)
        got = self.over_shard(mine)
        both = self.join(got, self.over_core(got), self.pair, cut)
        return self.join(value, both, self.shard, axis)

    def scatter_shard(self, value, axis):
        if self.sizes[0] != 2:
            return lax.psum_scatter(value.astype(BF), "shard", scatter_dimension=axis, tiled=True).astype(F32)
        mine, other = self.halves(value, self.shard, axis)
        return mine.astype(F32) + self.over_shard(other.astype(BF)).astype(F32)

    def scatter_core(self, value, axis):
        mine, other = self.halves(value, self.pair, axis)
        return mine.astype(F32) + self.over_core(other.astype(BF)).astype(F32)

    def scatter_heads(self, value, axis):
        mine, other = self.halves(value, self.head // 2, axis)
        return mine.astype(F32) + self.over_heads(other.astype(BF)).astype(F32)

    def line_gather(self, value):
        ups, downs = [value], [value]
        for _ in range(3):
            ups.append(self.up(ups[-1]))
            downs.append(self.down(downs[-1]))
        out = [value]
        for back in (1, 2, 3):
            out.append(jnp.where(self.tensor >= back, ups[back], downs[4 - back]))
        return out

    def line_scatter(self, parts):
        high, low = parts[1].astype(BF), parts[3].astype(BF)
        high = (parts[2].astype(F32) + self.up(high).astype(F32)).astype(BF)
        low = (parts[2].astype(F32) + self.down(low).astype(F32)).astype(BF)
        high = (parts[3].astype(F32) + self.up(high).astype(F32)).astype(BF)
        low = (parts[1].astype(F32) + self.down(low).astype(F32)).astype(BF)
        return parts[0].astype(F32) + self.up(high).astype(F32) + self.down(low).astype(F32)

    def join_slots(self, values):
        own = jnp.zeros((4,) + values[0].shape, values[0].dtype)
        for back, value in enumerate(values):
            own = lax.dynamic_update_index_in_dim(own, value, (self.tensor + 4 - back) % 4, 0)
        return self.join(own, self.over_core(own), self.pair, 0)

    def collect(self, value):
        mine, other = self.halves(value, self.pair, 0)
        mine = mine.astype(F32) + self.over_core(other).astype(F32)
        return self.line_scatter(
            [lax.dynamic_index_in_dim(mine, (self.tensor + 4 - k) % 4, 0, False) for k in range(4)]
        )


def local(
    tokens, ln1_gain, ln1_bias, qkv_weight, out_weight, ln2_gain, ln2_bias, router_weight,
    expert_in, expert_out, route_noise, expert_ids, cotangent,
):
    comm = Comm()
    rows, width = tokens.shape
    experts = expert_in.shape[0]
    images = rows // SEQ
    half = experts // 2
    padded = images * PAD

    def pad(value):
        value = value.reshape(images, SEQ, value.shape[1])
        return jnp.pad(value, ((0, 0), (0, PAD - SEQ), (0, 0))).reshape(padded, value.shape[2])

    def pad_turned(value, tall, fill):
        value = value.reshape(images, SEQ, value.shape[1]).transpose(2, 0, 1)
        value = jnp.pad(value, ((0, tall - value.shape[0]), (0, 0), (0, PAD - SEQ)), constant_values=fill)
        return value.reshape(tall, padded)

    def unpad(value):
        return value.reshape(images, PAD, value.shape[1])[:, :SEQ].reshape(rows, value.shape[1])

    small = jnp.concatenate(
        (router_weight.T, ln1_gain[None], ln1_bias[None], ln2_gain[None], ln2_bias[None]), 0
    )
    small = jnp.pad(small, ((0, TALL - small.shape[0]), (0, 0)))
    cot, x = pad(cotangent), pad(tokens)
    noise, ids = pad_turned(route_noise, TALL, 0), pad_turned(expert_ids, 8, -1)
    place = jnp.stack((comm.pair, comm.shard if comm.sizes[0] == 2 else 0 * comm.shard)).astype(jnp.int32)
    if comm.sizes[0] == 2:
        (
            small, proj_qkv, proj_out, normed_a, packed, attended, middle, prob,
            rows_all, flags_all, grad_rows, got_in, got_out,
        ) = head(x, cot, small, qkv_weight, out_weight, expert_in, expert_out, noise, ids)
        weights = (expert_in, got_in, expert_out, got_out)
    else:
        small = lax.all_gather(small, "shard", axis=1, tiled=True)
        small = small.reshape(TALL, 2, width // 2).transpose(1, 0, 2)
        proj_qkv = lax.all_gather(qkv_weight, "shard", axis=0, tiled=True)
        proj_out = lax.all_gather(out_weight, "shard", axis=0, tiled=True)
        inner = lax.all_gather(lax.dynamic_slice_in_dim(expert_in, comm.pair * half, half, 0), "shard", axis=1, tiled=True)
        outer = lax.all_gather(lax.dynamic_slice_in_dim(expert_out, comm.pair * half, half, 0), "shard", axis=2, tiled=True)
        cut = width // 2
        weights = (
            jnp.concatenate((inner[:, :cut], inner[:, :cut]), 0), inner[:, cut:],
            jnp.concatenate((outer[:, :, :cut], outer[:, :, :cut]), 0), outer[:, :, cut:],
        )
        normed_a, packed, attended, middle, sent, flags, prob = front(x, small, proj_qkv, proj_out, noise, ids)

        def gather(value):
            return comm.join_slots(comm.line_gather(value))

        grad_rows, rows_all, flags_all = gather(cot), gather(sent), gather(flags)
    total, back_all, gate_all, grads_in, grads_out = expert_pass(place, rows_all, flags_all, grad_rows, *weights)

    if comm.sizes[0] == 2:
        mixed, grad_tokens, dense, grad_small, grad_in, grad_outer, _, _ = tail(
            back_all, gate_all, total, grads_in, grads_out, rows_all, flags_all,
            cot, x, middle, prob, attended, packed, normed_a, small, proj_qkv, proj_out,
        )
        dense = dense.astype(F32)
        return (
            unpad(mixed),
            unpad(grad_tokens),
            grad_small[experts],
            grad_small[experts + 1],
            dense[:, width:],
            dense[:, :width],
            grad_small[experts + 2],
            grad_small[experts + 3],
            grad_small[:experts].T,
            grad_in.astype(F32),
            grad_outer.astype(F32),
        )

    def reduce_expert(grad, axis, other):
        part = comm.scatter_shard(grad, axis)
        part = comm.scatter_heads(part, other).astype(BF)
        return comm.join(part, comm.over_heads(part), comm.head // 2, other)

    inner_grads = [reduce_expert(grads_in[e], 0, 1) for e in range(half)]
    outer_grads = [reduce_expert(grads_out[e], 1, 0) for e in range(half)]

    moe_grad = comm.collect(back_all)
    gate_grad = comm.collect(gate_all)
    moe = comm.collect(total)
    mixed = (unpad(middle) + unpad(moe)).astype(BF)
    grad_tokens, grad_qkv, grad_out, grad_small = back(
        moe_grad, gate_grad, cot, x, middle, sent, flags, prob, attended, packed, normed_a, small, proj_qkv, proj_out
    )
    grad_tokens = unpad(grad_tokens)

    grad_small = jnp.pad(grad_small.T, ((0, 0), (0, 128 - TALL)))
    shares = jnp.concatenate((grad_qkv, grad_out, grad_small, jnp.zeros_like(grad_small)), 1)
    shares = comm.scatter_core(shares, 1)
    shares = comm.scatter_shard(shares, 0)
    shares = comm.scatter_heads(shares, 1)
    cut = shares.shape[0] // 4
    rolled = [
        lax.dynamic_slice_in_dim(shares, ((comm.tensor + 4 - k) % 4) * cut, cut, 0) for k in range(4)
    ]
    summed = comm.line_scatter(rolled).astype(BF)
    pieces = comm.line_gather(summed)
    whole = jnp.zeros(shares.shape, BF)
    for k in range(4):
        whole = lax.dynamic_update_slice_in_dim(whole, pieces[k], ((comm.tensor + 4 - k) % 4) * cut, 0)
    whole = comm.join(whole, comm.over_heads(whole), comm.head // 2, 1)
    whole = comm.join(whole, comm.over_core(whole), comm.pair, 1).astype(F32)
    small = whole[:, 4 * width : 4 * width + 128]

    grad_in, grad_outer = jnp.stack(inner_grads, 0), jnp.stack(outer_grads, 0)
    grad_in = comm.join(grad_in, comm.over_core(grad_in), comm.pair, 0).astype(F32)
    grad_outer = comm.join(grad_outer, comm.over_core(grad_outer), comm.pair, 0).astype(F32)
    return (
        mixed,
        grad_tokens,
        small[:, experts],
        small[:, experts + 1],
        whole[:, : 3 * width],
        whole[:, 3 * width : 4 * width],
        small[:, experts + 2],
        small[:, experts + 3],
        small[:, :experts],
        grad_in,
        grad_outer,
    )


def solution(mesh):
    split = P(AXES, None)
    vector, matrix = P("shard"), P("shard", None)
    inner, outer = P(None, "shard", "tensor"), P(None, "tensor", "shard")
    return jax.shard_map(
        local,
        mesh=mesh,
        in_specs=(
            split, vector, vector, matrix, matrix, vector, vector, matrix, inner, outer, split, split, split,
        ),
        out_specs=(
            split, split, vector, vector, matrix, matrix, vector, vector, matrix, inner, outer,
        ),
        check_vma=False,
    )
```

```python
import jax
import jax.numpy as jnp
from jax import lax
from jax.experimental import pallas as pl
from jax.experimental.pallas import tpu as pltpu
from jax.sharding import PartitionSpec as P

HEAD_DIM = 64
SEQ = 197
EPS = 1e-06
AXES = ("shard", "heads", "tensor")
BF = jnp.bfloat16
F32 = jnp.float32


def contract_rows(left, right):
    return lax.dot_general(left, right, (((0,), (0,)), ((), ())), preferred_element_type=F32)


def contract_cols(left, right):
    return lax.dot_general(left, right, (((1,), (1,)), ((), ())), preferred_element_type=F32)


PAD = 208
TILE = 128
CHUNK = 256
FAR = 512.0
TALL = 16
LANES = 128
MASKED = -1e30
CUBIC = 0.044715
ROOT = (2.0 / 3.141592653589793) ** 0.5
BIG = 60 * 1024 * 1024
MESH = pl.DeviceIdType.MESH


def dot(left, right):
    return jnp.dot(left, right, preferred_element_type=F32)


def norm_parts(values):
    centred = values - jnp.mean(values, -1, keepdims=True)
    inverse = lax.rsqrt(jnp.mean(centred * centred, -1, keepdims=True) + EPS)
    return centred * inverse, inverse


def norm_back(grad, unit, inverse, gain):
    scaled = grad * gain
    along = jnp.mean(scaled * unit, -1, keepdims=True)
    return inverse * (scaled - jnp.mean(scaled, -1, keepdims=True) - unit * along)


def head_probs(query, keys, scale):
    scores = contract_cols(query, keys) * scale
    column = lax.broadcasted_iota(jnp.int32, scores.shape, 1)
    scores = jnp.where(column < SEQ, scores, MASKED)
    raised = jnp.exp(scores - jnp.max(scores, -1, keepdims=True))
    return raised / jnp.sum(raised, -1, keepdims=True)


def gain_row(small_ref, experts, index):
    row = slice(experts + index, experts + index + 1)
    return jnp.concatenate((small_ref[0, row, :], small_ref[1, row, :]), 1).astype(F32)


def router_rows(small_ref):
    return jnp.concatenate((small_ref[0], small_ref[1]), 1)


def attend(normed, at, qkv_ref, packed_ref):
    width = normed.shape[1]
    group = 3 * HEAD_DIM
    scale = HEAD_DIM ** (-0.5)
    lane = lax.broadcasted_iota(jnp.int32, (PAD, group), 1) // HEAD_DIM
    outs = []
    for double in range(width // group // 2):
        cols = pl.ds(double * 6 * group, 6 * group)
        packed = dot(normed, qkv_ref[:, cols])
        packed_ref[at, cols] = packed.astype(BF)
        for side in range(2):
            query, keys, values = (
                packed[:, (3 * side + k) * group : (3 * side + k + 1) * group].astype(BF)
                for k in range(3)
            )
            total = jnp.zeros((PAD, group), F32)
            for head in range(3):
                mask = lane == head
                probs = head_probs(jnp.where(mask, query, jnp.zeros_like(query)), keys, scale)
                total = jnp.where(mask, dot(probs.astype(BF), values), total)
            outs.append(total)
    return jnp.concatenate(outs, 1).astype(BF)


def route(normed, small_ref, noise, ids, experts):
    logits = contract_cols(router_rows(small_ref), normed) + noise
    row = lax.broadcasted_iota(jnp.int32, logits.shape, 0)
    logits = jnp.where(row < experts, logits, MASKED)
    raised = jnp.exp(logits - jnp.max(logits, 0, keepdims=True))
    probs = raised / jnp.sum(raised, 0, keepdims=True)
    chosen = ((row == ids[0:1]) | (row == ids[1:2])).astype(F32)
    shifted = row - experts
    flags = (((shifted == ids[0:1]) | (shifted == ids[1:2])) & (shifted >= 0)).astype(F32)
    return probs, probs * chosen + flags


def front_image(image, experts, x_ref, small_ref, qkv_ref, out_ref, noise_ref, ids_ref, keep, ready=None):
    normed_ref, packed_ref, attended_ref, middle_ref = keep
    at = pl.ds(image * PAD, PAD)
    x = x_ref[at, :].astype(F32)
    unit, _ = norm_parts(x)
    normed = (unit * gain_row(small_ref, experts, 0) + gain_row(small_ref, experts, 1)).astype(BF)
    normed_ref[at, :] = normed
    attended = attend(normed, at, qkv_ref, packed_ref)
    attended_ref[at, :] = attended
    if ready is not None:
        ready()
    middle = x + dot(attended, out_ref[...])
    middle_ref[at, :] = middle
    unit, _ = norm_parts(middle)
    normed = (unit * gain_row(small_ref, experts, 2) + gain_row(small_ref, experts, 3)).astype(BF)
    cols = slice(image * PAD, (image + 1) * PAD)
    probs, flags = route(normed, small_ref, noise_ref[:, cols], ids_ref[:, cols], experts)
    return normed, probs, flags


def front_kernel(
    x_ref, small_ref, qkv_ref, out_ref, noise_ref, ids_ref,
    normed_ref, packed_ref, attended_ref, middle_ref, rows_ref, flag_ref, prob_ref,
):
    keep = (normed_ref, packed_ref, attended_ref, middle_ref)
    probs, flags = [], []
    for image in range(x_ref.shape[0] // PAD):
        normed, prob, flag = front_image(
            image, TALL // 2, x_ref, small_ref, qkv_ref, out_ref, noise_ref, ids_ref, keep
        )
        rows_ref[pl.ds(image * PAD, PAD), :] = normed
        probs.append(prob)
        flags.append(flag)
    prob_ref[...] = jnp.concatenate(probs, 1)
    flag_ref[...] = jnp.concatenate(flags, 1).astype(BF)


def front(x, small, qkv, out, noise, ids):
    rows, width = x.shape
    shape = jax.ShapeDtypeStruct
    return pl.pallas_call(
        front_kernel,
        out_shape=(
            shape((rows, width), BF),
            shape((rows, 3 * width), BF),
            shape((rows, width), BF),
            shape((rows, width), F32),
            shape((rows, width), BF),
            shape((TALL, rows), BF),
            shape((TALL, rows), F32),
        ),
        compiler_params=pltpu.CompilerParams(vmem_limit_bytes=BIG),
        cost_estimate=pl.CostEstimate(flops=8 * 10**9, bytes_accessed=10**7, transcendentals=10**6),
        name="front",
    )(x, small, qkv, out, noise, ids)


class Place:
    def __init__(self):
        shard, head, tensor = (lax.axis_index(axis) for axis in AXES)
        self.shard, self.head, self.tensor = shard, head, tensor
        self.pair, self.side = lax.rem(head, 2), lax.div(head, 2)
        self.across = (1 - shard, head, tensor)
        self.beside = (shard, lax.rem(head + 2, 4), tensor)
        self.twin = (shard, head + 1 - 2 * self.pair, tensor)
        self.above = (shard, head, lax.rem(tensor + 1, 4))
        self.below = (shard, head, lax.rem(tensor + 3, 4))

    def greet(self, line=False):
        barrier = pltpu.get_barrier_semaphore()
        devices = [self.across, self.beside, self.twin, self.above, self.below]
        if line:
            devices.append((self.shard, self.head, lax.rem(self.tensor + 2, 4)))
        for device in devices:
            pl.semaphore_signal(barrier, inc=1, device_id=device, device_id_type=MESH)
        pl.semaphore_wait(barrier, len(devices))


class Links:
    def __init__(self, send, recv):
        self.send, self.recv, self.used = send, recv, 0
        self.sent = []

    def copy(self, source, target, device):
        index = self.used
        self.used += 1
        return pltpu.make_async_remote_copy(
            src_ref=source, dst_ref=target, send_sem=self.send.at[index], recv_sem=self.recv.at[index],
            device_id=device, device_id_type=MESH,
        )

    def start(self, source, target, device):
        copy = self.copy(source, target, device)
        copy.start()
        self.sent.append((None, copy))
        return copy

    def skip(self, done):
        self.sent = [(when, copy) for when, copy in self.sent if copy is not done]

    def finish(self):
        for when, copy in self.sent:
            if when is None:
                copy.wait_send()
            else:
                pl.when(when)(copy.wait_send)


class LineGather:
    def __init__(self, links, place, view, own, parts):
        self.links, self.place, self.view, self.own = links, place, view, own
        self.copies = {}
        self.parts = parts

    def start(self, part, step):
        t = self.place.tensor
        for name, slot, device, sends in (
            ("up", t - step, self.place.above, (t >= step) & (t < 3)),
            ("down", t + step, self.place.below, (t + step <= 3) & (t > 0)),
        ):
            slot = jnp.clip(slot, 0, 3)
            source = self.own(part) if step == 0 else self.view(slot, part)
            copy = self.links.copy(source, self.view(slot, part), device)
            pl.when(sends)(copy.start)
            self.links.sent.append((sends, copy))
            self.copies[name, part, step] = copy

    def wait(self, part, step, then=None):
        t = self.place.tensor
        for name, slot, comes in (("up", t - 1 - step, t >= step + 1), ("down", t + 1 + step, t + 1 + step <= 3)):
            copy = self.copies[name, part, step]

            @pl.when(comes)
            def _():
                copy.wait_recv()

    def arrived(self, step):
        t = self.place.tensor
        return (
            (jnp.clip(t - 1 - step, 0, 3), t >= step + 1),
            (jnp.clip(t + 1 + step, 0, 3), t + 1 + step <= 3),
        )


def pad_images(source, target):
    value = source[...].astype(F32)
    empty = jnp.zeros((PAD - SEQ, value.shape[1]), F32)
    for image in range(2):
        part = value[image * SEQ : (image + 1) * SEQ]
        target[pl.ds(image * PAD, PAD), :] = jnp.concatenate((part, empty), 0).astype(BF)


def head_kernel(
    tokens_own, cot_own, small_own, qkv_own, out_own, expert_in, expert_out, noise_ref, ids_ref,
    small_ref, qkv_ref, out_ref, normed_ref, packed_ref, attended_ref, middle_ref, prob_ref,
    x_ref, cot_ref, rows_all, flags_all, cot_all, got_in, got_out,
    sent_rows, sent_flags, send, recv, local_sem,
):
    pad_images(cot_own, cot_ref)
    place = Place()
    links = Links(send, recv)
    width = x_ref.shape[1]
    experts = expert_in.shape[0]
    depth = qkv_own.shape[0]
    quarter = depth // 4
    shard, pair, side, tensor = place.shard, place.pair, place.side, place.tensor
    mine = pair * 4 + tensor
    place.greet()

    def dense_rows(owner, across_side, across_pair, start, size):
        return pl.ds(pl.multiple_of(owner * depth + (across_side * 2 + across_pair) * quarter + start, TALL), size)

    pieces = ((qkv_own, qkv_ref, 0, quarter // 2), (qkv_own, qkv_ref, quarter // 2, quarter // 2), (out_own, out_ref, 0, quarter))
    smalls = links.start(small_own, small_ref.at[shard], place.across)
    cross = []
    for own, full, start, size in pieces:
        source = own.at[pl.ds(pl.multiple_of((side * 2 + pair) * quarter + start, TALL), size), :]
        cross.append(links.start(source, full.at[dense_rows(shard, side, pair, start, size), :], place.across))

    def expert_item(item):
        index = side * 2 + item // 2
        source, target = (expert_in, got_in) if item % 2 == 0 else (expert_out, got_out)
        return source.at[pair * (experts // 2) + index], target.at[index]

    fetched = [links.start(*expert_item(item), place.across) for item in range(4)]
    here = pl.ds(pl.multiple_of(shard * depth, TALL), depth)
    locals_ = [
        pltpu.make_async_copy(qkv_own, qkv_ref.at[here, :], local_sem.at[0]),
        pltpu.make_async_copy(out_own, out_ref.at[here, :], local_sem.at[1]),
        pltpu.make_async_copy(small_own, small_ref.at[shard], local_sem.at[2]),
        pltpu.make_async_copy(cot_ref, cot_all.at[mine], local_sem.at[3]),
    ]
    for copy in locals_:
        copy.start()

    def slots(array):
        def view(slot, part):
            return array.at[pair * 4 + slot, pl.ds(part * PAD, PAD), :]

        return view

    cot_line = LineGather(links, place, slots(cot_all), lambda part: cot_ref.at[pl.ds(part * PAD, PAD), :], 2)
    for part in range(2):
        cot_line.start(part, 0)

    pad_images(tokens_own, x_ref)

    beside, twins = [], []
    for index, (own, full, start, size) in enumerate(pieces):
        cross[index].wait_recv()
        rows = full.at[dense_rows(1 - shard, side, pair, start, size), :]
        beside.append(links.start(rows, rows, place.beside))
        twins.append(links.start(rows, rows, place.twin))
    for part in range(2):
        cot_line.wait(part, 0)
        cot_line.start(part, 1)
    for index, (own, full, start, size) in enumerate(pieces):
        beside[index].wait_recv()
        rows = full.at[dense_rows(1 - shard, 1 - side, pair, start, size), :]
        twins.append(links.start(rows, rows, place.twin))

    for part in range(2):
        cot_line.wait(part, 1)
        cot_line.start(part, 2)
    smalls.wait_recv()
    for index, copy in enumerate(twins):
        if index % len(pieces) < 2:
            copy.wait_recv()
    for copy in locals_:
        copy.wait()

    keep = (normed_ref, packed_ref, attended_ref, middle_ref)
    row_line = LineGather(links, place, slots(rows_all), lambda part: sent_rows.at[pl.ds(part * PAD, PAD), :], 2)
    flag_line = LineGather(links, place, lambda slot, part: flags_all.at[pair * 4 + slot], lambda part: sent_flags, 1)
    probs, flags = [], []

    def out_ready():
        for index, copy in enumerate(twins):
            if index % len(pieces) == 2:
                copy.wait_recv()

    twin_rows = []
    forwarded = []

    def forward_expert(item):
        fetched[item].wait_recv()
        _, target = expert_item(item)
        forwarded.append(links.start(target, target, place.beside))

    for image in range(2):
        normed, prob, flag = front_image(
            image, experts, x_ref, small_ref, qkv_ref, out_ref, noise_ref, ids_ref, keep,
            out_ready if image == 0 else None,
        )
        at = pl.ds(image * PAD, PAD)
        sent_rows[at, :] = normed
        row_line.start(image, 0)
        twin_rows.append(links.start(sent_rows.at[at, :], rows_all.at[mine, at, :], place.twin))
        probs.append(prob)
        flags.append(flag)
        forward_expert(image)
    prob_ref[...] = jnp.concatenate(probs, 1)
    sent_flags[...] = jnp.concatenate(flags, 1).astype(BF)
    flag_line.start(0, 0)
    twin_flags = [links.start(sent_flags, flags_all.at[mine], place.twin)]
    keep_own = [
        pltpu.make_async_copy(sent_rows, rows_all.at[mine], local_sem.at[0]),
        pltpu.make_async_copy(sent_flags, flags_all.at[mine], local_sem.at[1]),
    ]
    for copy in keep_own:
        copy.start()

    def share(line, array, part, step, copies, whole):
        for slot, comes in line.arrived(step):
            index = pair * 4 + slot
            ref = array.at[index] if whole else array.at[index, pl.ds(part * PAD, PAD), :]
            copy = links.copy(ref, ref, place.twin)
            pl.when(comes)(copy.start)
            links.sent.append((comes, copy))
            copies.append((comes, copy))

    twin_steps = []
    for step in range(3):
        for part in range(2):
            row_line.wait(part, step)
            if step < 2:
                row_line.start(part, step + 1)
            share(row_line, rows_all, part, step, twin_steps, False)
        if step < 2:
            forward_expert(step + 2)
        flag_line.wait(0, step)
        if step < 2:
            flag_line.start(0, step + 1)
        share(flag_line, flags_all, 0, step, twin_steps, True)
        if step == 0:
            for part in range(2):
                cot_line.wait(part, 2)
            ours = cot_all.at[pl.ds(pair * 4, 4)]
            twin_cot = links.start(ours, ours, place.twin)

    for copy in twin_rows + twin_flags + [twin_cot] + forwarded:
        copy.wait_recv()
    for comes, copy in twin_steps:
        pl.when(comes)(copy.wait_recv)
    for copy in keep_own:
        copy.wait()
    links.finish()


def head(x, cot, small, qkv, out, expert_in, expert_out, noise, ids):
    rows, width = x.shape[0] // SEQ * PAD, x.shape[1]
    depth = qkv.shape[0]
    count = expert_in.shape[0] // 2
    shape = jax.ShapeDtypeStruct
    anywhere = pl.BlockSpec(memory_space=pl.ANY)
    vmem = pl.BlockSpec(memory_space=pltpu.VMEM)
    return pl.pallas_call(
        head_kernel,
        out_shape=(
            shape((2, TALL, depth), BF),
            shape((width, 3 * width), BF),
            shape((width, width), BF),
            shape((rows, width), BF),
            shape((rows, 3 * width), BF),
            shape((rows, width), BF),
            shape((rows, width), F32),
            shape((TALL, rows), F32),
            shape((rows, width), BF),
            shape((rows, width), BF),
            shape((8, rows, width), BF),
            shape((8, TALL, rows), BF),
            shape((8, rows, width), BF),
            shape((count,) + expert_in.shape[1:], BF),
            shape((count,) + expert_out.shape[1:], BF),
        ),
        in_specs=[vmem] * 3 + [anywhere] * 4 + [vmem] * 2,
        out_specs=(vmem,) * 10 + (anywhere,) * 5,
        scratch_shapes=[
            pltpu.VMEM((rows, width), BF),
            pltpu.VMEM((TALL, rows), BF),
            pltpu.SemaphoreType.DMA((96,)),
            pltpu.SemaphoreType.DMA((96,)),
            pltpu.SemaphoreType.DMA((4,)),
        ],
        compiler_params=pltpu.CompilerParams(vmem_limit_bytes=BIG, collective_id=1, has_side_effects=True),
        cost_estimate=pl.CostEstimate(flops=8 * 10**9, bytes_accessed=3 * 10**7, transcendentals=10**6),
        name="head",
    )(x, cot, small, qkv, out, expert_in, expert_out, noise, ids)


def expert_kernel(
    place_ref, flag_ref, rows_all, cot_all, own_in, got_in, own_out, got_out,
    total_all, back_all, gate_ref, grad_in, grad_out,
    inner, outer, picked, grads, gate, active, hidden_grad, made, made_back, made_gate, ranks,
    rows_buf, cot_buf, total_buf, back_buf, stage_in, stage_out, load_sem, store_sem, fetch_sem, put_sem, old_sem,
):
    blocks, length, width = cot_all.shape
    count = got_in.shape[0]
    depth = got_in.shape[1]
    pair, shard = place_ref[0], place_ref[1]
    experts = 2 * count

    def loads(expert, slot):
        mine = pl.ds(pl.multiple_of(shard * depth, LANES), depth)
        other = pl.ds(pl.multiple_of((1 - shard) * depth, LANES), depth)
        index = pair * count + expert
        return (
            pltpu.make_async_copy(own_in.at[index], inner.at[slot, mine, :], load_sem.at[slot, 0]),
            pltpu.make_async_copy(got_in.at[expert], inner.at[slot, other, :], load_sem.at[slot, 1]),
            pltpu.make_async_copy(own_out.at[index], outer.at[slot, :, mine], load_sem.at[slot, 2]),
            pltpu.make_async_copy(got_out.at[expert], outer.at[slot, :, other], load_sem.at[slot, 3]),
        )

    def stores(expert, slot):
        return (
            pltpu.make_async_copy(stage_in.at[slot], grad_in.at[expert], store_sem.at[slot, 0]),
            pltpu.make_async_copy(stage_out.at[slot], grad_out.at[expert], store_sem.at[slot, 1]),
        )

    def fetches(block, slot):
        return (
            pltpu.make_async_copy(rows_all.at[block], rows_buf.at[slot], fetch_sem.at[slot, 0]),
            pltpu.make_async_copy(cot_all.at[block], cot_buf.at[slot], fetch_sem.at[slot, 1]),
        )

    def puts(block, slot):
        return (
            pltpu.make_async_copy(total_buf.at[slot], total_all.at[block], put_sem.at[slot, 0]),
            pltpu.make_async_copy(back_buf.at[slot], back_all.at[block], put_sem.at[slot, 1]),
        )

    def start(copies):
        for copy in copies:
            copy.start()

    def wait(copies):
        for copy in copies:
            copy.wait()

    def reload(pairs):
        copies = [pltpu.make_async_copy(source, target, old_sem.at[n]) for n, (source, target) in enumerate(pairs)]
        start(copies)
        wait(copies)

    start(fetches(0, 0) + fetches(1, 1) + loads(0, 0))
    ahead = lax.broadcasted_iota(jnp.int32, (length, length), 0)
    behind = lax.broadcasted_iota(jnp.int32, (length, length), 1)
    order = jnp.where(behind < ahead, 1.0, jnp.where(behind == ahead, FAR, 0.0)).astype(BF)
    for block in range(blocks):
        ranks[block] = contract_cols(flag_ref[block], order) - FAR

    def line(expert):
        return pl.ds(experts + pair * count + expert, 1)

    def passes_of(expert):
        highest = ranks[0, line(expert), :]
        for block in range(1, blocks):
            highest = jnp.maximum(highest, ranks[block, line(expert), :])
        return (jnp.maximum(jnp.max(highest), -1.0).astype(jnp.int32) + TILE) // TILE

    highest = ranks[0, line(0), :]
    for block in range(blocks):
        for expert in range(count):
            highest = jnp.maximum(highest, ranks[block, line(expert), :])
    rounds = (jnp.maximum(jnp.max(highest), 0.0).astype(jnp.int32) + TILE) // TILE

    def take(block, slot, step):
        at = pl.ds(pl.multiple_of(block * TILE, TILE), TILE)
        choose = choices(block, step)
        columns = jnp.where(lane == wanted, contract_cols(choose, flag_ref[block]), 0.0)
        column = jnp.broadcast_to(jnp.sum(columns, -1, keepdims=True), (count * TILE, LANES))
        wait(fetches(block, slot))
        both = dot(choose, rows_buf[slot]).astype(BF)
        other = dot(choose, cot_buf[slot]).astype(BF)
        for expert in range(count):
            part = slice(expert * TILE, (expert + 1) * TILE)
            picked[expert, at, :] = both[part]
            grads[expert, at, :] = other[part]
            gate[expert, at, :] = column[part]

    def compute(expert, slot):
        def chunk(index, carry):
            at = pl.ds(pl.multiple_of(index * CHUNK, CHUNK), CHUNK)
            value = dot(picked[expert, at, :], inner[slot])
            grad_active = contract_cols(grads[expert, at, :], outer[slot])
            gate_column = gate[expert, at, 0:1]
            square = value * value
            bent = jnp.tanh(ROOT * value * (1.0 + CUBIC * square))
            plus = 0.5 * (1.0 + bent)
            bowed = value * plus
            slope = plus + (0.5 * ROOT) * value * (1.0 - bent * bent) * (1.0 + (3.0 * CUBIC) * square)
            active[at, :] = (bowed * gate_column).astype(BF)
            back = (grad_active * gate_column * slope).astype(BF)
            hidden_grad[at, :] = back
            lane = lax.broadcasted_iota(jnp.int32, (CHUNK, TALL), 1)
            gate_grad = jnp.sum(grad_active * bowed, -1, keepdims=True)
            made_gate[expert, at, :] = jnp.where(lane == pair * count + expert, gate_grad, 0.0).astype(BF)
            made[expert, at, :] = dot(active[at, :], outer[slot]).astype(BF)
            made_back[expert, at, :] = contract_cols(back, inner[slot]).astype(BF)
            return carry

        lax.fori_loop(0, blocks * TILE // CHUNK, chunk, 0)

    def weigh(expert, slot, again):
        for stage, grad, left, right in (
            (stage_out, grad_out, active, grads.at[expert]), (stage_in, grad_in, picked.at[expert], hidden_grad),
        ):
            if again:
                reload([(grad.at[expert], stage.at[slot])])
            for begin in range(0, left.shape[1], CHUNK):
                at = pl.ds(begin, CHUNK)
                value = contract_rows(left[:, at], right[...])
                if again:
                    value = value + stage[slot, at, :].astype(F32)
                stage[slot, at, :] = value.astype(BF)

    def give(block, slot, step, again):
        at = pl.ds(pl.multiple_of(block * TILE, TILE), TILE)
        choose = choices(block, step)

        def joined(source):
            return jnp.concatenate([source[expert, at, :] for expert in range(count)], 0)

        if again:
            reload([(total_all.at[block], rows_buf.at[0]), (back_all.at[block], rows_buf.at[1])])
        for target, source, old in ((total_buf, made, 0), (back_buf, made_back, 1)):
            value = contract_rows(choose, joined(source))
            if again:
                value = value + rows_buf[old].astype(F32)
            target[slot] = value.astype(BF)
        start(puts(block, slot))
        gates = contract_rows(joined(made_gate), choose)
        if again:
            gates = gates + gate_ref[block].astype(F32)
        gate_ref[block] = gates.astype(BF)

    def choices(block, step):
        slots = lax.broadcasted_iota(jnp.int32, (TILE, length), 0).astype(F32) + (step * TILE).astype(F32)
        return jnp.concatenate([(ranks[block, line(expert), :] == slots).astype(BF) for expert in range(count)], 0)

    lane = lax.broadcasted_iota(jnp.int32, (count * TILE, TALL), 1)
    wanted = lax.broadcasted_iota(jnp.int32, (count * TILE, TALL), 0) // TILE + pair * count
    first = jnp.int32(0)
    for block in range(blocks):
        take(block, block % 2, first)
        if block + 2 < blocks:
            start(fetches(block + 2, block % 2))
    for expert in range(count):
        slot = expert % 2
        if expert + 1 < count:
            start(loads(expert + 1, 1 - slot))
        wait(loads(expert, slot))
        compute(expert, slot)
        if expert >= 2:
            wait(stores(expert - 2, slot))
        weigh(expert, slot, False)
        start(stores(expert, slot))
    for block in range(blocks):
        if block >= 2:
            wait(puts(block - 2, block % 2))
        give(block, block % 2, first, False)
    for block in range(blocks - 2, blocks):
        wait(puts(block, block % 2))
    for expert in range(count - 2, count):
        wait(stores(expert, expert % 2))

    def more(step, carry):
        def take_one(block, carry):
            start(fetches(block, 0))
            take(block, 0, step)
            return carry

        def expert_one(expert, carry):
            @pl.when(passes_of(expert) > step)
            def _():
                start(loads(expert, 0))
                wait(loads(expert, 0))
                compute(expert, 0)
                weigh(expert, 0, True)
                start(stores(expert, 0))
                wait(stores(expert, 0))

            return carry

        def give_one(block, carry):
            give(block, 0, step, True)
            wait(puts(block, 0))
            return carry

        lax.fori_loop(0, blocks, take_one, 0)
        lax.fori_loop(0, count, expert_one, 0)
        lax.fori_loop(0, blocks, give_one, 0)
        return carry

    lax.fori_loop(1, rounds, more, 0)


def expert_pass(place, rows, flags, cot, own_in, got_in, own_out, got_out):
    blocks, length, width = cot.shape
    count, _, hidden = got_in.shape
    capacity = blocks * TILE
    shape = jax.ShapeDtypeStruct
    anywhere = pl.BlockSpec(memory_space=pl.ANY)
    vmem = pl.BlockSpec(memory_space=pltpu.VMEM)
    return pl.pallas_call(
        expert_kernel,
        out_shape=(
            shape((blocks, length, width), BF),
            shape((blocks, length, width), BF),
            shape((blocks, TALL, length), BF),
            shape((count, width, hidden), BF),
            shape((count, hidden, width), BF),
        ),
        in_specs=[pl.BlockSpec(memory_space=pltpu.SMEM), vmem] + [anywhere] * 6,
        out_specs=(anywhere, anywhere, vmem, anywhere, anywhere),
        scratch_shapes=[
            pltpu.VMEM((2, width, hidden), BF),
            pltpu.VMEM((2, hidden, width), BF),
            pltpu.VMEM((count, capacity, width), BF),
            pltpu.VMEM((count, capacity, width), BF),
            pltpu.VMEM((count, capacity, LANES), F32),
            pltpu.VMEM((capacity, hidden), BF),
            pltpu.VMEM((capacity, hidden), BF),
            pltpu.VMEM((count, capacity, width), BF),
            pltpu.VMEM((count, capacity, width), BF),
            pltpu.VMEM((count, capacity, TALL), BF),
            pltpu.VMEM((blocks, TALL, length), F32),
            pltpu.VMEM((2, length, width), BF),
            pltpu.VMEM((2, length, width), BF),
            pltpu.VMEM((2, length, width), BF),
            pltpu.VMEM((2, length, width), BF),
            pltpu.VMEM((2, width, hidden), BF),
            pltpu.VMEM((2, hidden, width), BF),
            pltpu.SemaphoreType.DMA((2, 4)),
            pltpu.SemaphoreType.DMA((2, 2)),
            pltpu.SemaphoreType.DMA((2, 2)),
            pltpu.SemaphoreType.DMA((2, 2)),
            pltpu.SemaphoreType.DMA((2,)),
        ],
        compiler_params=pltpu.CompilerParams(vmem_limit_bytes=BIG),
        cost_estimate=pl.CostEstimate(flops=50 * 10**9, bytes_accessed=5 * 10**7, transcendentals=10**6),
        name="experts",
    )(place, flags, rows, cot, own_in, got_in, own_out, got_out)


def back_middle(at, moe, gates, cot, middle, rows, probs, flags, small_ref, sums):
    experts = TALL // 2
    row = lax.broadcasted_iota(jnp.int32, flags.shape, 0)
    chosen = jnp.where(row < experts, pltpu.roll(flags, experts, 0), 0.0)
    asked = gates * chosen
    grad_logits = probs * (asked - jnp.sum(probs * asked, 0, keepdims=True))
    coarse = grad_logits.astype(BF)
    fine = (grad_logits - coarse.astype(F32)).astype(BF)
    router = router_rows(small_ref)
    sums[4] = sums[4] + dot(coarse, rows) + dot(fine, rows)
    grad = moe + contract_rows(coarse, router) + contract_rows(fine, router)
    unit, inverse = norm_parts(middle)
    sums[2] = sums[2] + jnp.sum(grad * unit, 0, keepdims=True)
    sums[3] = sums[3] + jnp.sum(grad, 0, keepdims=True)
    return cot + norm_back(grad, unit, inverse, gain_row(small_ref, experts, 2))


def back_probs(at, double, packed_ref, take):
    group = 3 * HEAD_DIM
    scale = HEAD_DIM ** (-0.5)
    lanes = lax.broadcasted_iota(jnp.int32, (PAD, group), 1) // HEAD_DIM
    packed = packed_ref[at, pl.ds(double * 6 * group, 6 * group)]
    for side in range(2):
        query, keys = (packed[:, (3 * side + k) * group : (3 * side + k + 1) * group] for k in range(2))
        for head in range(3):
            masked = jnp.where(lanes == head, query, jnp.zeros_like(query))
            take(side * 3 + head, head_probs(masked, keys, scale))


def back_heads(at, double, grad_proj, packed_ref, out_ref, stacked, give):
    width = grad_proj.shape[1]
    group = 3 * HEAD_DIM
    scale = HEAD_DIM ** (-0.5)
    lanes = lax.broadcasted_iota(jnp.int32, (PAD, group), 1) // HEAD_DIM
    made = []
    packed = packed_ref[at, pl.ds(double * 6 * group, 6 * group)]
    for side in range(2):
        query, keys, values = (packed[:, (3 * side + k) * group : (3 * side + k + 1) * group] for k in range(3))
        index = double * 2 + side
        grad_att = contract_cols(grad_proj, out_ref[pl.ds(index * group, group), :]).astype(BF)
        outs = [jnp.zeros((PAD, group), F32) for _ in range(3)]
        for head in range(3):
            mask = lanes == head
            low = give(side * 3 + head)
            probs = low.astype(F32)
            part = jnp.where(mask, grad_att, jnp.zeros_like(grad_att))
            grad_weights = contract_cols(part, values)
            inner_sum = jnp.sum(probs * grad_weights, -1, keepdims=True)
            grad_scores = (probs * (grad_weights - inner_sum)).astype(BF)
            outs[0] = jnp.where(mask, dot(grad_scores, keys), outs[0])
            outs[1] = jnp.where(mask, contract_rows(grad_scores, query), outs[1])
            outs[2] = jnp.where(mask, contract_rows(low, grad_att), outs[2])
        made += [outs[0] * scale, outs[1] * scale, outs[2]]
    stacked[at, pl.ds(double * 6 * group, 6 * group)] = jnp.concatenate(made, 1).astype(BF)


def back_kernel(
    moe_ref, gate_ref, cot_ref, x_ref, middle_ref, rows_ref, flag_ref, prob_ref, attended_ref, packed_ref, normed_ref,
    small_ref, qkv_ref, out_ref,
    tokens_ref, grad_qkv, grad_out, grad_small,
    stacked, projected,
):
    rows, width = x_ref.shape
    experts = TALL // 2
    sums = [jnp.zeros((1, width), F32) for _ in range(4)] + [jnp.zeros((TALL, width), F32)]
    for image in range(rows // PAD):
        at = pl.ds(image * PAD, PAD)
        cols = slice(image * PAD, (image + 1) * PAD)
        grad_middle = back_middle(
            at, moe_ref[at, :].astype(F32), gate_ref[:, cols].astype(F32), cot_ref[at, :].astype(F32),
            middle_ref[at, :], rows_ref[at, :], prob_ref[:, cols], flag_ref[:, cols].astype(F32), small_ref, sums,
        )
        grad_proj = grad_middle.astype(BF)
        projected[at, :] = grad_proj
        for double in range(width // (6 * HEAD_DIM)):
            saved = {}
            back_probs(at, double, packed_ref, lambda index, value: saved.update({index: value.astype(BF)}))
            back_heads(at, double, grad_proj, packed_ref, out_ref, stacked, saved.get)
        grad = contract_cols(stacked[at, :], qkv_ref[...])
        unit, inverse = norm_parts(x_ref[at, :].astype(F32))
        sums[0] = sums[0] + jnp.sum(grad * unit, 0, keepdims=True)
        sums[1] = sums[1] + jnp.sum(grad, 0, keepdims=True)
        tokens_ref[at, :] = (grad_middle + norm_back(grad, unit, inverse, gain_row(small_ref, experts, 0))).astype(BF)
    grad_small[...] = jnp.concatenate([sums[4][0:experts]] + sums[:4] + [jnp.zeros((4, width), F32)], 0).astype(BF)
    grad_out[...] = contract_rows(attended_ref[...], projected[...]).astype(BF)
    for third in range(3):
        cols = pl.ds(third * width, width)
        grad_qkv[:, cols] = contract_rows(normed_ref[...], stacked[:, cols]).astype(BF)


def back(moe, gates, cot, x, middle, sent, flags, prob, attended, packed, normed, small, qkv, out):
    rows, width = x.shape
    shape = jax.ShapeDtypeStruct
    return pl.pallas_call(
        back_kernel,
        out_shape=(
            shape((rows, width), BF),
            shape((width, 3 * width), BF),
            shape((width, width), BF),
            shape((TALL, width), BF),
        ),
        scratch_shapes=[pltpu.VMEM((rows, 3 * width), BF), pltpu.VMEM((rows, width), BF)],
        compiler_params=pltpu.CompilerParams(vmem_limit_bytes=BIG),
        cost_estimate=pl.CostEstimate(flops=16 * 10**9, bytes_accessed=2 * 10**7, transcendentals=10**6),
        name="back",
    )(moe, gates, cot, x, middle, sent, flags, prob, attended, packed, normed, small, qkv, out)


ORDER = [[('x', 0), ('n', 3)], [('a', 0), ('x', 1), ('n', 4)], [], [('b', 0), ('n', 5), ('x', 2), ('y', 0), ('y', 1)], [('n', 6), ('a', 1)], [('x', 3), ('c', 0)], [('da', 1), ('x', 4)], [('x', 5), ('da', 0), ('n', 7), ('dl', 1), ('y', 2), ('x', 6)], [('dl', 0)], [('da', 3), ('db', 1), ('x', 7), ('n', 8), ('db', 0), ('n', 9), ('da', 2), ('dl', 3), ('y', 3), ('n', 10), ('b', 1), ('ds', 1), ('ds', 0), ('x', 8)], [('y', 4), ('c', 1), ('y', 5), ('x', 9), ('dl', 2), ('s', 0), ('db', 3), ('n', 11), ('y', 6), ('d1', 0), ('y', 7), ('ds', 3), ('s', 1), ('db', 2), ('x', 10), ('y', 8)], [('d2', 0), ('ds', 2), ('d1', 1), ('x', 11), ('dt', 3), ('s', 2), ('d1', 2), ('d2', 1), ('y', 9), ('dt', 0), ('y', 10), ('d2', 2), ('y', 11), ('s', 3), ('dt', 1), ('dt', 2)]]


class LineScatter:
    def __init__(self, links, place, sums, up, down):
        self.links, self.place = links, place
        self.sums, self.up, self.down = sums, up, down
        self.copies = {}

    def ways(self, step):
        t = self.place.tensor
        return (
            ("up", self.up, t + 3 - step, t <= step, t >= 1, self.place.above),
            ("down", self.down, t - 3 + step, t >= 3 - step, t <= 2, self.place.below),
        )

    def send(self, part, step):
        for name, got, slot, sends, comes, device in self.ways(step):
            slot = jnp.clip(slot, 0, 3)
            if step > 0:
                before = self.copies[name, part, step - 1]

                @pl.when(sends & comes)
                def _():
                    before.wait_recv()
                    ref = self.sums(slot, part)
                    ref[...] = (ref[...].astype(F32) + got(step - 1, part)[...].astype(F32)).astype(BF)

            copy = self.links.copy(self.sums(slot, part), got(step, part), device)
            pl.when(sends)(copy.start)
            self.links.sent.append((sends, copy))
            self.copies[name, part, step] = copy

    def finish(self, part, total):
        total[...] = self.sums(self.place.tensor, part)[...].astype(F32)
        for name, got, slot, sends, comes, device in self.ways(2):
            copy = self.copies[name, part, 2]

            @pl.when(comes)
            def _():
                copy.wait_recv()
                total[...] += got(2, part)[...].astype(F32)


def tail_kernel(
    back_all, gate_all, total_all, grads_in, grads_out, rows_all, flags_all,
    cot_ref, x_ref, middle_ref, prob_ref, attended_ref, packed_ref, normed_ref, small_ref, qkv_ref, out_ref,
    mixed_ref, tokens_ref, dense_ref, grad_small, final_in, final_out, beside_in, beside_out,
    back_sum, back_got, back_up, back_down, gate_sum, gate_got, gate_up, gate_down,
    total_sum, total_got, total_up, total_down, moe, gates, rows_ref, flag_ref, projected, stacked, weights_ref,
    chunks, core_got, across_sent, across_got, line_sum, line_got, side_sum, side_got, line_final,
    own_in, own_out, across_in, across_out, read_in, read_out, half_in, half_out, mine_in, mine_out, both_in, both_out,
    small_sent, small_core, small_half, small_across, small_side, small_beside, small_line_sent, small_line,
    send, recv, local_sem,
):
    place = Place()
    links = Links(send, recv)
    rows, width = x_ref.shape
    experts = TALL // 2
    count = grads_in.shape[0]
    depth = width // 2
    shard, pair, side, tensor = place.shard, place.pair, place.side, place.tensor
    mine = pair * 4 + tensor
    place.greet(True)
    ours, theirs = pl.ds(pair * 4, 4), pl.ds((1 - pair) * 4, 4)

    locals_ = [
        pltpu.make_async_copy(back_all.at[ours], back_sum, local_sem.at[0]),
        pltpu.make_async_copy(gate_all.at[ours], gate_sum, local_sem.at[1]),
        pltpu.make_async_copy(total_all.at[ours], total_sum, local_sem.at[2]),
        pltpu.make_async_copy(rows_all.at[mine], rows_ref, local_sem.at[3]),
        pltpu.make_async_copy(flags_all.at[mine], flag_ref, local_sem.at[4]),
    ]
    for copy in locals_:
        copy.start()
    from_twin = [links.start(gate_all.at[theirs], gate_got, place.twin)]
    for part in range(2):
        at = pl.ds(part * PAD, PAD)
        from_twin.append(links.start(back_all.at[theirs, at, :], back_got.at[:, at, :], place.twin))
    from_twin.append(links.start(total_all.at[theirs], total_got, place.twin))

    here = pl.ds(pl.multiple_of(shard * depth, LANES), depth)
    there = pl.ds(pl.multiple_of((1 - shard) * depth, LANES), depth)
    hidden = grads_in.shape[2]
    tall, wide = depth // 2, hidden // 2
    pieces = []
    for expert in range(1, count):
        for half in range(2):
            at = pl.ds(half * tall, tall)
            pieces.append((
                grads_in.at[expert, pl.ds(pl.multiple_of((1 - shard) * depth + half * tall, TALL), tall), :],
                grads_in.at[expert, pl.ds(pl.multiple_of(shard * depth + half * tall, TALL), tall), :],
                across_in.at[expert - 1, at, :], beside_in.at[expert - 1, at, :],
                final_in.at[pair * count + expert, at, :], own_in.at[at, :], read_in.at[at, :],
            ))
        for half in range(2):
            at = pl.ds(half * wide, wide)
            pieces.append((
                grads_out.at[expert, at, there], grads_out.at[expert, at, here],
                across_out.at[expert - 1, at, :], beside_out.at[expert - 1, at, :],
                final_out.at[pair * count + expert, at, :], own_out.at[at, :], read_out.at[at, :],
            ))
    loads = [pltpu.make_async_copy(piece[1], piece[5], local_sem.at[8 + m]) for m, piece in enumerate(pieces)]
    at_across, at_beside, at_twin, kept = {}, {}, [], []
    started = [0]

    def add(target, source):
        target[...] = (target[...].astype(F32) + source[...].astype(F32)).astype(BF)

    def keep(source, target):
        copy = pltpu.make_async_copy(source, target, local_sem.at[32 + len(kept)])
        copy.start()
        kept.append(copy)

    def send_across():
        m = started[0]
        if m < len(pieces):
            at_across[m] = links.start(pieces[m][0], pieces[m][2], place.across)
            started[0] += 1

    def take_across(m):
        at_across[m].wait_recv()
        loads[m].wait()
        add(pieces[m][2], pieces[m][5])
        at_beside[m] = links.start(pieces[m][2], pieces[m][3], place.beside)
        if m + 4 < len(pieces):
            loads[m + 4].start()

    def take_beside(m):
        at_beside[m].wait_recv()
        load = pltpu.make_async_copy(pieces[m][3], pieces[m][6], local_sem.at[5])
        load.start()
        at_beside[m].wait_send()
        links.skip(at_beside[m])
        load.wait()
        add(pieces[m][2], pieces[m][6])
        at_twin.append(links.start(pieces[m][2], pieces[m][4], place.twin))
        keep(pieces[m][2], pieces[m][4])

    our_half = pl.ds(pl.multiple_of(side * wide, LANES), wide)
    other_half = pl.ds(pl.multiple_of((1 - side) * wide, LANES), wide)
    first = (
        (grads_in.at[0, :, other_half], grads_in.at[0, :, our_half], half_in, mine_in,
         half_in.at[there, :], half_in.at[here, :], both_in,
         final_in.at[pair * count, :, our_half], final_in.at[pair * count, :, other_half]),
        (grads_out.at[0, other_half, :], grads_out.at[0, our_half, :], half_out, mine_out,
         half_out.at[:, there], half_out.at[:, here], both_out,
         final_out.at[pair * count, our_half, :], final_out.at[pair * count, other_half, :]),
    )
    first_loads = [pltpu.make_async_copy(item[1], item[3], local_sem.at[6 + q]) for q, item in enumerate(first)]
    first_beside, first_across, first_back = {}, {}, {}

    def first_send(q):
        first_loads[q].start()
        first_beside[q] = links.start(first[q][0], first[q][2], place.beside)

    def first_sum(q):
        first_beside[q].wait_recv()
        first_loads[q].wait()
        add(first[q][2], first[q][3])
        first_across[q] = links.start(first[q][4], first[q][6], place.across)

    def first_total(q):
        first_across[q].wait_recv()
        add(first[q][6], first[q][5])
        first_back[q] = links.start(first[q][6], first[q][7], place.beside)
        at_twin.append(links.start(first[q][6], first[q][7], place.twin))
        keep(first[q][6], first[q][7])

    def first_share(q):
        first_back[q].wait_recv()
        at_twin.append(links.start(first[q][8], first[q][8], place.twin))

    share = depth // 2
    piece = share // 4
    stage = {}

    def dense_core(k):
        stage["core", k] = []
        for owner in range(2):
            source = chunks.at[k, pl.ds(pl.multiple_of(owner * depth + (1 - pair) * share, TALL), share), :]
            stage["core", k].append(links.start(source, core_got.at[k, owner], place.twin))

    def core_sum(k, owner):
        at = pl.ds(pl.multiple_of(owner * depth + pair * share, TALL), share)
        return chunks[k, at, :].astype(F32) + core_got[k, owner].astype(F32)

    def dense_across(k):
        for copy in stage["core", k]:
            copy.wait_recv()
        across_sent[k] = core_sum(k, 1 - shard).astype(BF)
        stage["across", k] = links.start(across_sent.at[k], across_got.at[k], place.across)

    def around(offset):
        return (shard, place.head, lax.rem(tensor + offset, 4))

    def dense_line(k):
        stage["across", k].wait_recv()
        line_sum[k] = (core_sum(k, shard) + across_got[k].astype(F32)).astype(BF)
        stage["line", k] = []
        for offset in (2, 1, 3):
            at = pl.ds(pl.multiple_of(lax.rem(tensor + offset, 4) * piece, TALL), piece)
            stage["line", k].append(links.start(line_sum.at[k, at, :], line_got.at[k, offset - 1], around(offset)))

    def dense_beside(k):
        for copy in stage["line", k]:
            copy.wait_recv()
        at = pl.ds(pl.multiple_of(tensor * piece, TALL), piece)
        value = line_sum[k, at, :].astype(F32)
        for offset in range(3):
            value = value + line_got[k, offset].astype(F32)
        side_sum[k] = value.astype(BF)
        stage["beside", k] = links.start(side_sum.at[k], side_got.at[k], place.beside)

    def dense_spread(k):
        stage["beside", k].wait_recv()
        line_final[k] = (side_sum[k].astype(F32) + side_got[k].astype(F32)).astype(BF)
        target = dense_ref.at[
            pl.ds(pl.multiple_of(pair * share + tensor * piece, TALL), piece), pl.ds(k * width, width)
        ]
        stage["keep", k] = pltpu.make_async_copy(line_final.at[k], target, local_sem.at[24 + k])
        stage["keep", k].start()
        if k < 3:
            dense_line_back.start(k, 0)
        else:
            stage["spread", k] = [links.start(line_final.at[k], target, around(offset)) for offset in (2, 1, 3)]

    def dense_hop(k, step):
        dense_line_back.wait(k, step)
        dense_line_back.start(k, step + 1)

    dense_line_back = LineGather(
        links, place,
        lambda slot, k: dense_ref.at[
            pl.ds(pl.multiple_of(pair * share + slot * piece, TALL), piece), pl.ds(k * width, width)
        ],
        lambda k: line_final.at[k], 3,
    )

    def dense_twin(k):
        if k < 3:
            dense_line_back.wait(k, 2)
        else:
            for copy in stage["spread", k]:
                copy.wait_recv()
        stage["keep", k].wait()
        block = dense_ref.at[pl.ds(pl.multiple_of(pair * share, TALL), share), pl.ds(k * width, width)]
        stage["twin", k] = links.start(block, block, place.twin)

    def small_core_stage():
        small_core_copy.wait_recv()
        other = pl.ds(pl.multiple_of((1 - shard) * depth, LANES), depth)
        small_half[...] = small_sent[:, other] + small_core[:, other]
        stage["small", 1] = links.start(small_half, small_across, place.across)

    def small_across_stage():
        stage["small", 1].wait_recv()
        own = pl.ds(pl.multiple_of(shard * depth, LANES), depth)
        small_side[...] = small_sent[:, own] + small_core[:, own] + small_across[...]
        stage["small", 2] = links.start(small_side, small_beside, place.beside)

    def small_beside_stage():
        stage["small", 2].wait_recv()
        small_line_sent[...] = small_side[...] + small_beside[...]
        stage["small", 3] = [
            links.start(small_line_sent, small_line.at[offset - 1], around(offset)) for offset in (2, 1, 3)
        ]

    def small_line_stage():
        for copy in stage["small", 3]:
            copy.wait_recv()
        grad_small[...] = small_line_sent[...] + small_line[0] + small_line[1] + small_line[2]

    def slots(array):
        def view(slot, part):
            return array.at[slot, pl.ds(part * PAD, PAD), :]

        return view

    back_line = LineScatter(links, place, slots(back_sum), slots(back_up), slots(back_down))
    total_line = LineScatter(links, place, slots(total_sum), slots(total_up), slots(total_down))
    gate_line = LineScatter(
        links, place, lambda slot, part: gate_sum.at[slot], lambda step, part: gate_up.at[step],
        lambda step, part: gate_down.at[step],
    )

    steps = {
        "d1": lambda index: dense_hop(index, 0), "d2": lambda index: dense_hop(index, 1),
        "n": lambda index: send_across(), "x": take_across, "y": take_beside, "a": first_sum, "b": first_total, "c": first_share,
        "da": dense_across, "dl": dense_line, "db": dense_beside, "ds": dense_spread, "dt": dense_twin,
        "s": lambda index: (small_core_stage, small_across_stage, small_beside_stage, small_line_stage)[index](),
    }

    def go(slot):
        for name, index in ORDER[slot]:
            steps[name](index)

    def save_probs(double, image):
        at = pl.ds(image * PAD, PAD)

        def take(index, value):
            weights_ref[(image * 2 + double) * 6 + index] = value.astype(BF)

        back_probs(at, double, packed_ref, take)

    def use_heads(double, image):
        at = pl.ds(image * PAD, PAD)
        back_heads(
            at, double, projected[at, :], packed_ref, out_ref, stacked,
            lambda index: weights_ref[(image * 2 + double) * 6 + index],
        )

    def middle_of(image):
        at = pl.ds(image * PAD, PAD)
        cols = slice(image * PAD, (image + 1) * PAD)
        back_line.finish(image, moe.at[at, :])
        grad = back_middle(
            at, moe[at, :], gates[:, cols], cot_ref[at, :].astype(F32), middle_ref[at, :], rows_ref[at, :],
            prob_ref[:, cols], flag_ref[:, cols].astype(F32), small_ref, sums,
        )
        moe[at, :] = grad
        projected[at, :] = grad.astype(BF)

    first_send(0)
    for _ in range(3):
        send_across()
    first_send(1)
    for m in range(4):
        loads[m].start()
    locals_[1].wait()
    from_twin[0].wait_recv()
    add(gate_sum, gate_got)
    gate_line.send(0, 0)
    locals_[0].wait()
    for part in range(2):
        from_twin[1 + part].wait_recv()
        at = pl.ds(part * PAD, PAD)
        for slot in range(4):
            add(back_sum.at[slot, at, :], back_got.at[slot, at, :])
        back_line.send(part, 0)
    locals_[2].wait()
    from_twin[3].wait_recv()
    for slot in range(4):
        add(total_sum.at[slot], total_got.at[slot])
    save_probs(0, 0)
    go(0)
    gate_line.send(0, 1)
    back_line.send(0, 1)
    save_probs(0, 1)
    back_line.send(1, 1)
    go(1)
    save_probs(1, 0)
    gate_line.send(0, 2)
    back_line.send(0, 2)
    go(2)
    back_line.send(1, 2)
    save_probs(1, 1)
    go(3)
    for part in range(2):
        total_line.send(part, 0)
    gate_line.finish(0, gates)
    locals_[3].wait()
    locals_[4].wait()
    sums = [jnp.zeros((1, width), F32) for _ in range(4)] + [jnp.zeros((TALL, width), F32)]
    middle_of(0)
    use_heads(0, 0)
    go(4)
    middle_of(1)
    chunks[0] = contract_rows(attended_ref[...], projected[...]).astype(BF)
    dense_core(0)
    go(5)
    use_heads(0, 1)
    chunks[1] = contract_rows(normed_ref[...], stacked[:, pl.ds(0, width)]).astype(BF)
    dense_core(1)
    go(6)
    for part in range(2):
        total_line.send(part, 1)
    use_heads(1, 0)
    go(7)
    use_heads(1, 1)
    for k in (2, 3):
        chunks[k] = contract_rows(normed_ref[...], stacked[:, pl.ds((k - 1) * width, width)]).astype(BF)
        dense_core(k)
    go(8)
    for part in range(2):
        total_line.send(part, 2)
    go(9)
    joined = []
    for image in range(2):
        at = pl.ds(image * PAD, PAD)
        grad = contract_cols(stacked[at, :], qkv_ref[...])
        unit, inverse = norm_parts(x_ref[at, :].astype(F32))
        sums[0] = sums[0] + jnp.sum(grad * unit, 0, keepdims=True)
        sums[1] = sums[1] + jnp.sum(grad, 0, keepdims=True)
        grad = moe[at, :] + norm_back(grad, unit, inverse, gain_row(small_ref, experts, 0))
        joined.append(grad[:SEQ])
    tokens_ref[...] = jnp.concatenate(joined, 0).astype(BF)
    small_sent[...] = jnp.concatenate([sums[4][0:experts]] + sums[:4] + [jnp.zeros((4, width), F32)], 0)
    small_core_copy = links.start(small_sent, small_core, place.twin)
    go(10)
    joined = []
    for part in range(2):
        at = pl.ds(part * PAD, PAD)
        total_line.finish(part, moe.at[at, :])
        joined.append((middle_ref[at, :] + moe[at, :])[:SEQ])
    mixed_ref[...] = jnp.concatenate(joined, 0).astype(BF)
    go(11)
    for copy in at_twin + [stage["twin", k] for k in range(4)]:
        copy.wait_recv()
    for copy in kept:
        copy.wait()
    links.finish()


def tail(back_all, gate_all, total_all, grads_in, grads_out, rows_all, flags_all, cot, x, middle, prob, attended, packed, normed, small, qkv, out):
    rows, width = x.shape
    count, _, hidden = grads_in.shape
    depth = width // 2
    shape = jax.ShapeDtypeStruct
    anywhere = pl.BlockSpec(memory_space=pl.ANY)
    vmem = pl.BlockSpec(memory_space=pltpu.VMEM)
    share, piece = depth // 2, depth // 8

    def scatter_buffers(tall, wide):
        return [pltpu.VMEM((4, tall, wide), BF)] * 2 + [pltpu.VMEM((3, tall, wide), BF)] * 2

    return pl.pallas_call(
        tail_kernel,
        out_shape=(
            shape((rows // PAD * SEQ, width), BF),
            shape((rows // PAD * SEQ, width), BF),
            shape((depth, 4 * width), BF),
            shape((TALL, depth), F32),
            shape((2 * count, depth, hidden), BF),
            shape((2 * count, hidden, depth), BF),
            shape((count - 1, depth, hidden), BF),
            shape((count - 1, hidden, depth), BF),
        ),
        in_specs=[anywhere] * 7 + [vmem] * 10,
        out_specs=(vmem,) * 4 + (anywhere,) * 4,
        scratch_shapes=scatter_buffers(rows, width)
        + scatter_buffers(TALL, rows)
        + scatter_buffers(rows, width)
        + [
            pltpu.VMEM((rows, width), F32),
            pltpu.VMEM((TALL, rows), F32),
            pltpu.VMEM((rows, width), BF),
            pltpu.VMEM((TALL, rows), BF),
            pltpu.VMEM((rows, width), BF),
            pltpu.VMEM((rows, 3 * width), BF),
            pltpu.VMEM((24, PAD, PAD), BF),
            pltpu.VMEM((4, width, width), BF),
            pltpu.VMEM((4, 2, share, width), BF),
            pltpu.VMEM((4, share, width), BF),
            pltpu.VMEM((4, share, width), BF),
            pltpu.VMEM((4, share, width), BF),
            pltpu.VMEM((4, 3, piece, width), BF),
            pltpu.VMEM((4, piece, width), BF),
            pltpu.VMEM((4, piece, width), BF),
            pltpu.VMEM((4, piece, width), BF),
        ]
        + [pltpu.VMEM((depth, hidden), BF), pltpu.VMEM((hidden, depth), BF)]
        + [pltpu.VMEM((count - 1, depth, hidden), BF), pltpu.VMEM((count - 1, hidden, depth), BF)]
        + [pltpu.VMEM((depth, hidden), BF), pltpu.VMEM((hidden, depth), BF)]
        + [pltpu.VMEM((width, hidden // 2), BF), pltpu.VMEM((hidden // 2, width), BF)] * 2
        + [pltpu.VMEM((depth, hidden // 2), BF), pltpu.VMEM((hidden // 2, depth), BF)]
        + [
            pltpu.VMEM((TALL, width), F32),
            pltpu.VMEM((TALL, width), F32),
            pltpu.VMEM((TALL, depth), F32),
            pltpu.VMEM((TALL, depth), F32),
            pltpu.VMEM((TALL, depth), F32),
            pltpu.VMEM((TALL, depth), F32),
            pltpu.VMEM((TALL, depth), F32),
            pltpu.VMEM((3, TALL, depth), F32),
            pltpu.SemaphoreType.DMA((192,)),
            pltpu.SemaphoreType.DMA((192,)),
            pltpu.SemaphoreType.DMA((48,)),
        ],
        compiler_params=pltpu.CompilerParams(vmem_limit_bytes=BIG + 3 * 512 * 1024, collective_id=2, has_side_effects=True),
        cost_estimate=pl.CostEstimate(flops=16 * 10**9, bytes_accessed=5 * 10**7, transcendentals=10**6),
        name="tail",
    )(back_all, gate_all, total_all, grads_in, grads_out, rows_all, flags_all, cot, x, middle, prob, attended, packed, normed, small, qkv, out)


class Comm:
    def __init__(self):
        self.sizes = tuple(lax.axis_size(axis) for axis in AXES)
        self.shard = lax.axis_index("shard")
        self.head = lax.axis_index("heads")
        self.tensor = lax.axis_index("tensor")
        self.pair = self.head % 2

    def move(self, value, step):
        shards, heads, tensors = self.sizes
        pairs = []
        for s in range(shards):
            for h in range(heads):
                for t in range(tensors):
                    to = step(s, h, t)
                    if 0 <= to[2] < tensors:
                        source = (s * heads + h) * tensors + t
                        pairs.append((source, (to[0] * heads + to[1]) * tensors + to[2]))
        return lax.ppermute(value, AXES, pairs)

    def over_core(self, value):
        return self.move(value, lambda s, h, t: (s, h ^ 1, t))

    def over_heads(self, value):
        return self.move(value, lambda s, h, t: (s, (h + 2) % 4, t))

    def over_shard(self, value):
        return self.move(value, lambda s, h, t: (1 - s, h, t))

    def up(self, value):
        return self.move(value, lambda s, h, t: (s, h, t + 1))

    def down(self, value):
        return self.move(value, lambda s, h, t: (s, h, t - 1))

    def halves(self, value, index, axis):
        size = value.shape[axis] // 2
        mine = lax.dynamic_slice_in_dim(value, index * size, size, axis)
        other = lax.dynamic_slice_in_dim(value, (1 - index) * size, size, axis)
        return mine, other

    def join(self, mine, other, index, axis):
        first = jnp.where(index == 0, mine, other)
        second = jnp.where(index == 0, other, mine)
        return jnp.concatenate((first, second), axis)

    def gather_shard(self, value, axis):
        if self.sizes[0] != 2:
            return lax.all_gather(value, "shard", axis=axis, tiled=True)
        return self.join(value, self.over_shard(value), self.shard, axis)

    def gather_shard_split(self, value, axis, cut):
        if self.sizes[0] != 2:
            return lax.all_gather(value, "shard", axis=axis, tiled=True)
        mine, _ = self.halves(value, self.pair, cut)
        got = self.over_shard(mine)
        both = self.join(got, self.over_core(got), self.pair, cut)
        return self.join(value, both, self.shard, axis)

    def scatter_shard(self, value, axis):
        if self.sizes[0] != 2:
            return lax.psum_scatter(value.astype(BF), "shard", scatter_dimension=axis, tiled=True).astype(F32)
        mine, other = self.halves(value, self.shard, axis)
        return mine.astype(F32) + self.over_shard(other.astype(BF)).astype(F32)

    def scatter_core(self, value, axis):
        mine, other = self.halves(value, self.pair, axis)
        return mine.astype(F32) + self.over_core(other.astype(BF)).astype(F32)

    def scatter_heads(self, value, axis):
        mine, other = self.halves(value, self.head // 2, axis)
        return mine.astype(F32) + self.over_heads(other.astype(BF)).astype(F32)

    def line_gather(self, value):
        ups, downs = [value], [value]
        for _ in range(3):
            ups.append(self.up(ups[-1]))
            downs.append(self.down(downs[-1]))
        out = [value]
        for back in (1, 2, 3):
            out.append(jnp.where(self.tensor >= back, ups[back], downs[4 - back]))
        return out

    def line_scatter(self, parts):
        high, low = parts[1].astype(BF), parts[3].astype(BF)
        high = (parts[2].astype(F32) + self.up(high).astype(F32)).astype(BF)
        low = (parts[2].astype(F32) + self.down(low).astype(F32)).astype(BF)
        high = (parts[3].astype(F32) + self.up(high).astype(F32)).astype(BF)
        low = (parts[1].astype(F32) + self.down(low).astype(F32)).astype(BF)
        return parts[0].astype(F32) + self.up(high).astype(F32) + self.down(low).astype(F32)

    def join_slots(self, values):
        own = jnp.zeros((4,) + values[0].shape, values[0].dtype)
        for back, value in enumerate(values):
            own = lax.dynamic_update_index_in_dim(own, value, (self.tensor + 4 - back) % 4, 0)
        return self.join(own, self.over_core(own), self.pair, 0)

    def collect(self, value):
        mine, other = self.halves(value, self.pair, 0)
        mine = mine.astype(F32) + self.over_core(other).astype(F32)
        return self.line_scatter(
            [lax.dynamic_index_in_dim(mine, (self.tensor + 4 - k) % 4, 0, False) for k in range(4)]
        )


def local(
    tokens, ln1_gain, ln1_bias, qkv_weight, out_weight, ln2_gain, ln2_bias, router_weight,
    expert_in, expert_out, route_noise, expert_ids, cotangent,
):
    comm = Comm()
    rows, width = tokens.shape
    experts = expert_in.shape[0]
    images = rows // SEQ
    half = experts // 2
    padded = images * PAD

    def pad(value):
        value = value.reshape(images, SEQ, value.shape[1])
        return jnp.pad(value, ((0, 0), (0, PAD - SEQ), (0, 0))).reshape(padded, value.shape[2])

    def pad_turned(value, tall, fill):
        value = value.reshape(images, SEQ, value.shape[1]).transpose(2, 0, 1)
        value = jnp.pad(value, ((0, tall - value.shape[0]), (0, 0), (0, PAD - SEQ)), constant_values=fill)
        return value.reshape(tall, padded)

    def unpad(value):
        return value.reshape(images, PAD, value.shape[1])[:, :SEQ].reshape(rows, value.shape[1])

    vectors = jnp.concatenate((ln1_gain, ln1_bias, ln2_gain, ln2_bias, jnp.zeros_like(jnp.tile(ln1_gain, 4))))
    vectors = lax.optimization_barrier(vectors).reshape(8, ln1_gain.shape[0])
    small = jnp.concatenate((router_weight.T, vectors), 0)
    noise, ids = pad_turned(route_noise, TALL, 0), pad_turned(expert_ids, 8, -1)
    place = jnp.stack((comm.pair, comm.shard if comm.sizes[0] == 2 else 0 * comm.shard)).astype(jnp.int32)
    if comm.sizes[0] == 2:
        (
            small, proj_qkv, proj_out, normed_a, packed, attended, middle, prob,
            x, cot, rows_all, flags_all, grad_rows, got_in, got_out,
        ) = head(tokens, cotangent, small, qkv_weight, out_weight, expert_in, expert_out, noise, ids)
        weights = (expert_in, got_in, expert_out, got_out)
    else:
        cot, x = pad(cotangent), pad(tokens)
        small = lax.all_gather(small, "shard", axis=1, tiled=True)
        small = small.reshape(TALL, 2, width // 2).transpose(1, 0, 2)
        proj_qkv = lax.all_gather(qkv_weight, "shard", axis=0, tiled=True)
        proj_out = lax.all_gather(out_weight, "shard", axis=0, tiled=True)
        inner = lax.all_gather(lax.dynamic_slice_in_dim(expert_in, comm.pair * half, half, 0), "shard", axis=1, tiled=True)
        outer = lax.all_gather(lax.dynamic_slice_in_dim(expert_out, comm.pair * half, half, 0), "shard", axis=2, tiled=True)
        cut = width // 2
        weights = (
            jnp.concatenate((inner[:, :cut], inner[:, :cut]), 0), inner[:, cut:],
            jnp.concatenate((outer[:, :, :cut], outer[:, :, :cut]), 0), outer[:, :, cut:],
        )
        normed_a, packed, attended, middle, sent, flags, prob = front(x, small, proj_qkv, proj_out, noise, ids)

        def gather(value):
            return comm.join_slots(comm.line_gather(value))

        grad_rows, rows_all, flags_all = gather(cot), gather(sent), gather(flags)
    total, back_all, gate_all, grads_in, grads_out = expert_pass(place, rows_all, flags_all, grad_rows, *weights)

    if comm.sizes[0] == 2:
        mixed, grad_tokens, dense, grad_small, grad_in, grad_outer, _, _ = tail(
            back_all, gate_all, total, grads_in, grads_out, rows_all, flags_all,
            cot, x, middle, prob, attended, packed, normed_a, small, proj_qkv, proj_out,
        )
        dense = dense.astype(F32)
        return (
            mixed,
            grad_tokens,
            grad_small[experts],
            grad_small[experts + 1],
            dense[:, width:],
            dense[:, :width],
            grad_small[experts + 2],
            grad_small[experts + 3],
            grad_small[:experts].T,
            grad_in.astype(F32),
            grad_outer.astype(F32),
        )

    def reduce_expert(grad, axis, other):
        part = comm.scatter_shard(grad, axis)
        part = comm.scatter_heads(part, other).astype(BF)
        return comm.join(part, comm.over_heads(part), comm.head // 2, other)

    inner_grads = [reduce_expert(grads_in[e], 0, 1) for e in range(half)]
    outer_grads = [reduce_expert(grads_out[e], 1, 0) for e in range(half)]

    moe_grad = comm.collect(back_all)
    gate_grad = comm.collect(gate_all)
    moe = comm.collect(total)
    mixed = (unpad(middle) + unpad(moe)).astype(BF)
    grad_tokens, grad_qkv, grad_out, grad_small = back(
        moe_grad, gate_grad, cot, x, middle, sent, flags, prob, attended, packed, normed_a, small, proj_qkv, proj_out
    )
    grad_tokens = unpad(grad_tokens)

    grad_small = jnp.pad(grad_small.T, ((0, 0), (0, 128 - TALL)))
    shares = jnp.concatenate((grad_qkv, grad_out, grad_small, jnp.zeros_like(grad_small)), 1)
    shares = comm.scatter_core(shares, 1)
    shares = comm.scatter_shard(shares, 0)
    shares = comm.scatter_heads(shares, 1)
    cut = shares.shape[0] // 4
    rolled = [
        lax.dynamic_slice_in_dim(shares, ((comm.tensor + 4 - k) % 4) * cut, cut, 0) for k in range(4)
    ]
    summed = comm.line_scatter(rolled).astype(BF)
    pieces = comm.line_gather(summed)
    whole = jnp.zeros(shares.shape, BF)
    for k in range(4):
        whole = lax.dynamic_update_slice_in_dim(whole, pieces[k], ((comm.tensor + 4 - k) % 4) * cut, 0)
    whole = comm.join(whole, comm.over_heads(whole), comm.head // 2, 1)
    whole = comm.join(whole, comm.over_core(whole), comm.pair, 1).astype(F32)
    small = whole[:, 4 * width : 4 * width + 128]

    grad_in, grad_outer = jnp.stack(inner_grads, 0), jnp.stack(outer_grads, 0)
    grad_in = comm.join(grad_in, comm.over_core(grad_in), comm.pair, 0).astype(F32)
    grad_outer = comm.join(grad_outer, comm.over_core(grad_outer), comm.pair, 0).astype(F32)
    return (
        mixed,
        grad_tokens,
        small[:, experts],
        small[:, experts + 1],
        whole[:, : 3 * width],
        whole[:, 3 * width : 4 * width],
        small[:, experts + 2],
        small[:, experts + 3],
        small[:, :experts],
        grad_in,
        grad_outer,
    )


def solution(mesh):
    split = P(AXES, None)
    vector, matrix = P("shard"), P("shard", None)
    inner, outer = P(None, "shard", "tensor"), P(None, "tensor", "shard")
    return jax.shard_map(
        local,
        mesh=mesh,
        in_specs=(
            split, vector, vector, matrix, matrix, vector, vector, matrix, inner, outer, split, split, split,
        ),
        out_specs=(
            split, split, vector, vector, matrix, matrix, vector, vector, matrix, inner, outer,
        ),
        check_vma=False,
    )
```

```python
import jax
import jax.numpy as jnp
from jax import lax
from jax.experimental import pallas as pl
from jax.experimental.pallas import tpu as pltpu
from jax.sharding import PartitionSpec as P

HEAD_DIM = 64
SEQ = 197
EPS = 1e-06
AXES = ("shard", "heads", "tensor")
BF = jnp.bfloat16
F32 = jnp.float32


def contract_rows(left, right):
    return lax.dot_general(left, right, (((0,), (0,)), ((), ())), preferred_element_type=F32)


def contract_cols(left, right):
    return lax.dot_general(left, right, (((1,), (1,)), ((), ())), preferred_element_type=F32)


PAD = 208
TILE = 128
CHUNK = 256
FAR = 512.0
TALL = 16
LANES = 128
MASKED = -1e30
CUBIC = 0.044715
ROOT = (2.0 / 3.141592653589793) ** 0.5
BIG = 60 * 1024 * 1024
MESH = pl.DeviceIdType.MESH


def dot(left, right):
    return jnp.dot(left, right, preferred_element_type=F32)


def norm_parts(values):
    centred = values - jnp.mean(values, -1, keepdims=True)
    inverse = lax.rsqrt(jnp.mean(centred * centred, -1, keepdims=True) + EPS)
    return centred * inverse, inverse


def norm_back(grad, unit, inverse, gain):
    scaled = grad * gain
    along = jnp.mean(scaled * unit, -1, keepdims=True)
    return inverse * (scaled - jnp.mean(scaled, -1, keepdims=True) - unit * along)


def head_probs(query, keys, scale):
    scores = contract_cols(query, keys) * scale
    column = lax.broadcasted_iota(jnp.int32, scores.shape, 1)
    scores = jnp.where(column < SEQ, scores, MASKED)
    raised = jnp.exp(scores - jnp.max(scores, -1, keepdims=True))
    return raised / jnp.sum(raised, -1, keepdims=True)


def gain_row(small_ref, experts, index):
    row = slice(experts + index, experts + index + 1)
    return jnp.concatenate((small_ref[0, row, :], small_ref[1, row, :]), 1).astype(F32)


def router_rows(small_ref):
    return jnp.concatenate((small_ref[0], small_ref[1]), 1)


def attend(normed, at, qkv_ref, packed_ref):
    width = normed.shape[1]
    group = 3 * HEAD_DIM
    scale = HEAD_DIM ** (-0.5)
    lane = lax.broadcasted_iota(jnp.int32, (PAD, group), 1) // HEAD_DIM
    outs = []
    for double in range(width // group // 2):
        cols = pl.ds(double * 6 * group, 6 * group)
        packed = dot(normed, qkv_ref[:, cols])
        packed_ref[at, cols] = packed.astype(BF)
        for side in range(2):
            query, keys, values = (
                packed[:, (3 * side + k) * group : (3 * side + k + 1) * group].astype(BF)
                for k in range(3)
            )
            total = jnp.zeros((PAD, group), F32)
            for head in range(3):
                mask = lane == head
                probs = head_probs(jnp.where(mask, query, jnp.zeros_like(query)), keys, scale)
                total = jnp.where(mask, dot(probs.astype(BF), values), total)
            outs.append(total)
    return jnp.concatenate(outs, 1).astype(BF)


def route(normed, small_ref, noise, ids, experts):
    logits = contract_cols(router_rows(small_ref), normed) + noise
    row = lax.broadcasted_iota(jnp.int32, logits.shape, 0)
    logits = jnp.where(row < experts, logits, MASKED)
    raised = jnp.exp(logits - jnp.max(logits, 0, keepdims=True))
    probs = raised / jnp.sum(raised, 0, keepdims=True)
    chosen = ((row == ids[0:1]) | (row == ids[1:2])).astype(F32)
    shifted = row - experts
    flags = (((shifted == ids[0:1]) | (shifted == ids[1:2])) & (shifted >= 0)).astype(F32)
    return probs, probs * chosen + flags


def front_image(image, experts, x_ref, small_ref, qkv_ref, out_ref, noise_ref, ids_ref, keep, ready=None):
    normed_ref, packed_ref, attended_ref, middle_ref = keep
    at = pl.ds(image * PAD, PAD)
    x = x_ref[at, :].astype(F32)
    unit, _ = norm_parts(x)
    normed = (unit * gain_row(small_ref, experts, 0) + gain_row(small_ref, experts, 1)).astype(BF)
    normed_ref[at, :] = normed
    attended = attend(normed, at, qkv_ref, packed_ref)
    attended_ref[at, :] = attended
    if ready is not None:
        ready()
    middle = x + dot(attended, out_ref[...])
    middle_ref[at, :] = middle
    unit, _ = norm_parts(middle)
    normed = (unit * gain_row(small_ref, experts, 2) + gain_row(small_ref, experts, 3)).astype(BF)
    cols = slice(image * PAD, (image + 1) * PAD)
    probs, flags = route(normed, small_ref, noise_ref[:, cols], ids_ref[:, cols], experts)
    return normed, probs, flags


def front_kernel(
    x_ref, small_ref, qkv_ref, out_ref, noise_ref, ids_ref,
    normed_ref, packed_ref, attended_ref, middle_ref, rows_ref, flag_ref, prob_ref,
):
    keep = (normed_ref, packed_ref, attended_ref, middle_ref)
    probs, flags = [], []
    for image in range(x_ref.shape[0] // PAD):
        normed, prob, flag = front_image(
            image, TALL // 2, x_ref, small_ref, qkv_ref, out_ref, noise_ref, ids_ref, keep
        )
        rows_ref[pl.ds(image * PAD, PAD), :] = normed
        probs.append(prob)
        flags.append(flag)
    prob_ref[...] = jnp.concatenate(probs, 1)
    flag_ref[...] = jnp.concatenate(flags, 1).astype(BF)


def front(x, small, qkv, out, noise, ids):
    rows, width = x.shape
    shape = jax.ShapeDtypeStruct
    return pl.pallas_call(
        front_kernel,
        out_shape=(
            shape((rows, width), BF),
            shape((rows, 3 * width), BF),
            shape((rows, width), BF),
            shape((rows, width), F32),
            shape((rows, width), BF),
            shape((TALL, rows), BF),
            shape((TALL, rows), F32),
        ),
        compiler_params=pltpu.CompilerParams(vmem_limit_bytes=BIG),
        cost_estimate=pl.CostEstimate(flops=8 * 10**9, bytes_accessed=10**7, transcendentals=10**6),
        name="front",
    )(x, small, qkv, out, noise, ids)


class Place:
    def __init__(self):
        shard, head, tensor = (lax.axis_index(axis) for axis in AXES)
        self.shard, self.head, self.tensor = shard, head, tensor
        self.pair, self.side = lax.rem(head, 2), lax.div(head, 2)
        self.across = (1 - shard, head, tensor)
        self.beside = (shard, lax.rem(head + 2, 4), tensor)
        self.twin = (shard, head + 1 - 2 * self.pair, tensor)
        self.above = (shard, head, lax.rem(tensor + 1, 4))
        self.below = (shard, head, lax.rem(tensor + 3, 4))

    def greet(self, line=False):
        barrier = pltpu.get_barrier_semaphore()
        devices = [self.across, self.beside, self.twin, self.above, self.below]
        if line:
            devices.append((self.shard, self.head, lax.rem(self.tensor + 2, 4)))
        for device in devices:
            pl.semaphore_signal(barrier, inc=1, device_id=device, device_id_type=MESH)
        pl.semaphore_wait(barrier, len(devices))


class Links:
    def __init__(self, send, recv):
        self.send, self.recv, self.used = send, recv, 0
        self.sent = []

    def copy(self, source, target, device):
        index = self.used
        self.used += 1
        return pltpu.make_async_remote_copy(
            src_ref=source, dst_ref=target, send_sem=self.send.at[index], recv_sem=self.recv.at[index],
            device_id=device, device_id_type=MESH,
        )

    def start(self, source, target, device):
        copy = self.copy(source, target, device)
        copy.start()
        self.sent.append((None, copy))
        return copy

    def skip(self, done):
        self.sent = [(when, copy) for when, copy in self.sent if copy is not done]

    def finish(self):
        for when, copy in self.sent:
            if when is None:
                copy.wait_send()
            else:
                pl.when(when)(copy.wait_send)


class LineGather:
    def __init__(self, links, place, view, own, parts):
        self.links, self.place, self.view, self.own = links, place, view, own
        self.copies = {}
        self.parts = parts

    def start(self, part, step):
        t = self.place.tensor
        for name, slot, device, sends in (
            ("up", t - step, self.place.above, (t >= step) & (t < 3)),
            ("down", t + step, self.place.below, (t + step <= 3) & (t > 0)),
        ):
            slot = jnp.clip(slot, 0, 3)
            source = self.own(part) if step == 0 else self.view(slot, part)
            copy = self.links.copy(source, self.view(slot, part), device)
            pl.when(sends)(copy.start)
            self.links.sent.append((sends, copy))
            self.copies[name, part, step] = copy

    def wait(self, part, step, then=None):
        t = self.place.tensor
        for name, slot, comes in (("up", t - 1 - step, t >= step + 1), ("down", t + 1 + step, t + 1 + step <= 3)):
            copy = self.copies[name, part, step]

            @pl.when(comes)
            def _():
                copy.wait_recv()

    def arrived(self, step):
        t = self.place.tensor
        return (
            (jnp.clip(t - 1 - step, 0, 3), t >= step + 1),
            (jnp.clip(t + 1 + step, 0, 3), t + 1 + step <= 3),
        )


def pad_images(source, target):
    value = source[...].astype(F32)
    empty = jnp.zeros((PAD - SEQ, source.shape[1]), F32)
    for image in range(2):
        part = value[image * SEQ : (image + 1) * SEQ]
        target[pl.ds(image * PAD, PAD), :] = jnp.concatenate((part, empty), 0).astype(BF)


def head_kernel(
    tokens_own, cot_own, small_own, qkv_own, out_own, expert_in, expert_out, noise_ref, ids_ref,
    small_ref, qkv_ref, out_ref, normed_ref, packed_ref, attended_ref, middle_ref, prob_ref,
    x_ref, cot_ref, rows_all, flags_all, cot_all, got_in, got_out,
    sent_rows, sent_flags, send, recv, local_sem,
):
    pad_images(cot_own, cot_ref)
    place = Place()
    links = Links(send, recv)
    width = x_ref.shape[1]
    experts = expert_in.shape[0]
    depth = qkv_own.shape[0]
    quarter = depth // 4
    shard, pair, side, tensor = place.shard, place.pair, place.side, place.tensor
    mine = pair * 4 + tensor
    place.greet()

    def dense_rows(owner, across_side, across_pair, start, size):
        return pl.ds(pl.multiple_of(owner * depth + (across_side * 2 + across_pair) * quarter + start, TALL), size)

    pieces = ((qkv_own, qkv_ref, 0, quarter // 2), (qkv_own, qkv_ref, quarter // 2, quarter // 2), (out_own, out_ref, 0, quarter))
    smalls = links.start(small_own, small_ref.at[shard], place.across)
    cross = []
    for own, full, start, size in pieces:
        source = own.at[pl.ds(pl.multiple_of((side * 2 + pair) * quarter + start, TALL), size), :]
        cross.append(links.start(source, full.at[dense_rows(shard, side, pair, start, size), :], place.across))

    def expert_item(item):
        index = side * 2 + item // 2
        source, target = (expert_in, got_in) if item % 2 == 0 else (expert_out, got_out)
        return source.at[pair * (experts // 2) + index], target.at[index]

    fetched = [links.start(*expert_item(item), place.across) for item in range(4)]
    here = pl.ds(pl.multiple_of(shard * depth, TALL), depth)
    locals_ = [
        pltpu.make_async_copy(qkv_own, qkv_ref.at[here, :], local_sem.at[0]),
        pltpu.make_async_copy(out_own, out_ref.at[here, :], local_sem.at[1]),
        pltpu.make_async_copy(small_own, small_ref.at[shard], local_sem.at[2]),
        pltpu.make_async_copy(cot_ref, cot_all.at[mine], local_sem.at[3]),
    ]
    for copy in locals_:
        copy.start()

    def slots(array):
        def view(slot, part):
            return array.at[pair * 4 + slot, pl.ds(part * PAD, PAD), :]

        return view

    cot_line = LineGather(links, place, slots(cot_all), lambda part: cot_ref.at[pl.ds(part * PAD, PAD), :], 2)
    for part in range(2):
        cot_line.start(part, 0)

    pad_images(tokens_own, x_ref)

    beside, twins = [], []
    for index, (own, full, start, size) in enumerate(pieces):
        cross[index].wait_recv()
        rows = full.at[dense_rows(1 - shard, side, pair, start, size), :]
        beside.append(links.start(rows, rows, place.beside))
        twins.append(links.start(rows, rows, place.twin))
    for part in range(2):
        cot_line.wait(part, 0)
        cot_line.start(part, 1)
    for index, (own, full, start, size) in enumerate(pieces):
        beside[index].wait_recv()
        rows = full.at[dense_rows(1 - shard, 1 - side, pair, start, size), :]
        twins.append(links.start(rows, rows, place.twin))

    for part in range(2):
        cot_line.wait(part, 1)
        cot_line.start(part, 2)
    smalls.wait_recv()
    for index, copy in enumerate(twins):
        if index % len(pieces) < 2:
            copy.wait_recv()
    for copy in locals_:
        copy.wait()

    keep = (normed_ref, packed_ref, attended_ref, middle_ref)
    row_line = LineGather(links, place, slots(rows_all), lambda part: sent_rows.at[pl.ds(part * PAD, PAD), :], 2)
    flag_line = LineGather(links, place, lambda slot, part: flags_all.at[pair * 4 + slot], lambda part: sent_flags, 1)
    probs, flags = [], []

    def out_ready():
        for index, copy in enumerate(twins):
            if index % len(pieces) == 2:
                copy.wait_recv()

    twin_rows = []
    forwarded = []

    def forward_expert(item):
        fetched[item].wait_recv()
        _, target = expert_item(item)
        forwarded.append(links.start(target, target, place.beside))

    forward_expert(0)
    for image in range(2):
        normed, prob, flag = front_image(
            image, experts, x_ref, small_ref, qkv_ref, out_ref, noise_ref, ids_ref, keep,
            out_ready if image == 0 else None,
        )
        at = pl.ds(image * PAD, PAD)
        sent_rows[at, :] = normed
        row_line.start(image, 0)
        twin_rows.append(links.start(sent_rows.at[at, :], rows_all.at[mine, at, :], place.twin))
        probs.append(prob)
        flags.append(flag)
        if image == 1:
            forward_expert(1)
    prob_ref[...] = jnp.concatenate(probs, 1)
    sent_flags[...] = jnp.concatenate(flags, 1).astype(BF)
    flag_line.start(0, 0)
    twin_flags = [links.start(sent_flags, flags_all.at[mine], place.twin)]
    keep_own = [
        pltpu.make_async_copy(sent_rows, rows_all.at[mine], local_sem.at[0]),
        pltpu.make_async_copy(sent_flags, flags_all.at[mine], local_sem.at[1]),
    ]
    for copy in keep_own:
        copy.start()

    def share(line, array, part, step, copies, whole):
        for slot, comes in line.arrived(step):
            index = pair * 4 + slot
            ref = array.at[index] if whole else array.at[index, pl.ds(part * PAD, PAD), :]
            copy = links.copy(ref, ref, place.twin)
            pl.when(comes)(copy.start)
            links.sent.append((comes, copy))
            copies.append((comes, copy))

    twin_steps = []
    for step in range(3):
        for part in range(2):
            row_line.wait(part, step)
            if step < 2:
                row_line.start(part, step + 1)
            share(row_line, rows_all, part, step, twin_steps, False)
        if step < 2:
            forward_expert(step + 2)
        flag_line.wait(0, step)
        if step < 2:
            flag_line.start(0, step + 1)
        share(flag_line, flags_all, 0, step, twin_steps, True)
        if step == 0:
            for part in range(2):
                cot_line.wait(part, 2)
            ours = cot_all.at[pl.ds(pair * 4, 4)]
            twin_cot = links.start(ours, ours, place.twin)

    for copy in twin_rows + twin_flags + [twin_cot] + forwarded:
        copy.wait_recv()
    for comes, copy in twin_steps:
        pl.when(comes)(copy.wait_recv)
    for copy in keep_own:
        copy.wait()
    links.finish()


def head(x, cot, small, qkv, out, expert_in, expert_out, noise, ids):
    rows, width = x.shape[0] // SEQ * PAD, x.shape[1]
    depth = qkv.shape[0]
    count = expert_in.shape[0] // 2
    shape = jax.ShapeDtypeStruct
    anywhere = pl.BlockSpec(memory_space=pl.ANY)
    vmem = pl.BlockSpec(memory_space=pltpu.VMEM)
    return pl.pallas_call(
        head_kernel,
        out_shape=(
            shape((2, TALL, depth), BF),
            shape((width, 3 * width), BF),
            shape((width, width), BF),
            shape((rows, width), BF),
            shape((rows, 3 * width), BF),
            shape((rows, width), BF),
            shape((rows, width), F32),
            shape((TALL, rows), F32),
            shape((rows, width), BF),
            shape((rows, width), BF),
            shape((8, rows, width), BF),
            shape((8, TALL, rows), BF),
            shape((8, rows, width), BF),
            shape((count,) + expert_in.shape[1:], BF),
            shape((count,) + expert_out.shape[1:], BF),
        ),
        in_specs=[vmem] * 3 + [anywhere] * 4 + [vmem] * 2,
        out_specs=(vmem,) * 10 + (anywhere,) * 5,
        scratch_shapes=[
            pltpu.VMEM((rows, width), BF),
            pltpu.VMEM((TALL, rows), BF),
            pltpu.SemaphoreType.DMA((96,)),
            pltpu.SemaphoreType.DMA((96,)),
            pltpu.SemaphoreType.DMA((4,)),
        ],
        compiler_params=pltpu.CompilerParams(vmem_limit_bytes=BIG, collective_id=1, has_side_effects=True),
        cost_estimate=pl.CostEstimate(flops=8 * 10**9, bytes_accessed=3 * 10**7, transcendentals=10**6),
        name="head",
    )(x, cot, small, qkv, out, expert_in, expert_out, noise, ids)


def expert_kernel(
    place_ref, flag_ref, rows_all, cot_all, own_in, got_in, own_out, got_out,
    total_all, back_all, gate_ref, grad_in, grad_out,
    inner, outer, picked, grads, gate, active, hidden_grad, made, made_back, made_gate, ranks,
    rows_buf, cot_buf, total_buf, back_buf, stage_in, stage_out, load_sem, store_sem, fetch_sem, put_sem, old_sem,
):
    blocks, length, width = cot_all.shape
    count = got_in.shape[0]
    depth = got_in.shape[1]
    pair, shard = place_ref[0], place_ref[1]
    experts = 2 * count

    def loads(expert, slot):
        mine = pl.ds(pl.multiple_of(shard * depth, LANES), depth)
        other = pl.ds(pl.multiple_of((1 - shard) * depth, LANES), depth)
        index = pair * count + expert
        return (
            pltpu.make_async_copy(own_in.at[index], inner.at[slot, mine, :], load_sem.at[slot, 0]),
            pltpu.make_async_copy(got_in.at[expert], inner.at[slot, other, :], load_sem.at[slot, 1]),
            pltpu.make_async_copy(own_out.at[index], outer.at[slot, :, mine], load_sem.at[slot, 2]),
            pltpu.make_async_copy(got_out.at[expert], outer.at[slot, :, other], load_sem.at[slot, 3]),
        )

    def stores(expert, slot):
        return (
            pltpu.make_async_copy(stage_in.at[slot], grad_in.at[expert], store_sem.at[slot, 0]),
            pltpu.make_async_copy(stage_out.at[slot], grad_out.at[expert], store_sem.at[slot, 1]),
        )

    def fetches(block, slot):
        return (
            pltpu.make_async_copy(rows_all.at[block], rows_buf.at[slot], fetch_sem.at[slot, 0]),
            pltpu.make_async_copy(cot_all.at[block], cot_buf.at[slot], fetch_sem.at[slot, 1]),
        )

    def puts(block, slot):
        return (
            pltpu.make_async_copy(total_buf.at[slot], total_all.at[block], put_sem.at[slot, 0]),
            pltpu.make_async_copy(back_buf.at[slot], back_all.at[block], put_sem.at[slot, 1]),
        )

    def start(copies):
        for copy in copies:
            copy.start()

    def wait(copies):
        for copy in copies:
            copy.wait()

    def reload(pairs):
        copies = [pltpu.make_async_copy(source, target, old_sem.at[n]) for n, (source, target) in enumerate(pairs)]
        start(copies)
        wait(copies)

    start(fetches(0, 0) + fetches(1, 1) + loads(0, 0))
    ahead = lax.broadcasted_iota(jnp.int32, (length, length), 0)
    behind = lax.broadcasted_iota(jnp.int32, (length, length), 1)
    order = jnp.where(behind < ahead, 1.0, jnp.where(behind == ahead, FAR, 0.0)).astype(BF)
    for block in range(blocks):
        ranks[block] = contract_cols(flag_ref[block], order) - FAR

    def line(expert):
        return pl.ds(experts + pair * count + expert, 1)

    def passes_of(expert):
        highest = ranks[0, line(expert), :]
        for block in range(1, blocks):
            highest = jnp.maximum(highest, ranks[block, line(expert), :])
        return (jnp.maximum(jnp.max(highest), -1.0).astype(jnp.int32) + TILE) // TILE

    highest = ranks[0, line(0), :]
    for block in range(blocks):
        for expert in range(count):
            highest = jnp.maximum(highest, ranks[block, line(expert), :])
    rounds = (jnp.maximum(jnp.max(highest), 0.0).astype(jnp.int32) + TILE) // TILE

    def take(block, slot, step):
        at = pl.ds(pl.multiple_of(block * TILE, TILE), TILE)
        choose = choices(block, step)
        columns = jnp.where(lane == wanted, contract_cols(choose, flag_ref[block]), 0.0)
        column = jnp.broadcast_to(jnp.sum(columns, -1, keepdims=True), (count * TILE, LANES))
        wait(fetches(block, slot))
        both = dot(choose, rows_buf[slot]).astype(BF)
        other = dot(choose, cot_buf[slot]).astype(BF)
        for expert in range(count):
            part = slice(expert * TILE, (expert + 1) * TILE)
            picked[expert, at, :] = both[part]
            grads[expert, at, :] = other[part]
            gate[expert, at, :] = column[part]

    def compute(expert, slot):
        def chunk(index, carry):
            at = pl.ds(pl.multiple_of(index * CHUNK, CHUNK), CHUNK)
            value = dot(picked[expert, at, :], inner[slot])
            grad_active = contract_cols(grads[expert, at, :], outer[slot])
            gate_column = gate[expert, at, 0:1]
            square = value * value
            bent = jnp.tanh(ROOT * value * (1.0 + CUBIC * square))
            plus = 0.5 * (1.0 + bent)
            bowed = value * plus
            slope = plus + (0.5 * ROOT) * value * (1.0 - bent * bent) * (1.0 + (3.0 * CUBIC) * square)
            active[at, :] = (bowed * gate_column).astype(BF)
            back = (grad_active * gate_column * slope).astype(BF)
            hidden_grad[at, :] = back
            lane = lax.broadcasted_iota(jnp.int32, (CHUNK, TALL), 1)
            gate_grad = jnp.sum(grad_active * bowed, -1, keepdims=True)
            made_gate[expert, at, :] = jnp.where(lane == pair * count + expert, gate_grad, 0.0).astype(BF)
            made[expert, at, :] = dot(active[at, :], outer[slot]).astype(BF)
            made_back[expert, at, :] = contract_cols(back, inner[slot]).astype(BF)
            return carry

        lax.fori_loop(0, blocks * TILE // CHUNK, chunk, 0)

    def weigh(expert, slot, again):
        for stage, grad, left, right in (
            (stage_out, grad_out, active, grads.at[expert]), (stage_in, grad_in, picked.at[expert], hidden_grad),
        ):
            if again:
                reload([(grad.at[expert], stage.at[slot])])
            for begin in range(0, left.shape[1], CHUNK):
                at = pl.ds(begin, CHUNK)
                value = contract_rows(left[:, at], right[...])
                if again:
                    value = value + stage[slot, at, :].astype(F32)
                stage[slot, at, :] = value.astype(BF)

    def give(block, slot, step, again):
        at = pl.ds(pl.multiple_of(block * TILE, TILE), TILE)
        choose = choices(block, step)

        def joined(source):
            return jnp.concatenate([source[expert, at, :] for expert in range(count)], 0)

        if again:
            reload([(total_all.at[block], rows_buf.at[0]), (back_all.at[block], rows_buf.at[1])])
        for target, source, old in ((total_buf, made, 0), (back_buf, made_back, 1)):
            value = contract_rows(choose, joined(source))
            if again:
                value = value + rows_buf[old].astype(F32)
            target[slot] = value.astype(BF)
        start(puts(block, slot))
        gates = contract_rows(joined(made_gate), choose)
        if again:
            gates = gates + gate_ref[block].astype(F32)
        gate_ref[block] = gates.astype(BF)

    def choices(block, step):
        slots = lax.broadcasted_iota(jnp.int32, (TILE, length), 0).astype(F32) + (step * TILE).astype(F32)
        return jnp.concatenate([(ranks[block, line(expert), :] == slots).astype(BF) for expert in range(count)], 0)

    lane = lax.broadcasted_iota(jnp.int32, (count * TILE, TALL), 1)
    wanted = lax.broadcasted_iota(jnp.int32, (count * TILE, TALL), 0) // TILE + pair * count
    first = jnp.int32(0)
    for block in range(blocks):
        take(block, block % 2, first)
        if block + 2 < blocks:
            start(fetches(block + 2, block % 2))
    for expert in range(count):
        slot = expert % 2
        if expert + 1 < count:
            start(loads(expert + 1, 1 - slot))
        wait(loads(expert, slot))
        compute(expert, slot)
        if expert >= 2:
            wait(stores(expert - 2, slot))
        weigh(expert, slot, False)
        start(stores(expert, slot))
    for block in range(blocks):
        if block >= 2:
            wait(puts(block - 2, block % 2))
        give(block, block % 2, first, False)
    for block in range(blocks - 2, blocks):
        wait(puts(block, block % 2))
    for expert in range(count - 2, count):
        wait(stores(expert, expert % 2))

    def more(step, carry):
        def take_one(block, carry):
            start(fetches(block, 0))
            take(block, 0, step)
            return carry

        def expert_one(expert, carry):
            @pl.when(passes_of(expert) > step)
            def _():
                start(loads(expert, 0))
                wait(loads(expert, 0))
                compute(expert, 0)
                weigh(expert, 0, True)
                start(stores(expert, 0))
                wait(stores(expert, 0))

            return carry

        def give_one(block, carry):
            give(block, 0, step, True)
            wait(puts(block, 0))
            return carry

        lax.fori_loop(0, blocks, take_one, 0)
        lax.fori_loop(0, count, expert_one, 0)
        lax.fori_loop(0, blocks, give_one, 0)
        return carry

    lax.fori_loop(1, rounds, more, 0)


def expert_pass(place, rows, flags, cot, own_in, got_in, own_out, got_out):
    blocks, length, width = cot.shape
    count, _, hidden = got_in.shape
    capacity = blocks * TILE
    shape = jax.ShapeDtypeStruct
    anywhere = pl.BlockSpec(memory_space=pl.ANY)
    vmem = pl.BlockSpec(memory_space=pltpu.VMEM)
    return pl.pallas_call(
        expert_kernel,
        out_shape=(
            shape((blocks, length, width), BF),
            shape((blocks, length, width), BF),
            shape((blocks, TALL, length), BF),
            shape((count, width, hidden), BF),
            shape((count, hidden, width), BF),
        ),
        in_specs=[pl.BlockSpec(memory_space=pltpu.SMEM), vmem] + [anywhere] * 6,
        out_specs=(anywhere, anywhere, vmem, anywhere, anywhere),
        scratch_shapes=[
            pltpu.VMEM((2, width, hidden), BF),
            pltpu.VMEM((2, hidden, width), BF),
            pltpu.VMEM((count, capacity, width), BF),
            pltpu.VMEM((count, capacity, width), BF),
            pltpu.VMEM((count, capacity, LANES), F32),
            pltpu.VMEM((capacity, hidden), BF),
            pltpu.VMEM((capacity, hidden), BF),
            pltpu.VMEM((count, capacity, width), BF),
            pltpu.VMEM((count, capacity, width), BF),
            pltpu.VMEM((count, capacity, TALL), BF),
            pltpu.VMEM((blocks, TALL, length), F32),
            pltpu.VMEM((2, length, width), BF),
            pltpu.VMEM((2, length, width), BF),
            pltpu.VMEM((2, length, width), BF),
            pltpu.VMEM((2, length, width), BF),
            pltpu.VMEM((2, width, hidden), BF),
            pltpu.VMEM((2, hidden, width), BF),
            pltpu.SemaphoreType.DMA((2, 4)),
            pltpu.SemaphoreType.DMA((2, 2)),
            pltpu.SemaphoreType.DMA((2, 2)),
            pltpu.SemaphoreType.DMA((2, 2)),
            pltpu.SemaphoreType.DMA((2,)),
        ],
        compiler_params=pltpu.CompilerParams(vmem_limit_bytes=BIG),
        cost_estimate=pl.CostEstimate(flops=50 * 10**9, bytes_accessed=5 * 10**7, transcendentals=10**6),
        name="experts",
    )(place, flags, rows, cot, own_in, got_in, own_out, got_out)


def back_middle(at, moe, gates, cot, middle, rows, probs, flags, small_ref, sums):
    experts = TALL // 2
    row = lax.broadcasted_iota(jnp.int32, flags.shape, 0)
    chosen = jnp.where(row < experts, pltpu.roll(flags, experts, 0), 0.0)
    asked = gates * chosen
    grad_logits = probs * (asked - jnp.sum(probs * asked, 0, keepdims=True))
    coarse = grad_logits.astype(BF)
    fine = (grad_logits - coarse.astype(F32)).astype(BF)
    router = router_rows(small_ref)
    sums[4] = sums[4] + dot(coarse, rows) + dot(fine, rows)
    grad = moe + contract_rows(coarse, router) + contract_rows(fine, router)
    unit, inverse = norm_parts(middle)
    sums[2] = sums[2] + jnp.sum(grad * unit, 0, keepdims=True)
    sums[3] = sums[3] + jnp.sum(grad, 0, keepdims=True)
    return cot + norm_back(grad, unit, inverse, gain_row(small_ref, experts, 2))


def back_probs(at, double, packed_ref, take):
    group = 3 * HEAD_DIM
    scale = HEAD_DIM ** (-0.5)
    lanes = lax.broadcasted_iota(jnp.int32, (PAD, group), 1) // HEAD_DIM
    packed = packed_ref[at, pl.ds(double * 6 * group, 6 * group)]
    for side in range(2):
        query, keys = (packed[:, (3 * side + k) * group : (3 * side + k + 1) * group] for k in range(2))
        for head in range(3):
            masked = jnp.where(lanes == head, query, jnp.zeros_like(query))
            take(side * 3 + head, head_probs(masked, keys, scale))


def back_heads(at, double, grad_proj, packed_ref, out_ref, stacked, give):
    width = grad_proj.shape[1]
    group = 3 * HEAD_DIM
    scale = HEAD_DIM ** (-0.5)
    lanes = lax.broadcasted_iota(jnp.int32, (PAD, group), 1) // HEAD_DIM
    made = []
    packed = packed_ref[at, pl.ds(double * 6 * group, 6 * group)]
    for side in range(2):
        query, keys, values = (packed[:, (3 * side + k) * group : (3 * side + k + 1) * group] for k in range(3))
        index = double * 2 + side
        grad_att = contract_cols(grad_proj, out_ref[pl.ds(index * group, group), :]).astype(BF)
        outs = [jnp.zeros((PAD, group), F32) for _ in range(3)]
        for head in range(3):
            mask = lanes == head
            low = give(side * 3 + head)
            probs = low.astype(F32)
            part = jnp.where(mask, grad_att, jnp.zeros_like(grad_att))
            grad_weights = contract_cols(part, values)
            inner_sum = jnp.sum(probs * grad_weights, -1, keepdims=True)
            grad_scores = (probs * (grad_weights - inner_sum)).astype(BF)
            outs[0] = jnp.where(mask, dot(grad_scores, keys), outs[0])
            outs[1] = jnp.where(mask, contract_rows(grad_scores, query), outs[1])
            outs[2] = jnp.where(mask, contract_rows(low, grad_att), outs[2])
        made += [outs[0] * scale, outs[1] * scale, outs[2]]
    stacked[at, pl.ds(double * 6 * group, 6 * group)] = jnp.concatenate(made, 1).astype(BF)


def back_kernel(
    moe_ref, gate_ref, cot_ref, x_ref, middle_ref, rows_ref, flag_ref, prob_ref, attended_ref, packed_ref, normed_ref,
    small_ref, qkv_ref, out_ref,
    tokens_ref, grad_qkv, grad_out, grad_small,
    stacked, projected,
):
    rows, width = x_ref.shape
    experts = TALL // 2
    sums = [jnp.zeros((1, width), F32) for _ in range(4)] + [jnp.zeros((TALL, width), F32)]
    for image in range(rows // PAD):
        at = pl.ds(image * PAD, PAD)
        cols = slice(image * PAD, (image + 1) * PAD)
        grad_middle = back_middle(
            at, moe_ref[at, :].astype(F32), gate_ref[:, cols].astype(F32), cot_ref[at, :].astype(F32),
            middle_ref[at, :], rows_ref[at, :], prob_ref[:, cols], flag_ref[:, cols].astype(F32), small_ref, sums,
        )
        grad_proj = grad_middle.astype(BF)
        projected[at, :] = grad_proj
        for double in range(width // (6 * HEAD_DIM)):
            saved = {}
            back_probs(at, double, packed_ref, lambda index, value: saved.update({index: value.astype(BF)}))
            back_heads(at, double, grad_proj, packed_ref, out_ref, stacked, saved.get)
        grad = contract_cols(stacked[at, :], qkv_ref[...])
        unit, inverse = norm_parts(x_ref[at, :].astype(F32))
        sums[0] = sums[0] + jnp.sum(grad * unit, 0, keepdims=True)
        sums[1] = sums[1] + jnp.sum(grad, 0, keepdims=True)
        tokens_ref[at, :] = (grad_middle + norm_back(grad, unit, inverse, gain_row(small_ref, experts, 0))).astype(BF)
    grad_small[...] = jnp.concatenate([sums[4][0:experts]] + sums[:4] + [jnp.zeros((4, width), F32)], 0).astype(BF)
    grad_out[...] = contract_rows(attended_ref[...], projected[...]).astype(BF)
    for third in range(3):
        cols = pl.ds(third * width, width)
        grad_qkv[:, cols] = contract_rows(normed_ref[...], stacked[:, cols]).astype(BF)


def back(moe, gates, cot, x, middle, sent, flags, prob, attended, packed, normed, small, qkv, out):
    rows, width = x.shape
    shape = jax.ShapeDtypeStruct
    return pl.pallas_call(
        back_kernel,
        out_shape=(
            shape((rows, width), BF),
            shape((width, 3 * width), BF),
            shape((width, width), BF),
            shape((TALL, width), BF),
        ),
        scratch_shapes=[pltpu.VMEM((rows, 3 * width), BF), pltpu.VMEM((rows, width), BF)],
        compiler_params=pltpu.CompilerParams(vmem_limit_bytes=BIG),
        cost_estimate=pl.CostEstimate(flops=16 * 10**9, bytes_accessed=2 * 10**7, transcendentals=10**6),
        name="back",
    )(moe, gates, cot, x, middle, sent, flags, prob, attended, packed, normed, small, qkv, out)


ORDER = [[('x', 0), ('a', 0), ('n', 3), ('n', 4)], [('x', 1)], [], [('x', 2), ('y', 0), ('x', 3), ('n', 5), ('b', 0), ('x', 4)], [('n', 6), ('a', 1)], [], [('x', 5), ('da', 1)], [('da', 0), ('y', 1), ('dl', 1), ('x', 6), ('b', 1), ('n', 7), ('n', 8)], [('da', 3), ('dl', 0), ('n', 9), ('x', 7)], [('db', 0), ('db', 1)], [('y', 2), ('x', 8), ('da', 2), ('ds', 0), ('y', 3), ('dl', 3), ('y', 4), ('s', 0), ('n', 10), ('c', 0), ('y', 5), ('x', 9), ('dl', 2), ('s', 1), ('y', 6), ('d1', 0), ('db', 3), ('ds', 1), ('n', 11), ('y', 7), ('c', 1), ('db', 2), ('x', 10), ('d2', 0), ('ds', 3), ('ds', 2), ('d1', 1), ('dt', 0), ('x', 11), ('y', 8), ('dt', 3), ('s', 2), ('d1', 2), ('y', 9)], [('d2', 1), ('y', 10), ('s', 3), ('d2', 2), ('y', 11), ('dt', 1), ('dt', 2)]]


class LineScatter:
    def __init__(self, links, place, sums, up, down):
        self.links, self.place = links, place
        self.sums, self.up, self.down = sums, up, down
        self.copies = {}

    def ways(self, step):
        t = self.place.tensor
        return (
            ("up", self.up, t + 3 - step, t <= step, t >= 1, self.place.above),
            ("down", self.down, t - 3 + step, t >= 3 - step, t <= 2, self.place.below),
        )

    def send(self, part, step):
        for name, got, slot, sends, comes, device in self.ways(step):
            slot = jnp.clip(slot, 0, 3)
            if step > 0:
                before = self.copies[name, part, step - 1]

                @pl.when(sends & comes)
                def _():
                    before.wait_recv()
                    ref = self.sums(slot, part)
                    ref[...] = (ref[...].astype(F32) + got(step - 1, part)[...].astype(F32)).astype(BF)

            copy = self.links.copy(self.sums(slot, part), got(step, part), device)
            pl.when(sends)(copy.start)
            self.links.sent.append((sends, copy))
            self.copies[name, part, step] = copy

    def finish(self, part, total):
        total[...] = self.sums(self.place.tensor, part)[...].astype(F32)
        for name, got, slot, sends, comes, device in self.ways(2):
            copy = self.copies[name, part, 2]

            @pl.when(comes)
            def _():
                copy.wait_recv()
                total[...] += got(2, part)[...].astype(F32)


def tail_kernel(
    back_all, gate_all, total_all, grads_in, grads_out, rows_all, flags_all,
    cot_ref, x_ref, middle_ref, prob_ref, attended_ref, packed_ref, normed_ref, small_ref, qkv_ref, out_ref,
    mixed_ref, tokens_ref, dense_ref, grad_small, final_in, final_out, beside_in, beside_out,
    back_sum, back_got, back_up, back_down, gate_sum, gate_got, gate_up, gate_down,
    total_sum, total_got, total_up, total_down, moe, gates, rows_ref, flag_ref, projected, stacked, weights_ref,
    chunks, core_got, across_sent, across_got, line_sum, line_got, side_sum, side_got, line_final,
    own_in, own_out, across_in, across_out, read_in, read_out, half_in, half_out, mine_in, mine_out, both_in, both_out,
    small_sent, small_core, small_half, small_across, small_side, small_beside, small_line_sent, small_line,
    send, recv, local_sem,
):
    place = Place()
    links = Links(send, recv)
    rows, width = x_ref.shape
    experts = TALL // 2
    count = grads_in.shape[0]
    depth = width // 2
    shard, pair, side, tensor = place.shard, place.pair, place.side, place.tensor
    mine = pair * 4 + tensor
    place.greet(True)
    ours, theirs = pl.ds(pair * 4, 4), pl.ds((1 - pair) * 4, 4)

    locals_ = [
        pltpu.make_async_copy(back_all.at[ours], back_sum, local_sem.at[0]),
        pltpu.make_async_copy(gate_all.at[ours], gate_sum, local_sem.at[1]),
        pltpu.make_async_copy(total_all.at[ours], total_sum, local_sem.at[2]),
        pltpu.make_async_copy(rows_all.at[mine], rows_ref, local_sem.at[3]),
        pltpu.make_async_copy(flags_all.at[mine], flag_ref, local_sem.at[4]),
    ]
    for copy in locals_:
        copy.start()
    from_twin = [links.start(gate_all.at[theirs], gate_got, place.twin)]
    for part in range(2):
        at = pl.ds(part * PAD, PAD)
        from_twin.append(links.start(back_all.at[theirs, at, :], back_got.at[:, at, :], place.twin))
    from_twin.append(links.start(total_all.at[theirs], total_got, place.twin))

    here = pl.ds(pl.multiple_of(shard * depth, LANES), depth)
    there = pl.ds(pl.multiple_of((1 - shard) * depth, LANES), depth)
    hidden = grads_in.shape[2]
    tall, wide = depth // 2, hidden // 2
    pieces = []
    for expert in range(1, count):
        for half in range(2):
            at = pl.ds(half * tall, tall)
            pieces.append((
                grads_in.at[expert, pl.ds(pl.multiple_of((1 - shard) * depth + half * tall, TALL), tall), :],
                grads_in.at[expert, pl.ds(pl.multiple_of(shard * depth + half * tall, TALL), tall), :],
                across_in.at[expert - 1, at, :], beside_in.at[expert - 1, at, :],
                final_in.at[pair * count + expert, at, :], own_in.at[at, :], read_in.at[at, :],
            ))
        for half in range(2):
            at = pl.ds(half * wide, wide)
            pieces.append((
                grads_out.at[expert, at, there], grads_out.at[expert, at, here],
                across_out.at[expert - 1, at, :], beside_out.at[expert - 1, at, :],
                final_out.at[pair * count + expert, at, :], own_out.at[at, :], read_out.at[at, :],
            ))
    loads = [pltpu.make_async_copy(piece[1], piece[5], local_sem.at[8 + m]) for m, piece in enumerate(pieces)]
    at_across, at_beside, at_twin, kept = {}, {}, [], []
    started = [0]

    def add(target, source):
        target[...] = (target[...].astype(F32) + source[...].astype(F32)).astype(BF)

    def keep(source, target):
        copy = pltpu.make_async_copy(source, target, local_sem.at[32 + len(kept)])
        copy.start()
        kept.append(copy)

    def send_across():
        m = started[0]
        if m < len(pieces):
            at_across[m] = links.start(pieces[m][0], pieces[m][2], place.across)
            started[0] += 1

    def take_across(m):
        at_across[m].wait_recv()
        loads[m].wait()
        add(pieces[m][2], pieces[m][5])
        at_beside[m] = links.start(pieces[m][2], pieces[m][3], place.beside)
        if m + 4 < len(pieces):
            loads[m + 4].start()

    def take_beside(m):
        at_beside[m].wait_recv()
        load = pltpu.make_async_copy(pieces[m][3], pieces[m][6], local_sem.at[5])
        load.start()
        at_beside[m].wait_send()
        links.skip(at_beside[m])
        load.wait()
        add(pieces[m][2], pieces[m][6])
        at_twin.append(links.start(pieces[m][2], pieces[m][4], place.twin))
        keep(pieces[m][2], pieces[m][4])

    our_half = pl.ds(pl.multiple_of(side * wide, LANES), wide)
    other_half = pl.ds(pl.multiple_of((1 - side) * wide, LANES), wide)
    first = (
        (grads_in.at[0, :, other_half], grads_in.at[0, :, our_half], half_in, mine_in,
         half_in.at[there, :], half_in.at[here, :], both_in,
         final_in.at[pair * count, :, our_half], final_in.at[pair * count, :, other_half]),
        (grads_out.at[0, other_half, :], grads_out.at[0, our_half, :], half_out, mine_out,
         half_out.at[:, there], half_out.at[:, here], both_out,
         final_out.at[pair * count, our_half, :], final_out.at[pair * count, other_half, :]),
    )
    first_loads = [pltpu.make_async_copy(item[1], item[3], local_sem.at[6 + q]) for q, item in enumerate(first)]
    first_beside, first_across, first_back = {}, {}, {}

    def first_send(q):
        first_loads[q].start()
        first_beside[q] = links.start(first[q][0], first[q][2], place.beside)

    def first_sum(q):
        first_beside[q].wait_recv()
        first_loads[q].wait()
        add(first[q][2], first[q][3])
        first_across[q] = links.start(first[q][4], first[q][6], place.across)

    def first_total(q):
        first_across[q].wait_recv()
        add(first[q][6], first[q][5])
        first_back[q] = links.start(first[q][6], first[q][7], place.beside)
        at_twin.append(links.start(first[q][6], first[q][7], place.twin))
        keep(first[q][6], first[q][7])

    def first_share(q):
        first_back[q].wait_recv()
        at_twin.append(links.start(first[q][8], first[q][8], place.twin))

    share = depth // 2
    piece = share // 4
    stage = {}
    early, late = width * 5 // 2, width * 2 // 3
    spans = (
        pl.ds(0, width), pl.ds(width, early - width), pl.ds(early, late), pl.ds(early + late, 4 * width - early - late),
    )

    def fill(k):
        columns = pl.ds(spans[k].start - width, spans[k].size)
        chunks[:, spans[k]] = contract_rows(normed_ref[...], stacked[:, columns]).astype(BF)
        dense_core(k)

    def dense_core(k):
        stage["core", k] = []
        for owner in range(2):
            source = chunks.at[pl.ds(pl.multiple_of(owner * depth + (1 - pair) * share, TALL), share), spans[k]]
            stage["core", k].append(links.start(source, core_got.at[owner, :, spans[k]], place.twin))

    def core_sum(k, owner):
        at = pl.ds(pl.multiple_of(owner * depth + pair * share, TALL), share)
        return chunks[at, spans[k]].astype(F32) + core_got[owner, :, spans[k]].astype(F32)

    def dense_across(k):
        for copy in stage["core", k]:
            copy.wait_recv()
        across_sent[:, spans[k]] = core_sum(k, 1 - shard).astype(BF)
        stage["across", k] = links.start(across_sent.at[:, spans[k]], across_got.at[:, spans[k]], place.across)

    def around(offset):
        return (shard, place.head, lax.rem(tensor + offset, 4))

    def dense_line(k):
        stage["across", k].wait_recv()
        line_sum[:, spans[k]] = (core_sum(k, shard) + across_got[:, spans[k]].astype(F32)).astype(BF)
        stage["line", k] = []
        for offset in (2, 1, 3):
            at = pl.ds(pl.multiple_of(lax.rem(tensor + offset, 4) * piece, TALL), piece)
            stage["line", k].append(links.start(line_sum.at[at, spans[k]], line_got.at[offset - 1, :, spans[k]], around(offset)))

    def dense_beside(k):
        for copy in stage["line", k]:
            copy.wait_recv()
        at = pl.ds(pl.multiple_of(tensor * piece, TALL), piece)
        value = line_sum[at, spans[k]].astype(F32)
        for offset in range(3):
            value = value + line_got[offset, :, spans[k]].astype(F32)
        side_sum[:, spans[k]] = value.astype(BF)
        stage["beside", k] = links.start(side_sum.at[:, spans[k]], side_got.at[:, spans[k]], place.beside)

    def dense_spread(k):
        stage["beside", k].wait_recv()
        line_final[:, spans[k]] = (side_sum[:, spans[k]].astype(F32) + side_got[:, spans[k]].astype(F32)).astype(BF)
        target = dense_ref.at[
            pl.ds(pl.multiple_of(pair * share + tensor * piece, TALL), piece), spans[k]
        ]
        stage["keep", k] = pltpu.make_async_copy(line_final.at[:, spans[k]], target, local_sem.at[24 + k])
        stage["keep", k].start()
        if k < 3:
            dense_line_back.start(k, 0)
        else:
            stage["spread", k] = [links.start(line_final.at[:, spans[k]], target, around(offset)) for offset in (2, 1, 3)]

    def dense_hop(k, step):
        dense_line_back.wait(k, step)
        dense_line_back.start(k, step + 1)

    dense_line_back = LineGather(
        links, place,
        lambda slot, k: dense_ref.at[
            pl.ds(pl.multiple_of(pair * share + slot * piece, TALL), piece), spans[k]
        ],
        lambda k: line_final.at[:, spans[k]], 3,
    )

    def dense_twin(k):
        if k < 3:
            dense_line_back.wait(k, 2)
        else:
            for copy in stage["spread", k]:
                copy.wait_recv()
        stage["keep", k].wait()
        block = dense_ref.at[pl.ds(pl.multiple_of(pair * share, TALL), share), spans[k]]
        stage["twin", k] = links.start(block, block, place.twin)

    def small_core_stage():
        small_core_copy.wait_recv()
        other = pl.ds(pl.multiple_of((1 - shard) * depth, LANES), depth)
        small_half[...] = small_sent[:, other] + small_core[:, other]
        stage["small", 1] = links.start(small_half, small_across, place.across)

    def small_across_stage():
        stage["small", 1].wait_recv()
        own = pl.ds(pl.multiple_of(shard * depth, LANES), depth)
        small_side[...] = small_sent[:, own] + small_core[:, own] + small_across[...]
        stage["small", 2] = links.start(small_side, small_beside, place.beside)

    def small_beside_stage():
        stage["small", 2].wait_recv()
        small_line_sent[...] = small_side[...] + small_beside[...]
        stage["small", 3] = [
            links.start(small_line_sent, small_line.at[offset - 1], around(offset)) for offset in (2, 1, 3)
        ]

    def small_line_stage():
        for copy in stage["small", 3]:
            copy.wait_recv()
        grad_small[...] = small_line_sent[...] + small_line[0] + small_line[1] + small_line[2]

    def slots(array):
        def view(slot, part):
            return array.at[slot, pl.ds(part * PAD, PAD), :]

        return view

    back_line = LineScatter(links, place, slots(back_sum), slots(back_up), slots(back_down))
    total_line = LineScatter(links, place, slots(total_sum), slots(total_up), slots(total_down))
    gate_line = LineScatter(
        links, place, lambda slot, part: gate_sum.at[slot], lambda step, part: gate_up.at[step],
        lambda step, part: gate_down.at[step],
    )

    steps = {
        "d1": lambda index: dense_hop(index, 0), "d2": lambda index: dense_hop(index, 1),
        "n": lambda index: send_across(), "x": take_across, "y": take_beside, "a": first_sum, "b": first_total, "c": first_share,
        "da": dense_across, "dl": dense_line, "db": dense_beside, "ds": dense_spread, "dt": dense_twin,
        "s": lambda index: (small_core_stage, small_across_stage, small_beside_stage, small_line_stage)[index](),
    }

    def go(slot):
        for name, index in ORDER[slot]:
            steps[name](index)

    def save_probs(double, image):
        at = pl.ds(image * PAD, PAD)

        def take(index, value):
            weights_ref[(image * 2 + double) * 6 + index] = value.astype(BF)

        back_probs(at, double, packed_ref, take)

    def use_heads(double, image):
        at = pl.ds(image * PAD, PAD)
        back_heads(
            at, double, projected[at, :], packed_ref, out_ref, stacked,
            lambda index: weights_ref[(image * 2 + double) * 6 + index],
        )

    def middle_of(image):
        at = pl.ds(image * PAD, PAD)
        cols = slice(image * PAD, (image + 1) * PAD)
        back_line.finish(image, moe.at[at, :])
        grad = back_middle(
            at, moe[at, :], gates[:, cols], cot_ref[at, :].astype(F32), middle_ref[at, :], rows_ref[at, :],
            prob_ref[:, cols], flag_ref[:, cols].astype(F32), small_ref, sums,
        )
        moe[at, :] = grad
        projected[at, :] = grad.astype(BF)

    first_send(0)
    for _ in range(3):
        send_across()
    first_send(1)
    for m in range(4):
        loads[m].start()
    locals_[1].wait()
    from_twin[0].wait_recv()
    add(gate_sum, gate_got)
    gate_line.send(0, 0)
    locals_[0].wait()
    for part in range(2):
        from_twin[1 + part].wait_recv()
        at = pl.ds(part * PAD, PAD)
        for slot in range(4):
            add(back_sum.at[slot, at, :], back_got.at[slot, at, :])
        back_line.send(part, 0)
    locals_[2].wait()
    from_twin[3].wait_recv()
    for slot in range(4):
        add(total_sum.at[slot], total_got.at[slot])
    save_probs(0, 0)
    go(0)
    gate_line.send(0, 1)
    back_line.send(0, 1)
    save_probs(0, 1)
    back_line.send(1, 1)
    go(1)
    save_probs(1, 0)
    gate_line.send(0, 2)
    back_line.send(0, 2)
    go(2)
    back_line.send(1, 2)
    save_probs(1, 1)
    go(3)
    for part in range(2):
        total_line.send(part, 0)
    gate_line.finish(0, gates)
    locals_[3].wait()
    locals_[4].wait()
    sums = [jnp.zeros((1, width), F32) for _ in range(4)] + [jnp.zeros((TALL, width), F32)]
    middle_of(0)
    use_heads(0, 0)
    go(4)
    middle_of(1)
    chunks[:, spans[0]] = contract_rows(attended_ref[...], projected[...]).astype(BF)
    dense_core(0)
    go(5)
    use_heads(0, 1)
    fill(1)
    go(6)
    for part in range(2):
        total_line.send(part, 1)
    use_heads(1, 0)
    go(7)
    use_heads(1, 1)
    for k in (2, 3):
        fill(k)
    go(8)
    for part in range(2):
        total_line.send(part, 2)
    go(9)
    joined = []
    for image in range(2):
        at = pl.ds(image * PAD, PAD)
        grad = contract_cols(stacked[at, :], qkv_ref[...])
        unit, inverse = norm_parts(x_ref[at, :].astype(F32))
        sums[0] = sums[0] + jnp.sum(grad * unit, 0, keepdims=True)
        sums[1] = sums[1] + jnp.sum(grad, 0, keepdims=True)
        grad = moe[at, :] + norm_back(grad, unit, inverse, gain_row(small_ref, experts, 0))
        joined.append(grad[:SEQ])
    tokens_ref[...] = jnp.concatenate(joined, 0).astype(BF)
    small_sent[...] = jnp.concatenate([sums[4][0:experts]] + sums[:4] + [jnp.zeros((4, width), F32)], 0)
    small_core_copy = links.start(small_sent, small_core, place.twin)
    go(10)
    joined = []
    for part in range(2):
        at = pl.ds(part * PAD, PAD)
        total_line.finish(part, moe.at[at, :])
        joined.append((middle_ref[at, :] + moe[at, :])[:SEQ])
    mixed_ref[...] = jnp.concatenate(joined, 0).astype(BF)
    go(11)
    for copy in at_twin + [stage["twin", k] for k in range(4)]:
        copy.wait_recv()
    for copy in kept:
        copy.wait()
    links.finish()


def tail(back_all, gate_all, total_all, grads_in, grads_out, rows_all, flags_all, cot, x, middle, prob, attended, packed, normed, small, qkv, out):
    rows, width = x.shape
    count, _, hidden = grads_in.shape
    depth = width // 2
    shape = jax.ShapeDtypeStruct
    anywhere = pl.BlockSpec(memory_space=pl.ANY)
    vmem = pl.BlockSpec(memory_space=pltpu.VMEM)
    share, piece = depth // 2, depth // 8

    def scatter_buffers(tall, wide):
        return [pltpu.VMEM((4, tall, wide), BF)] * 2 + [pltpu.VMEM((3, tall, wide), BF)] * 2

    return pl.pallas_call(
        tail_kernel,
        out_shape=(
            shape((rows // PAD * SEQ, width), BF),
            shape((rows // PAD * SEQ, width), BF),
            shape((depth, 4 * width), BF),
            shape((TALL, depth), F32),
            shape((2 * count, depth, hidden), BF),
            shape((2 * count, hidden, depth), BF),
            shape((count - 1, depth, hidden), BF),
            shape((count - 1, hidden, depth), BF),
        ),
        in_specs=[anywhere] * 7 + [vmem] * 10,
        out_specs=(vmem,) * 4 + (anywhere,) * 4,
        scratch_shapes=scatter_buffers(rows, width)
        + scatter_buffers(TALL, rows)
        + scatter_buffers(rows, width)
        + [
            pltpu.VMEM((rows, width), F32),
            pltpu.VMEM((TALL, rows), F32),
            pltpu.VMEM((rows, width), BF),
            pltpu.VMEM((TALL, rows), BF),
            pltpu.VMEM((rows, width), BF),
            pltpu.VMEM((rows, 3 * width), BF),
            pltpu.VMEM((24, PAD, PAD), BF),
            pltpu.VMEM((width, 4 * width), BF),
            pltpu.VMEM((2, share, 4 * width), BF),
            pltpu.VMEM((share, 4 * width), BF),
            pltpu.VMEM((share, 4 * width), BF),
            pltpu.VMEM((share, 4 * width), BF),
            pltpu.VMEM((3, piece, 4 * width), BF),
            pltpu.VMEM((piece, 4 * width), BF),
            pltpu.VMEM((piece, 4 * width), BF),
            pltpu.VMEM((piece, 4 * width), BF),
        ]
        + [pltpu.VMEM((depth, hidden), BF), pltpu.VMEM((hidden, depth), BF)]
        + [pltpu.VMEM((count - 1, depth, hidden), BF), pltpu.VMEM((count - 1, hidden, depth), BF)]
        + [pltpu.VMEM((depth, hidden), BF), pltpu.VMEM((hidden, depth), BF)]
        + [pltpu.VMEM((width, hidden // 2), BF), pltpu.VMEM((hidden // 2, width), BF)] * 2
        + [pltpu.VMEM((depth, hidden // 2), BF), pltpu.VMEM((hidden // 2, depth), BF)]
        + [
            pltpu.VMEM((TALL, width), F32),
            pltpu.VMEM((TALL, width), F32),
            pltpu.VMEM((TALL, depth), F32),
            pltpu.VMEM((TALL, depth), F32),
            pltpu.VMEM((TALL, depth), F32),
            pltpu.VMEM((TALL, depth), F32),
            pltpu.VMEM((TALL, depth), F32),
            pltpu.VMEM((3, TALL, depth), F32),
            pltpu.SemaphoreType.DMA((192,)),
            pltpu.SemaphoreType.DMA((192,)),
            pltpu.SemaphoreType.DMA((48,)),
        ],
        compiler_params=pltpu.CompilerParams(vmem_limit_bytes=BIG + 3 * 512 * 1024, collective_id=2, has_side_effects=True),
        cost_estimate=pl.CostEstimate(flops=16 * 10**9, bytes_accessed=5 * 10**7, transcendentals=10**6),
        name="tail",
    )(back_all, gate_all, total_all, grads_in, grads_out, rows_all, flags_all, cot, x, middle, prob, attended, packed, normed, small, qkv, out)


class Comm:
    def __init__(self):
        self.sizes = tuple(lax.axis_size(axis) for axis in AXES)
        self.shard = lax.axis_index("shard")
        self.head = lax.axis_index("heads")
        self.tensor = lax.axis_index("tensor")
        self.pair = self.head % 2

    def move(self, value, step):
        shards, heads, tensors = self.sizes
        pairs = []
        for s in range(shards):
            for h in range(heads):
                for t in range(tensors):
                    to = step(s, h, t)
                    if 0 <= to[2] < tensors:
                        source = (s * heads + h) * tensors + t
                        pairs.append((source, (to[0] * heads + to[1]) * tensors + to[2]))
        return lax.ppermute(value, AXES, pairs)

    def over_core(self, value):
        return self.move(value, lambda s, h, t: (s, h ^ 1, t))

    def over_heads(self, value):
        return self.move(value, lambda s, h, t: (s, (h + 2) % 4, t))

    def over_shard(self, value):
        return self.move(value, lambda s, h, t: (1 - s, h, t))

    def up(self, value):
        return self.move(value, lambda s, h, t: (s, h, t + 1))

    def down(self, value):
        return self.move(value, lambda s, h, t: (s, h, t - 1))

    def halves(self, value, index, axis):
        size = value.shape[axis] // 2
        mine = lax.dynamic_slice_in_dim(value, index * size, size, axis)
        other = lax.dynamic_slice_in_dim(value, (1 - index) * size, size, axis)
        return mine, other

    def join(self, mine, other, index, axis):
        first = jnp.where(index == 0, mine, other)
        second = jnp.where(index == 0, other, mine)
        return jnp.concatenate((first, second), axis)

    def gather_shard(self, value, axis):
        if self.sizes[0] != 2:
            return lax.all_gather(value, "shard", axis=axis, tiled=True)
        return self.join(value, self.over_shard(value), self.shard, axis)

    def gather_shard_split(self, value, axis, cut):
        if self.sizes[0] != 2:
            return lax.all_gather(value, "shard", axis=axis, tiled=True)
        mine, _ = self.halves(value, self.pair, cut)
        got = self.over_shard(mine)
        both = self.join(got, self.over_core(got), self.pair, cut)
        return self.join(value, both, self.shard, axis)

    def scatter_shard(self, value, axis):
        if self.sizes[0] != 2:
            return lax.psum_scatter(value.astype(BF), "shard", scatter_dimension=axis, tiled=True).astype(F32)
        mine, other = self.halves(value, self.shard, axis)
        return mine.astype(F32) + self.over_shard(other.astype(BF)).astype(F32)

    def scatter_core(self, value, axis):
        mine, other = self.halves(value, self.pair, axis)
        return mine.astype(F32) + self.over_core(other.astype(BF)).astype(F32)

    def scatter_heads(self, value, axis):
        mine, other = self.halves(value, self.head // 2, axis)
        return mine.astype(F32) + self.over_heads(other.astype(BF)).astype(F32)

    def line_gather(self, value):
        ups, downs = [value], [value]
        for _ in range(3):
            ups.append(self.up(ups[-1]))
            downs.append(self.down(downs[-1]))
        out = [value]
        for back in (1, 2, 3):
            out.append(jnp.where(self.tensor >= back, ups[back], downs[4 - back]))
        return out

    def line_scatter(self, parts):
        high, low = parts[1].astype(BF), parts[3].astype(BF)
        high = (parts[2].astype(F32) + self.up(high).astype(F32)).astype(BF)
        low = (parts[2].astype(F32) + self.down(low).astype(F32)).astype(BF)
        high = (parts[3].astype(F32) + self.up(high).astype(F32)).astype(BF)
        low = (parts[1].astype(F32) + self.down(low).astype(F32)).astype(BF)
        return parts[0].astype(F32) + self.up(high).astype(F32) + self.down(low).astype(F32)

    def join_slots(self, values):
        own = jnp.zeros((4,) + values[0].shape, values[0].dtype)
        for back, value in enumerate(values):
            own = lax.dynamic_update_index_in_dim(own, value, (self.tensor + 4 - back) % 4, 0)
        return self.join(own, self.over_core(own), self.pair, 0)

    def collect(self, value):
        mine, other = self.halves(value, self.pair, 0)
        mine = mine.astype(F32) + self.over_core(other).astype(F32)
        return self.line_scatter(
            [lax.dynamic_index_in_dim(mine, (self.tensor + 4 - k) % 4, 0, False) for k in range(4)]
        )


def local(
    tokens, ln1_gain, ln1_bias, qkv_weight, out_weight, ln2_gain, ln2_bias, router_weight,
    expert_in, expert_out, route_noise, expert_ids, cotangent,
):
    comm = Comm()
    rows, width = tokens.shape
    experts = expert_in.shape[0]
    images = rows // SEQ
    half = experts // 2
    padded = images * PAD

    def pad(value):
        value = value.reshape(images, SEQ, value.shape[1])
        return jnp.pad(value, ((0, 0), (0, PAD - SEQ), (0, 0))).reshape(padded, value.shape[2])

    def pad_turned(value, tall, fill):
        value = value.reshape(images, SEQ, value.shape[1]).transpose(2, 0, 1)
        value = jnp.pad(value, ((0, tall - value.shape[0]), (0, 0), (0, PAD - SEQ)), constant_values=fill)
        return value.reshape(tall, padded)

    def unpad(value):
        return value.reshape(images, PAD, value.shape[1])[:, :SEQ].reshape(rows, value.shape[1])

    vectors = jnp.concatenate((ln1_gain, ln1_bias, ln2_gain, ln2_bias, jnp.zeros_like(jnp.tile(ln1_gain, 4))))
    vectors = lax.optimization_barrier(vectors).reshape(8, ln1_gain.shape[0])
    small = jnp.concatenate((router_weight.T, vectors), 0)
    noise, ids = pad_turned(route_noise, TALL, 0), pad_turned(expert_ids, 8, -1)
    place = jnp.stack((comm.pair, comm.shard if comm.sizes[0] == 2 else 0 * comm.shard)).astype(jnp.int32)
    if comm.sizes[0] == 2:
        (
            small, proj_qkv, proj_out, normed_a, packed, attended, middle, prob,
            x, cot, rows_all, flags_all, grad_rows, got_in, got_out,
        ) = head(tokens, cotangent, small, qkv_weight, out_weight, expert_in, expert_out, noise, ids)
        weights = (expert_in, got_in, expert_out, got_out)
    else:
        cot, x = pad(cotangent), pad(tokens)
        small = lax.all_gather(small, "shard", axis=1, tiled=True)
        small = small.reshape(TALL, 2, width // 2).transpose(1, 0, 2)
        proj_qkv = lax.all_gather(qkv_weight, "shard", axis=0, tiled=True)
        proj_out = lax.all_gather(out_weight, "shard", axis=0, tiled=True)
        inner = lax.all_gather(lax.dynamic_slice_in_dim(expert_in, comm.pair * half, half, 0), "shard", axis=1, tiled=True)
        outer = lax.all_gather(lax.dynamic_slice_in_dim(expert_out, comm.pair * half, half, 0), "shard", axis=2, tiled=True)
        cut = width // 2
        weights = (
            jnp.concatenate((inner[:, :cut], inner[:, :cut]), 0), inner[:, cut:],
            jnp.concatenate((outer[:, :, :cut], outer[:, :, :cut]), 0), outer[:, :, cut:],
        )
        normed_a, packed, attended, middle, sent, flags, prob = front(x, small, proj_qkv, proj_out, noise, ids)

        def gather(value):
            return comm.join_slots(comm.line_gather(value))

        grad_rows, rows_all, flags_all = gather(cot), gather(sent), gather(flags)
    total, back_all, gate_all, grads_in, grads_out = expert_pass(place, rows_all, flags_all, grad_rows, *weights)

    if comm.sizes[0] == 2:
        mixed, grad_tokens, dense, grad_small, grad_in, grad_outer, _, _ = tail(
            back_all, gate_all, total, grads_in, grads_out, rows_all, flags_all,
            cot, x, middle, prob, attended, packed, normed_a, small, proj_qkv, proj_out,
        )
        dense = dense.astype(F32)
        return (
            mixed,
            grad_tokens,
            grad_small[experts],
            grad_small[experts + 1],
            dense[:, width:],
            dense[:, :width],
            grad_small[experts + 2],
            grad_small[experts + 3],
            grad_small[:experts].T,
            grad_in.astype(F32),
            grad_outer.astype(F32),
        )

    def reduce_expert(grad, axis, other):
        part = comm.scatter_shard(grad, axis)
        part = comm.scatter_heads(part, other).astype(BF)
        return comm.join(part, comm.over_heads(part), comm.head // 2, other)

    inner_grads = [reduce_expert(grads_in[e], 0, 1) for e in range(half)]
    outer_grads = [reduce_expert(grads_out[e], 1, 0) for e in range(half)]

    moe_grad = comm.collect(back_all)
    gate_grad = comm.collect(gate_all)
    moe = comm.collect(total)
    mixed = (unpad(middle) + unpad(moe)).astype(BF)
    grad_tokens, grad_qkv, grad_out, grad_small = back(
        moe_grad, gate_grad, cot, x, middle, sent, flags, prob, attended, packed, normed_a, small, proj_qkv, proj_out
    )
    grad_tokens = unpad(grad_tokens)

    grad_small = jnp.pad(grad_small.T, ((0, 0), (0, 128 - TALL)))
    shares = jnp.concatenate((grad_qkv, grad_out, grad_small, jnp.zeros_like(grad_small)), 1)
    shares = comm.scatter_core(shares, 1)
    shares = comm.scatter_shard(shares, 0)
    shares = comm.scatter_heads(shares, 1)
    cut = shares.shape[0] // 4
    rolled = [
        lax.dynamic_slice_in_dim(shares, ((comm.tensor + 4 - k) % 4) * cut, cut, 0) for k in range(4)
    ]
    summed = comm.line_scatter(rolled).astype(BF)
    pieces = comm.line_gather(summed)
    whole = jnp.zeros(shares.shape, BF)
    for k in range(4):
        whole = lax.dynamic_update_slice_in_dim(whole, pieces[k], ((comm.tensor + 4 - k) % 4) * cut, 0)
    whole = comm.join(whole, comm.over_heads(whole), comm.head // 2, 1)
    whole = comm.join(whole, comm.over_core(whole), comm.pair, 1).astype(F32)
    small = whole[:, 4 * width : 4 * width + 128]

    grad_in, grad_outer = jnp.stack(inner_grads, 0), jnp.stack(outer_grads, 0)
    grad_in = comm.join(grad_in, comm.over_core(grad_in), comm.pair, 0).astype(F32)
    grad_outer = comm.join(grad_outer, comm.over_core(grad_outer), comm.pair, 0).astype(F32)
    return (
        mixed,
        grad_tokens,
        small[:, experts],
        small[:, experts + 1],
        whole[:, : 3 * width],
        whole[:, 3 * width : 4 * width],
        small[:, experts + 2],
        small[:, experts + 3],
        small[:, :experts],
        grad_in,
        grad_outer,
    )


def solution(mesh):
    split = P(AXES, None)
    vector, matrix = P("shard"), P("shard", None)
    inner, outer = P(None, "shard", "tensor"), P(None, "tensor", "shard")
    return jax.shard_map(
        local,
        mesh=mesh,
        in_specs=(
            split, vector, vector, matrix, matrix, vector, vector, matrix, inner, outer, split, split, split,
        ),
        out_specs=(
            split, split, vector, vector, matrix, matrix, vector, vector, matrix, inner, outer,
        ),
        check_vma=False,
    )
```
